32 devices in a mesh: groups: 2 (over y), mx: 4 (over z), my: 4 (over x, core).
Axes of the slice: x: 2, y: 2, z: 4, core: 2. Of those that a mesh axis runs over, the one named last changes fastest.
Arguments:
- tokens: bfloat16 [2048, 8192], P(('groups', 'mx'), 'my'), parts along dimension 0, may hold values from -6 to 6
- w_gate: bfloat16 [8192, 26624], P('my', 'mx'), may hold values from -0.0625 to 0.0625
- w_up: bfloat16 [8192, 26624], P('my', 'mx'), may hold values from -0.0625 to 0.0625
- adapter_in: bfloat16 [8, 8192, 32], P(None, 'my'), may hold values from -0.0625 to 0.0625
- adapter_out: bfloat16 [8, 2, 16, 26624], P(None, None, None, 'mx'), may hold values from -0.75 to 0.75
- magnitude: float32 [8, 2, 26624], P(None, None, 'mx'), may hold values from 0.5 to 2
- partial_norms: float32 [4, 8, 2, 26624], P('my', None, None, 'mx'), may hold values from 0.06 to 2.8125, as said below
- block_tenant: int32 [16], P('groups'), parts along dimension 0, may hold values from 0 to 7
- block_rows: int32 [16], P('groups'), parts along dimension 0, may hold values from 1 to 128, 768 in all
Outputs:
- hidden: bfloat16 [2048, 26624], P('groups', ('mx', 'my')), parts along dimension 0
The draws below stay inside these ranges and needn't reach their ends.
There are 2 independent parts, one for each index of `groups`. The reference program is written for one: setup_inputs(seed, part) draws one part's arguments, and reference() takes and returns one part's arrays. A program takes and returns all parts, laid end to end along the dimension named above; an argument that names none is the same for every part. Nothing has to cross between parts.
Inputs may be any that keep to these rules, and one draw needn't show every extreme that they name: `partial_norms`: positive.
All inputs are finite; a program needn't handle non-finite values.
Results may differ from the reference program's by a relative error of at most 0.0038.
Values may be sent and summed in bfloat16 or wider, within the bound.
No kernel may reach another device: no remote copies, remote signals or barrier semaphores. Data moves between devices by JAX's collectives and lax.ppermute only.
A program may use at most 384 MiB of HBM per device.

```python
import math
import jax
import jax.numpy as jnp
import numpy as np
from jax import lax

D = 8192
FF = 26624
RANK = 16
BLOCK_ROWS = 128
BLOCKS = 8
TEN = 8
ROWS = 1024
NORM_SHARDS = 4


def draw_partial_norms(key, part):
    key = jax.random.fold_in(key, 7)
    key_column, key_element = jax.random.split(key)
    column_scale = jnp.exp(jax.random.uniform(key_column, (TEN, 2, FF), jnp.float32, jnp.log(0.3), jnp.log(3.0)))
    element_scale = jnp.exp(jax.random.uniform(key_element, (NORM_SHARDS, TEN, 2, FF), jnp.float32, jnp.log(0.8), jnp.log(1.25)))
    rise_factor = 1.0 + 2.0 * jnp.arange(NORM_SHARDS, dtype=jnp.float32) / max(NORM_SHARDS - 1, 1)
    values = rise_factor[:, None, None, None] * column_scale[None] * element_scale / NORM_SHARDS
    return values.astype(jnp.float32)


def with_ends(drawn, own_key, least, largest):
    shape = drawn.shape
    place = [jax.random.randint(jax.random.fold_in(own_key, axis), (), 0, shape[axis]) for axis in range(len(shape))]
    drawn = drawn.at[tuple(place)].set(least)
    longest = shape.index(max(shape))
    place[longest] = (place[longest] + 1) % shape[longest]
    return drawn.at[tuple(place)].set(largest)


def block_scale(rng, dims, cuts, smallest, top_value):
    gain = 1.0
    for dim, blocks in cuts:
        heights = jax.random.uniform(jax.random.fold_in(jax.random.fold_in(rng, 6), dim), (blocks,), jnp.float32, smallest / len(cuts), top_value / len(cuts))
        gain = gain * jnp.repeat(jnp.exp(heights), dims[dim] // blocks).reshape((-1,) + (1,) * (len(dims) - 1 - dim))
    return gain


def length_profile(count, total, most, lean):
    weights = [(1 << 20) // math.isqrt(standing ** lean) + 1 for standing in range(2, count + 1)]
    rest, given = total - most - (count - 1), [1] * (count - 1)
    while rest > 0:
        candidates = [i for i in range(count - 1) if given[i] < most]
        pool, budget = sum([weights[i] for i in candidates]), rest
        for i in candidates:
            more = min(most - given[i], max(1, budget * weights[i] // pool), rest)
            given[i] = given[i] + more
            rest = rest - more
    return np.array([most] + given)


def ragged(key, number_of, total, most, lean):
    if number_of == 2:
        one = jax.random.randint(key, (), max(1, total - most), min(most, total - 1) + 1)
        return jnp.stack([one, total - one])
    sizes = jnp.asarray(length_profile(number_of, total, most, lean), jnp.int32)
    twos = (number_of - 1) // 2
    donor, receiver = sizes[1:1 + 2 * twos:2], sizes[2:2 + 2 * twos:2]
    room = jnp.minimum(donor - 1, most - receiver)
    shifted = jax.random.randint(jax.random.fold_in(key, 1), (twos,), 0, 1 << 20) % (room + 1)
    sizes = sizes.at[1:1 + 2 * twos:2].set(donor - shifted).at[2:2 + 2 * twos:2].set(receiver + shifted)
    return sizes[jax.random.permutation(jax.random.fold_in(key, 2), number_of)]


def normal_values(own_key, dims, scale, bound, shards=(), kind=jnp.bfloat16):
    drawn = scale * jax.random.normal(own_key, dims, jnp.float32)
    if shards:
        drawn = drawn * block_scale(own_key, dims, shards, -0.22, 0.18)
    return jnp.clip(drawn, -bound, bound).astype(kind)


def setup_inputs(seed: int = 0, part: int = 0) -> dict:
    seeds = jax.random.split(jax.random.key(seed), 10)
    part_splits = jax.random.split(jax.random.fold_in(seeds[9], part), 10)
    return {
        "tokens": normal_values(part_splits[0], (ROWS, D), 1.0, 6.0, ((0, 4), (1, 4))),
        "w_gate": normal_values(seeds[1], (D, FF), D ** -0.5, 0.0625, ((0, 4), (1, 4))),
        "w_up": normal_values(seeds[2], (D, FF), D ** -0.5, 0.0625, ((0, 4), (1, 4))),
        "adapter_in": normal_values(seeds[3], (TEN, D, 2 * RANK), D ** -0.5, 0.0625, ((1, 4),)),
        "adapter_out": normal_values(seeds[4], (TEN, 2, RANK, FF), 0.125, 0.75, ((3, 4),)),
        "magnitude": jnp.clip(jnp.exp(math.log(2.0) - 1.3862944 * jax.random.uniform(seeds[5], (TEN, 2, FF), jnp.float32) ** block_scale(seeds[5], (TEN, 2, FF), ((2, 4),), -0.2, 0.2)), 0.5, 2.0),
        "partial_norms": draw_partial_norms(jax.random.fold_in(seeds[9], 71), part),
        "block_tenant": with_ends(jax.random.randint(part_splits[7], (BLOCKS,), 0, TEN), jax.random.fold_in(part_splits[7], 1), 0, TEN - 1).astype(jnp.int32),
        "block_rows": ragged(part_splits[8], BLOCKS, BLOCKS * 96, BLOCK_ROWS, 1).astype(jnp.int32),
    }


def reference(tokens, w_gate, w_up, adapter_in, adapter_out, magnitude, partial_norms, block_tenant, block_rows):
    base_gate = jnp.dot(tokens, w_gate, preferred_element_type=jnp.float32)
    base_up = jnp.dot(tokens, w_up, preferred_element_type=jnp.float32)
    block_grouped = tokens.reshape(BLOCKS, BLOCK_ROWS, D).astype(jnp.float32)
    tenant_tables = adapter_in[block_tenant].astype(jnp.float32)
    reduced_rank_factor = jnp.einsum('jgi,jio->jgo', block_grouped, tenant_tables).astype(jnp.bfloat16)
    low_pair = reduced_rank_factor.reshape(BLOCKS, BLOCK_ROWS, 2, RANK).astype(jnp.float32)
    col_scale = magnitude * lax.rsqrt(lax.optimization_barrier(jnp.sum(partial_norms, axis=0)))
    chosen_scale = col_scale[block_tenant]
    chosen_out = adapter_out[block_tenant].astype(jnp.float32)
    adapted_gate = jnp.einsum('bkr,brf->bkf', low_pair[:, :, 0], chosen_out[:, 0])
    adapted_up = jnp.einsum('bkr,brf->bkf', low_pair[:, :, 1], chosen_out[:, 1])
    pre_gate = (base_gate.reshape(BLOCKS, BLOCK_ROWS, FF) + adapted_gate) * chosen_scale[:, 0][:, None, :]
    up_preactivation = (base_up.reshape(BLOCKS, BLOCK_ROWS, FF) + adapted_up) * chosen_scale[:, 1][:, None, :]
    hidden = jax.nn.silu(pre_gate) * up_preactivation
    positions = jnp.arange(BLOCK_ROWS, dtype=jnp.int32)
    live_mask = positions[None, :] < block_rows[:, None]
    hidden = jnp.where(live_mask[:, :, None], hidden, jnp.zeros_like(hidden))
    return hidden.reshape(BLOCKS * BLOCK_ROWS, FF).astype(jnp.bfloat16)
```

```python
import functools
import math

import jax
import jax.numpy as jnp
from jax import lax
from jax.experimental import pallas as pl
from jax.experimental.pallas import tpu as pltpu
from jax.sharding import PartitionSpec as P

RANK = 16
BLOCK_ROWS = 128
LIVE_ROWS = 768
VMEM_LIMIT = 56 * 1024 * 1024

SLOTS = (
    (0, 0), (0, 1),
    (-1, 0), (1, 0), (-1, 1), (1, 1),
    (-2, 0), (2, 0), (-2, 1), (2, 1),
    (-3, 0), (3, 0), (-3, 1), (3, 1),
)
CHUNKS = ((0, 128, 4), (128, 256, 8), (384, 384, 14))


def slot_table(ids, rows, tenants, mx_count):
    place = ids[0]
    start = jnp.int32(0)
    table = []
    for distance, half in SLOTS:
        source = place + distance
        valid = (source >= 0) & (source < mx_count)
        block = jnp.clip(source, 0, mx_count - 1) * 2 + half
        count = jnp.where(valid, rows[block], 0)
        table.append((start, count, tenants[block], jnp.where(valid, block, -1)))
        start = start + count
    return table


def row_tenants(table, first, shape):
    row = lax.broadcasted_iota(jnp.int32, shape, 0) + first
    tenant = jnp.full(shape, -1, jnp.int32)
    for start, count, owner, _ in table:
        tenant = jnp.where((row >= start) & (row < start + count), owner, tenant)
    return tenant


def pack_kernel(mx_count, first, rows_out, slots, ids, rows, tenants, *refs):
    token_refs = refs[:slots]
    down_ref = refs[slots]
    x_ref, low_ref, acc = refs[-3:]
    table = slot_table(ids, rows, tenants, mx_count)
    acc[...] = jnp.zeros_like(acc)
    for slot in range(slots):
        start, count, _, _ = table[slot]

        @pl.when((count > 0) & (start < first + rows_out) & (start + count > first))
        def _():
            target = lax.broadcasted_iota(jnp.int32, (rows_out, BLOCK_ROWS), 0) + first
            position = lax.broadcasted_iota(jnp.int32, (rows_out, BLOCK_ROWS), 1)
            chosen = (position < count) & (target == position + start)
            acc[...] += jnp.dot(
                chosen.astype(jnp.bfloat16), token_refs[slot][...], preferred_element_type=jnp.float32
            )

    x = acc[...].astype(jnp.bfloat16)
    x_ref[...] = x
    for tile in range(rows_out // BLOCK_ROWS):
        low = jnp.dot(
            x[tile * BLOCK_ROWS:(tile + 1) * BLOCK_ROWS], down_ref[...], preferred_element_type=jnp.float32
        )
        tenant = row_tenants(table, first + tile * BLOCK_ROWS, low.shape)
        lane = lax.broadcasted_iota(jnp.int32, low.shape, 1)
        low = jnp.where(lane // (2 * RANK) == tenant, low, 0.0)
        low = low[:, :128] + low[:, 128:]
        low = low + pltpu.roll(low, 64, 1)
        low = low + pltpu.roll(low, 32, 1)
        group = lax.broadcasted_iota(jnp.int32, (32, 128), 1) // 32
        packed = jnp.where(group == 0, low[0:32], 0.0)
        for part in range(1, 4):
            packed = jnp.where(group == part, low[part * 32:(part + 1) * 32], packed)
        low_ref[tile * 32:(tile + 1) * 32, :] = packed


def pack_rows(mx_count, first, rows_out, scalars, blocks, down, after):
    width = blocks[0].shape[1]
    slots = len(blocks)
    in_specs = [pl.BlockSpec((BLOCK_ROWS, width), lambda i, *_: (0, 0))] * slots
    in_specs.append(pl.BlockSpec(down.shape, lambda i, *_: (0, 0)))
    in_specs += [pl.BlockSpec(memory_space=pl.ANY)] * len(after)
    return pl.pallas_call(
        functools.partial(pack_kernel, mx_count, first, rows_out, slots),
        out_shape=(
            jax.ShapeDtypeStruct((rows_out, width), jnp.bfloat16),
            jax.ShapeDtypeStruct((rows_out // 4, 128), jnp.float32),
        ),
        grid_spec=pltpu.PrefetchScalarGridSpec(
            num_scalar_prefetch=3,
            grid=(1,),
            in_specs=in_specs,
            out_specs=(
                pl.BlockSpec((rows_out, width), lambda i, *_: (0, 0)),
                pl.BlockSpec((rows_out // 4, 128), lambda i, *_: (0, 0)),
            ),
            scratch_shapes=[pltpu.VMEM((rows_out, width), jnp.float32)],
        ),
        compiler_params=pltpu.CompilerParams(vmem_limit_bytes=VMEM_LIMIT),
        cost_estimate=pl.CostEstimate(
            flops=2 * rows_out * width * (256 + 512),
            bytes_accessed=slots * BLOCK_ROWS * width * 2 + rows_out * width * 2,
            transcendentals=0,
        ),
        name="pack_rows",
    )(*scalars, *blocks, down, *after)


def dot_kernel(steps, has_term, ids, x_ref, w_ref, *refs):
    out_ref, acc = refs[-2:]
    step = pl.program_id(0)
    part = jnp.dot(x_ref[...], w_ref[...], preferred_element_type=jnp.float32)

    @pl.when(step == 0)
    def _():
        acc[...] = part + refs[0][...].astype(jnp.float32) if has_term else part

    @pl.when((step > 0) & (step < steps - 1))
    def _():
        acc[...] += part

    @pl.when(step == steps - 1)
    def _():
        out_ref[...] = (acc[...] + part).astype(out_ref.dtype)


def dot_quarter(x, w, flip, narrow, ids, out_dtype, term=None, after=()):
    rows, depth = x.shape
    step_depth = 512
    steps = depth // step_depth
    in_specs = [
        pl.BlockSpec((rows, step_depth), lambda k, ids: (0, k)),
        pl.BlockSpec((step_depth, narrow), lambda k, ids: (k, ids[1] ^ flip)),
    ]
    terms = []
    if term is not None:
        terms.append(term)
        in_specs.append(pl.BlockSpec((rows, narrow), lambda k, ids: (0, 0)))
    in_specs += [pl.BlockSpec(memory_space=pl.ANY)] * len(after)
    return pl.pallas_call(
        functools.partial(dot_kernel, steps, term is not None),
        out_shape=jax.ShapeDtypeStruct((rows, narrow), out_dtype),
        grid_spec=pltpu.PrefetchScalarGridSpec(
            num_scalar_prefetch=1,
            grid=(steps,),
            in_specs=in_specs,
            out_specs=pl.BlockSpec((rows, narrow), lambda k, ids: (0, 0)),
            scratch_shapes=[pltpu.VMEM((rows, narrow), jnp.float32)],
        ),
        compiler_params=pltpu.CompilerParams(vmem_limit_bytes=VMEM_LIMIT),
        cost_estimate=pl.CostEstimate(
            flops=2 * rows * depth * narrow,
            bytes_accessed=depth * narrow * 2 + rows * depth * 2 + rows * narrow * 4,
            transcendentals=0,
        ),
        name="dot_quarter",
    )(ids, x, w, *terms, *after)


def finish_kernel(mx_count, first, ids, rows, tenants, *refs):
    sums, far, (low_a, low_b, up_ref, scale_ref) = refs[0:2], refs[2:4], refs[4:8]
    out_ref = refs[-1]
    base = first + pl.program_id(0) * BLOCK_ROWS
    table = slot_table(ids, rows, tenants, mx_count)
    low = low_a[...] + low_b[...]
    group = lax.broadcasted_iota(jnp.int32, (32, 128), 1) // 32
    spread = jnp.concatenate([jnp.where(group == part, low, 0.0) for part in range(4)], axis=0)
    spread = spread.astype(jnp.bfloat16)
    tenant = row_tenants(table, base, (BLOCK_ROWS, 128))
    lane = lax.broadcasted_iota(jnp.int32, (BLOCK_ROWS, 128), 1)
    source = lax.broadcasted_iota(jnp.int32, (128, 128), 0) % (2 * RANK)
    goal = lax.broadcasted_iota(jnp.int32, (128, 128), 1) % RANK
    expanded = []
    for side in range(2):
        table_side = (source == goal + side * RANK).astype(jnp.bfloat16)
        full = jnp.dot(spread, table_side, preferred_element_type=jnp.float32)
        expanded.append(jnp.where(lane // RANK == tenant, full, 0.0).astype(jnp.bfloat16))
    pick = ((lane % 8 == tenant) & (lane < 24)).astype(jnp.bfloat16)
    columns = out_ref.shape[1]
    for left in range(0, columns, 256):
        right = min(left + 256, columns)
        pre = []
        for side in range(2):
            scale = scale_ref[side, :, left:right]
            high = scale.astype(jnp.bfloat16)
            rest = scale - high.astype(jnp.float32)
            middle = rest.astype(jnp.bfloat16)
            final = (rest - middle.astype(jnp.float32)).astype(jnp.bfloat16)
            stacked = jnp.concatenate(
                [high.astype(jnp.float32), middle.astype(jnp.float32), final.astype(jnp.float32),
                 jnp.zeros((104, right - left), jnp.float32)], axis=0
            ).astype(jnp.bfloat16)
            row_scale = jnp.dot(pick, stacked, preferred_element_type=jnp.float32)
            maps = up_ref[:, side, :, left:right].reshape(8 * RANK, right - left)
            adapted = jnp.dot(expanded[side], maps, preferred_element_type=jnp.float32)
            total = sums[side][:, left:right] + far[side][:, left:right].astype(jnp.float32) + adapted
            pre.append(total * row_scale)
        hidden = pre[0] * (1.0 / (1.0 + jnp.exp(-pre[0]))) * pre[1]
        out_ref[:, left:right] = hidden.astype(jnp.bfloat16)


def finish_rows(mx_count, first, scalars, sums, far, lows, adapter_out, scale, after):
    row_count, narrow = sums[0].shape
    tenants = adapter_out.shape[0]
    wide = pl.BlockSpec((BLOCK_ROWS, narrow), lambda i, *_: (i, 0))
    low_spec = pl.BlockSpec((32, 128), lambda i, *_: (i, 0))
    in_specs = [wide] * 4 + [low_spec] * 2
    in_specs.append(
        pl.BlockSpec((tenants, 2, RANK, narrow), lambda i, ids, *_: (0, 0, 0, ids[1]))
    )
    in_specs.append(pl.BlockSpec((2, tenants, narrow), lambda i, *_: (0, 0, 0)))
    in_specs += [pl.BlockSpec(memory_space=pl.ANY)] * len(after)
    return pl.pallas_call(
        functools.partial(finish_kernel, mx_count, first),
        out_shape=jax.ShapeDtypeStruct((row_count, narrow), jnp.bfloat16),
        grid_spec=pltpu.PrefetchScalarGridSpec(
            num_scalar_prefetch=3,
            grid=(row_count // BLOCK_ROWS,),
            in_specs=in_specs,
            out_specs=wide,
        ),
        compiler_params=pltpu.CompilerParams(vmem_limit_bytes=VMEM_LIMIT),
        cost_estimate=pl.CostEstimate(
            flops=2 * row_count * narrow * 2 * 256 + 20 * row_count * narrow,
            bytes_accessed=row_count * narrow * 14,
            transcendentals=row_count * narrow,
        ),
        name="finish_rows",
    )(*scalars, *sums, *far, *lows, adapter_out, scale, *after)


def unpack_kernel(mx_count, chunks, ids, rows, tenants, *refs):
    out_ref = refs[-1]
    block = pl.program_id(0)
    start = jnp.int32(0)
    for first, _, _, owner in slot_table(ids, rows, tenants, mx_count):
        start = jnp.where(owner == block, first, start)
    count = rows[block]
    total = None
    for (first, row_count, _), hidden in zip(chunks, refs):
        shape = (BLOCK_ROWS, row_count)
        position = lax.broadcasted_iota(jnp.int32, shape, 0)
        column = lax.broadcasted_iota(jnp.int32, shape, 1) + first
        chosen = (position < count) & (column == position + start)
        part = jnp.dot(chosen.astype(jnp.bfloat16), hidden[...], preferred_element_type=jnp.float32)
        total = part if total is None else total + part
    out_ref[...] = total.astype(jnp.bfloat16)


def unpack_rows(mx_count, chunks, scalars, hidden, blocks):
    narrow = hidden[0].shape[1]
    return pl.pallas_call(
        functools.partial(unpack_kernel, mx_count, chunks),
        out_shape=jax.ShapeDtypeStruct((blocks * BLOCK_ROWS, narrow), jnp.bfloat16),
        grid_spec=pltpu.PrefetchScalarGridSpec(
            num_scalar_prefetch=3,
            grid=(blocks,),
            in_specs=[pl.BlockSpec(part.shape, lambda i, *_: (0, 0)) for part in hidden],
            out_specs=pl.BlockSpec((BLOCK_ROWS, narrow), lambda i, *_: (i, 0)),
        ),
        compiler_params=pltpu.CompilerParams(vmem_limit_bytes=VMEM_LIMIT),
        cost_estimate=pl.CostEstimate(
            flops=2 * blocks * BLOCK_ROWS * LIVE_ROWS * narrow,
            bytes_accessed=(blocks * BLOCK_ROWS + LIVE_ROWS) * narrow * 2,
            transcendentals=0,
        ),
        name="unpack_rows",
    )(*scalars, *hidden)


def quarter(array, index, narrow):
    return lax.dynamic_slice_in_dim(array, index * narrow, narrow, array.ndim - 1)


def pipelined(
    tokens, w_gate, w_up, adapter_in, adapter_out, magnitude, partial_norms, block_tenant, block_rows
):
    mx_count = lax.axis_size("mx")
    my_count = lax.axis_size("my")
    narrow = w_gate.shape[1] // my_count
    mine = lax.axis_index("my")
    ids = jnp.stack([lax.axis_index("mx"), mine]).astype(jnp.int32)
    scalars = (ids, block_rows, block_tenant)
    weights = (w_gate, w_up)
    near = [(i, i ^ 1) for i in range(my_count)]
    across = [(i, i ^ 2) for i in range(my_count)]

    blocks = {(0, half): tokens[half * BLOCK_ROWS:(half + 1) * BLOCK_ROWS] for half in range(2)}
    for hop in range(1, mx_count):
        for half in range(2):
            up = [(i, i + 1) for i in range(hop - 1, mx_count - 1)]
            down = [(i + 1, i) for i in range(0, mx_count - hop)]
            blocks[-hop, half] = lax.ppermute(blocks[1 - hop, half], "mx", up)
            blocks[hop, half] = lax.ppermute(blocks[hop - 1, half], "mx", down)
    ordered = [blocks[slot] for slot in SLOTS]

    norms = partial_norms[0]
    pair = jnp.stack([quarter(norms, mine, narrow), quarter(norms, mine ^ 2, narrow)])
    other = jnp.stack([quarter(norms, mine ^ 1, narrow), quarter(norms, mine ^ 3, narrow)])
    pair = pair + lax.ppermute(other, "my", near)
    norm_total = pair[0] + lax.ppermute(pair[1], "my", across)
    scale = quarter(magnitude, mine, narrow) * lax.rsqrt(norm_total)
    scale = jnp.transpose(scale, (1, 0, 2))

    down = jnp.transpose(adapter_in, (1, 0, 2)).reshape(adapter_in.shape[1], -1)

    last = []

    def chain(result):
        last[:] = [result]
        return result

    packed, far, lows, near_got, sums, hidden = {}, {}, {}, {}, {}, {}

    def pack(c):
        first, row_count, slots = CHUNKS[c]
        packed[c], low = pack_rows(mx_count, first, row_count, scalars, ordered[:slots], down, tuple(last))
        chain(packed[c])
        low = low + lax.ppermute(low, "my", near)
        lows[c] = (low, lax.ppermute(low, "my", across))

    def send_far(c):
        got = []
        for w in weights:
            part = chain(dot_quarter(packed[c], w, 3, narrow, ids, jnp.bfloat16, after=tuple(last)))
            got.append(lax.ppermute(part, "my", near))
        far[c] = []
        for w, term in zip(weights, got):
            part = chain(dot_quarter(packed[c], w, 2, narrow, ids, jnp.bfloat16, term, after=tuple(last)))
            far[c].append(lax.ppermute(part, "my", across))

    def send_near(c):
        near_got[c] = []
        for w in weights:
            part = chain(dot_quarter(packed[c], w, 1, narrow, ids, jnp.bfloat16, after=tuple(last)))
            near_got[c].append(lax.ppermute(part, "my", near))

    def keep(c):
        sums[c] = [
            chain(dot_quarter(packed[c], w, 0, narrow, ids, jnp.float32, term, after=tuple(last)))
            for w, term in zip(weights, near_got[c])
        ]

    def finish(c):
        hidden[c] = chain(
            finish_rows(
                mx_count, CHUNKS[c][0], scalars, sums[c], far[c], lows[c], adapter_out, scale, tuple(last)
            )
        )

    pack(0)
    send_far(0)
    send_near(0)
    pack(1)
    send_far(1)
    keep(0)
    send_near(1)
    pack(2)
    send_far(2)
    send_near(2)
    keep(1)
    keep(2)
    finish(0)
    finish(1)
    finish(2)
    return unpack_rows(mx_count, CHUNKS, scalars, [hidden[c] for c in range(len(CHUNKS))], block_rows.shape[0])


def adapter_low(rows_piece, aligned_row_total, adapter_in, block_tenant):
    row_count = rows_piece.shape[0]
    seg_rows = math.gcd(math.gcd(row_count, BLOCK_ROWS), aligned_row_total)
    seg_count = row_count // seg_rows
    seg_block = jnp.arange(seg_count, dtype=jnp.int32) * seg_rows // BLOCK_ROWS
    tenant_tables = adapter_in[block_tenant[seg_block]]
    grouped = rows_piece.reshape(seg_count, seg_rows, rows_piece.shape[1])
    low_terms = jnp.einsum(
        "skd,sdr->skr", grouped, tenant_tables, preferred_element_type=jnp.float32
    )
    return low_terms.reshape(row_count, tenant_tables.shape[2])


def finish_plain(
    summed, reduced_rank_factor, norm_total, mag_cols, adapter_cols, first_row, block_tenant, block_rows
):
    row_count = summed.shape[0]
    col_count = summed.shape[2]
    seg_rows = math.gcd(row_count, BLOCK_ROWS)
    seg_count = row_count // seg_rows
    seg_block = (first_row + jnp.arange(seg_count, dtype=jnp.int32) * seg_rows) // BLOCK_ROWS
    tenants = block_tenant[seg_block]
    col_scale = mag_cols * lax.rsqrt(norm_total)
    seg_scale = col_scale[tenants]
    seg_tables = adapter_cols[tenants]
    low_pair = reduced_rank_factor.reshape(seg_count, seg_rows, 2, RANK)
    adapted = jnp.einsum(
        "skpr,sprc->skpc", low_pair, seg_tables, preferred_element_type=jnp.float32
    )
    pre_act = (summed.reshape(seg_count, seg_rows, 2, col_count) + adapted) * seg_scale[:, None]
    hidden = jax.nn.silu(pre_act[:, :, 0]) * pre_act[:, :, 1]
    offsets = (first_row + jnp.arange(row_count, dtype=jnp.int32)).reshape(
        seg_count, seg_rows
    ) % BLOCK_ROWS
    live_mask = offsets < block_rows[seg_block][:, None]
    hidden = jnp.where(live_mask[:, :, None], hidden, jnp.zeros_like(hidden))
    return hidden.reshape(row_count, col_count).astype(jnp.bfloat16)


def plain(
    tokens, w_gate, w_up, adapter_in, adapter_out, magnitude, partial_norms, block_tenant, block_rows
):
    local_rows = tokens.shape[0]
    col_local = w_gate.shape[1]
    my_count = lax.axis_size("my")
    device_position = lax.axis_index("my")
    rows_piece = lax.all_gather(tokens, "mx", axis=0, tiled=True)
    gate_part = jnp.dot(rows_piece, w_gate, preferred_element_type=jnp.float32)
    up_part = jnp.dot(rows_piece, w_up, preferred_element_type=jnp.float32)
    main_part = jnp.stack((gate_part, up_part), axis=1)
    low_terms = adapter_low(rows_piece, local_rows, adapter_in, block_tenant)
    reduced_rank_factor = lax.psum(low_terms, "my").astype(jnp.bfloat16)
    summed = lax.psum_scatter(main_part, "my", scatter_dimension=2, tiled=True)
    norm_total = lax.psum_scatter(partial_norms[0], "my", scatter_dimension=2, tiled=True)
    narrow = col_local // my_count
    mag_cols = lax.dynamic_slice_in_dim(magnitude, device_position * narrow, narrow, 2)
    adapter_cols = lax.dynamic_slice_in_dim(adapter_out, device_position * narrow, narrow, 3)
    return finish_plain(
        summed, reduced_rank_factor, norm_total, mag_cols, adapter_cols, 0, block_tenant, block_rows
    )


def on_device(tokens, w_gate, *rest):
    my_count = lax.axis_size("my")
    fits = (
        my_count == 4
        and lax.axis_size("mx") == 4
        and tokens.shape[0] == 2 * BLOCK_ROWS
        and tokens.shape[1] % 512 == 0
        and w_gate.shape[1] % (my_count * 128) == 0
    )
    return (pipelined if fits else plain)(tokens, w_gate, *rest)


def solution(mesh):
    return jax.shard_map(
        on_device,
        mesh=mesh,
        in_specs=(
            P(("groups", "mx"), "my"),
            P("my", "mx"),
            P("my", "mx"),
            P(None, "my", None),
            P(None, None, None, "mx"),
            P(None, None, "mx"),
            P("my", None, None, "mx"),
            P("groups"),
            P("groups"),
        ),
        out_specs=P("groups", ("mx", "my")),
        check_vma=False,
    )
```

```python
import functools
import math

import jax
import jax.numpy as jnp
from jax import lax
from jax.experimental import pallas as pl
from jax.experimental.pallas import tpu as pltpu
from jax.sharding import PartitionSpec as P

RANK = 16
BLOCK_ROWS = 128
LIVE_ROWS = 768
STEP_DEPTH = 512
VMEM_LIMIT = 48 * 1024 * 1024

SLOTS = (
    (0, 0), (0, 1),
    (-1, 0), (1, 0), (-1, 1), (1, 1),
    (-2, 0), (-2, 1), (2, 0), (2, 1),
    (-3, 0), (-3, 1), (3, 0), (3, 1),
)
CHUNKS = ((0, 128, 4), (128, 128, 6), (256, 256, 10), (512, 256, 14))
ANY = pl.BlockSpec(memory_space=pl.ANY)
COST = pl.CostEstimate(flops=0, bytes_accessed=0, transcendentals=0)


def slot_table(ids, rows, tenants, mx_count):
    place = ids[0]
    start = jnp.int32(0)
    table = []
    for distance, half in SLOTS:
        source = place + distance
        valid = (source >= 0) & (source < mx_count)
        block = jnp.clip(source, 0, mx_count - 1) * 2 + half
        count = jnp.where(valid, rows[block], 0)
        table.append((start, count, tenants[block], jnp.where(valid, block, -1)))
        start = start + count
    return table


def row_tenants(table, first, shape):
    row = lax.broadcasted_iota(jnp.int32, shape, 0) + first
    tenant = jnp.full(shape, -1, jnp.int32)
    for start, count, owner, _ in table:
        tenant = jnp.where((row >= start) & (row < start + count), owner, tenant)
    return tenant


def pack_kernel(mx_count, first, rows_out, places, copied, ids, rows, tenants, *refs):
    slots = len(places)
    tokens = max(ref for ref, _ in places) + 1
    token_refs = refs[:tokens]
    down_ref = refs[tokens]
    scratch = refs[-6:]
    x_ref, low_ref = refs[-9:-7] if copied is not None else refs[-8:-6]
    buffer, down, acc, sems, down_sem, copy_sem = scratch
    table = slot_table(ids, rows, tenants, mx_count)
    needed, copies = [], []
    for slot, (ref, row) in enumerate(places):
        start, count, _, _ = table[slot]
        needed.append((count > 0) & (start < first + rows_out) & (start + count > first))
        copies.append(
            pltpu.make_async_copy(token_refs[ref].at[pl.ds(row, BLOCK_ROWS)], buffer.at[slot], sems.at[slot])
        )
    for need, copy in zip(needed, copies):
        pl.when(need)(copy.start)
    down_copy = pltpu.make_async_copy(down_ref, down, down_sem)
    down_copy.start()
    if copied is not None:
        hand_on = pltpu.make_async_copy(token_refs[copied], refs[-7], copy_sem)
        hand_on.start()
    acc[...] = jnp.zeros_like(acc)
    for slot in range(slots):
        start, count, _, _ = table[slot]

        @pl.when(needed[slot])
        def _():
            copies[slot].wait()
            target = lax.broadcasted_iota(jnp.int32, (rows_out, BLOCK_ROWS), 0) + first
            position = lax.broadcasted_iota(jnp.int32, (rows_out, BLOCK_ROWS), 1)
            chosen = (position < count) & (target == position + start)
            acc[...] += jnp.dot(
                chosen.astype(jnp.bfloat16), buffer[slot], preferred_element_type=jnp.float32
            )

    x = acc[...].astype(jnp.bfloat16)
    x_ref[...] = x
    down_copy.wait()
    for tile in range(rows_out // BLOCK_ROWS):
        low = lax.dot_general(
            x[tile * BLOCK_ROWS:(tile + 1) * BLOCK_ROWS], down[...], (((1,), (1,)), ((), ())),
            preferred_element_type=jnp.float32,
        )
        tenant = row_tenants(table, first + tile * BLOCK_ROWS, low.shape)
        lane = lax.broadcasted_iota(jnp.int32, low.shape, 1)
        low = jnp.where(lane // (2 * RANK) == tenant, low, 0.0)
        low = low[:, :128] + low[:, 128:]
        low = low + pltpu.roll(low, 64, 1)
        low = low + pltpu.roll(low, 32, 1)
        group = lax.broadcasted_iota(jnp.int32, (32, 128), 1) // 32
        packed = jnp.where(group == 0, low[0:32], 0.0)
        for part in range(1, 4):
            packed = jnp.where(group == part, low[part * 32:(part + 1) * 32], packed)
        low_ref[tile * 32:(tile + 1) * 32, :] = packed
    if copied is not None:
        hand_on.wait()


def pack_rows(mx_count, first, rows_out, scalars, tokens, places, down, after, copied=None):
    width = down.shape[1]
    outs = [
        jax.ShapeDtypeStruct((rows_out, width), jnp.bfloat16),
        jax.ShapeDtypeStruct((rows_out // 4, 128), jnp.float32),
    ]
    out_specs = [
        pl.BlockSpec((rows_out, width), lambda i, *_: (0, 0)),
        pl.BlockSpec((rows_out // 4, 128), lambda i, *_: (0, 0)),
    ]
    if copied is not None:
        outs.append(jax.ShapeDtypeStruct(tokens[copied].shape, tokens[copied].dtype))
        out_specs.append(ANY)
    return pl.pallas_call(
        functools.partial(pack_kernel, mx_count, first, rows_out, places, copied),
        out_shape=outs,
        grid_spec=pltpu.PrefetchScalarGridSpec(
            num_scalar_prefetch=3,
            grid=(1,),
            in_specs=[ANY] * (len(tokens) + 1 + len(after)),
            out_specs=out_specs,
            scratch_shapes=[
                pltpu.VMEM((len(places), BLOCK_ROWS, width), jnp.bfloat16),
                pltpu.VMEM(down.shape, jnp.bfloat16),
                pltpu.VMEM((rows_out, width), jnp.float32),
                pltpu.SemaphoreType.DMA((len(places),)),
                pltpu.SemaphoreType.DMA,
                pltpu.SemaphoreType.DMA,
            ],
        ),
        compiler_params=pltpu.CompilerParams(vmem_limit_bytes=VMEM_LIMIT),
        cost_estimate=COST,
        name="pack_rows",
    )(*scalars, *tokens, down, *after)


def dot_kernel(flip, row_counts, has_term, passed, joined, narrow, steps, ids, *refs):
    x_refs, refs = refs[:len(row_counts)], refs[len(row_counts):]
    w_refs, refs = refs[:2], refs[2:]
    term_refs = refs[:2] if has_term else None
    x, w, acc, out, x_sem, w_sem, term_sem, out_sem = refs[-8:]
    if joined:
        out_refs = [refs[-9 - passed].at[side] for side in range(2)]
    else:
        out_refs = refs[-10 - passed:-8 - passed]
    left = pl.multiple_of((ids[1] ^ flip) * narrow, 128)

    x_copies, row = [], 0
    for part, (x_ref, count) in enumerate(zip(x_refs, row_counts)):
        x_copies.append(pltpu.make_async_copy(x_ref, x.at[pl.ds(row, count)], x_sem.at[part]))
        row += count
    for copy in x_copies:
        copy.start()

    def piece(side, step):
        return pltpu.make_async_copy(
            w_refs[side].at[pl.ds(step * STEP_DEPTH, STEP_DEPTH), pl.ds(left, narrow)],
            w.at[side * steps + step], w_sem.at[side * steps + step],
        )

    for side in range(2):
        for step in range(steps):
            piece(side, step).start()
    if has_term:
        term_copies = [
            pltpu.make_async_copy(term_refs[side], out.at[side], term_sem.at[side]) for side in range(2)
        ]
        for copy in term_copies:
            copy.start()
        for side in range(2):
            term_copies[side].wait()
            acc[side] = out[side].astype(jnp.float32)
    else:
        acc[...] = jnp.zeros_like(acc)
    for copy in x_copies:
        copy.wait()

    def out_copy(side):
        source = acc if out_refs[side].dtype == jnp.float32 else out
        return pltpu.make_async_copy(source.at[side], out_refs[side], out_sem.at[side])

    for side in range(2):
        @pl.loop(0, steps)
        def _(step):
            piece(side, step).wait()
            columns = pl.ds(pl.multiple_of(step * STEP_DEPTH, STEP_DEPTH), STEP_DEPTH)
            acc[side] += jnp.dot(x[:, columns], w[side * steps + step], preferred_element_type=jnp.float32)

        if out_refs[side].dtype != jnp.float32:
            out[side] = acc[side].astype(out.dtype)
        out_copy(side).start()
    for side in range(2):
        out_copy(side).wait()


def dot_pair(xs, weights, flip, narrow, ids, out_dtype, terms=(), after=(), passed=(), joined=False):
    row_counts = tuple(x.shape[0] for x in xs)
    rows, depth = sum(row_counts), xs[0].shape[1]
    steps = depth // STEP_DEPTH
    operands = [ids, *xs, *weights, *terms, *after]
    if joined:
        outs = [jax.ShapeDtypeStruct((2, rows, narrow), out_dtype)]
    else:
        outs = [jax.ShapeDtypeStruct((rows, narrow), out_dtype)] * 2
    aliases = {len(operands) + i: len(outs) + i for i in range(len(passed))}
    operands += list(passed)
    return pl.pallas_call(
        functools.partial(dot_kernel, flip, row_counts, len(terms) > 0, len(passed), joined, narrow, steps),
        out_shape=outs + [jax.ShapeDtypeStruct(array.shape, array.dtype) for array in passed],
        grid_spec=pltpu.PrefetchScalarGridSpec(
            num_scalar_prefetch=1,
            grid=(1,),
            in_specs=[ANY] * (len(operands) - 1),
            out_specs=[ANY] * (len(outs) + len(passed)),
            scratch_shapes=[
                pltpu.VMEM((rows, depth), jnp.bfloat16),
                pltpu.VMEM((2 * steps, STEP_DEPTH, narrow), jnp.bfloat16),
                pltpu.VMEM((2, rows, narrow), jnp.float32),
                pltpu.VMEM((2, rows, narrow), jnp.bfloat16),
                pltpu.SemaphoreType.DMA((len(xs),)),
                pltpu.SemaphoreType.DMA((2 * steps,)),
                pltpu.SemaphoreType.DMA((2,)),
                pltpu.SemaphoreType.DMA((2,)),
            ],
        ),
        input_output_aliases=aliases,
        compiler_params=pltpu.CompilerParams(vmem_limit_bytes=VMEM_LIMIT),
        cost_estimate=COST,
        name="dot_pair",
    )(*operands)


def finish_tile(base, table, sums, far, low, up_ref, scale_ref, store):
    group = lax.broadcasted_iota(jnp.int32, (32, 128), 1) // 32
    spread = jnp.concatenate([jnp.where(group == part, low, 0.0) for part in range(4)], axis=0)
    spread = spread.astype(jnp.bfloat16)
    tenant = row_tenants(table, base, (BLOCK_ROWS, 128))
    lane = lax.broadcasted_iota(jnp.int32, (BLOCK_ROWS, 128), 1)
    source = lax.broadcasted_iota(jnp.int32, (128, 128), 0) % (2 * RANK)
    goal = lax.broadcasted_iota(jnp.int32, (128, 128), 1) % RANK
    expanded = []
    for side in range(2):
        table_side = (source == goal + side * RANK).astype(jnp.bfloat16)
        full = jnp.dot(spread, table_side, preferred_element_type=jnp.float32)
        expanded.append(jnp.where(lane // RANK == tenant, full, 0.0).astype(jnp.bfloat16))
    pick = ((lane % 8 == tenant) & (lane < 24)).astype(jnp.bfloat16)
    columns = scale_ref.shape[2]
    for left in range(0, columns, 256):
        right = min(left + 256, columns)
        pre = []
        for side in range(2):
            scale = scale_ref[side, :, left:right]
            high = scale.astype(jnp.bfloat16)
            rest = scale - high.astype(jnp.float32)
            middle = rest.astype(jnp.bfloat16)
            final = (rest - middle.astype(jnp.float32)).astype(jnp.bfloat16)
            stacked = jnp.concatenate(
                [high.astype(jnp.float32), middle.astype(jnp.float32), final.astype(jnp.float32),
                 jnp.zeros((104, right - left), jnp.float32)], axis=0
            ).astype(jnp.bfloat16)
            row_scale = jnp.dot(pick, stacked, preferred_element_type=jnp.float32)
            maps = up_ref[:, side, :, left:right].reshape(8 * RANK, right - left)
            adapted = jnp.dot(expanded[side], maps, preferred_element_type=jnp.float32)
            total = sums(side, left, right) + far(side, left, right).astype(jnp.float32) + adapted
            pre.append(total * row_scale)
        hidden = pre[0] * (1.0 / (1.0 + jnp.exp(-pre[0]))) * pre[1]
        store(left, right, hidden.astype(jnp.bfloat16))


def finish_kernel(
    mx_count, first, ids, rows, tenants, gate_sum, up_sum, far, low_a, low_b, up_ref, scale_ref, *refs
):
    out_ref = refs[-1]
    sums = (gate_sum, up_sum)
    base = first + pl.program_id(0) * BLOCK_ROWS
    table = slot_table(ids, rows, tenants, mx_count)

    def store(left, right, value):
        out_ref[:, left:right] = value

    finish_tile(
        base, table, lambda side, left, right: sums[side][:, left:right],
        lambda side, left, right: far[side, :, left:right], low_a[...] + low_b[...], up_ref, scale_ref, store,
    )


def finish_rows(mx_count, first, scalars, sums, far, lows, adapter_out, scale, after):
    _, row_count, narrow = far.shape
    tenants = adapter_out.shape[0]
    place = first // BLOCK_ROWS
    low_spec = pl.BlockSpec((32, 128), lambda i, *_: (place + i, 0))
    in_specs = [
        *[pl.BlockSpec((BLOCK_ROWS, narrow), lambda i, *_: (place + i, 0))] * 2,
        pl.BlockSpec((2, BLOCK_ROWS, narrow), lambda i, *_: (0, i, 0)),
        low_spec, low_spec,
        pl.BlockSpec((tenants, 2, RANK, narrow), lambda i, ids, *_: (0, 0, 0, ids[1])),
        pl.BlockSpec((2, tenants, narrow), lambda i, *_: (0, 0, 0)),
    ]
    return pl.pallas_call(
        functools.partial(finish_kernel, mx_count, first),
        out_shape=jax.ShapeDtypeStruct((row_count, narrow), jnp.bfloat16),
        grid_spec=pltpu.PrefetchScalarGridSpec(
            num_scalar_prefetch=3,
            grid=(row_count // BLOCK_ROWS,),
            in_specs=in_specs + [ANY] * len(after),
            out_specs=pl.BlockSpec((BLOCK_ROWS, narrow), lambda i, *_: (i, 0)),
        ),
        compiler_params=pltpu.CompilerParams(vmem_limit_bytes=VMEM_LIMIT),
        cost_estimate=COST,
        name="finish_rows",
    )(*scalars, *sums, far, *lows, adapter_out, scale, *after)


def last_kernel(
    mx_count, first, ids, rows, tenants, gate_sum, up_sum, far, low_a, low_b, up_ref, scale_ref, *refs
):
    earlier, out_ref, held = refs[:-2], refs[-2], refs[-1]
    sums = (gate_sum, up_sum)
    table = slot_table(ids, rows, tenants, mx_count)
    block = pl.program_id(0)

    @pl.when(block == 0)
    def _():
        row = 0
        for part in earlier:
            held[row:row + part.shape[0], :] = part[...]
            row += part.shape[0]
        held[LIVE_ROWS:, :] = jnp.zeros((BLOCK_ROWS, held.shape[1]), held.dtype)

        @pl.loop(0, far.shape[1] // BLOCK_ROWS)
        def _(tile):
            here = pl.ds(pl.multiple_of(tile * BLOCK_ROWS, BLOCK_ROWS), BLOCK_ROWS)
            there = pl.ds(pl.multiple_of(first + tile * BLOCK_ROWS, BLOCK_ROWS), BLOCK_ROWS)
            lanes = pl.ds(pl.multiple_of(tile * 32, 32), 32)

            def store(left, right, value):
                held[there, left:right] = value

            finish_tile(
                first + tile * BLOCK_ROWS, table, lambda side, left, right: sums[side][here, left:right],
                lambda side, left, right: far[side, here, left:right], low_a[lanes, :] + low_b[lanes, :],
                up_ref, scale_ref, store,
            )

    start = jnp.int32(0)
    for begin, _, _, owner in table:
        start = jnp.where(owner == block, begin, start)
    count = rows[block]
    base = pl.multiple_of(jnp.minimum(start // BLOCK_ROWS * BLOCK_ROWS, LIVE_ROWS - BLOCK_ROWS), BLOCK_ROWS)
    shape = (BLOCK_ROWS, 2 * BLOCK_ROWS)
    position = lax.broadcasted_iota(jnp.int32, shape, 0)
    column = lax.broadcasted_iota(jnp.int32, shape, 1) + base
    chosen = (position < count) & (column == position + start)
    out_ref[...] = jnp.dot(
        chosen.astype(jnp.bfloat16), held[pl.ds(base, 2 * BLOCK_ROWS), :], preferred_element_type=jnp.float32
    ).astype(jnp.bfloat16)


def last_rows(mx_count, first, scalars, sums, far, lows, adapter_out, scale, earlier, blocks):
    _, row_count, narrow = far.shape
    tenants = adapter_out.shape[0]
    place = first // row_count
    low_spec = pl.BlockSpec((row_count // 4, 128), lambda i, *_: (place, 0))
    in_specs = [
        *[pl.BlockSpec((row_count, narrow), lambda i, *_: (0, 0))] * 2,
        pl.BlockSpec((2, row_count, narrow), lambda i, *_: (0, 0, 0)),
        low_spec, low_spec,
        pl.BlockSpec((tenants, 2, RANK, narrow), lambda i, ids, *_: (0, 0, 0, ids[1])),
        pl.BlockSpec((2, tenants, narrow), lambda i, *_: (0, 0, 0)),
    ] + [pl.BlockSpec(part.shape, lambda i, *_: (0, 0)) for part in earlier]
    return pl.pallas_call(
        functools.partial(last_kernel, mx_count, first),
        out_shape=jax.ShapeDtypeStruct((blocks * BLOCK_ROWS, narrow), jnp.bfloat16),
        grid_spec=pltpu.PrefetchScalarGridSpec(
            num_scalar_prefetch=3,
            grid=(blocks,),
            in_specs=in_specs,
            out_specs=pl.BlockSpec((BLOCK_ROWS, narrow), lambda i, *_: (i, 0)),
            scratch_shapes=[pltpu.VMEM((LIVE_ROWS + BLOCK_ROWS, narrow), jnp.bfloat16)],
        ),
        compiler_params=pltpu.CompilerParams(vmem_limit_bytes=VMEM_LIMIT),
        cost_estimate=COST,
        name="last_rows",
    )(*scalars, *sums, far, *lows, adapter_out, scale, *earlier)


def quarter(array, index, narrow):
    return lax.dynamic_slice_in_dim(array, index * narrow, narrow, array.ndim - 1)


def pipelined(
    tokens, w_gate, w_up, adapter_in, adapter_out, magnitude, partial_norms, block_tenant, block_rows
):
    mx_count = lax.axis_size("mx")
    my_count = lax.axis_size("my")
    narrow = w_gate.shape[1] // my_count
    mine = lax.axis_index("my")
    ids = jnp.stack([lax.axis_index("mx"), mine]).astype(jnp.int32)
    scalars = (ids, block_rows, block_tenant)
    weights = (w_gate, w_up)
    near = [(i, i ^ 1) for i in range(my_count)]
    across = [(i, i ^ 2) for i in range(my_count)]

    def hop(block, distance, least=0):
        if distance > 0:
            pairs = [(i, i + distance) for i in range(least, mx_count - distance)]
        else:
            pairs = [(i, i + distance) for i in range(-distance, mx_count - least)]
        return lax.ppermute(block, "mx", pairs)

    halves = [tokens[half * BLOCK_ROWS:(half + 1) * BLOCK_ROWS] for half in range(2)]
    first_hop = [(hop(block, 1), hop(block, -1)) for block in halves]

    norms = partial_norms[0]
    pair = jnp.stack([quarter(norms, mine, narrow), quarter(norms, mine ^ 2, narrow)])
    other = jnp.stack([quarter(norms, mine ^ 1, narrow), quarter(norms, mine ^ 3, narrow)])
    pair = pair + lax.ppermute(other, "my", near)
    norm_total = pair[0] + lax.ppermute(pair[1], "my", across)
    scale = quarter(magnitude, mine, narrow) * lax.rsqrt(norm_total)
    scale = jnp.transpose(scale, (1, 0, 2))

    down = jnp.transpose(adapter_in, (0, 2, 1)).reshape(-1, adapter_in.shape[1])

    def pack(c, blocks, places, after, copied=None):
        first, row_count, slots = CHUNKS[c]
        return pack_rows(mx_count, first, row_count, scalars, blocks, places[:slots], down, after, copied)

    def swap(parts, pairs):
        return [lax.ppermute(part, "my", pairs) for part in parts]

    def send_far(x, passed=()):
        parts = dot_pair([x], weights, 3, narrow, ids, jnp.bfloat16)
        got = swap(parts, near)
        part, *handed = dot_pair([x], weights, 2, narrow, ids, jnp.bfloat16, got, passed=passed, joined=True)
        return part, lax.ppermute(part, "my", across), handed

    blocks = [tokens, *first_hop[0]]
    places = [(0, 0), (0, BLOCK_ROWS), (1, 0), (2, 0)]
    x0, low0, again = pack(0, blocks, places, (scale,), copied=0)
    second_hop = [hop(again, 2), hop(again, -2)]
    mark, far0, _ = send_far(x0)

    blocks += first_hop[1]
    places += [(3, 0), (4, 0)]
    x1, low1 = pack(1, blocks, places, (mark,))
    mark, far1, second_hop = send_far(x1, passed=second_hop)
    third_hop = [hop(second_hop[0], 1, 2), hop(second_hop[1], -1, 2)]

    blocks += second_hop
    places += [(5, 0), (5, BLOCK_ROWS), (6, 0), (6, BLOCK_ROWS)]
    x2, low2 = pack(2, blocks, places, (mark, far0))
    mark, far2, _ = send_far(x2)

    early = [x0, x1, x2]
    parts = dot_pair(early, weights, 1, narrow, ids, jnp.bfloat16, after=(mark,))
    early_got = swap(parts, near)

    blocks += third_hop
    places += [(7, 0), (7, BLOCK_ROWS), (8, 0), (8, BLOCK_ROWS)]
    x3, low3 = pack(3, blocks, places, (parts[0], far1))
    mark, far3, _ = send_far(x3)

    low = jnp.concatenate([low0, low1, low2, low3], axis=0)
    low = low + lax.ppermute(low, "my", near)
    lows = (low, lax.ppermute(low, "my", across))

    parts = dot_pair([x3], weights, 1, narrow, ids, jnp.bfloat16, after=(mark,))
    late_got = swap(parts, near)
    early_sums = dot_pair(early, weights, 0, narrow, ids, jnp.float32, early_got, after=(parts[0],))
    late_sums = dot_pair([x3], weights, 0, narrow, ids, jnp.float32, late_got, after=(early_sums[0], far2))
    hidden, mark = [], late_sums[0]
    for c, far in enumerate([far0, far1, far2]):
        mark = finish_rows(
            mx_count, CHUNKS[c][0], scalars, early_sums, far, lows, adapter_out, scale, (mark,)
        )
        hidden.append(mark)
    return last_rows(
        mx_count, CHUNKS[3][0], scalars, late_sums, far3, lows, adapter_out, scale, hidden, block_rows.shape[0]
    )


def adapter_low(rows_piece, aligned_row_total, adapter_in, block_tenant):
    row_count = rows_piece.shape[0]
    seg_rows = math.gcd(math.gcd(row_count, BLOCK_ROWS), aligned_row_total)
    seg_count = row_count // seg_rows
    seg_block = jnp.arange(seg_count, dtype=jnp.int32) * seg_rows // BLOCK_ROWS
    tenant_tables = adapter_in[block_tenant[seg_block]]
    grouped = rows_piece.reshape(seg_count, seg_rows, rows_piece.shape[1])
    low_terms = jnp.einsum(
        "skd,sdr->skr", grouped, tenant_tables, preferred_element_type=jnp.float32
    )
    return low_terms.reshape(row_count, tenant_tables.shape[2])


def finish_plain(
    summed, reduced_rank_factor, norm_total, mag_cols, adapter_cols, first_row, block_tenant, block_rows
):
    row_count = summed.shape[0]
    col_count = summed.shape[2]
    seg_rows = math.gcd(row_count, BLOCK_ROWS)
    seg_count = row_count // seg_rows
    seg_block = (first_row + jnp.arange(seg_count, dtype=jnp.int32) * seg_rows) // BLOCK_ROWS
    tenants = block_tenant[seg_block]
    col_scale = mag_cols * lax.rsqrt(norm_total)
    seg_scale = col_scale[tenants]
    seg_tables = adapter_cols[tenants]
    low_pair = reduced_rank_factor.reshape(seg_count, seg_rows, 2, RANK)
    adapted = jnp.einsum(
        "skpr,sprc->skpc", low_pair, seg_tables, preferred_element_type=jnp.float32
    )
    pre_act = (summed.reshape(seg_count, seg_rows, 2, col_count) + adapted) * seg_scale[:, None]
    hidden = jax.nn.silu(pre_act[:, :, 0]) * pre_act[:, :, 1]
    offsets = (first_row + jnp.arange(row_count, dtype=jnp.int32)).reshape(
        seg_count, seg_rows
    ) % BLOCK_ROWS
    live_mask = offsets < block_rows[seg_block][:, None]
    hidden = jnp.where(live_mask[:, :, None], hidden, jnp.zeros_like(hidden))
    return hidden.reshape(row_count, col_count).astype(jnp.bfloat16)


def plain(
    tokens, w_gate, w_up, adapter_in, adapter_out, magnitude, partial_norms, block_tenant, block_rows
):
    local_rows = tokens.shape[0]
    col_local = w_gate.shape[1]
    my_count = lax.axis_size("my")
    device_position = lax.axis_index("my")
    rows_piece = lax.all_gather(tokens, "mx", axis=0, tiled=True)
    gate_part = jnp.dot(rows_piece, w_gate, preferred_element_type=jnp.float32)
    up_part = jnp.dot(rows_piece, w_up, preferred_element_type=jnp.float32)
    main_part = jnp.stack((gate_part, up_part), axis=1)
    low_terms = adapter_low(rows_piece, local_rows, adapter_in, block_tenant)
    reduced_rank_factor = lax.psum(low_terms, "my").astype(jnp.bfloat16)
    summed = lax.psum_scatter(main_part, "my", scatter_dimension=2, tiled=True)
    norm_total = lax.psum_scatter(partial_norms[0], "my", scatter_dimension=2, tiled=True)
    narrow = col_local // my_count
    mag_cols = lax.dynamic_slice_in_dim(magnitude, device_position * narrow, narrow, 2)
    adapter_cols = lax.dynamic_slice_in_dim(adapter_out, device_position * narrow, narrow, 3)
    return finish_plain(
        summed, reduced_rank_factor, norm_total, mag_cols, adapter_cols, 0, block_tenant, block_rows
    )


def on_device(tokens, w_gate, *rest):
    my_count = lax.axis_size("my")
    fits = (
        my_count == 4
        and lax.axis_size("mx") == 4
        and tokens.shape[0] == 2 * BLOCK_ROWS
        and tokens.shape[1] % 512 == 0
        and w_gate.shape[1] % (my_count * 128) == 0
    )
    return (pipelined if fits else plain)(tokens, w_gate, *rest)


def solution(mesh):
    return jax.shard_map(
        on_device,
        mesh=mesh,
        in_specs=(
            P(("groups", "mx"), "my"),
            P("my", "mx"),
            P("my", "mx"),
            P(None, "my", None),
            P(None, None, None, "mx"),
            P(None, None, "mx"),
            P("my", None, None, "mx"),
            P("groups"),
            P("groups"),
        ),
        out_specs=P("groups", ("mx", "my")),
        check_vma=False,
    )
```

```python
import functools
import math

import jax
import jax.numpy as jnp
from jax import lax
from jax.experimental import pallas as pl
from jax.experimental.pallas import tpu as pltpu
from jax.sharding import PartitionSpec as P

RANK = 16
BLOCK_ROWS = 128
LIVE_ROWS = 768
TILE = 256
VMEM_LIMIT = 52 * 1024 * 1024

SLOTS = tuple((distance, half) for distance in (0, -1, 1, -2, 2, -3, 3) for half in range(2))
CHUNKS = ((0, 256, 6), (256, 192, 10), (448, 320, 14))
ANY = pl.BlockSpec(memory_space=pl.ANY)
COST = pl.CostEstimate(flops=0, bytes_accessed=0, transcendentals=0)


def fill_table(table, ids, rows, tenants, mx_count):
    start = jnp.int32(0)
    for slot, (distance, half) in enumerate(SLOTS):
        source = ids[0] + distance
        valid = (source >= 0) & (source < mx_count)
        block = jnp.clip(source, 0, mx_count - 1) * 2 + half
        count = jnp.where(valid, rows[block], 0)
        table[0, slot] = start
        table[1, slot] = count
        table[2, slot] = tenants[block]
        table[3, slot] = jnp.where(valid, block, -1)
        start = start + count


def pack_kernel(mx_count, first, rows_out, slots, passed, ids, rows, tenants, *refs):
    token_refs, down_ref = refs[:slots // 2], refs[slots // 2]
    outs, scratch = refs[-9 - passed:-6], refs[-6:]
    x_ref, low_ref, pick_ref = outs[:3]
    table, buffer, down, acc, sems, down_sem = scratch
    fill_table(table, ids, rows, tenants, mx_count)

    def needed(slot):
        start, count = table[0, slot], table[1, slot]
        return (count > 0) & (start < first + rows_out) & (start + count > first)

    for slot in range(slots):
        @pl.when(needed(slot))
        def _():
            here = pl.ds(slot % 2 * BLOCK_ROWS, BLOCK_ROWS)
            pltpu.make_async_copy(token_refs[slot // 2].at[here], buffer.at[slot], sems.at[slot]).start()

    down_copy = pltpu.make_async_copy(down_ref, down, down_sem)
    down_copy.start()
    acc[...] = jnp.zeros_like(acc)

    @pl.loop(0, slots)
    def _(slot):
        @pl.when(needed(slot))
        def _():
            start, count = table[0, slot], table[1, slot]
            pltpu.make_async_copy(buffer.at[slot], buffer.at[slot], sems.at[slot]).wait()
            target = lax.broadcasted_iota(jnp.int32, (rows_out, BLOCK_ROWS), 0) + first
            position = lax.broadcasted_iota(jnp.int32, (rows_out, BLOCK_ROWS), 1)
            chosen = (position < count) & (target == position + start)
            acc[...] += jnp.dot(
                chosen.astype(jnp.bfloat16), buffer[slot], preferred_element_type=jnp.float32
            )

    x_ref[...] = acc[...].astype(jnp.bfloat16)
    row = lax.broadcasted_iota(jnp.int32, (rows_out, 128), 0) + first

    def own(slot, tenant):
        start, count = table[0, slot], table[1, slot]
        return jnp.where((row >= start) & (row < start + count), table[2, slot], tenant)

    tenant = lax.fori_loop(0, slots, own, jnp.full((rows_out, 128), -1, jnp.int32))
    lane = lax.broadcasted_iota(jnp.int32, (rows_out, 128), 1)
    pick_ref[...] = ((lane % 8 == tenant) & (lane < 24)).astype(jnp.bfloat16)

    down_copy.wait()
    low = lax.dot_general(x_ref[...], down[...], (((1,), (1,)), ((), ())), preferred_element_type=jnp.float32)
    owner = jnp.concatenate([lane // 32, lane // 32 + 4], axis=1)
    low = jnp.where(owner == jnp.concatenate([tenant, tenant], axis=1), low, 0.0)
    high = low.astype(jnp.bfloat16)
    rest = (low - high.astype(jnp.float32)).astype(jnp.bfloat16)
    source = lax.broadcasted_iota(jnp.int32, (256, 256), 0)
    goal = lax.broadcasted_iota(jnp.int32, (256, 256), 1)
    place = source // 32 * RANK + source % RANK
    for side in range(2):
        mine = source // RANK % 2 == side
        to_high = (mine & (place == goal)).astype(jnp.bfloat16)
        to_rest = (mine & (place + 128 == goal)).astype(jnp.bfloat16)
        moved = jnp.dot(high, to_high, preferred_element_type=jnp.float32)
        moved += jnp.dot(rest, to_rest, preferred_element_type=jnp.float32)
        low_ref[side] = moved.astype(jnp.bfloat16)


def pack_rows(mx_count, chunk, scalars, tokens, down, after=(), passed=()):
    first, rows_out, slots = chunk
    width = down.shape[1]
    outs = [
        jax.ShapeDtypeStruct((rows_out, width), jnp.bfloat16),
        jax.ShapeDtypeStruct((2, rows_out, 256), jnp.bfloat16),
        jax.ShapeDtypeStruct((rows_out, 128), jnp.bfloat16),
    ]
    out_specs = [
        pl.BlockSpec((rows_out, width), lambda i, *_: (0, 0)),
        pl.BlockSpec((2, rows_out, 256), lambda i, *_: (0, 0, 0)),
        pl.BlockSpec((rows_out, 128), lambda i, *_: (0, 0)),
    ] + [ANY] * len(passed)
    return pl.pallas_call(
        functools.partial(pack_kernel, mx_count, first, rows_out, slots, len(passed)),
        out_shape=outs + [jax.ShapeDtypeStruct(tokens[i].shape, tokens[i].dtype) for i in passed],
        grid_spec=pltpu.PrefetchScalarGridSpec(
            num_scalar_prefetch=3,
            grid=(1,),
            in_specs=[ANY] * (len(tokens) + 1 + len(after)),
            out_specs=out_specs,
            scratch_shapes=[
                pltpu.SMEM((4, len(SLOTS)), jnp.int32),
                pltpu.VMEM((slots, BLOCK_ROWS, width), jnp.bfloat16),
                pltpu.VMEM(down.shape, jnp.bfloat16),
                pltpu.VMEM((rows_out, width), jnp.float32),
                pltpu.SemaphoreType.DMA((slots,)),
                pltpu.SemaphoreType.DMA,
            ],
        ),
        input_output_aliases={3 + place: 3 + i for i, place in enumerate(passed)},
        compiler_params=pltpu.CompilerParams(vmem_limit_bytes=VMEM_LIMIT),
        cost_estimate=COST,
        name="pack_rows",
    )(*scalars, *tokens, down, *after)


def activate(gate, up):
    return (gate * (1.0 / (1.0 + jnp.exp(-gate))) * up).astype(jnp.bfloat16)


def dot_kernel(flip, counts, splits, terms, far_counts, narrow, ids, *refs):
    parts = len(counts)
    finish = len(far_counts) > 0
    x_refs, low_refs, refs = refs[:parts], refs[parts:2 * parts], refs[2 * parts:]
    w_refs, up_ref, refs = refs[:2], refs[2], refs[3:]
    term_refs, refs = refs[:2 * terms], refs[2 * terms:]
    if finish:
        far_refs, refs = refs[:parts], refs[parts:]
        pick_refs, scale_ref, refs = refs[:parts], refs[parts], refs[parts + 1:]
    x, low, w, maps, term, out, far, pick, scale, in_sem, w_sem, out_sem = refs[-12:]
    outs = refs[-12 - max(1, 2 * len(splits)):-12]
    rows, depth = x.shape
    left = pl.multiple_of((ids[1] ^ flip) * narrow, 128)
    tiles = [(at, min(TILE, narrow - at)) for at in range(0, narrow, TILE)]
    whole = sum(size == TILE for _, size in tiles)

    loads = []

    def load(source, target):
        copy = pltpu.make_async_copy(source, target, in_sem.at[len(loads)])
        copy.start()
        loads.append(copy)

    row = 0
    for part, count in enumerate(counts):
        here = pl.ds(row, count)
        load(x_refs[part], x.at[here])
        load(low_refs[part], low.at[:, here])
        row += count

    def piece(side, at, size, place):
        return pltpu.make_async_copy(
            w_refs[side].at[:, pl.ds(pl.multiple_of(left + at, 128), size)],
            w.at[side, :, pl.ds(at, size)], w_sem.at[side, place],
        )

    def start_piece(place):
        for side in range(2):
            piece(side, *tiles[place], place).start()

    start_piece(0)
    for side in range(2):
        for copy in range(2):
            load(up_ref.at[:, side, :, pl.ds(left, narrow)], maps.at[side, copy])
    row = 0
    if terms:
        count = rows // terms
        for side in range(2):
            for part in range(terms):
                load(term_refs[side * terms + part], term.at[side, pl.ds(part * count, count)])
    if finish:
        for part, count in enumerate(counts):
            here = pl.ds(row, count)
            load(far_refs[part], far.at[:, here])
            load(pick_refs[part], pick.at[here])
            row += count
        load(scale_ref, scale)
    for place in range(1, len(tiles)):
        start_piece(place)
    for copy in loads:
        copy.wait()

    def tile(at, size, place):
        columns = pl.ds(at, size)
        values = []
        for side in range(2):
            piece(side, at, size, place).wait()
            value = jnp.dot(x[...], w[side, :, columns], preferred_element_type=jnp.float32)
            value += jnp.dot(
                low[side], maps[side, :, :, :, columns].reshape(256, size), preferred_element_type=jnp.float32
            )
            if terms:
                value += term[side, :, columns].astype(jnp.float32)
            if finish:
                value += far[side, :, columns].astype(jnp.float32)
                value *= jnp.dot(pick[...], scale[side, :, columns], preferred_element_type=jnp.float32)
                values.append(value)
            else:
                out[side, :, columns] = value.astype(out.dtype)
        if finish:
            out[0, :, columns] = activate(*values)

    @pl.loop(0, whole)
    def _(place):
        tile(pl.multiple_of(place * TILE, TILE), TILE, place)

    for place in range(whole, len(tiles)):
        tile(*tiles[place], place)

    copies = []

    def store(source, target):
        copy = pltpu.make_async_copy(source, target, out_sem.at[len(copies)])
        copy.start()
        copies.append(copy)

    if finish:
        store(out.at[0], outs[0])
    elif not splits:
        store(out, outs[0])
    else:
        for side in range(2):
            row = 0
            for part, count in enumerate(splits):
                store(out.at[side, pl.ds(row, count)], outs[side * len(splits) + part])
                row += count
    for copy in copies:
        copy.wait()


def dot_pair(chunks, weights, adapter_out, flip, narrow, ids, out_dtype, splits=(), terms=(), finish=None, after=()):
    xs, lows, picks = zip(*chunks)
    counts = tuple(x.shape[0] for x in xs)
    rows, depth = sum(counts), xs[0].shape[1]
    tenants = adapter_out.shape[0]
    operands = [ids, *xs, *lows, *weights, adapter_out, *terms]
    if finish is not None:
        operands += [*finish[0], *picks, finish[1]]
        out_shape = [jax.ShapeDtypeStruct((rows, narrow), out_dtype)]
    elif splits:
        out_shape = [jax.ShapeDtypeStruct((count, narrow), out_dtype) for _ in range(2) for count in splits]
    else:
        out_shape = [jax.ShapeDtypeStruct((2, rows, narrow), out_dtype)]
    operands += list(after)
    few = (8, 128)
    pieces = -(-narrow // TILE)
    return pl.pallas_call(
        functools.partial(
            dot_kernel, flip, counts, splits, len(terms) // 2, counts if finish is not None else (), narrow
        ),
        out_shape=out_shape,
        grid_spec=pltpu.PrefetchScalarGridSpec(
            num_scalar_prefetch=1,
            grid=(1,),
            in_specs=[ANY] * (len(operands) - 1),
            out_specs=[ANY] * len(out_shape),
            scratch_shapes=[
                pltpu.VMEM((rows, depth), jnp.bfloat16),
                pltpu.VMEM((2, rows, 256), jnp.bfloat16),
                pltpu.VMEM((2, depth, narrow), jnp.bfloat16),
                pltpu.VMEM((2, 2, tenants, RANK, narrow), jnp.bfloat16),
                pltpu.VMEM((2, rows, narrow) if terms else few, jnp.bfloat16),
                pltpu.VMEM((1 if finish is not None else 2, rows, narrow), out_dtype),
                pltpu.VMEM((2, rows, narrow) if finish is not None else few, jnp.bfloat16),
                pltpu.VMEM((rows, 128) if finish is not None else few, jnp.bfloat16),
                pltpu.VMEM((2, 128, narrow) if finish is not None else few, jnp.bfloat16),
                pltpu.SemaphoreType.DMA((4 * len(xs) + 8,)),
                pltpu.SemaphoreType.DMA((2, pieces)),
                pltpu.SemaphoreType.DMA((4,)),
            ],
        ),
        compiler_params=pltpu.CompilerParams(vmem_limit_bytes=VMEM_LIMIT),
        cost_estimate=COST,
        name="finish_dots" if finish is not None else "dot_pair",
    )(*operands)


def last_kernel(mx_count, first, ids, rows, tenants, sums, far, pick, scale, earlier, out_ref, table, held):
    block = pl.program_id(0)

    @pl.when(block == 0)
    def _():
        fill_table(table, ids, rows, tenants, mx_count)
        held[0:first, :] = earlier[...]
        held[LIVE_ROWS:, :] = jnp.zeros((BLOCK_ROWS, held.shape[1]), held.dtype)
        columns = held.shape[1]

        @pl.loop(0, far.shape[1] // 64)
        def _(tile):
            here = pl.ds(pl.multiple_of(tile * 64, 64), 64)
            there = pl.ds(pl.multiple_of(first + tile * 64, 64), 64)
            for left in range(0, columns, TILE):
                right = min(left + TILE, columns)
                pre = [
                    (sums[side, here, left:right] + far[side, here, left:right].astype(jnp.float32))
                    * jnp.dot(pick[here, :], scale[side, :, left:right], preferred_element_type=jnp.float32)
                    for side in range(2)
                ]
                held[there, left:right] = activate(*pre)

    def find(slot, start):
        return jnp.where(table[3, slot] == block, table[0, slot], start)

    start = lax.fori_loop(0, len(SLOTS), find, jnp.int32(0))
    count = rows[block]
    base = pl.multiple_of(jnp.minimum(start // BLOCK_ROWS * BLOCK_ROWS, LIVE_ROWS - BLOCK_ROWS), BLOCK_ROWS)
    shape = (BLOCK_ROWS, 2 * BLOCK_ROWS)
    position = lax.broadcasted_iota(jnp.int32, shape, 0)
    column = lax.broadcasted_iota(jnp.int32, shape, 1) + base
    chosen = (position < count) & (column == position + start)
    out_ref[...] = jnp.dot(
        chosen.astype(jnp.bfloat16), held[pl.ds(base, 2 * BLOCK_ROWS), :], preferred_element_type=jnp.float32
    ).astype(jnp.bfloat16)


def last_rows(mx_count, first, scalars, sums, far, pick, scale, earlier, blocks):
    narrow = far.shape[2]
    operands = (sums, far, pick, scale, earlier)
    return pl.pallas_call(
        functools.partial(last_kernel, mx_count, first),
        out_shape=jax.ShapeDtypeStruct((blocks * BLOCK_ROWS, narrow), jnp.bfloat16),
        grid_spec=pltpu.PrefetchScalarGridSpec(
            num_scalar_prefetch=3,
            grid=(blocks,),
            in_specs=[
                pl.BlockSpec(part.shape, lambda i, *_, dims=part.ndim: (0,) * dims) for part in operands
            ],
            out_specs=pl.BlockSpec((BLOCK_ROWS, narrow), lambda i, *_: (i, 0)),
            scratch_shapes=[
                pltpu.SMEM((4, len(SLOTS)), jnp.int32),
                pltpu.VMEM((LIVE_ROWS + BLOCK_ROWS, narrow), jnp.bfloat16),
            ],
        ),
        compiler_params=pltpu.CompilerParams(vmem_limit_bytes=VMEM_LIMIT),
        cost_estimate=COST,
        name="last_rows",
    )(*scalars, *operands)


def quarter(array, index, narrow):
    return lax.dynamic_slice_in_dim(array, index * narrow, narrow, array.ndim - 1)


def pipelined(
    tokens, w_gate, w_up, adapter_in, adapter_out, magnitude, partial_norms, block_tenant, block_rows
):
    mx_count = lax.axis_size("mx")
    my_count = lax.axis_size("my")
    narrow = w_gate.shape[1] // my_count
    mine = lax.axis_index("my")
    ids = jnp.stack([lax.axis_index("mx"), mine]).astype(jnp.int32)
    scalars = (ids, block_rows, block_tenant)
    near = [(i, i ^ 1) for i in range(my_count)]
    across = [(i, i ^ 2) for i in range(my_count)]

    def hop(block, distance, least=0):
        if distance > 0:
            pairs = [(i, i + distance) for i in range(least, mx_count - distance)]
        else:
            pairs = [(i, i + distance) for i in range(-distance, mx_count - least)]
        return lax.ppermute(block, "mx", pairs)

    blocks = [tokens] + [hop(tokens, distance) for distance in (1, -1, 2, -2)]

    norms = partial_norms[0]
    pair = jnp.stack([quarter(norms, mine, narrow), quarter(norms, mine ^ 2, narrow)])
    other = jnp.stack([quarter(norms, mine ^ 1, narrow), quarter(norms, mine ^ 3, narrow)])
    pair = pair + lax.ppermute(other, "my", near)
    norm_total = pair[0] + lax.ppermute(pair[1], "my", across)
    scale = quarter(magnitude, mine, narrow) * lax.rsqrt(norm_total)
    scale = jnp.transpose(scale, (1, 0, 2))
    high = lax.reduce_precision(scale, 8, 7)
    middle = lax.reduce_precision(scale - high, 8, 7)
    rest = scale - high - middle
    scale = jnp.concatenate(
        [high, middle, rest, jnp.zeros((2, 128 - 3 * scale.shape[1], narrow), jnp.float32)], axis=1
    ).astype(jnp.bfloat16)

    down = jnp.transpose(adapter_in, (0, 2, 1)).reshape(-1, adapter_in.shape[1])

    dots = functools.partial(
        dot_pair, weights=(w_gate, w_up), adapter_out=adapter_out, narrow=narrow, ids=ids
    )

    def swap(parts, pairs):
        return [lax.ppermute(part, "my", pairs) for part in parts]

    def send_far(chunk, pieces=1):
        rows = chunk[0].shape[0] // pieces
        parts = dots([chunk], flip=3, out_dtype=jnp.bfloat16, splits=(rows,) * pieces)
        got = swap(parts, near)
        part, = dots([chunk], flip=2, out_dtype=jnp.bfloat16, terms=got)
        return part, lax.ppermute(part, "my", across)

    *chunk0, = pack_rows(mx_count, CHUNKS[0], scalars, blocks[:3], down, after=(scale,))
    mark, far0 = send_far(chunk0)

    *chunk1, second, third = pack_rows(
        mx_count, CHUNKS[1], scalars, blocks, down, after=(mark,), passed=(3, 4)
    )
    blocks = [*blocks[:3], second, third, hop(second, 1, 2), hop(third, -1, 2)]
    mark, far1 = send_far(chunk1)

    *chunk2, = pack_rows(mx_count, CHUNKS[2], scalars, blocks, down, after=(mark, far0))
    mark, far2 = send_far(chunk2, 2)

    first, last = CHUNKS[2][:2]
    parts = dots([chunk0, chunk1, chunk2], flip=1, out_dtype=jnp.bfloat16, splits=(first, last), after=(mark, far1))
    early_gate, late_gate, early_up, late_up = swap(parts, near)
    sums, = dots([chunk2], flip=0, out_dtype=jnp.float32, terms=(late_gate, late_up))
    hidden, = dots(
        [chunk0, chunk1], flip=0, out_dtype=jnp.bfloat16, terms=(early_gate, early_up),
        finish=((far0, far1), scale), after=(sums,),
    )
    return last_rows(mx_count, first, scalars, sums, far2, chunk2[2], scale, hidden, block_rows.shape[0])


def adapter_low(rows_piece, aligned_row_total, adapter_in, block_tenant):
    row_count = rows_piece.shape[0]
    seg_rows = math.gcd(math.gcd(row_count, BLOCK_ROWS), aligned_row_total)
    seg_count = row_count // seg_rows
    seg_block = jnp.arange(seg_count, dtype=jnp.int32) * seg_rows // BLOCK_ROWS
    tenant_tables = adapter_in[block_tenant[seg_block]]
    grouped = rows_piece.reshape(seg_count, seg_rows, rows_piece.shape[1])
    low_terms = jnp.einsum(
        "skd,sdr->skr", grouped, tenant_tables, preferred_element_type=jnp.float32
    )
    return low_terms.reshape(row_count, tenant_tables.shape[2])


def finish_plain(
    summed, reduced_rank_factor, norm_total, mag_cols, adapter_cols, first_row, block_tenant, block_rows
):
    row_count = summed.shape[0]
    col_count = summed.shape[2]
    seg_rows = math.gcd(row_count, BLOCK_ROWS)
    seg_count = row_count // seg_rows
    seg_block = (first_row + jnp.arange(seg_count, dtype=jnp.int32) * seg_rows) // BLOCK_ROWS
    tenants = block_tenant[seg_block]
    col_scale = mag_cols * lax.rsqrt(norm_total)
    seg_scale = col_scale[tenants]
    seg_tables = adapter_cols[tenants]
    low_pair = reduced_rank_factor.reshape(seg_count, seg_rows, 2, RANK)
    adapted = jnp.einsum(
        "skpr,sprc->skpc", low_pair, seg_tables, preferred_element_type=jnp.float32
    )
    pre_act = (summed.reshape(seg_count, seg_rows, 2, col_count) + adapted) * seg_scale[:, None]
    hidden = jax.nn.silu(pre_act[:, :, 0]) * pre_act[:, :, 1]
    offsets = (first_row + jnp.arange(row_count, dtype=jnp.int32)).reshape(
        seg_count, seg_rows
    ) % BLOCK_ROWS
    live_mask = offsets < block_rows[seg_block][:, None]
    hidden = jnp.where(live_mask[:, :, None], hidden, jnp.zeros_like(hidden))
    return hidden.reshape(row_count, col_count).astype(jnp.bfloat16)


def plain(
    tokens, w_gate, w_up, adapter_in, adapter_out, magnitude, partial_norms, block_tenant, block_rows
):
    local_rows = tokens.shape[0]
    col_local = w_gate.shape[1]
    my_count = lax.axis_size("my")
    device_position = lax.axis_index("my")
    rows_piece = lax.all_gather(tokens, "mx", axis=0, tiled=True)
    gate_part = jnp.dot(rows_piece, w_gate, preferred_element_type=jnp.float32)
    up_part = jnp.dot(rows_piece, w_up, preferred_element_type=jnp.float32)
    main_part = jnp.stack((gate_part, up_part), axis=1)
    low_terms = adapter_low(rows_piece, local_rows, adapter_in, block_tenant)
    reduced_rank_factor = lax.psum(low_terms, "my").astype(jnp.bfloat16)
    summed = lax.psum_scatter(main_part, "my", scatter_dimension=2, tiled=True)
    norm_total = lax.psum_scatter(partial_norms[0], "my", scatter_dimension=2, tiled=True)
    narrow = col_local // my_count
    mag_cols = lax.dynamic_slice_in_dim(magnitude, device_position * narrow, narrow, 2)
    adapter_cols = lax.dynamic_slice_in_dim(adapter_out, device_position * narrow, narrow, 3)
    return finish_plain(
        summed, reduced_rank_factor, norm_total, mag_cols, adapter_cols, 0, block_tenant, block_rows
    )


def on_device(tokens, w_gate, *rest):
    my_count = lax.axis_size("my")
    fits = (
        my_count == 4
        and lax.axis_size("mx") == 4
        and tokens.shape[0] == 2 * BLOCK_ROWS
        and tokens.shape[1] % 512 == 0
        and w_gate.shape[1] % (my_count * 128) == 0
    )
    return (pipelined if fits else plain)(tokens, w_gate, *rest)


def solution(mesh):
    return jax.shard_map(
        on_device,
        mesh=mesh,
        in_specs=(
            P(("groups", "mx"), "my"),
            P("my", "mx"),
            P("my", "mx"),
            P(None, "my", None),
            P(None, None, None, "mx"),
            P(None, None, "mx"),
            P("my", None, None, "mx"),
            P("groups"),
            P("groups"),
        ),
        out_specs=P("groups", ("mx", "my")),
        check_vma=False,
    )
```

```python
import functools
import math

import jax
import jax.numpy as jnp
from jax import lax
from jax.experimental import pallas as pl
from jax.experimental.pallas import tpu as pltpu
from jax.sharding import PartitionSpec as P

RANK = 16
BLOCK_ROWS = 128
LIVE_ROWS = 768
TILE = 256
VMEM_LIMIT = 60 * 1024 * 1024

SLOTS = tuple((distance, half) for distance in (0, -1, 1, -2, 2, -3, 3) for half in range(2))
CHUNKS = ((0, 256, 6), (256, 192, 10), (448, 320, 14))
ANY = pl.BlockSpec(memory_space=pl.ANY)
COST = pl.CostEstimate(flops=0, bytes_accessed=0, transcendentals=0)


def fill_table(table, ids, rows, tenants, mx_count):
    start = jnp.int32(0)
    for slot, (distance, half) in enumerate(SLOTS):
        source = ids[0] + distance
        valid = (source >= 0) & (source < mx_count)
        block = jnp.clip(source, 0, mx_count - 1) * 2 + half
        count = jnp.where(valid, rows[block], 0)
        table[0, slot] = start
        table[1, slot] = count
        table[2, slot] = tenants[block]
        table[3, slot] = jnp.where(valid, block, -1)
        start = start + count


def pack_kernel(mx_count, first, rows_out, slots, passed, ids, rows, tenants, *refs):
    token_refs, down_ref = refs[:slots // 2], refs[slots // 2]
    outs, scratch = refs[-9 - passed:-6], refs[-6:]
    x_ref, low_ref, pick_ref = outs[:3]
    table, buffer, down, acc, sems, down_sem = scratch
    fill_table(table, ids, rows, tenants, mx_count)

    def needed(slot):
        start, count = table[0, slot], table[1, slot]
        return (count > 0) & (start < first + rows_out) & (start + count > first)

    for slot in range(slots):
        @pl.when(needed(slot))
        def _():
            here = pl.ds(slot % 2 * BLOCK_ROWS, BLOCK_ROWS)
            pltpu.make_async_copy(token_refs[slot // 2].at[here], buffer.at[slot], sems.at[slot]).start()

    down_copy = pltpu.make_async_copy(down_ref, down, down_sem)
    down_copy.start()
    acc[...] = jnp.zeros_like(acc)

    @pl.loop(0, slots)
    def _(slot):
        @pl.when(needed(slot))
        def _():
            start, count = table[0, slot], table[1, slot]
            pltpu.make_async_copy(buffer.at[slot], buffer.at[slot], sems.at[slot]).wait()
            target = lax.broadcasted_iota(jnp.int32, (rows_out, BLOCK_ROWS), 0) + first
            position = lax.broadcasted_iota(jnp.int32, (rows_out, BLOCK_ROWS), 1)
            chosen = (position < count) & (target == position + start)
            acc[...] += jnp.dot(
                chosen.astype(jnp.bfloat16), buffer[slot], preferred_element_type=jnp.float32
            )

    x_ref[...] = acc[...].astype(jnp.bfloat16)
    row = lax.broadcasted_iota(jnp.int32, (rows_out, 128), 0) + first

    def own(slot, tenant):
        start, count = table[0, slot], table[1, slot]
        return jnp.where((row >= start) & (row < start + count), table[2, slot], tenant)

    tenant = lax.fori_loop(0, slots, own, jnp.full((rows_out, 128), -1, jnp.int32))
    lane = lax.broadcasted_iota(jnp.int32, (rows_out, 128), 1)
    pick_ref[...] = ((lane % 8 == tenant) & (lane < 24)).astype(jnp.bfloat16)

    down_copy.wait()
    low = lax.dot_general(x_ref[...], down[...], (((1,), (1,)), ((), ())), preferred_element_type=jnp.float32)
    owner = jnp.concatenate([lane // 32, lane // 32 + 4], axis=1)
    low = jnp.where(owner == jnp.concatenate([tenant, tenant], axis=1), low, 0.0)
    high = low.astype(jnp.bfloat16)
    rest = (low - high.astype(jnp.float32)).astype(jnp.bfloat16)
    source = lax.broadcasted_iota(jnp.int32, (256, 256), 0)
    goal = lax.broadcasted_iota(jnp.int32, (256, 256), 1)
    place = source // 32 * RANK + source % RANK
    for side in range(2):
        mine = source // RANK % 2 == side
        to_high = (mine & (place == goal)).astype(jnp.bfloat16)
        to_rest = (mine & (place + 128 == goal)).astype(jnp.bfloat16)
        moved = jnp.dot(high, to_high, preferred_element_type=jnp.float32)
        moved += jnp.dot(rest, to_rest, preferred_element_type=jnp.float32)
        low_ref[side] = moved.astype(jnp.bfloat16)


def pack_rows(mx_count, chunk, scalars, tokens, down, after=(), passed=()):
    first, rows_out, slots = chunk
    width = down.shape[1]
    outs = [
        jax.ShapeDtypeStruct((rows_out, width), jnp.bfloat16),
        jax.ShapeDtypeStruct((2, rows_out, 256), jnp.bfloat16),
        jax.ShapeDtypeStruct((rows_out, 128), jnp.bfloat16),
    ]
    out_specs = [
        pl.BlockSpec((rows_out, width), lambda i, *_: (0, 0)),
        pl.BlockSpec((2, rows_out, 256), lambda i, *_: (0, 0, 0)),
        pl.BlockSpec((rows_out, 128), lambda i, *_: (0, 0)),
    ] + [ANY] * len(passed)
    return pl.pallas_call(
        functools.partial(pack_kernel, mx_count, first, rows_out, slots, len(passed)),
        out_shape=outs + [jax.ShapeDtypeStruct(tokens[i].shape, tokens[i].dtype) for i in passed],
        grid_spec=pltpu.PrefetchScalarGridSpec(
            num_scalar_prefetch=3,
            grid=(1,),
            in_specs=[ANY] * (len(tokens) + 1 + len(after)),
            out_specs=out_specs,
            scratch_shapes=[
                pltpu.SMEM((4, len(SLOTS)), jnp.int32),
                pltpu.VMEM((slots, BLOCK_ROWS, width), jnp.bfloat16),
                pltpu.VMEM(down.shape, jnp.bfloat16),
                pltpu.VMEM((rows_out, width), jnp.float32),
                pltpu.SemaphoreType.DMA((slots,)),
                pltpu.SemaphoreType.DMA,
            ],
        ),
        input_output_aliases={3 + place: 3 + i for i, place in enumerate(passed)},
        compiler_params=pltpu.CompilerParams(vmem_limit_bytes=VMEM_LIMIT),
        cost_estimate=COST,
        name="pack_rows",
    )(*scalars, *tokens, down, *after)


def activate(gate, up):
    return (gate * (1.0 / (1.0 + jnp.exp(-gate))) * up).astype(jnp.bfloat16)


def dot_kernel(flip, counts, splits, terms, far_counts, narrow, ids, *refs):
    parts = len(counts)
    finish = len(far_counts) > 0
    x_refs, low_refs, refs = refs[:parts], refs[parts:2 * parts], refs[2 * parts:]
    w_refs, up_ref, refs = refs[:2], refs[2], refs[3:]
    term_refs, refs = refs[:2 * terms], refs[2 * terms:]
    if finish:
        far_refs, refs = refs[:parts], refs[parts:]
        pick_refs, scale_ref, refs = refs[:parts], refs[parts], refs[parts + 1:]
    x, low, w, maps, term, out, far, pick, scale, in_sem, w_sem, out_sem = refs[-12:]
    outs = refs[-12 - max(1, 2 * len(splits)):-12]
    rows, depth = x.shape
    left = pl.multiple_of((ids[1] ^ flip) * narrow, 128)
    tiles = [(at, min(TILE, narrow - at)) for at in range(0, narrow, TILE)]
    whole = sum(size == TILE for _, size in tiles)

    loads = []

    def load(source, target):
        copy = pltpu.make_async_copy(source, target, in_sem.at[len(loads)])
        copy.start()
        loads.append(copy)

    row = 0
    for part, count in enumerate(counts):
        here = pl.ds(row, count)
        load(x_refs[part], x.at[here])
        load(low_refs[part], low.at[:, here])
        row += count

    def piece(side, at, size, place):
        return pltpu.make_async_copy(
            w_refs[side].at[:, pl.ds(pl.multiple_of(left + at, 128), size)],
            w.at[place, :, pl.ds(side * size, size)], w_sem.at[side, place],
        )

    def start_piece(place):
        for side in range(2):
            piece(side, *tiles[place], place).start()

    start_piece(0)
    for side in range(2):
        for copy in range(2):
            load(up_ref.at[:, side, :, pl.ds(left, narrow)], maps.at[side, copy])
    row = 0
    if terms:
        count = rows // terms
        for side in range(2):
            for part in range(terms):
                load(term_refs[side * terms + part], term.at[side, pl.ds(part * count, count)])
    if finish:
        for part, count in enumerate(counts):
            here = pl.ds(row, count)
            load(far_refs[part], far.at[:, here])
            load(pick_refs[part], pick.at[here])
            row += count
        load(scale_ref, scale)
    for place in range(1, len(tiles)):
        start_piece(place)
    for copy in loads:
        copy.wait()

    def tile(at, size, place):
        columns = pl.ds(at, size)
        values = []
        for side in range(2):
            piece(side, at, size, place).wait()
        both = jnp.dot(x[...], w[place, :, 0:2 * size], preferred_element_type=jnp.float32)
        for side in range(2):
            value = both[:, side * size:(side + 1) * size]
            value += jnp.dot(
                low[side], maps[side, :, :, :, columns].reshape(256, size), preferred_element_type=jnp.float32
            )
            if terms:
                value += term[side, :, columns].astype(jnp.float32)
            if finish:
                value += far[side, :, columns].astype(jnp.float32)
                value *= jnp.dot(pick[...], scale[side, :, columns], preferred_element_type=jnp.float32)
                values.append(value)
            else:
                out[side, :, columns] = value.astype(out.dtype)
        if finish:
            out[0, :, columns] = activate(*values)

    @pl.loop(0, whole)
    def _(place):
        tile(pl.multiple_of(place * TILE, TILE), TILE, place)

    for place in range(whole, len(tiles)):
        tile(*tiles[place], place)

    copies = []

    def store(source, target):
        copy = pltpu.make_async_copy(source, target, out_sem.at[len(copies)])
        copy.start()
        copies.append(copy)

    if finish:
        store(out.at[0], outs[0])
    elif not splits:
        store(out, outs[0])
    else:
        for side in range(2):
            row = 0
            for part, count in enumerate(splits):
                store(out.at[side, pl.ds(row, count)], outs[side * len(splits) + part])
                row += count
    for copy in copies:
        copy.wait()


def dot_pair(chunks, weights, adapter_out, flip, narrow, ids, out_dtype, splits=(), terms=(), finish=None, after=()):
    xs, lows, picks = zip(*chunks)
    counts = tuple(x.shape[0] for x in xs)
    rows, depth = sum(counts), xs[0].shape[1]
    tenants = adapter_out.shape[0]
    operands = [ids, *xs, *lows, *weights, adapter_out, *terms]
    if finish is not None:
        operands += [*finish[0], *picks, finish[1]]
        out_shape = [jax.ShapeDtypeStruct((rows, narrow), out_dtype)]
    elif splits:
        out_shape = [jax.ShapeDtypeStruct((count, narrow), out_dtype) for _ in range(2) for count in splits]
    else:
        out_shape = [jax.ShapeDtypeStruct((2, rows, narrow), out_dtype)]
    operands += list(after)
    few = (8, 128)
    pieces = -(-narrow // TILE)
    return pl.pallas_call(
        functools.partial(
            dot_kernel, flip, counts, splits, len(terms) // 2, counts if finish is not None else (), narrow
        ),
        out_shape=out_shape,
        grid_spec=pltpu.PrefetchScalarGridSpec(
            num_scalar_prefetch=1,
            grid=(1,),
            in_specs=[ANY] * (len(operands) - 1),
            out_specs=[ANY] * len(out_shape),
            scratch_shapes=[
                pltpu.VMEM((rows, depth), jnp.bfloat16),
                pltpu.VMEM((2, rows, 256), jnp.bfloat16),
                pltpu.VMEM((pieces, depth, 2 * TILE), jnp.bfloat16),
                pltpu.VMEM((2, 2, tenants, RANK, narrow), jnp.bfloat16),
                pltpu.VMEM((2, rows, narrow) if terms else few, jnp.bfloat16),
                pltpu.VMEM((1 if finish is not None else 2, rows, narrow), out_dtype),
                pltpu.VMEM((2, rows, narrow) if finish is not None else few, jnp.bfloat16),
                pltpu.VMEM((rows, 128) if finish is not None else few, jnp.bfloat16),
                pltpu.VMEM((2, 128, narrow) if finish is not None else few, jnp.bfloat16),
                pltpu.SemaphoreType.DMA((4 * len(xs) + 8,)),
                pltpu.SemaphoreType.DMA((2, pieces)),
                pltpu.SemaphoreType.DMA((4,)),
            ],
        ),
        compiler_params=pltpu.CompilerParams(vmem_limit_bytes=VMEM_LIMIT),
        cost_estimate=COST,
        name="finish_dots" if finish is not None else "dot_pair",
    )(*operands)


def last_kernel(mx_count, first, ids, rows, tenants, sums, far, pick, scale, earlier, out_ref, table, held):
    block = pl.program_id(0)

    @pl.when(block == 0)
    def _():
        fill_table(table, ids, rows, tenants, mx_count)
        held[0:first, :] = earlier[...]
        held[LIVE_ROWS:, :] = jnp.zeros((BLOCK_ROWS, held.shape[1]), held.dtype)
        columns = held.shape[1]

        @pl.loop(0, far.shape[1] // 64)
        def _(tile):
            here = pl.ds(pl.multiple_of(tile * 64, 64), 64)
            there = pl.ds(pl.multiple_of(first + tile * 64, 64), 64)
            for left in range(0, columns, TILE):
                right = min(left + TILE, columns)
                pre = [
                    (sums[side, here, left:right] + far[side, here, left:right].astype(jnp.float32))
                    * jnp.dot(pick[here, :], scale[side, :, left:right], preferred_element_type=jnp.float32)
                    for side in range(2)
                ]
                held[there, left:right] = activate(*pre)

    def find(slot, start):
        return jnp.where(table[3, slot] == block, table[0, slot], start)

    start = lax.fori_loop(0, len(SLOTS), find, jnp.int32(0))
    count = rows[block]
    base = pl.multiple_of(jnp.minimum(start // BLOCK_ROWS * BLOCK_ROWS, LIVE_ROWS - BLOCK_ROWS), BLOCK_ROWS)
    shape = (BLOCK_ROWS, 2 * BLOCK_ROWS)
    position = lax.broadcasted_iota(jnp.int32, shape, 0)
    column = lax.broadcasted_iota(jnp.int32, shape, 1) + base
    chosen = (position < count) & (column == position + start)
    out_ref[...] = jnp.dot(
        chosen.astype(jnp.bfloat16), held[pl.ds(base, 2 * BLOCK_ROWS), :], preferred_element_type=jnp.float32
    ).astype(jnp.bfloat16)


def last_rows(mx_count, first, scalars, sums, far, pick, scale, earlier, blocks):
    narrow = far.shape[2]
    operands = (sums, far, pick, scale, earlier)
    return pl.pallas_call(
        functools.partial(last_kernel, mx_count, first),
        out_shape=jax.ShapeDtypeStruct((blocks * BLOCK_ROWS, narrow), jnp.bfloat16),
        grid_spec=pltpu.PrefetchScalarGridSpec(
            num_scalar_prefetch=3,
            grid=(blocks,),
            in_specs=[
                pl.BlockSpec(part.shape, lambda i, *_, dims=part.ndim: (0,) * dims) for part in operands
            ],
            out_specs=pl.BlockSpec((BLOCK_ROWS, narrow), lambda i, *_: (i, 0)),
            scratch_shapes=[
                pltpu.SMEM((4, len(SLOTS)), jnp.int32),
                pltpu.VMEM((LIVE_ROWS + BLOCK_ROWS, narrow), jnp.bfloat16),
            ],
        ),
        compiler_params=pltpu.CompilerParams(vmem_limit_bytes=VMEM_LIMIT),
        cost_estimate=COST,
        name="last_rows",
    )(*scalars, *operands)


def quarter(array, index, narrow):
    return lax.dynamic_slice_in_dim(array, index * narrow, narrow, array.ndim - 1)


def pipelined(
    tokens, w_gate, w_up, adapter_in, adapter_out, magnitude, partial_norms, block_tenant, block_rows
):
    mx_count = lax.axis_size("mx")
    my_count = lax.axis_size("my")
    narrow = w_gate.shape[1] // my_count
    mine = lax.axis_index("my")
    ids = jnp.stack([lax.axis_index("mx"), mine]).astype(jnp.int32)
    scalars = (ids, block_rows, block_tenant)
    near = [(i, i ^ 1) for i in range(my_count)]
    across = [(i, i ^ 2) for i in range(my_count)]

    def hop(block, distance, least=0):
        if distance > 0:
            pairs = [(i, i + distance) for i in range(least, mx_count - distance)]
        else:
            pairs = [(i, i + distance) for i in range(-distance, mx_count - least)]
        return lax.ppermute(block, "mx", pairs)

    first_up, first_down = hop(tokens, 1), hop(tokens, -1)
    blocks = [tokens, first_up, first_down, hop(first_up, 1, 1), hop(first_down, -1, 1)]

    norms = partial_norms[0]
    pair = jnp.stack([quarter(norms, mine, narrow), quarter(norms, mine ^ 2, narrow)])
    other = jnp.stack([quarter(norms, mine ^ 1, narrow), quarter(norms, mine ^ 3, narrow)])
    pair = pair + lax.ppermute(other, "my", near)
    norm_total = pair[0] + lax.ppermute(pair[1], "my", across)
    scale = quarter(magnitude, mine, narrow) * lax.rsqrt(norm_total)
    scale = jnp.transpose(scale, (1, 0, 2))
    high = lax.reduce_precision(scale, 8, 7)
    middle = lax.reduce_precision(scale - high, 8, 7)
    rest = scale - high - middle
    scale = jnp.concatenate(
        [high, middle, rest, jnp.zeros((2, 128 - 3 * scale.shape[1], narrow), jnp.float32)], axis=1
    ).astype(jnp.bfloat16)

    down = jnp.transpose(adapter_in, (0, 2, 1)).reshape(-1, adapter_in.shape[1])

    dots = functools.partial(
        dot_pair, weights=(w_gate, w_up), adapter_out=adapter_out, narrow=narrow, ids=ids
    )

    def swap(parts, pairs):
        return [lax.ppermute(part, "my", pairs) for part in parts]

    def send_far(chunk, pieces=1):
        rows = chunk[0].shape[0] // pieces
        parts = dots([chunk], flip=3, out_dtype=jnp.bfloat16, splits=(rows,) * pieces)
        got = swap(parts, near)
        part, = dots([chunk], flip=2, out_dtype=jnp.bfloat16, terms=got)
        return part, lax.ppermute(part, "my", across)

    *chunk0, = pack_rows(mx_count, CHUNKS[0], scalars, blocks[:3], down, after=(scale,))
    mark, far0 = send_far(chunk0)

    *chunk1, second, third = pack_rows(
        mx_count, CHUNKS[1], scalars, blocks, down, after=(mark,), passed=(3, 4)
    )
    blocks = [*blocks[:3], second, third, hop(second, 1, 2), hop(third, -1, 2)]
    mark, far1 = send_far(chunk1)

    *chunk2, = pack_rows(mx_count, CHUNKS[2], scalars, blocks, down, after=(mark, far0))
    mark, far2 = send_far(chunk2, 2)

    first, last = CHUNKS[2][:2]
    parts = dots([chunk0, chunk1, chunk2], flip=1, out_dtype=jnp.bfloat16, splits=(first, last), after=(mark, far1))
    early_gate, late_gate, early_up, late_up = swap(parts, near)
    sums, = dots([chunk2], flip=0, out_dtype=jnp.float32, terms=(late_gate, late_up))
    hidden, = dots(
        [chunk0, chunk1], flip=0, out_dtype=jnp.bfloat16, terms=(early_gate, early_up),
        finish=((far0, far1), scale), after=(sums,),
    )
    return last_rows(mx_count, first, scalars, sums, far2, chunk2[2], scale, hidden, block_rows.shape[0])


def adapter_low(rows_piece, aligned_row_total, adapter_in, block_tenant):
    row_count = rows_piece.shape[0]
    seg_rows = math.gcd(math.gcd(row_count, BLOCK_ROWS), aligned_row_total)
    seg_count = row_count // seg_rows
    seg_block = jnp.arange(seg_count, dtype=jnp.int32) * seg_rows // BLOCK_ROWS
    tenant_tables = adapter_in[block_tenant[seg_block]]
    grouped = rows_piece.reshape(seg_count, seg_rows, rows_piece.shape[1])
    low_terms = jnp.einsum(
        "skd,sdr->skr", grouped, tenant_tables, preferred_element_type=jnp.float32
    )
    return low_terms.reshape(row_count, tenant_tables.shape[2])


def finish_plain(
    summed, reduced_rank_factor, norm_total, mag_cols, adapter_cols, first_row, block_tenant, block_rows
):
    row_count = summed.shape[0]
    col_count = summed.shape[2]
    seg_rows = math.gcd(row_count, BLOCK_ROWS)
    seg_count = row_count // seg_rows
    seg_block = (first_row + jnp.arange(seg_count, dtype=jnp.int32) * seg_rows) // BLOCK_ROWS
    tenants = block_tenant[seg_block]
    col_scale = mag_cols * lax.rsqrt(norm_total)
    seg_scale = col_scale[tenants]
    seg_tables = adapter_cols[tenants]
    low_pair = reduced_rank_factor.reshape(seg_count, seg_rows, 2, RANK)
    adapted = jnp.einsum(
        "skpr,sprc->skpc", low_pair, seg_tables, preferred_element_type=jnp.float32
    )
    pre_act = (summed.reshape(seg_count, seg_rows, 2, col_count) + adapted) * seg_scale[:, None]
    hidden = jax.nn.silu(pre_act[:, :, 0]) * pre_act[:, :, 1]
    offsets = (first_row + jnp.arange(row_count, dtype=jnp.int32)).reshape(
        seg_count, seg_rows
    ) % BLOCK_ROWS
    live_mask = offsets < block_rows[seg_block][:, None]
    hidden = jnp.where(live_mask[:, :, None], hidden, jnp.zeros_like(hidden))
    return hidden.reshape(row_count, col_count).astype(jnp.bfloat16)


def plain(
    tokens, w_gate, w_up, adapter_in, adapter_out, magnitude, partial_norms, block_tenant, block_rows
):
    local_rows = tokens.shape[0]
    col_local = w_gate.shape[1]
    my_count = lax.axis_size("my")
    device_position = lax.axis_index("my")
    rows_piece = lax.all_gather(tokens, "mx", axis=0, tiled=True)
    gate_part = jnp.dot(rows_piece, w_gate, preferred_element_type=jnp.float32)
    up_part = jnp.dot(rows_piece, w_up, preferred_element_type=jnp.float32)
    main_part = jnp.stack((gate_part, up_part), axis=1)
    low_terms = adapter_low(rows_piece, local_rows, adapter_in, block_tenant)
    reduced_rank_factor = lax.psum(low_terms, "my").astype(jnp.bfloat16)
    summed = lax.psum_scatter(main_part, "my", scatter_dimension=2, tiled=True)
    norm_total = lax.psum_scatter(partial_norms[0], "my", scatter_dimension=2, tiled=True)
    narrow = col_local // my_count
    mag_cols = lax.dynamic_slice_in_dim(magnitude, device_position * narrow, narrow, 2)
    adapter_cols = lax.dynamic_slice_in_dim(adapter_out, device_position * narrow, narrow, 3)
    return finish_plain(
        summed, reduced_rank_factor, norm_total, mag_cols, adapter_cols, 0, block_tenant, block_rows
    )


def on_device(tokens, w_gate, *rest):
    my_count = lax.axis_size("my")
    fits = (
        my_count == 4
        and lax.axis_size("mx") == 4
        and tokens.shape[0] == 2 * BLOCK_ROWS
        and tokens.shape[1] % 512 == 0
        and w_gate.shape[1] % (my_count * 128) == 0
    )
    return (pipelined if fits else plain)(tokens, w_gate, *rest)


def solution(mesh):
    return jax.shard_map(
        on_device,
        mesh=mesh,
        in_specs=(
            P(("groups", "mx"), "my"),
            P("my", "mx"),
            P("my", "mx"),
            P(None, "my", None),
            P(None, None, None, "mx"),
            P(None, None, "mx"),
            P("my", None, None, "mx"),
            P("groups"),
            P("groups"),
        ),
        out_specs=P("groups", ("mx", "my")),
        check_vma=False,
    )
```

```python
import functools
import math

import jax
import jax.numpy as jnp
from jax import lax
from jax.experimental import pallas as pl
from jax.experimental.pallas import tpu as pltpu
from jax.sharding import PartitionSpec as P

RANK = 16
BLOCK_ROWS = 128
LIVE_ROWS = 768
TILE = 256
VMEM_LIMIT = 60 * 1024 * 1024

SLOTS = tuple((distance, half) for distance in (0, -1, 1, -2, 2, -3, 3) for half in range(2))
CHUNKS = ((0, 256, 6), (256, 192, 10), (448, 320, 14))
ANY = pl.BlockSpec(memory_space=pl.ANY)
COST = pl.CostEstimate(flops=0, bytes_accessed=0, transcendentals=0)


def fill_table(table, ids, rows, tenants, mx_count):
    start = jnp.int32(0)
    for slot, (distance, half) in enumerate(SLOTS):
        source = ids[0] + distance
        valid = (source >= 0) & (source < mx_count)
        block = jnp.clip(source, 0, mx_count - 1) * 2 + half
        count = jnp.where(valid, rows[block], 0)
        table[0, slot] = start
        table[1, slot] = count
        table[2, slot] = tenants[block]
        table[3, slot] = jnp.where(valid, block, -1)
        start = start + count


def pack_kernel(mx_count, first, rows_out, slots, passed, ids, rows, tenants, *refs):
    token_refs, down_ref = refs[:slots // 2], refs[slots // 2]
    outs, scratch = refs[-9 - passed:-6], refs[-6:]
    x_ref, low_ref, pick_ref = outs[:3]
    table, buffer, down, acc, sems, down_sem = scratch
    fill_table(table, ids, rows, tenants, mx_count)

    def needed(slot):
        start, count = table[0, slot], table[1, slot]
        return (count > 0) & (start < first + rows_out) & (start + count > first)

    for slot in range(slots):
        @pl.when(needed(slot))
        def _():
            here = pl.ds(slot % 2 * BLOCK_ROWS, BLOCK_ROWS)
            pltpu.make_async_copy(token_refs[slot // 2].at[here], buffer.at[slot], sems.at[slot]).start()

    down_copy = pltpu.make_async_copy(down_ref, down, down_sem)
    down_copy.start()
    acc[...] = jnp.zeros_like(acc)

    @pl.loop(0, slots)
    def _(slot):
        @pl.when(needed(slot))
        def _():
            start, count = table[0, slot], table[1, slot]
            pltpu.make_async_copy(buffer.at[slot], buffer.at[slot], sems.at[slot]).wait()
            target = lax.broadcasted_iota(jnp.int32, (rows_out, BLOCK_ROWS), 0) + first
            position = lax.broadcasted_iota(jnp.int32, (rows_out, BLOCK_ROWS), 1)
            chosen = (position < count) & (target == position + start)
            acc[...] += jnp.dot(
                chosen.astype(jnp.bfloat16), buffer[slot], preferred_element_type=jnp.float32
            )

    x_ref[...] = acc[...].astype(jnp.bfloat16)
    row = lax.broadcasted_iota(jnp.int32, (rows_out, 128), 0) + first

    def own(slot, tenant):
        start, count = table[0, slot], table[1, slot]
        return jnp.where((row >= start) & (row < start + count), table[2, slot], tenant)

    tenant = lax.fori_loop(0, slots, own, jnp.full((rows_out, 128), -1, jnp.int32))
    lane = lax.broadcasted_iota(jnp.int32, (rows_out, 128), 1)
    pick_ref[...] = ((lane % 8 == tenant) & (lane < 24)).astype(jnp.bfloat16)

    down_copy.wait()
    low = lax.dot_general(x_ref[...], down[...], (((1,), (1,)), ((), ())), preferred_element_type=jnp.float32)
    owner = jnp.concatenate([lane // 32, lane // 32 + 4], axis=1)
    low = jnp.where(owner == jnp.concatenate([tenant, tenant], axis=1), low, 0.0)
    high = low.astype(jnp.bfloat16)
    rest = (low - high.astype(jnp.float32)).astype(jnp.bfloat16)
    source = lax.broadcasted_iota(jnp.int32, (256, 256), 0)
    goal = lax.broadcasted_iota(jnp.int32, (256, 256), 1)
    place = source // 32 * RANK + source % RANK
    for side in range(2):
        mine = source // RANK % 2 == side
        to_high = (mine & (place == goal)).astype(jnp.bfloat16)
        to_rest = (mine & (place + 128 == goal)).astype(jnp.bfloat16)
        moved = jnp.dot(high, to_high, preferred_element_type=jnp.float32)
        moved += jnp.dot(rest, to_rest, preferred_element_type=jnp.float32)
        low_ref[side] = moved.astype(jnp.bfloat16)


def pack_rows(mx_count, chunk, scalars, tokens, down, after=(), passed=()):
    first, rows_out, slots = chunk
    width = down.shape[1]
    outs = [
        jax.ShapeDtypeStruct((rows_out, width), jnp.bfloat16),
        jax.ShapeDtypeStruct((2, rows_out, 256), jnp.bfloat16),
        jax.ShapeDtypeStruct((rows_out, 128), jnp.bfloat16),
    ]
    out_specs = [
        pl.BlockSpec((rows_out, width), lambda i, *_: (0, 0)),
        pl.BlockSpec((2, rows_out, 256), lambda i, *_: (0, 0, 0)),
        pl.BlockSpec((rows_out, 128), lambda i, *_: (0, 0)),
    ] + [ANY] * len(passed)
    return pl.pallas_call(
        functools.partial(pack_kernel, mx_count, first, rows_out, slots, len(passed)),
        out_shape=outs + [jax.ShapeDtypeStruct(tokens[i].shape, tokens[i].dtype) for i in passed],
        grid_spec=pltpu.PrefetchScalarGridSpec(
            num_scalar_prefetch=3,
            grid=(1,),
            in_specs=[ANY] * (len(tokens) + 1 + len(after)),
            out_specs=out_specs,
            scratch_shapes=[
                pltpu.SMEM((4, len(SLOTS)), jnp.int32),
                pltpu.VMEM((slots, BLOCK_ROWS, width), jnp.bfloat16),
                pltpu.VMEM(down.shape, jnp.bfloat16),
                pltpu.VMEM((rows_out, width), jnp.float32),
                pltpu.SemaphoreType.DMA((slots,)),
                pltpu.SemaphoreType.DMA,
            ],
        ),
        input_output_aliases={3 + place: 3 + i for i, place in enumerate(passed)},
        compiler_params=pltpu.CompilerParams(vmem_limit_bytes=VMEM_LIMIT),
        cost_estimate=COST,
        name="pack_rows",
    )(*scalars, *tokens, down, *after)


def activate(gate, up):
    return (gate * (1.0 / (1.0 + jnp.exp(-gate))) * up).astype(jnp.bfloat16)


def dot_kernel(flip, counts, splits, terms, far_counts, narrow, ids, *refs):
    parts = len(counts)
    finish = len(far_counts) > 0
    x_refs, low_refs, refs = refs[:parts], refs[parts:2 * parts], refs[2 * parts:]
    w_refs, up_ref, refs = refs[:2], refs[2], refs[3:]
    term_refs, refs = refs[:2 * terms], refs[2 * terms:]
    if finish:
        far_refs, refs = refs[:parts], refs[parts:]
        pick_refs, scale_ref, refs = refs[:parts], refs[parts], refs[parts + 1:]
    x, low, w, maps, term, out, far, pick, scale, in_sem, w_sem, out_sem = refs[-12:]
    outs = refs[-12 - max(1, 2 * len(splits)):-12]
    rows, depth = x.shape
    left = pl.multiple_of((ids[1] ^ flip) * narrow, 128)
    tiles = [(at, min(TILE, narrow - at)) for at in range(0, narrow, TILE)]
    whole = sum(size == TILE for _, size in tiles)

    loads = []

    def load(source, target):
        copy = pltpu.make_async_copy(source, target, in_sem.at[len(loads)])
        copy.start()
        loads.append(copy)

    def wait_loads(begin, end):
        for copy in loads[begin:end]:
            copy.wait()

    def piece(side, at, size, place):
        return pltpu.make_async_copy(
            w_refs[side].at[:, pl.ds(pl.multiple_of(left + at, 128), size)],
            w.at[place, :, pl.ds(side * size, size)], w_sem.at[side, place],
        )

    def start_piece(at, size, place):
        for side in range(2):
            piece(side, at, size, place).start()

    def stores(at, size, place):
        columns = pl.ds(at, size)
        if finish:
            pairs = [(out.at[0, :, columns], outs[0].at[:, columns])]
        elif not splits:
            pairs = [(out.at[side, :, columns], outs[0].at[side, :, columns]) for side in range(2)]
        else:
            pairs = []
            for side in range(2):
                row = 0
                for part, count in enumerate(splits):
                    target = outs[side * len(splits) + part].at[:, columns]
                    pairs.append((out.at[side, pl.ds(row, count), columns], target))
                    row += count
        return [
            pltpu.make_async_copy(source, target, out_sem.at[place, i]) for i, (source, target) in enumerate(pairs)
        ]

    def tile(at, size, place, before_sums=lambda: None):
        columns = pl.ds(at, size)
        values = []
        for side in range(2):
            piece(side, at, size, place).wait()
        both = jnp.dot(x[...], w[place, :, 0:2 * size], preferred_element_type=jnp.float32)
        before_sums()
        for side in range(2):
            value = both[:, side * size:(side + 1) * size]
            value += jnp.dot(
                low[side], maps[side, :, :, :, columns].reshape(256, size), preferred_element_type=jnp.float32
            )
            if terms:
                value += term[side, :, columns].astype(jnp.float32)
            if finish:
                value += far[side, :, columns].astype(jnp.float32)
                value *= jnp.dot(pick[...], scale[side, :, columns], preferred_element_type=jnp.float32)
                values.append(value)
            else:
                out[side, :, columns] = value.astype(out.dtype)
        if finish:
            out[0, :, columns] = activate(*values)
        for copy in stores(at, size, place):
            copy.start()

    row = 0
    for part, count in enumerate(counts):
        load(x_refs[part], x.at[pl.ds(row, count)])
        row += count
    start_piece(*tiles[0], 0)
    first_loads = len(loads)
    start_piece(*tiles[1], 1)
    row = 0
    for part, count in enumerate(counts):
        load(low_refs[part], low.at[:, pl.ds(row, count)])
        row += count
    for side in range(2):
        load(up_ref.at[:, side, :, pl.ds(left, narrow)], maps.at[side, 0])
    if terms:
        count = rows // terms
        for side in range(2):
            for part in range(terms):
                load(term_refs[side * terms + part], term.at[side, pl.ds(part * count, count)])
    if finish:
        row = 0
        for part, count in enumerate(counts):
            here = pl.ds(row, count)
            load(far_refs[part], far.at[:, here])
            load(pick_refs[part], pick.at[here])
            row += count
        load(scale_ref, scale)
    wait_loads(0, first_loads)

    def rest():
        start_piece(*tiles[2], 2)
        wait_loads(first_loads, len(loads))
        for side in range(2):
            maps[side, 1] = maps[side, 0]

    tile(*tiles[0], 0, rest)

    @pl.loop(1, whole)
    def _(place):
        at = pl.multiple_of(place * TILE, TILE)

        @pl.when(place + 2 < whole)
        def _():
            start_piece(pl.multiple_of(at + 2 * TILE, TILE), TILE, place + 2)

        if whole < len(tiles):
            @pl.when(place + 2 == whole)
            def _():
                start_piece(*tiles[whole], whole)

        tile(at, TILE, place)

    for place in range(whole, len(tiles)):
        tile(*tiles[place], place)
    for place, (at, size) in enumerate(tiles):
        for copy in stores(at, size, place):
            copy.wait()


def dot_pair(chunks, weights, adapter_out, flip, narrow, ids, out_dtype, splits=(), terms=(), finish=None, after=()):
    xs, lows, picks = zip(*chunks)
    counts = tuple(x.shape[0] for x in xs)
    rows, depth = sum(counts), xs[0].shape[1]
    tenants = adapter_out.shape[0]
    operands = [ids, *xs, *lows, *weights, adapter_out, *terms]
    if finish is not None:
        operands += [*finish[0], *picks, finish[1]]
        out_shape = [jax.ShapeDtypeStruct((rows, narrow), out_dtype)]
    elif splits:
        out_shape = [jax.ShapeDtypeStruct((count, narrow), out_dtype) for _ in range(2) for count in splits]
    else:
        out_shape = [jax.ShapeDtypeStruct((2, rows, narrow), out_dtype)]
    operands += list(after)
    few = (8, 128)
    pieces = -(-narrow // TILE)
    return pl.pallas_call(
        functools.partial(
            dot_kernel, flip, counts, splits, len(terms) // 2, counts if finish is not None else (), narrow
        ),
        out_shape=out_shape,
        grid_spec=pltpu.PrefetchScalarGridSpec(
            num_scalar_prefetch=1,
            grid=(1,),
            in_specs=[ANY] * (len(operands) - 1),
            out_specs=[ANY] * len(out_shape),
            scratch_shapes=[
                pltpu.VMEM((rows, depth), jnp.bfloat16),
                pltpu.VMEM((2, rows, 256), jnp.bfloat16),
                pltpu.VMEM((pieces, depth, 2 * TILE), jnp.bfloat16),
                pltpu.VMEM((2, 2, tenants, RANK, narrow), jnp.bfloat16),
                pltpu.VMEM((2, rows, narrow) if terms else few, jnp.bfloat16),
                pltpu.VMEM((1 if finish is not None else 2, rows, narrow), out_dtype),
                pltpu.VMEM((2, rows, narrow) if finish is not None else few, jnp.bfloat16),
                pltpu.VMEM((rows, 128) if finish is not None else few, jnp.bfloat16),
                pltpu.VMEM((2, 128, narrow) if finish is not None else few, jnp.bfloat16),
                pltpu.SemaphoreType.DMA((4 * len(xs) + 8,)),
                pltpu.SemaphoreType.DMA((2, pieces)),
                pltpu.SemaphoreType.DMA((pieces, 4)),
            ],
        ),
        compiler_params=pltpu.CompilerParams(vmem_limit_bytes=VMEM_LIMIT),
        cost_estimate=COST,
        name="finish_dots" if finish is not None else "dot_pair",
    )(*operands)


def last_kernel(mx_count, first, ids, rows, tenants, sums, far, pick, scale, earlier, out_ref, table, held):
    block = pl.program_id(0)

    @pl.when(block == 0)
    def _():
        fill_table(table, ids, rows, tenants, mx_count)
        held[0:first, :] = earlier[...]
        held[LIVE_ROWS:, :] = jnp.zeros((BLOCK_ROWS, held.shape[1]), held.dtype)
        columns = held.shape[1]

        @pl.loop(0, far.shape[1] // 64)
        def _(tile):
            here = pl.ds(pl.multiple_of(tile * 64, 64), 64)
            there = pl.ds(pl.multiple_of(first + tile * 64, 64), 64)
            for left in range(0, columns, TILE):
                right = min(left + TILE, columns)
                pre = [
                    (sums[side, here, left:right] + far[side, here, left:right].astype(jnp.float32))
                    * jnp.dot(pick[here, :], scale[side, :, left:right], preferred_element_type=jnp.float32)
                    for side in range(2)
                ]
                held[there, left:right] = activate(*pre)

    def find(slot, start):
        return jnp.where(table[3, slot] == block, table[0, slot], start)

    start = lax.fori_loop(0, len(SLOTS), find, jnp.int32(0))
    count = rows[block]
    base = pl.multiple_of(jnp.minimum(start // BLOCK_ROWS * BLOCK_ROWS, LIVE_ROWS - BLOCK_ROWS), BLOCK_ROWS)
    shape = (BLOCK_ROWS, 2 * BLOCK_ROWS)
    position = lax.broadcasted_iota(jnp.int32, shape, 0)
    column = lax.broadcasted_iota(jnp.int32, shape, 1) + base
    chosen = (position < count) & (column == position + start)
    out_ref[...] = jnp.dot(
        chosen.astype(jnp.bfloat16), held[pl.ds(base, 2 * BLOCK_ROWS), :], preferred_element_type=jnp.float32
    ).astype(jnp.bfloat16)


def last_rows(mx_count, first, scalars, sums, far, pick, scale, earlier, blocks):
    narrow = far.shape[2]
    operands = (sums, far, pick, scale, earlier)
    return pl.pallas_call(
        functools.partial(last_kernel, mx_count, first),
        out_shape=jax.ShapeDtypeStruct((blocks * BLOCK_ROWS, narrow), jnp.bfloat16),
        grid_spec=pltpu.PrefetchScalarGridSpec(
            num_scalar_prefetch=3,
            grid=(blocks,),
            in_specs=[
                pl.BlockSpec(part.shape, lambda i, *_, dims=part.ndim: (0,) * dims) for part in operands
            ],
            out_specs=pl.BlockSpec((BLOCK_ROWS, narrow), lambda i, *_: (i, 0)),
            scratch_shapes=[
                pltpu.SMEM((4, len(SLOTS)), jnp.int32),
                pltpu.VMEM((LIVE_ROWS + BLOCK_ROWS, narrow), jnp.bfloat16),
            ],
        ),
        compiler_params=pltpu.CompilerParams(vmem_limit_bytes=VMEM_LIMIT),
        cost_estimate=COST,
        name="last_rows",
    )(*scalars, *operands)


def quarter(array, index, narrow):
    return lax.dynamic_slice_in_dim(array, index * narrow, narrow, array.ndim - 1)


def pipelined(
    tokens, w_gate, w_up, adapter_in, adapter_out, magnitude, partial_norms, block_tenant, block_rows
):
    mx_count = lax.axis_size("mx")
    my_count = lax.axis_size("my")
    narrow = w_gate.shape[1] // my_count
    mine = lax.axis_index("my")
    ids = jnp.stack([lax.axis_index("mx"), mine]).astype(jnp.int32)
    scalars = (ids, block_rows, block_tenant)
    near = [(i, i ^ 1) for i in range(my_count)]
    across = [(i, i ^ 2) for i in range(my_count)]

    def hop(block, distance, least=0):
        if distance > 0:
            pairs = [(i, i + distance) for i in range(least, mx_count - distance)]
        else:
            pairs = [(i, i + distance) for i in range(-distance, mx_count - least)]
        return lax.ppermute(block, "mx", pairs)

    first_up, first_down = hop(tokens, 1), hop(tokens, -1)
    blocks = [tokens, first_up, first_down, hop(first_up, 1, 1), hop(first_down, -1, 1)]

    norms = partial_norms[0]
    pair = jnp.stack([quarter(norms, mine, narrow), quarter(norms, mine ^ 2, narrow)])
    other = jnp.stack([quarter(norms, mine ^ 1, narrow), quarter(norms, mine ^ 3, narrow)])
    pair = pair + lax.ppermute(other, "my", near)
    norm_total = pair[0] + lax.ppermute(pair[1], "my", across)
    scale = quarter(magnitude, mine, narrow) * lax.rsqrt(norm_total)
    scale = jnp.transpose(scale, (1, 0, 2))
    high = lax.reduce_precision(scale, 8, 7)
    middle = lax.reduce_precision(scale - high, 8, 7)
    rest = scale - high - middle
    scale = jnp.concatenate(
        [high, middle, rest, jnp.zeros((2, 128 - 3 * scale.shape[1], narrow), jnp.float32)], axis=1
    ).astype(jnp.bfloat16)

    down = jnp.transpose(adapter_in, (0, 2, 1)).reshape(-1, adapter_in.shape[1])

    dots = functools.partial(
        dot_pair, weights=(w_gate, w_up), adapter_out=adapter_out, narrow=narrow, ids=ids
    )

    def swap(parts, pairs):
        return [lax.ppermute(part, "my", pairs) for part in parts]

    def send_far(chunk, pieces=1):
        rows = chunk[0].shape[0] // pieces
        parts = dots([chunk], flip=3, out_dtype=jnp.bfloat16, splits=(rows,) * pieces)
        got = swap(parts, near)
        part, = dots([chunk], flip=2, out_dtype=jnp.bfloat16, terms=got)
        return part, lax.ppermute(part, "my", across)

    *chunk0, = pack_rows(mx_count, CHUNKS[0], scalars, blocks[:3], down, after=(scale,))
    mark, far0 = send_far(chunk0)

    *chunk1, second, third = pack_rows(
        mx_count, CHUNKS[1], scalars, blocks, down, after=(mark,), passed=(3, 4)
    )
    blocks = [*blocks[:3], second, third, hop(second, 1, 2), hop(third, -1, 2)]
    mark, far1 = send_far(chunk1)

    *chunk2, = pack_rows(mx_count, CHUNKS[2], scalars, blocks, down, after=(mark, far0))
    mark, far2 = send_far(chunk2, 2)

    first, last = CHUNKS[2][:2]
    parts = dots([chunk0, chunk1], flip=1, out_dtype=jnp.bfloat16, splits=(first,), after=(mark, far1))
    early = swap(parts, near)
    parts = dots([chunk2], flip=1, out_dtype=jnp.bfloat16, splits=(last,), after=(parts[0],))
    late = swap(parts, near)
    hidden, = dots(
        [chunk0, chunk1], flip=0, out_dtype=jnp.bfloat16, terms=early, finish=((far0, far1), scale),
        after=(parts[0],),
    )
    sums, = dots([chunk2], flip=0, out_dtype=jnp.float32, terms=late, after=(hidden,))
    return last_rows(mx_count, first, scalars, sums, far2, chunk2[2], scale, hidden, block_rows.shape[0])


def adapter_low(rows_piece, aligned_row_total, adapter_in, block_tenant):
    row_count = rows_piece.shape[0]
    seg_rows = math.gcd(math.gcd(row_count, BLOCK_ROWS), aligned_row_total)
    seg_count = row_count // seg_rows
    seg_block = jnp.arange(seg_count, dtype=jnp.int32) * seg_rows // BLOCK_ROWS
    tenant_tables = adapter_in[block_tenant[seg_block]]
    grouped = rows_piece.reshape(seg_count, seg_rows, rows_piece.shape[1])
    low_terms = jnp.einsum(
        "skd,sdr->skr", grouped, tenant_tables, preferred_element_type=jnp.float32
    )
    return low_terms.reshape(row_count, tenant_tables.shape[2])


def finish_plain(
    summed, reduced_rank_factor, norm_total, mag_cols, adapter_cols, first_row, block_tenant, block_rows
):
    row_count = summed.shape[0]
    col_count = summed.shape[2]
    seg_rows = math.gcd(row_count, BLOCK_ROWS)
    seg_count = row_count // seg_rows
    seg_block = (first_row + jnp.arange(seg_count, dtype=jnp.int32) * seg_rows) // BLOCK_ROWS
    tenants = block_tenant[seg_block]
    col_scale = mag_cols * lax.rsqrt(norm_total)
    seg_scale = col_scale[tenants]
    seg_tables = adapter_cols[tenants]
    low_pair = reduced_rank_factor.reshape(seg_count, seg_rows, 2, RANK)
    adapted = jnp.einsum(
        "skpr,sprc->skpc", low_pair, seg_tables, preferred_element_type=jnp.float32
    )
    pre_act = (summed.reshape(seg_count, seg_rows, 2, col_count) + adapted) * seg_scale[:, None]
    hidden = jax.nn.silu(pre_act[:, :, 0]) * pre_act[:, :, 1]
    offsets = (first_row + jnp.arange(row_count, dtype=jnp.int32)).reshape(
        seg_count, seg_rows
    ) % BLOCK_ROWS
    live_mask = offsets < block_rows[seg_block][:, None]
    hidden = jnp.where(live_mask[:, :, None], hidden, jnp.zeros_like(hidden))
    return hidden.reshape(row_count, col_count).astype(jnp.bfloat16)


def plain(
    tokens, w_gate, w_up, adapter_in, adapter_out, magnitude, partial_norms, block_tenant, block_rows
):
    local_rows = tokens.shape[0]
    col_local = w_gate.shape[1]
    my_count = lax.axis_size("my")
    device_position = lax.axis_index("my")
    rows_piece = lax.all_gather(tokens, "mx", axis=0, tiled=True)
    gate_part = jnp.dot(rows_piece, w_gate, preferred_element_type=jnp.float32)
    up_part = jnp.dot(rows_piece, w_up, preferred_element_type=jnp.float32)
    main_part = jnp.stack((gate_part, up_part), axis=1)
    low_terms = adapter_low(rows_piece, local_rows, adapter_in, block_tenant)
    reduced_rank_factor = lax.psum(low_terms, "my").astype(jnp.bfloat16)
    summed = lax.psum_scatter(main_part, "my", scatter_dimension=2, tiled=True)
    norm_total = lax.psum_scatter(partial_norms[0], "my", scatter_dimension=2, tiled=True)
    narrow = col_local // my_count
    mag_cols = lax.dynamic_slice_in_dim(magnitude, device_position * narrow, narrow, 2)
    adapter_cols = lax.dynamic_slice_in_dim(adapter_out, device_position * narrow, narrow, 3)
    return finish_plain(
        summed, reduced_rank_factor, norm_total, mag_cols, adapter_cols, 0, block_tenant, block_rows
    )


def on_device(tokens, w_gate, *rest):
    my_count = lax.axis_size("my")
    fits = (
        my_count == 4
        and lax.axis_size("mx") == 4
        and tokens.shape[0] == 2 * BLOCK_ROWS
        and tokens.shape[1] % 512 == 0
        and w_gate.shape[1] % (my_count * 128) == 0
    )
    return (pipelined if fits else plain)(tokens, w_gate, *rest)


def solution(mesh):
    return jax.shard_map(
        on_device,
        mesh=mesh,
        in_specs=(
            P(("groups", "mx"), "my"),
            P("my", "mx"),
            P("my", "mx"),
            P(None, "my", None),
            P(None, None, None, "mx"),
            P(None, None, "mx"),
            P("my", None, None, "mx"),
            P("groups"),
            P("groups"),
        ),
        out_specs=P("groups", ("mx", "my")),
        check_vma=False,
    )
```

```python
import functools
import math

import jax
import jax.numpy as jnp
from jax import lax
from jax.experimental import pallas as pl
from jax.experimental.pallas import tpu as pltpu
from jax.sharding import PartitionSpec as P

RANK = 16
BLOCK_ROWS = 128
LIVE_ROWS = 768
STEP_DEPTH = 512
TILE = 512
VMEM_LIMIT = 60 * 1024 * 1024

SLOTS = tuple((distance, half) for distance in (0, -1, 1, -2, 2, -3, 3) for half in range(2))
CHUNKS = ((0, 256, 6), (256, 192, 10), (448, 320, 14))
ANY = pl.BlockSpec(memory_space=pl.ANY)
COST = pl.CostEstimate(flops=0, bytes_accessed=0, transcendentals=0)
LONG = pl.CostEstimate(flops=10**12, bytes_accessed=0, transcendentals=0)


def fill_table(table, ids, rows, tenants, mx_count):
    start = jnp.int32(0)
    for slot, (distance, half) in enumerate(SLOTS):
        source = ids[0] + distance
        valid = (source >= 0) & (source < mx_count)
        block = jnp.clip(source, 0, mx_count - 1) * 2 + half
        count = jnp.where(valid, rows[block], 0)
        table[0, slot] = start
        table[1, slot] = count
        table[2, slot] = tenants[block]
        table[3, slot] = jnp.where(valid, block, -1)
        start = start + count


def pack_kernel(mx_count, first, rows_out, slots, passed, ids, rows, tenants, *refs):
    token_refs, down_ref = refs[:slots // 2], refs[slots // 2]
    outs, scratch = refs[-9 - passed:-6], refs[-6:]
    x_ref, low_ref, pick_ref = outs[:3]
    table, buffer, down, acc, sems, down_sem = scratch
    fill_table(table, ids, rows, tenants, mx_count)

    def needed(slot):
        start, count = table[0, slot], table[1, slot]
        return (count > 0) & (start < first + rows_out) & (start + count > first)

    for slot in range(slots):
        @pl.when(needed(slot))
        def _():
            here = pl.ds(slot % 2 * BLOCK_ROWS, BLOCK_ROWS)
            pltpu.make_async_copy(token_refs[slot // 2].at[here], buffer.at[slot], sems.at[slot]).start()

    down_copy = pltpu.make_async_copy(down_ref, down, down_sem)
    down_copy.start()
    acc[...] = jnp.zeros_like(acc)

    @pl.loop(0, slots)
    def _(slot):
        @pl.when(needed(slot))
        def _():
            start, count = table[0, slot], table[1, slot]
            pltpu.make_async_copy(buffer.at[slot], buffer.at[slot], sems.at[slot]).wait()
            target = lax.broadcasted_iota(jnp.int32, (rows_out, BLOCK_ROWS), 0) + first
            position = lax.broadcasted_iota(jnp.int32, (rows_out, BLOCK_ROWS), 1)
            chosen = (position < count) & (target == position + start)
            acc[...] += jnp.dot(
                chosen.astype(jnp.bfloat16), buffer[slot], preferred_element_type=jnp.float32
            )

    x_ref[...] = acc[...].astype(jnp.bfloat16)
    row = lax.broadcasted_iota(jnp.int32, (rows_out, 128), 0) + first

    def own(slot, tenant):
        start, count = table[0, slot], table[1, slot]
        return jnp.where((row >= start) & (row < start + count), table[2, slot], tenant)

    tenant = lax.fori_loop(0, slots, own, jnp.full((rows_out, 128), -1, jnp.int32))
    lane = lax.broadcasted_iota(jnp.int32, (rows_out, 128), 1)
    pick_ref[...] = ((lane % 8 == tenant) & (lane < 24)).astype(jnp.bfloat16)

    down_copy.wait()
    low = lax.dot_general(x_ref[...], down[...], (((1,), (1,)), ((), ())), preferred_element_type=jnp.float32)
    owner = jnp.concatenate([lane // 32, lane // 32 + 4], axis=1)
    low = jnp.where(owner == jnp.concatenate([tenant, tenant], axis=1), low, 0.0)
    high = low.astype(jnp.bfloat16)
    rest = (low - high.astype(jnp.float32)).astype(jnp.bfloat16)
    source = lax.broadcasted_iota(jnp.int32, (256, 256), 0)
    goal = lax.broadcasted_iota(jnp.int32, (256, 256), 1)
    place = source // 32 * RANK + source % RANK
    for side in range(2):
        mine = source // RANK % 2 == side
        to_high = (mine & (place == goal)).astype(jnp.bfloat16)
        to_rest = (mine & (place + 128 == goal)).astype(jnp.bfloat16)
        moved = jnp.dot(high, to_high, preferred_element_type=jnp.float32)
        moved += jnp.dot(rest, to_rest, preferred_element_type=jnp.float32)
        low_ref[side] = moved.astype(jnp.bfloat16)


def pack_rows(mx_count, chunk, scalars, tokens, down, after=(), passed=(), cost=COST):
    first, rows_out, slots = chunk
    width = down.shape[1]
    outs = [
        jax.ShapeDtypeStruct((rows_out, width), jnp.bfloat16),
        jax.ShapeDtypeStruct((2, rows_out, 256), jnp.bfloat16),
        jax.ShapeDtypeStruct((rows_out, 128), jnp.bfloat16),
    ]
    out_specs = [
        pl.BlockSpec((rows_out, width), lambda i, *_: (0, 0)),
        pl.BlockSpec((2, rows_out, 256), lambda i, *_: (0, 0, 0)),
        pl.BlockSpec((rows_out, 128), lambda i, *_: (0, 0)),
    ] + [ANY] * len(passed)
    return pl.pallas_call(
        functools.partial(pack_kernel, mx_count, first, rows_out, slots, len(passed)),
        out_shape=outs + [jax.ShapeDtypeStruct(tokens[i].shape, tokens[i].dtype) for i in passed],
        grid_spec=pltpu.PrefetchScalarGridSpec(
            num_scalar_prefetch=3,
            grid=(1,),
            in_specs=[ANY] * (len(tokens) + 1 + len(after)),
            out_specs=out_specs,
            scratch_shapes=[
                pltpu.SMEM((4, len(SLOTS)), jnp.int32),
                pltpu.VMEM((slots, BLOCK_ROWS, width), jnp.bfloat16),
                pltpu.VMEM(down.shape, jnp.bfloat16),
                pltpu.VMEM((rows_out, width), jnp.float32),
                pltpu.SemaphoreType.DMA((slots,)),
                pltpu.SemaphoreType.DMA,
            ],
        ),
        input_output_aliases={3 + place: 3 + i for i, place in enumerate(passed)},
        compiler_params=pltpu.CompilerParams(vmem_limit_bytes=VMEM_LIMIT),
        cost_estimate=cost,
        name="pack_rows",
    )(*scalars, *tokens, down, *after)


def activate(gate, up):
    return (gate * (1.0 / (1.0 + jnp.exp(-gate))) * up).astype(jnp.bfloat16)


def dot_kernel(flip, counts, splits, terms, far_counts, narrow, ids, *refs):
    parts = len(counts)
    finish = len(far_counts) > 0
    x_refs, low_refs, refs = refs[:parts], refs[parts:2 * parts], refs[2 * parts:]
    w_refs, up_ref, refs = refs[:2], refs[2], refs[3:]
    term_refs, refs = refs[:2 * terms], refs[2 * terms:]
    if finish:
        far_refs, refs = refs[:parts], refs[parts:]
        pick_refs, scale_ref, refs = refs[:parts], refs[parts], refs[parts + 1:]
    x, low, w, maps, term, acc, out, far, pick, scale, in_sem, w_sem, out_sem = refs[-13:]
    outs = refs[-13 - max(1, 2 * len(splits)):-13]
    rows, depth = x.shape
    steps = depth // STEP_DEPTH
    left = pl.multiple_of((ids[1] ^ flip) * narrow, 128)
    tiles = [(at, min(TILE, narrow - at)) for at in range(0, narrow, TILE)]
    loads = []

    def load(source, target):
        copy = pltpu.make_async_copy(source, target, in_sem.at[len(loads)])
        copy.start()
        loads.append(copy)

    def piece(side, step):
        return pltpu.make_async_copy(
            w_refs[side].at[pl.ds(step * STEP_DEPTH, STEP_DEPTH), pl.ds(left, narrow)],
            w.at[side, step], w_sem.at[side, step],
        )

    def start_step(step):
        for side in range(2):
            piece(side, step).start()

    def stores(place):
        at, size = tiles[place]
        columns = pl.ds(at, size)
        result = acc if outs[0].dtype == jnp.float32 else out
        if finish:
            pairs = [(result.at[0, :, columns], outs[0].at[:, columns])]
        elif not splits:
            pairs = [(result.at[side, :, columns], outs[0].at[side, :, columns]) for side in range(2)]
        else:
            pairs = []
            for side in range(2):
                row = 0
                for part, count in enumerate(splits):
                    target = outs[side * len(splits) + part].at[:, columns]
                    pairs.append((result.at[side, pl.ds(row, count), columns], target))
                    row += count
        return [
            pltpu.make_async_copy(source, target, out_sem.at[place, i]) for i, (source, target) in enumerate(pairs)
        ]

    def part_dot(side, step, columns):
        depths = pl.ds(step * STEP_DEPTH, STEP_DEPTH)
        return jnp.dot(x[:, depths], w[side, step, :, columns], preferred_element_type=jnp.float32)

    row = 0
    for part, count in enumerate(counts):
        load(x_refs[part], x.at[pl.ds(row, count)])
        row += count
    first_loads = len(loads)
    start_step(0)
    start_step(1)
    row = 0
    for part, count in enumerate(counts):
        load(low_refs[part], low.at[:, pl.ds(row, count)])
        row += count
    for side in range(2):
        load(up_ref.at[:, side, :, pl.ds(left, narrow)], maps.at[side, 0])
    if terms:
        count = rows // terms
        for side in range(2):
            for part in range(terms):
                load(term_refs[side * terms + part], term.at[side, pl.ds(part * count, count)])
    if finish:
        row = 0
        for part, count in enumerate(counts):
            here = pl.ds(row, count)
            load(far_refs[part], far.at[:, here])
            load(pick_refs[part], pick.at[here])
            row += count
        load(scale_ref, scale)

    for copy in loads[:first_loads]:
        copy.wait()
    for side in range(2):
        piece(side, 0).wait()
        if steps > 2:
            piece(side, 2).start()
        acc[side] = part_dot(side, 0, slice(None))

    @pl.loop(1, steps - 1)
    def _(step):
        for side in range(2):
            piece(side, step).wait()

            @pl.when(step + 2 < steps)
            def _():
                piece(side, step + 2).start()

            depths = pl.ds(pl.multiple_of(step * STEP_DEPTH, STEP_DEPTH), STEP_DEPTH)
            acc[side] += jnp.dot(x[:, depths], w[side, step], preferred_element_type=jnp.float32)

    for copy in loads[first_loads:]:
        copy.wait()
    for side in range(2):
        maps[side, 1] = maps[side, 0]
        piece(side, steps - 1).wait()
    for place, (at, size) in enumerate(tiles):
        columns = slice(at, at + size)
        values = []
        for side in range(2):
            value = acc[side, :, columns] + part_dot(side, steps - 1, columns)
            value += jnp.dot(
                low[side], maps[side, :, :, :, columns].reshape(256, size), preferred_element_type=jnp.float32
            )
            if terms:
                value += term[side, :, columns].astype(jnp.float32)
            if finish:
                value += far[side, :, columns].astype(jnp.float32)
                value *= jnp.dot(pick[...], scale[side, :, columns], preferred_element_type=jnp.float32)
                values.append(value)
            elif outs[0].dtype == jnp.float32:
                acc[side, :, columns] = value
            else:
                out[side, :, columns] = value.astype(out.dtype)
        if finish:
            out[0, :, columns] = activate(*values)
        for copy in stores(place):
            copy.start()
    for place in range(len(tiles)):
        for copy in stores(place):
            copy.wait()


def dot_pair(chunks, weights, adapter_out, flip, narrow, ids, out_dtype, splits=(), terms=(), finish=None, after=()):
    xs, lows, picks = zip(*chunks)
    counts = tuple(x.shape[0] for x in xs)
    rows, depth = sum(counts), xs[0].shape[1]
    tenants = adapter_out.shape[0]
    operands = [ids, *xs, *lows, *weights, adapter_out, *terms]
    if finish is not None:
        operands += [*finish[0], *picks, finish[1]]
        out_shape = [jax.ShapeDtypeStruct((rows, narrow), out_dtype)]
    elif splits:
        out_shape = [jax.ShapeDtypeStruct((count, narrow), out_dtype) for _ in range(2) for count in splits]
    else:
        out_shape = [jax.ShapeDtypeStruct((2, rows, narrow), out_dtype)]
    operands += list(after)
    few = (8, 128)
    steps = depth // STEP_DEPTH
    out_few = out_dtype == jnp.float32
    return pl.pallas_call(
        functools.partial(
            dot_kernel, flip, counts, splits, len(terms) // 2, counts if finish is not None else (), narrow
        ),
        out_shape=out_shape,
        grid_spec=pltpu.PrefetchScalarGridSpec(
            num_scalar_prefetch=1,
            grid=(1,),
            in_specs=[ANY] * (len(operands) - 1),
            out_specs=[ANY] * len(out_shape),
            scratch_shapes=[
                pltpu.VMEM((rows, depth), jnp.bfloat16),
                pltpu.VMEM((2, rows, 256), jnp.bfloat16),
                pltpu.VMEM((2, steps, STEP_DEPTH, narrow), jnp.bfloat16),
                pltpu.VMEM((2, 2, tenants, RANK, narrow), jnp.bfloat16),
                pltpu.VMEM((2, rows, narrow) if terms else few, jnp.bfloat16),
                pltpu.VMEM((2, rows, narrow), jnp.float32),
                pltpu.VMEM(few if out_few else (1 if finish is not None else 2, rows, narrow), jnp.bfloat16),
                pltpu.VMEM((2, rows, narrow) if finish is not None else few, jnp.bfloat16),
                pltpu.VMEM((rows, 128) if finish is not None else few, jnp.bfloat16),
                pltpu.VMEM((2, 128, narrow) if finish is not None else few, jnp.bfloat16),
                pltpu.SemaphoreType.DMA((4 * len(xs) + 8,)),
                pltpu.SemaphoreType.DMA((2, steps)),
                pltpu.SemaphoreType.DMA((-(-narrow // TILE), 4)),
            ],
        ),
        compiler_params=pltpu.CompilerParams(vmem_limit_bytes=VMEM_LIMIT),
        cost_estimate=COST,
        name="finish_dots" if finish is not None else "dot_pair",
    )(*operands)


def last_kernel(mx_count, first, ids, rows, tenants, sums, far, pick, scale, earlier, out_ref, table, held):
    block = pl.program_id(0)

    @pl.when(block == 0)
    def _():
        fill_table(table, ids, rows, tenants, mx_count)
        held[0:first, :] = earlier[...]
        held[LIVE_ROWS:, :] = jnp.zeros((BLOCK_ROWS, held.shape[1]), held.dtype)
        columns = held.shape[1]

        @pl.loop(0, far.shape[1] // 64)
        def _(tile):
            here = pl.ds(pl.multiple_of(tile * 64, 64), 64)
            there = pl.ds(pl.multiple_of(first + tile * 64, 64), 64)
            for left in range(0, columns, TILE):
                right = min(left + TILE, columns)
                pre = [
                    (sums[side, here, left:right] + far[side, here, left:right].astype(jnp.float32))
                    * jnp.dot(pick[here, :], scale[side, :, left:right], preferred_element_type=jnp.float32)
                    for side in range(2)
                ]
                held[there, left:right] = activate(*pre)

    def find(slot, start):
        return jnp.where(table[3, slot] == block, table[0, slot], start)

    start = lax.fori_loop(0, len(SLOTS), find, jnp.int32(0))
    count = rows[block]
    base = pl.multiple_of(jnp.minimum(start // BLOCK_ROWS * BLOCK_ROWS, LIVE_ROWS - BLOCK_ROWS), BLOCK_ROWS)
    shape = (BLOCK_ROWS, 2 * BLOCK_ROWS)
    position = lax.broadcasted_iota(jnp.int32, shape, 0)
    column = lax.broadcasted_iota(jnp.int32, shape, 1) + base
    chosen = (position < count) & (column == position + start)
    out_ref[...] = jnp.dot(
        chosen.astype(jnp.bfloat16), held[pl.ds(base, 2 * BLOCK_ROWS), :], preferred_element_type=jnp.float32
    ).astype(jnp.bfloat16)


def last_rows(mx_count, first, scalars, sums, far, pick, scale, earlier, blocks):
    narrow = far.shape[2]
    operands = (sums, far, pick, scale, earlier)
    return pl.pallas_call(
        functools.partial(last_kernel, mx_count, first),
        out_shape=jax.ShapeDtypeStruct((blocks * BLOCK_ROWS, narrow), jnp.bfloat16),
        grid_spec=pltpu.PrefetchScalarGridSpec(
            num_scalar_prefetch=3,
            grid=(blocks,),
            in_specs=[
                pl.BlockSpec(part.shape, lambda i, *_, dims=part.ndim: (0,) * dims) for part in operands
            ],
            out_specs=pl.BlockSpec((BLOCK_ROWS, narrow), lambda i, *_: (i, 0)),
            scratch_shapes=[
                pltpu.SMEM((4, len(SLOTS)), jnp.int32),
                pltpu.VMEM((LIVE_ROWS + BLOCK_ROWS, narrow), jnp.bfloat16),
            ],
        ),
        compiler_params=pltpu.CompilerParams(vmem_limit_bytes=VMEM_LIMIT),
        cost_estimate=COST,
        name="last_rows",
    )(*scalars, *operands)


def quarter(array, index, narrow):
    return lax.dynamic_slice_in_dim(array, index * narrow, narrow, array.ndim - 1)


def pipelined(
    tokens, w_gate, w_up, adapter_in, adapter_out, magnitude, partial_norms, block_tenant, block_rows
):
    mx_count = lax.axis_size("mx")
    my_count = lax.axis_size("my")
    narrow = w_gate.shape[1] // my_count
    mine = lax.axis_index("my")
    ids = jnp.stack([lax.axis_index("mx"), mine]).astype(jnp.int32)
    scalars = (ids, block_rows, block_tenant)
    near = [(i, i ^ 1) for i in range(my_count)]
    across = [(i, i ^ 2) for i in range(my_count)]

    def hop(block, distance, least=0):
        if distance > 0:
            pairs = [(i, i + distance) for i in range(least, mx_count - distance)]
        else:
            pairs = [(i, i + distance) for i in range(-distance, mx_count - least)]
        return lax.ppermute(block, "mx", pairs)

    first_up, first_down = hop(tokens, 1), hop(tokens, -1)
    blocks = [tokens, first_up, first_down, hop(first_up, 1, 1), hop(first_down, -1, 1)]

    norms = partial_norms[0]
    pair = jnp.stack([quarter(norms, mine, narrow), quarter(norms, mine ^ 2, narrow)])
    other = jnp.stack([quarter(norms, mine ^ 1, narrow), quarter(norms, mine ^ 3, narrow)])
    pair = pair + lax.ppermute(other, "my", near)
    norm_total = pair[0] + lax.ppermute(pair[1], "my", across)
    scale = quarter(magnitude, mine, narrow) * lax.rsqrt(norm_total)
    scale = jnp.transpose(scale, (1, 0, 2))
    high = lax.reduce_precision(scale, 8, 7)
    middle = lax.reduce_precision(scale - high, 8, 7)
    rest = scale - high - middle
    scale = jnp.concatenate(
        [high, middle, rest, jnp.zeros((2, 128 - 3 * scale.shape[1], narrow), jnp.float32)], axis=1
    ).astype(jnp.bfloat16)

    down = jnp.transpose(adapter_in, (0, 2, 1)).reshape(-1, adapter_in.shape[1])

    dots = functools.partial(
        dot_pair, weights=(w_gate, w_up), adapter_out=adapter_out, narrow=narrow, ids=ids
    )

    def swap(parts, pairs):
        return [lax.ppermute(part, "my", pairs) for part in parts]

    def send_far(chunk, pieces=1):
        rows = chunk[0].shape[0] // pieces
        parts = dots([chunk], flip=3, out_dtype=jnp.bfloat16, splits=(rows,) * pieces)
        got = swap(parts, near)
        part, = dots([chunk], flip=2, out_dtype=jnp.bfloat16, terms=got)
        return part, lax.ppermute(part, "my", across)

    *chunk0, = pack_rows(mx_count, CHUNKS[0], scalars, blocks[:3], down, after=(scale,))
    mark, far0 = send_far(chunk0)

    *chunk1, second, third = pack_rows(
        mx_count, CHUNKS[1], scalars, blocks, down, after=(mark,), passed=(3, 4), cost=LONG
    )
    blocks = [*blocks[:3], second, third, hop(second, 1, 2), hop(third, -1, 2)]
    mark, far1 = send_far(chunk1)

    *chunk2, = pack_rows(mx_count, CHUNKS[2], scalars, blocks, down, after=(mark, far0))
    mark, far2 = send_far(chunk2, 2)

    first, last = CHUNKS[2][:2]
    parts = dots([chunk0, chunk1], flip=1, out_dtype=jnp.bfloat16, splits=(first,), after=(mark, far1))
    early = swap(parts, near)
    parts = dots([chunk2], flip=1, out_dtype=jnp.bfloat16, splits=(last,), after=(parts[0],))
    late = swap(parts, near)
    hidden, = dots(
        [chunk0, chunk1], flip=0, out_dtype=jnp.bfloat16, terms=early, finish=((far0, far1), scale),
        after=(parts[0],),
    )
    sums, = dots([chunk2], flip=0, out_dtype=jnp.float32, terms=late, after=(hidden,))
    return last_rows(mx_count, first, scalars, sums, far2, chunk2[2], scale, hidden, block_rows.shape[0])


def adapter_low(rows_piece, aligned_row_total, adapter_in, block_tenant):
    row_count = rows_piece.shape[0]
    seg_rows = math.gcd(math.gcd(row_count, BLOCK_ROWS), aligned_row_total)
    seg_count = row_count // seg_rows
    seg_block = jnp.arange(seg_count, dtype=jnp.int32) * seg_rows // BLOCK_ROWS
    tenant_tables = adapter_in[block_tenant[seg_block]]
    grouped = rows_piece.reshape(seg_count, seg_rows, rows_piece.shape[1])
    low_terms = jnp.einsum(
        "skd,sdr->skr", grouped, tenant_tables, preferred_element_type=jnp.float32
    )
    return low_terms.reshape(row_count, tenant_tables.shape[2])


def finish_plain(
    summed, reduced_rank_factor, norm_total, mag_cols, adapter_cols, first_row, block_tenant, block_rows
):
    row_count = summed.shape[0]
    col_count = summed.shape[2]
    seg_rows = math.gcd(row_count, BLOCK_ROWS)
    seg_count = row_count // seg_rows
    seg_block = (first_row + jnp.arange(seg_count, dtype=jnp.int32) * seg_rows) // BLOCK_ROWS
    tenants = block_tenant[seg_block]
    col_scale = mag_cols * lax.rsqrt(norm_total)
    seg_scale = col_scale[tenants]
    seg_tables = adapter_cols[tenants]
    low_pair = reduced_rank_factor.reshape(seg_count, seg_rows, 2, RANK)
    adapted = jnp.einsum(
        "skpr,sprc->skpc", low_pair, seg_tables, preferred_element_type=jnp.float32
    )
    pre_act = (summed.reshape(seg_count, seg_rows, 2, col_count) + adapted) * seg_scale[:, None]
    hidden = jax.nn.silu(pre_act[:, :, 0]) * pre_act[:, :, 1]
    offsets = (first_row + jnp.arange(row_count, dtype=jnp.int32)).reshape(
        seg_count, seg_rows
    ) % BLOCK_ROWS
    live_mask = offsets < block_rows[seg_block][:, None]
    hidden = jnp.where(live_mask[:, :, None], hidden, jnp.zeros_like(hidden))
    return hidden.reshape(row_count, col_count).astype(jnp.bfloat16)


def plain(
    tokens, w_gate, w_up, adapter_in, adapter_out, magnitude, partial_norms, block_tenant, block_rows
):
    local_rows = tokens.shape[0]
    col_local = w_gate.shape[1]
    my_count = lax.axis_size("my")
    device_position = lax.axis_index("my")
    rows_piece = lax.all_gather(tokens, "mx", axis=0, tiled=True)
    gate_part = jnp.dot(rows_piece, w_gate, preferred_element_type=jnp.float32)
    up_part = jnp.dot(rows_piece, w_up, preferred_element_type=jnp.float32)
    main_part = jnp.stack((gate_part, up_part), axis=1)
    low_terms = adapter_low(rows_piece, local_rows, adapter_in, block_tenant)
    reduced_rank_factor = lax.psum(low_terms, "my").astype(jnp.bfloat16)
    summed = lax.psum_scatter(main_part, "my", scatter_dimension=2, tiled=True)
    norm_total = lax.psum_scatter(partial_norms[0], "my", scatter_dimension=2, tiled=True)
    narrow = col_local // my_count
    mag_cols = lax.dynamic_slice_in_dim(magnitude, device_position * narrow, narrow, 2)
    adapter_cols = lax.dynamic_slice_in_dim(adapter_out, device_position * narrow, narrow, 3)
    return finish_plain(
        summed, reduced_rank_factor, norm_total, mag_cols, adapter_cols, 0, block_tenant, block_rows
    )


def on_device(tokens, w_gate, *rest):
    my_count = lax.axis_size("my")
    fits = (
        my_count == 4
        and lax.axis_size("mx") == 4
        and tokens.shape[0] == 2 * BLOCK_ROWS
        and tokens.shape[1] % STEP_DEPTH == 0
        and tokens.shape[1] >= 2 * STEP_DEPTH
        and w_gate.shape[1] % (my_count * 128) == 0
    )
    return (pipelined if fits else plain)(tokens, w_gate, *rest)


def solution(mesh):
    return jax.shard_map(
        on_device,
        mesh=mesh,
        in_specs=(
            P(("groups", "mx"), "my"),
            P("my", "mx"),
            P("my", "mx"),
            P(None, "my", None),
            P(None, None, None, "mx"),
            P(None, None, "mx"),
            P("my", None, None, "mx"),
            P("groups"),
            P("groups"),
        ),
        out_specs=P("groups", ("mx", "my")),
        check_vma=False,
    )
```

```python
import functools
import math

import jax
import jax.numpy as jnp
from jax import lax
from jax.experimental import pallas as pl
from jax.experimental.pallas import tpu as pltpu
from jax.sharding import PartitionSpec as P

RANK = 16
BLOCK_ROWS = 128
LIVE_ROWS = 768
STEP_DEPTH = 512
TILE = 512
VMEM_LIMIT = 60 * 1024 * 1024

SLOTS = tuple((distance, half) for distance in (0, -1, 1, -2, 2, -3, 3) for half in range(2))
CHUNKS = ((0, 256, 6), (256, 256, 10), (512, 256, 14))
ANY = pl.BlockSpec(memory_space=pl.ANY)
COST = pl.CostEstimate(flops=0, bytes_accessed=0, transcendentals=0)
LONG = pl.CostEstimate(flops=10**12, bytes_accessed=0, transcendentals=0)


def fill_table(table, ids, rows, tenants, mx_count):
    start = jnp.int32(0)
    for slot, (distance, half) in enumerate(SLOTS):
        source = ids[0] + distance
        valid = (source >= 0) & (source < mx_count)
        block = jnp.clip(source, 0, mx_count - 1) * 2 + half
        count = jnp.where(valid, rows[block], 0)
        table[0, slot] = start
        table[1, slot] = count
        table[2, slot] = tenants[block]
        table[3, slot] = jnp.where(valid, block, -1)
        start = start + count


def pack_kernel(mx_count, first, rows_out, slots, passed, ids, rows, tenants, *refs):
    token_refs, down_ref = refs[:slots // 2], refs[slots // 2]
    outs, scratch = refs[-9 - passed:-6], refs[-6:]
    x_ref, low_ref, pick_ref = outs[:3]
    table, buffer, down, acc, sems, down_sem = scratch
    fill_table(table, ids, rows, tenants, mx_count)

    def needed(slot):
        start, count = table[0, slot], table[1, slot]
        return (count > 0) & (start < first + rows_out) & (start + count > first)

    for slot in range(slots):
        @pl.when(needed(slot))
        def _():
            here = pl.ds(slot % 2 * BLOCK_ROWS, BLOCK_ROWS)
            pltpu.make_async_copy(token_refs[slot // 2].at[here], buffer.at[slot], sems.at[slot]).start()

    down_copy = pltpu.make_async_copy(down_ref, down, down_sem)
    down_copy.start()
    acc[...] = jnp.zeros_like(acc)

    @pl.loop(0, slots)
    def _(slot):
        @pl.when(needed(slot))
        def _():
            start, count = table[0, slot], table[1, slot]
            pltpu.make_async_copy(buffer.at[slot], buffer.at[slot], sems.at[slot]).wait()
            target = lax.broadcasted_iota(jnp.int32, (rows_out, BLOCK_ROWS), 0) + first
            position = lax.broadcasted_iota(jnp.int32, (rows_out, BLOCK_ROWS), 1)
            chosen = (position < count) & (target == position + start)
            acc[...] += jnp.dot(
                chosen.astype(jnp.bfloat16), buffer[slot], preferred_element_type=jnp.float32
            )

    x_ref[...] = acc[...].astype(jnp.bfloat16)
    row = lax.broadcasted_iota(jnp.int32, (rows_out, 128), 0) + first

    def own(slot, tenant):
        start, count = table[0, slot], table[1, slot]
        return jnp.where((row >= start) & (row < start + count), table[2, slot], tenant)

    tenant = lax.fori_loop(0, slots, own, jnp.full((rows_out, 128), -1, jnp.int32))
    lane = lax.broadcasted_iota(jnp.int32, (rows_out, 128), 1)
    pick_ref[...] = ((lane % 8 == tenant) & (lane < 24)).astype(jnp.bfloat16)

    down_copy.wait()
    low = lax.dot_general(x_ref[...], down[...], (((1,), (1,)), ((), ())), preferred_element_type=jnp.float32)
    owner = jnp.concatenate([lane // 32, lane // 32 + 4], axis=1)
    low = jnp.where(owner == jnp.concatenate([tenant, tenant], axis=1), low, 0.0)
    high = low.astype(jnp.bfloat16)
    rest = (low - high.astype(jnp.float32)).astype(jnp.bfloat16)
    source = lax.broadcasted_iota(jnp.int32, (256, 256), 0)
    goal = lax.broadcasted_iota(jnp.int32, (256, 256), 1)
    place = source // 32 * RANK + source % RANK
    for side in range(2):
        mine = source // RANK % 2 == side
        to_high = (mine & (place == goal)).astype(jnp.bfloat16)
        to_rest = (mine & (place + 128 == goal)).astype(jnp.bfloat16)
        moved = jnp.dot(high, to_high, preferred_element_type=jnp.float32)
        moved += jnp.dot(rest, to_rest, preferred_element_type=jnp.float32)
        low_ref[side] = moved.astype(jnp.bfloat16)


def pack_rows(mx_count, chunk, scalars, tokens, down, after=(), passed=(), cost=COST):
    first, rows_out, slots = chunk
    width = down.shape[1]
    outs = [
        jax.ShapeDtypeStruct((rows_out, width), jnp.bfloat16),
        jax.ShapeDtypeStruct((2, rows_out, 256), jnp.bfloat16),
        jax.ShapeDtypeStruct((rows_out, 128), jnp.bfloat16),
    ]
    out_specs = [
        pl.BlockSpec((rows_out, width), lambda i, *_: (0, 0)),
        pl.BlockSpec((2, rows_out, 256), lambda i, *_: (0, 0, 0)),
        pl.BlockSpec((rows_out, 128), lambda i, *_: (0, 0)),
    ] + [ANY] * len(passed)
    return pl.pallas_call(
        functools.partial(pack_kernel, mx_count, first, rows_out, slots, len(passed)),
        out_shape=outs + [jax.ShapeDtypeStruct(tokens[i].shape, tokens[i].dtype) for i in passed],
        grid_spec=pltpu.PrefetchScalarGridSpec(
            num_scalar_prefetch=3,
            grid=(1,),
            in_specs=[ANY] * (len(tokens) + 1 + len(after)),
            out_specs=out_specs,
            scratch_shapes=[
                pltpu.SMEM((4, len(SLOTS)), jnp.int32),
                pltpu.VMEM((slots, BLOCK_ROWS, width), jnp.bfloat16),
                pltpu.VMEM(down.shape, jnp.bfloat16),
                pltpu.VMEM((rows_out, width), jnp.float32),
                pltpu.SemaphoreType.DMA((slots,)),
                pltpu.SemaphoreType.DMA,
            ],
        ),
        input_output_aliases={3 + place: 3 + i for i, place in enumerate(passed)},
        compiler_params=pltpu.CompilerParams(vmem_limit_bytes=VMEM_LIMIT),
        cost_estimate=cost,
        name="pack_rows",
    )(*scalars, *tokens, down, *after)


def activate(gate, up):
    return (gate * (1.0 / (1.0 + jnp.exp(-gate))) * up).astype(jnp.bfloat16)


def dot_kernel(flip, counts, splits, terms, far_counts, narrow, ids, *refs):
    parts = len(counts)
    finish = len(far_counts) > 0
    x_refs, low_refs, refs = refs[:parts], refs[parts:2 * parts], refs[2 * parts:]
    w_refs, up_ref, refs = refs[:2], refs[2], refs[3:]
    term_refs, refs = refs[:2 * terms], refs[2 * terms:]
    if finish:
        far_refs, refs = refs[:parts], refs[parts:]
        pick_refs, scale_ref, refs = refs[:parts], refs[parts], refs[parts + 1:]
    x, low, w, maps, term, acc, out, far, pick, scale, in_sem, w_sem, out_sem = refs[-13:]
    outs = refs[-13 - max(1, 2 * len(splits)):-13]
    rows, depth = x.shape
    steps = depth // STEP_DEPTH
    left = pl.multiple_of((ids[1] ^ flip) * narrow, 128)
    tiles = [(at, min(TILE, narrow - at)) for at in range(0, narrow, TILE)]
    loads = []

    def load(source, target):
        copy = pltpu.make_async_copy(source, target, in_sem.at[len(loads)])
        copy.start()
        loads.append(copy)

    def piece(side, step):
        return pltpu.make_async_copy(
            w_refs[side].at[pl.ds(step * STEP_DEPTH, STEP_DEPTH), pl.ds(left, narrow)],
            w.at[side, step], w_sem.at[side, step],
        )

    def start_step(step):
        for side in range(2):
            piece(side, step).start()

    def stores(place):
        at, size = tiles[place]
        columns = pl.ds(at, size)
        result = acc if outs[0].dtype == jnp.float32 else out
        if finish:
            pairs = [(result.at[0, :, columns], outs[0].at[:, columns])]
        elif not splits:
            pairs = [(result.at[side, :, columns], outs[0].at[side, :, columns]) for side in range(2)]
        else:
            pairs = []
            for side in range(2):
                row = 0
                for part, count in enumerate(splits):
                    target = outs[side * len(splits) + part].at[:, columns]
                    pairs.append((result.at[side, pl.ds(row, count), columns], target))
                    row += count
        return [
            pltpu.make_async_copy(source, target, out_sem.at[place, i]) for i, (source, target) in enumerate(pairs)
        ]

    def part_dot(side, step, columns):
        depths = pl.ds(step * STEP_DEPTH, STEP_DEPTH)
        return jnp.dot(x[:, depths], w[side, step, :, columns], preferred_element_type=jnp.float32)

    row = 0
    for part, count in enumerate(counts):
        load(x_refs[part], x.at[pl.ds(row, count)])
        row += count
    first_loads = len(loads)
    start_step(0)
    start_step(1)
    row = 0
    for part, count in enumerate(counts):
        load(low_refs[part], low.at[:, pl.ds(row, count)])
        row += count
    for side in range(2):
        load(up_ref.at[:, side, :, pl.ds(left, narrow)], maps.at[side, 0])
    if terms:
        count = rows // terms
        for side in range(2):
            for part in range(terms):
                load(term_refs[side * terms + part], term.at[side, pl.ds(part * count, count)])
    if finish:
        row = 0
        for part, count in enumerate(counts):
            here = pl.ds(row, count)
            load(far_refs[part], far.at[:, here])
            load(pick_refs[part], pick.at[here])
            row += count
        load(scale_ref, scale)

    for copy in loads[:first_loads]:
        copy.wait()
    for side in range(2):
        piece(side, 0).wait()
        if steps > 2:
            piece(side, 2).start()
        acc[side] = part_dot(side, 0, slice(None))

    @pl.loop(1, steps - 1)
    def _(step):
        for side in range(2):
            piece(side, step).wait()

            @pl.when(step + 2 < steps)
            def _():
                piece(side, step + 2).start()

            depths = pl.ds(pl.multiple_of(step * STEP_DEPTH, STEP_DEPTH), STEP_DEPTH)
            acc[side] += jnp.dot(x[:, depths], w[side, step], preferred_element_type=jnp.float32)

    for copy in loads[first_loads:]:
        copy.wait()
    for side in range(2):
        maps[side, 1] = maps[side, 0]
        piece(side, steps - 1).wait()
    for place, (at, size) in enumerate(tiles):
        columns = slice(at, at + size)
        values = []
        for side in range(2):
            value = acc[side, :, columns] + part_dot(side, steps - 1, columns)
            value += jnp.dot(
                low[side], maps[side, :, :, :, columns].reshape(256, size), preferred_element_type=jnp.float32
            )
            if terms:
                value += term[side, :, columns].astype(jnp.float32)
            if finish:
                value += far[side, :, columns].astype(jnp.float32)
                value *= jnp.dot(pick[...], scale[side, :, columns], preferred_element_type=jnp.float32)
                values.append(value)
            elif outs[0].dtype == jnp.float32:
                acc[side, :, columns] = value
            else:
                out[side, :, columns] = value.astype(out.dtype)
        if finish:
            out[0, :, columns] = activate(*values)
        for copy in stores(place):
            copy.start()
    for place in range(len(tiles)):
        for copy in stores(place):
            copy.wait()


def dot_pair(chunks, weights, adapter_out, flip, narrow, ids, out_dtype, splits=(), terms=(), finish=None, after=(), cost=COST):
    xs, lows, picks = zip(*chunks)
    counts = tuple(x.shape[0] for x in xs)
    rows, depth = sum(counts), xs[0].shape[1]
    tenants = adapter_out.shape[0]
    operands = [ids, *xs, *lows, *weights, adapter_out, *terms]
    if finish is not None:
        operands += [*finish[0], *picks, finish[1]]
        out_shape = [jax.ShapeDtypeStruct((rows, narrow), out_dtype)]
    elif splits:
        out_shape = [jax.ShapeDtypeStruct((count, narrow), out_dtype) for _ in range(2) for count in splits]
    else:
        out_shape = [jax.ShapeDtypeStruct((2, rows, narrow), out_dtype)]
    operands += list(after)
    few = (8, 128)
    steps = depth // STEP_DEPTH
    out_few = out_dtype == jnp.float32
    return pl.pallas_call(
        functools.partial(
            dot_kernel, flip, counts, splits, len(terms) // 2, counts if finish is not None else (), narrow
        ),
        out_shape=out_shape,
        grid_spec=pltpu.PrefetchScalarGridSpec(
            num_scalar_prefetch=1,
            grid=(1,),
            in_specs=[ANY] * (len(operands) - 1),
            out_specs=[ANY] * len(out_shape),
            scratch_shapes=[
                pltpu.VMEM((rows, depth), jnp.bfloat16),
                pltpu.VMEM((2, rows, 256), jnp.bfloat16),
                pltpu.VMEM((2, steps, STEP_DEPTH, narrow), jnp.bfloat16),
                pltpu.VMEM((2, 2, tenants, RANK, narrow), jnp.bfloat16),
                pltpu.VMEM((2, rows, narrow) if terms else few, jnp.bfloat16),
                pltpu.VMEM((2, rows, narrow), jnp.float32),
                pltpu.VMEM(few if out_few else (1 if finish is not None else 2, rows, narrow), jnp.bfloat16),
                pltpu.VMEM((2, rows, narrow) if finish is not None else few, jnp.bfloat16),
                pltpu.VMEM((rows, 128) if finish is not None else few, jnp.bfloat16),
                pltpu.VMEM((2, 128, narrow) if finish is not None else few, jnp.bfloat16),
                pltpu.SemaphoreType.DMA((4 * len(xs) + 8,)),
                pltpu.SemaphoreType.DMA((2, steps)),
                pltpu.SemaphoreType.DMA((-(-narrow // TILE), 4)),
            ],
        ),
        compiler_params=pltpu.CompilerParams(vmem_limit_bytes=VMEM_LIMIT),
        cost_estimate=cost,
        name="finish_dots" if finish is not None else "dot_pair",
    )(*operands)


def last_kernel(mx_count, first, ids, rows, tenants, sums, far, pick, scale, earlier, out_ref, table, held):
    block = pl.program_id(0)

    @pl.when(block == 0)
    def _():
        fill_table(table, ids, rows, tenants, mx_count)
        held[0:first, :] = earlier[...]
        held[LIVE_ROWS:, :] = jnp.zeros((BLOCK_ROWS, held.shape[1]), held.dtype)
        columns = held.shape[1]

        @pl.loop(0, far.shape[1] // 64)
        def _(tile):
            here = pl.ds(pl.multiple_of(tile * 64, 64), 64)
            there = pl.ds(pl.multiple_of(first + tile * 64, 64), 64)
            for left in range(0, columns, TILE):
                right = min(left + TILE, columns)
                pre = [
                    (sums[side, here, left:right] + far[side, here, left:right].astype(jnp.float32))
                    * jnp.dot(pick[here, :], scale[side, :, left:right], preferred_element_type=jnp.float32)
                    for side in range(2)
                ]
                held[there, left:right] = activate(*pre)

    def find(slot, start):
        return jnp.where(table[3, slot] == block, table[0, slot], start)

    start = lax.fori_loop(0, len(SLOTS), find, jnp.int32(0))
    count = rows[block]
    base = pl.multiple_of(jnp.minimum(start // BLOCK_ROWS * BLOCK_ROWS, LIVE_ROWS - BLOCK_ROWS), BLOCK_ROWS)
    shape = (BLOCK_ROWS, 2 * BLOCK_ROWS)
    position = lax.broadcasted_iota(jnp.int32, shape, 0)
    column = lax.broadcasted_iota(jnp.int32, shape, 1) + base
    chosen = (position < count) & (column == position + start)
    out_ref[...] = jnp.dot(
        chosen.astype(jnp.bfloat16), held[pl.ds(base, 2 * BLOCK_ROWS), :], preferred_element_type=jnp.float32
    ).astype(jnp.bfloat16)


def last_rows(mx_count, first, scalars, sums, far, pick, scale, earlier, blocks):
    narrow = far.shape[2]
    operands = (sums, far, pick, scale, earlier)
    return pl.pallas_call(
        functools.partial(last_kernel, mx_count, first),
        out_shape=jax.ShapeDtypeStruct((blocks * BLOCK_ROWS, narrow), jnp.bfloat16),
        grid_spec=pltpu.PrefetchScalarGridSpec(
            num_scalar_prefetch=3,
            grid=(blocks,),
            in_specs=[
                pl.BlockSpec(part.shape, lambda i, *_, dims=part.ndim: (0,) * dims) for part in operands
            ],
            out_specs=pl.BlockSpec((BLOCK_ROWS, narrow), lambda i, *_: (i, 0)),
            scratch_shapes=[
                pltpu.SMEM((4, len(SLOTS)), jnp.int32),
                pltpu.VMEM((LIVE_ROWS + BLOCK_ROWS, narrow), jnp.bfloat16),
            ],
        ),
        compiler_params=pltpu.CompilerParams(vmem_limit_bytes=VMEM_LIMIT),
        cost_estimate=COST,
        name="last_rows",
    )(*scalars, *operands)


def quarter(array, index, narrow):
    return lax.dynamic_slice_in_dim(array, index * narrow, narrow, array.ndim - 1)


def pipelined(
    tokens, w_gate, w_up, adapter_in, adapter_out, magnitude, partial_norms, block_tenant, block_rows
):
    mx_count = lax.axis_size("mx")
    my_count = lax.axis_size("my")
    narrow = w_gate.shape[1] // my_count
    mine = lax.axis_index("my")
    ids = jnp.stack([lax.axis_index("mx"), mine]).astype(jnp.int32)
    scalars = (ids, block_rows, block_tenant)
    near = [(i, i ^ 1) for i in range(my_count)]
    across = [(i, i ^ 2) for i in range(my_count)]

    def hop(block, distance, least=0):
        if distance > 0:
            pairs = [(i, i + distance) for i in range(least, mx_count - distance)]
        else:
            pairs = [(i, i + distance) for i in range(-distance, mx_count - least)]
        return lax.ppermute(block, "mx", pairs)

    first_up, first_down = hop(tokens, 1), hop(tokens, -1)
    blocks = [tokens, first_up, first_down, hop(first_up, 1, 1), hop(first_down, -1, 1)]

    norms = partial_norms[0]
    pair = jnp.stack([quarter(norms, mine, narrow), quarter(norms, mine ^ 2, narrow)])
    other = jnp.stack([quarter(norms, mine ^ 1, narrow), quarter(norms, mine ^ 3, narrow)])
    pair = pair + lax.ppermute(other, "my", near)
    norm_total = pair[0] + lax.ppermute(pair[1], "my", across)
    scale = quarter(magnitude, mine, narrow) * lax.rsqrt(norm_total)
    scale = jnp.transpose(scale, (1, 0, 2))
    high = lax.reduce_precision(scale, 8, 7)
    middle = lax.reduce_precision(scale - high, 8, 7)
    rest = scale - high - middle
    scale = jnp.concatenate(
        [high, middle, rest, jnp.zeros((2, 128 - 3 * scale.shape[1], narrow), jnp.float32)], axis=1
    ).astype(jnp.bfloat16)

    down = jnp.transpose(adapter_in, (0, 2, 1)).reshape(-1, adapter_in.shape[1])

    dots = functools.partial(
        dot_pair, weights=(w_gate, w_up), adapter_out=adapter_out, narrow=narrow, ids=ids
    )

    def swap(parts, pairs):
        return [lax.ppermute(part, "my", pairs) for part in parts]

    def send_far(chunk, pieces=1):
        rows = chunk[0].shape[0] // pieces
        parts = dots([chunk], flip=3, out_dtype=jnp.bfloat16, splits=(rows,) * pieces)
        got = swap(parts, near)
        part, = dots([chunk], flip=2, out_dtype=jnp.bfloat16, terms=got)
        return part, lax.ppermute(part, "my", across)

    *chunk0, = pack_rows(mx_count, CHUNKS[0], scalars, blocks[:3], down, after=(scale,))
    mark, far0 = send_far(chunk0)

    *chunk1, second, third = pack_rows(
        mx_count, CHUNKS[1], scalars, blocks, down, after=(mark,), passed=(3, 4), cost=LONG
    )
    blocks = [*blocks[:3], second, third, hop(second, 1, 2), hop(third, -1, 2)]
    mark, far1 = send_far(chunk1)

    parts = dots([chunk0, chunk1], flip=1, out_dtype=jnp.bfloat16, splits=(CHUNKS[2][0],), after=(mark,))
    early = swap(parts, near)

    *chunk2, = pack_rows(mx_count, CHUNKS[2], scalars, blocks, down, after=(parts[0], far0))
    mark, far2 = send_far(chunk2)

    first, last = CHUNKS[2][:2]
    parts = dots([chunk2], flip=1, out_dtype=jnp.bfloat16, splits=(last,), after=(mark, far1))
    late = swap(parts, near)
    hidden, = dots(
        [chunk0, chunk1], flip=0, out_dtype=jnp.bfloat16, terms=early, finish=((far0, far1), scale),
        after=(parts[0],),
    )
    sums, = dots([chunk2], flip=0, out_dtype=jnp.float32, terms=late, after=(hidden,))
    return last_rows(mx_count, first, scalars, sums, far2, chunk2[2], scale, hidden, block_rows.shape[0])


def adapter_low(rows_piece, aligned_row_total, adapter_in, block_tenant):
    row_count = rows_piece.shape[0]
    seg_rows = math.gcd(math.gcd(row_count, BLOCK_ROWS), aligned_row_total)
    seg_count = row_count // seg_rows
    seg_block = jnp.arange(seg_count, dtype=jnp.int32) * seg_rows // BLOCK_ROWS
    tenant_tables = adapter_in[block_tenant[seg_block]]
    grouped = rows_piece.reshape(seg_count, seg_rows, rows_piece.shape[1])
    low_terms = jnp.einsum(
        "skd,sdr->skr", grouped, tenant_tables, preferred_element_type=jnp.float32
    )
    return low_terms.reshape(row_count, tenant_tables.shape[2])


def finish_plain(
    summed, reduced_rank_factor, norm_total, mag_cols, adapter_cols, first_row, block_tenant, block_rows
):
    row_count = summed.shape[0]
    col_count = summed.shape[2]
    seg_rows = math.gcd(row_count, BLOCK_ROWS)
    seg_count = row_count // seg_rows
    seg_block = (first_row + jnp.arange(seg_count, dtype=jnp.int32) * seg_rows) // BLOCK_ROWS
    tenants = block_tenant[seg_block]
    col_scale = mag_cols * lax.rsqrt(norm_total)
    seg_scale = col_scale[tenants]
    seg_tables = adapter_cols[tenants]
    low_pair = reduced_rank_factor.reshape(seg_count, seg_rows, 2, RANK)
    adapted = jnp.einsum(
        "skpr,sprc->skpc", low_pair, seg_tables, preferred_element_type=jnp.float32
    )
    pre_act = (summed.reshape(seg_count, seg_rows, 2, col_count) + adapted) * seg_scale[:, None]
    hidden = jax.nn.silu(pre_act[:, :, 0]) * pre_act[:, :, 1]
    offsets = (first_row + jnp.arange(row_count, dtype=jnp.int32)).reshape(
        seg_count, seg_rows
    ) % BLOCK_ROWS
    live_mask = offsets < block_rows[seg_block][:, None]
    hidden = jnp.where(live_mask[:, :, None], hidden, jnp.zeros_like(hidden))
    return hidden.reshape(row_count, col_count).astype(jnp.bfloat16)


def plain(
    tokens, w_gate, w_up, adapter_in, adapter_out, magnitude, partial_norms, block_tenant, block_rows
):
    local_rows = tokens.shape[0]
    col_local = w_gate.shape[1]
    my_count = lax.axis_size("my")
    device_position = lax.axis_index("my")
    rows_piece = lax.all_gather(tokens, "mx", axis=0, tiled=True)
    gate_part = jnp.dot(rows_piece, w_gate, preferred_element_type=jnp.float32)
    up_part = jnp.dot(rows_piece, w_up, preferred_element_type=jnp.float32)
    main_part = jnp.stack((gate_part, up_part), axis=1)
    low_terms = adapter_low(rows_piece, local_rows, adapter_in, block_tenant)
    reduced_rank_factor = lax.psum(low_terms, "my").astype(jnp.bfloat16)
    summed = lax.psum_scatter(main_part, "my", scatter_dimension=2, tiled=True)
    norm_total = lax.psum_scatter(partial_norms[0], "my", scatter_dimension=2, tiled=True)
    narrow = col_local // my_count
    mag_cols = lax.dynamic_slice_in_dim(magnitude, device_position * narrow, narrow, 2)
    adapter_cols = lax.dynamic_slice_in_dim(adapter_out, device_position * narrow, narrow, 3)
    return finish_plain(
        summed, reduced_rank_factor, norm_total, mag_cols, adapter_cols, 0, block_tenant, block_rows
    )


def on_device(tokens, w_gate, *rest):
    my_count = lax.axis_size("my")
    fits = (
        my_count == 4
        and lax.axis_size("mx") == 4
        and tokens.shape[0] == 2 * BLOCK_ROWS
        and tokens.shape[1] % STEP_DEPTH == 0
        and tokens.shape[1] >= 2 * STEP_DEPTH
        and w_gate.shape[1] % (my_count * 128) == 0
    )
    return (pipelined if fits else plain)(tokens, w_gate, *rest)


def solution(mesh):
    return jax.shard_map(
        on_device,
        mesh=mesh,
        in_specs=(
            P(("groups", "mx"), "my"),
            P("my", "mx"),
            P("my", "mx"),
            P(None, "my", None),
            P(None, None, None, "mx"),
            P(None, None, "mx"),
            P("my", None, None, "mx"),
            P("groups"),
            P("groups"),
        ),
        out_specs=P("groups", ("mx", "my")),
        check_vma=False,
    )
```

```python
import functools
import math

import jax
import jax.numpy as jnp
from jax import lax
from jax.experimental import pallas as pl
from jax.experimental.pallas import tpu as pltpu
from jax.sharding import PartitionSpec as P

RANK = 16
BLOCK_ROWS = 128
LIVE_ROWS = 768
STEP_DEPTH = 256
AHEAD = 2
TILE = 512
VMEM_LIMIT = 60 * 1024 * 1024

SLOTS = tuple((distance, half) for distance in (0, -1, 1, -2, 2, -3, 3) for half in range(2))
CHUNKS = ((0, 256, 6), (256, 256, 10), (512, 256, 14))
ANY = pl.BlockSpec(memory_space=pl.ANY)
COST = pl.CostEstimate(flops=0, bytes_accessed=0, transcendentals=0)
LONG = pl.CostEstimate(flops=10**12, bytes_accessed=0, transcendentals=0)


def fill_table(table, ids, rows, tenants, mx_count):
    start = jnp.int32(0)
    for slot, (distance, half) in enumerate(SLOTS):
        source = ids[0] + distance
        valid = (source >= 0) & (source < mx_count)
        block = jnp.clip(source, 0, mx_count - 1) * 2 + half
        count = jnp.where(valid, rows[block], 0)
        table[0, slot] = start
        table[1, slot] = count
        table[2, slot] = tenants[block]
        table[3, slot] = jnp.where(valid, block, -1)
        start = start + count


def pack_kernel(mx_count, first, rows_out, slots, passed, ids, rows, tenants, *refs):
    token_refs, down_ref = refs[:slots // 2], refs[slots // 2]
    outs, scratch = refs[-9 - passed:-6], refs[-6:]
    x_ref, low_ref, pick_ref = outs[:3]
    table, buffer, down, acc, sems, down_sem = scratch
    fill_table(table, ids, rows, tenants, mx_count)

    def needed(source):
        start, count = table[0, 2 * source], table[1, 2 * source] + table[1, 2 * source + 1]
        return (count > 0) & (start < first + rows_out) & (start + count > first)

    for source in range(slots // 2):
        @pl.when(needed(source))
        def _():
            pltpu.make_async_copy(token_refs[source], buffer.at[source], sems.at[source]).start()

    down_copy = pltpu.make_async_copy(down_ref, down, down_sem)
    down_copy.start()
    acc[...] = jnp.zeros_like(acc)

    @pl.loop(0, slots // 2)
    def _(source):
        @pl.when(needed(source))
        def _():
            pltpu.make_async_copy(buffer.at[source], buffer.at[source], sems.at[source]).wait()
            target = lax.broadcasted_iota(jnp.int32, (rows_out, 2 * BLOCK_ROWS), 0) + first
            place = lax.broadcasted_iota(jnp.int32, (rows_out, 2 * BLOCK_ROWS), 1)
            upper = place >= BLOCK_ROWS
            position = jnp.where(upper, place - BLOCK_ROWS, place)
            start = jnp.where(upper, table[0, 2 * source + 1], table[0, 2 * source])
            count = jnp.where(upper, table[1, 2 * source + 1], table[1, 2 * source])
            chosen = (position < count) & (target == position + start)
            acc[...] += jnp.dot(
                chosen.astype(jnp.bfloat16), buffer[source], preferred_element_type=jnp.float32
            )

    x_ref[...] = acc[...].astype(jnp.bfloat16)
    row = lax.broadcasted_iota(jnp.int32, (rows_out, 128), 0) + first

    def own(slot, tenant):
        start, count = table[0, slot], table[1, slot]
        return jnp.where((row >= start) & (row < start + count), table[2, slot], tenant)

    tenant = lax.fori_loop(0, slots, own, jnp.full((rows_out, 128), -1, jnp.int32))
    lane = lax.broadcasted_iota(jnp.int32, (rows_out, 128), 1)
    pick_ref[...] = ((lane % 8 == tenant) & (lane < 24)).astype(jnp.bfloat16)

    down_copy.wait()
    low = lax.dot_general(x_ref[...], down[...], (((1,), (1,)), ((), ())), preferred_element_type=jnp.float32)
    owner = jnp.concatenate([lane // 32, lane // 32 + 4], axis=1)
    low = jnp.where(owner == jnp.concatenate([tenant, tenant], axis=1), low, 0.0)
    high = low.astype(jnp.bfloat16)
    rest = (low - high.astype(jnp.float32)).astype(jnp.bfloat16)
    source = lax.broadcasted_iota(jnp.int32, (256, 256), 0)
    goal = lax.broadcasted_iota(jnp.int32, (256, 256), 1)
    place = source // 32 * RANK + source % RANK
    for side in range(2):
        mine = source // RANK % 2 == side
        to_high = (mine & (place == goal)).astype(jnp.bfloat16)
        to_rest = (mine & (place + 128 == goal)).astype(jnp.bfloat16)
        moved = jnp.dot(high, to_high, preferred_element_type=jnp.float32)
        moved += jnp.dot(rest, to_rest, preferred_element_type=jnp.float32)
        low_ref[side] = moved.astype(jnp.bfloat16)


def pack_rows(mx_count, chunk, scalars, tokens, down, after=(), passed=(), cost=COST):
    first, rows_out, slots = chunk
    width = down.shape[1]
    outs = [
        jax.ShapeDtypeStruct((rows_out, width), jnp.bfloat16),
        jax.ShapeDtypeStruct((2, rows_out, 256), jnp.bfloat16),
        jax.ShapeDtypeStruct((rows_out, 128), jnp.bfloat16),
    ]
    out_specs = [
        pl.BlockSpec((rows_out, width), lambda i, *_: (0, 0)),
        pl.BlockSpec((2, rows_out, 256), lambda i, *_: (0, 0, 0)),
        pl.BlockSpec((rows_out, 128), lambda i, *_: (0, 0)),
    ] + [ANY] * len(passed)
    return pl.pallas_call(
        functools.partial(pack_kernel, mx_count, first, rows_out, slots, len(passed)),
        out_shape=outs + [jax.ShapeDtypeStruct(tokens[i].shape, tokens[i].dtype) for i in passed],
        grid_spec=pltpu.PrefetchScalarGridSpec(
            num_scalar_prefetch=3,
            grid=(1,),
            in_specs=[ANY] * (len(tokens) + 1 + len(after)),
            out_specs=out_specs,
            scratch_shapes=[
                pltpu.SMEM((4, len(SLOTS)), jnp.int32),
                pltpu.VMEM((slots // 2, 2 * BLOCK_ROWS, width), jnp.bfloat16),
                pltpu.VMEM(down.shape, jnp.bfloat16),
                pltpu.VMEM((rows_out, width), jnp.float32),
                pltpu.SemaphoreType.DMA((slots // 2,)),
                pltpu.SemaphoreType.DMA,
            ],
        ),
        input_output_aliases={3 + place: 3 + i for i, place in enumerate(passed)},
        compiler_params=pltpu.CompilerParams(vmem_limit_bytes=VMEM_LIMIT),
        cost_estimate=cost,
        name="pack_rows",
    )(*scalars, *tokens, down, *after)


def activate(gate, up):
    return (gate * (1.0 / (1.0 + jnp.exp(-gate))) * up).astype(jnp.bfloat16)


def dot_kernel(flip, counts, splits, terms, far_counts, narrow, ids, *refs):
    parts = len(counts)
    finish = len(far_counts) > 0
    x_refs, low_refs, refs = refs[:parts], refs[parts:2 * parts], refs[2 * parts:]
    w_refs, up_ref, refs = refs[:2], refs[2], refs[3:]
    term_refs, refs = refs[:2 * terms], refs[2 * terms:]
    if finish:
        far_refs, refs = refs[:parts], refs[parts:]
        pick_refs, scale_ref, refs = refs[:parts], refs[parts], refs[parts + 1:]
    x, low, w, maps, term, acc, out, far, pick, scale, in_sem, w_sem, out_sem = refs[-13:]
    outs = refs[-13 - max(1, 2 * len(splits)):-13]
    rows, depth = x.shape
    steps = depth // STEP_DEPTH
    left = pl.multiple_of((ids[1] ^ flip) * narrow, 128)
    tiles = [(at, min(TILE, narrow - at)) for at in range(0, narrow, TILE)]
    loads = []

    def load(source, target):
        loads.append(pltpu.make_async_copy(source, target, in_sem.at[len(loads)]))

    def piece(side, step):
        return pltpu.make_async_copy(
            w_refs[side].at[pl.ds(step * STEP_DEPTH, STEP_DEPTH), pl.ds(left, narrow)],
            w.at[side, step], w_sem.at[side, step],
        )

    def start_step(step):
        for side in range(2):
            piece(side, step).start()

    def stores(place):
        at, size = tiles[place]
        columns = pl.ds(at, size)
        result = acc if outs[0].dtype == jnp.float32 else out
        if finish:
            pairs = [(result.at[0, :, columns], outs[0].at[:, columns])]
        elif not splits:
            pairs = [(result.at[side, :, columns], outs[0].at[side, :, columns]) for side in range(2)]
        else:
            pairs = []
            for side in range(2):
                row = 0
                for part, count in enumerate(splits):
                    target = outs[side * len(splits) + part].at[:, columns]
                    pairs.append((result.at[side, pl.ds(row, count), columns], target))
                    row += count
        return [
            pltpu.make_async_copy(source, target, out_sem.at[place, i]) for i, (source, target) in enumerate(pairs)
        ]

    def part_dot(side, step, columns):
        depths = pl.ds(step * STEP_DEPTH, STEP_DEPTH)
        return jnp.dot(x[:, depths], w[side, step, :, columns], preferred_element_type=jnp.float32)

    row = 0
    for part, count in enumerate(counts):
        load(x_refs[part], x.at[pl.ds(row, count)])
        row += count
    first_loads = len(loads)
    for copy in loads:
        copy.start()
    for step in range(AHEAD):
        start_step(step)
    row = 0
    for part, count in enumerate(counts):
        load(low_refs[part], low.at[:, pl.ds(row, count)])
        row += count
    for side in range(2):
        load(up_ref.at[:, side, :, pl.ds(left, narrow)], maps.at[side, 0])
    if terms:
        count = rows // terms
        for side in range(2):
            for part in range(terms):
                load(term_refs[side * terms + part], term.at[side, pl.ds(part * count, count)])
    if finish:
        row = 0
        for part, count in enumerate(counts):
            here = pl.ds(row, count)
            load(far_refs[part], far.at[:, here])
            load(pick_refs[part], pick.at[here])
            row += count
        load(scale_ref, scale)

    for copy in loads[:first_loads]:
        copy.wait()
    for side in range(2):
        piece(side, 0).wait()
        piece(side, AHEAD).start()
        acc[side] = part_dot(side, 0, slice(None))

    @pl.loop(1, steps - 1)
    def _(step):
        @pl.when(step == steps // 2)
        def _():
            for copy in loads[first_loads:]:
                copy.start()

        for side in range(2):
            piece(side, step).wait()

            @pl.when(step + AHEAD < steps)
            def _():
                piece(side, step + AHEAD).start()

            depths = pl.ds(pl.multiple_of(step * STEP_DEPTH, STEP_DEPTH), STEP_DEPTH)
            acc[side] += jnp.dot(x[:, depths], w[side, step], preferred_element_type=jnp.float32)

    for copy in loads[first_loads:]:
        copy.wait()
    for side in range(2):
        maps[side, 1] = maps[side, 0]
        piece(side, steps - 1).wait()
    for place, (at, size) in enumerate(tiles):
        columns = slice(at, at + size)
        values = []
        for side in range(2):
            value = acc[side, :, columns] + part_dot(side, steps - 1, columns)
            value += jnp.dot(
                low[side], maps[side, :, :, :, columns].reshape(256, size), preferred_element_type=jnp.float32
            )
            if terms:
                value += term[side, :, columns].astype(jnp.float32)
            if finish:
                value += far[side, :, columns].astype(jnp.float32)
                value *= jnp.dot(pick[...], scale[side, :, columns], preferred_element_type=jnp.float32)
                values.append(value)
            elif outs[0].dtype == jnp.float32:
                acc[side, :, columns] = value
            else:
                out[side, :, columns] = value.astype(out.dtype)
        if finish:
            out[0, :, columns] = activate(*values)
        for copy in stores(place):
            copy.start()
    for place in range(len(tiles)):
        for copy in stores(place):
            copy.wait()


def dot_pair(chunks, weights, adapter_out, flip, narrow, ids, out_dtype, splits=(), terms=(), finish=None, after=(), cost=COST):
    xs, lows, picks = zip(*chunks)
    counts = tuple(x.shape[0] for x in xs)
    rows, depth = sum(counts), xs[0].shape[1]
    tenants = adapter_out.shape[0]
    operands = [ids, *xs, *lows, *weights, adapter_out, *terms]
    if finish is not None:
        operands += [*finish[0], *picks, finish[1]]
        out_shape = [jax.ShapeDtypeStruct((rows, narrow), out_dtype)]
    elif splits:
        out_shape = [jax.ShapeDtypeStruct((count, narrow), out_dtype) for _ in range(2) for count in splits]
    else:
        out_shape = [jax.ShapeDtypeStruct((2, rows, narrow), out_dtype)]
    operands += list(after)
    few = (8, 128)
    steps = depth // STEP_DEPTH
    out_few = out_dtype == jnp.float32
    return pl.pallas_call(
        functools.partial(
            dot_kernel, flip, counts, splits, len(terms) // 2, counts if finish is not None else (), narrow
        ),
        out_shape=out_shape,
        grid_spec=pltpu.PrefetchScalarGridSpec(
            num_scalar_prefetch=1,
            grid=(1,),
            in_specs=[ANY] * (len(operands) - 1),
            out_specs=[ANY] * len(out_shape),
            scratch_shapes=[
                pltpu.VMEM((rows, depth), jnp.bfloat16),
                pltpu.VMEM((2, rows, 256), jnp.bfloat16),
                pltpu.VMEM((2, steps, STEP_DEPTH, narrow), jnp.bfloat16),
                pltpu.VMEM((2, 2, tenants, RANK, narrow), jnp.bfloat16),
                pltpu.VMEM((2, rows, narrow) if terms else few, jnp.bfloat16),
                pltpu.VMEM((2, rows, narrow), jnp.float32),
                pltpu.VMEM(few if out_few else (1 if finish is not None else 2, rows, narrow), jnp.bfloat16),
                pltpu.VMEM((2, rows, narrow) if finish is not None else few, jnp.bfloat16),
                pltpu.VMEM((rows, 128) if finish is not None else few, jnp.bfloat16),
                pltpu.VMEM((2, 128, narrow) if finish is not None else few, jnp.bfloat16),
                pltpu.SemaphoreType.DMA((4 * len(xs) + 8,)),
                pltpu.SemaphoreType.DMA((2, steps)),
                pltpu.SemaphoreType.DMA((-(-narrow // TILE), 4)),
            ],
        ),
        compiler_params=pltpu.CompilerParams(vmem_limit_bytes=VMEM_LIMIT),
        cost_estimate=cost,
        name="finish_dots" if finish is not None else "dot_pair",
    )(*operands)


def last_kernel(
    mx_count, first, ids, rows, tenants, sums_ref, far_ref, pick, scale, earlier_ref, out_ref, table, sums, far, held,
    tile_sem, held_sem,
):
    block = pl.program_id(0)
    tiles = far.shape[1] // 64

    def tile_copies(tile):
        here = pl.ds(pl.multiple_of(tile * 64, 64), 64)
        return [
            pltpu.make_async_copy(source.at[:, here], target.at[:, here], tile_sem.at[tile, i])
            for i, (source, target) in enumerate([(sums_ref, sums), (far_ref, far)])
        ]

    @pl.when(block == 0)
    def _():
        for tile in range(tiles):
            for copy in tile_copies(tile):
                copy.start()
        held_copy = pltpu.make_async_copy(earlier_ref, held.at[pl.ds(0, first)], held_sem)
        held_copy.start()
        fill_table(table, ids, rows, tenants, mx_count)
        held[LIVE_ROWS:, :] = jnp.zeros((BLOCK_ROWS, held.shape[1]), held.dtype)
        columns = held.shape[1]

        @pl.loop(0, tiles)
        def _(tile):
            for copy in tile_copies(tile):
                copy.wait()
            here = pl.ds(pl.multiple_of(tile * 64, 64), 64)
            there = pl.ds(pl.multiple_of(first + tile * 64, 64), 64)
            for left in range(0, columns, TILE):
                right = min(left + TILE, columns)
                pre = [
                    (sums[side, here, left:right] + far[side, here, left:right].astype(jnp.float32))
                    * jnp.dot(pick[here, :], scale[side, :, left:right], preferred_element_type=jnp.float32)
                    for side in range(2)
                ]
                held[there, left:right] = activate(*pre)

        held_copy.wait()

    def find(slot, start):
        return jnp.where(table[3, slot] == block, table[0, slot], start)

    start = lax.fori_loop(0, len(SLOTS), find, jnp.int32(0))
    count = rows[block]
    base = pl.multiple_of(jnp.minimum(start // BLOCK_ROWS * BLOCK_ROWS, LIVE_ROWS - BLOCK_ROWS), BLOCK_ROWS)
    shape = (BLOCK_ROWS, 2 * BLOCK_ROWS)
    position = lax.broadcasted_iota(jnp.int32, shape, 0)
    column = lax.broadcasted_iota(jnp.int32, shape, 1) + base
    chosen = (position < count) & (column == position + start)
    out_ref[...] = jnp.dot(
        chosen.astype(jnp.bfloat16), held[pl.ds(base, 2 * BLOCK_ROWS), :], preferred_element_type=jnp.float32
    ).astype(jnp.bfloat16)


def last_rows(mx_count, first, scalars, sums, far, pick, scale, earlier, blocks):
    narrow = far.shape[2]
    operands = (sums, far, pick, scale, earlier)
    return pl.pallas_call(
        functools.partial(last_kernel, mx_count, first),
        out_shape=jax.ShapeDtypeStruct((blocks * BLOCK_ROWS, narrow), jnp.bfloat16),
        grid_spec=pltpu.PrefetchScalarGridSpec(
            num_scalar_prefetch=3,
            grid=(blocks,),
            in_specs=[
                ANY, ANY,
                pl.BlockSpec(pick.shape, lambda i, *_: (0, 0)),
                pl.BlockSpec(scale.shape, lambda i, *_: (0, 0, 0)),
                ANY,
            ],
            out_specs=pl.BlockSpec((BLOCK_ROWS, narrow), lambda i, *_: (i, 0)),
            scratch_shapes=[
                pltpu.SMEM((4, len(SLOTS)), jnp.int32),
                pltpu.VMEM(sums.shape, sums.dtype),
                pltpu.VMEM(far.shape, far.dtype),
                pltpu.VMEM((LIVE_ROWS + BLOCK_ROWS, narrow), jnp.bfloat16),
                pltpu.SemaphoreType.DMA((far.shape[1] // 64, 2)),
                pltpu.SemaphoreType.DMA,
            ],
        ),
        compiler_params=pltpu.CompilerParams(vmem_limit_bytes=VMEM_LIMIT),
        cost_estimate=COST,
        name="last_rows",
    )(*scalars, *operands)


def quarter(array, index, narrow):
    return lax.dynamic_slice_in_dim(array, index * narrow, narrow, array.ndim - 1)


def pipelined(
    tokens, w_gate, w_up, adapter_in, adapter_out, magnitude, partial_norms, block_tenant, block_rows
):
    mx_count = lax.axis_size("mx")
    my_count = lax.axis_size("my")
    narrow = w_gate.shape[1] // my_count
    mine = lax.axis_index("my")
    ids = jnp.stack([lax.axis_index("mx"), mine]).astype(jnp.int32)
    scalars = (ids, block_rows, block_tenant)
    near = [(i, i ^ 1) for i in range(my_count)]
    across = [(i, i ^ 2) for i in range(my_count)]

    def hop(block, distance, least=0):
        if distance > 0:
            pairs = [(i, i + distance) for i in range(least, mx_count - distance)]
        else:
            pairs = [(i, i + distance) for i in range(-distance, mx_count - least)]
        return lax.ppermute(block, "mx", pairs)

    first_up, first_down = hop(tokens, 1), hop(tokens, -1)
    blocks = [tokens, first_up, first_down, hop(first_up, 1, 1), hop(first_down, -1, 1)]

    norms = partial_norms[0]
    pair = jnp.stack([quarter(norms, mine, narrow), quarter(norms, mine ^ 2, narrow)])
    other = jnp.stack([quarter(norms, mine ^ 1, narrow), quarter(norms, mine ^ 3, narrow)])
    pair = pair + lax.ppermute(other, "my", near)
    norm_total = pair[0] + lax.ppermute(pair[1], "my", across)
    scale = quarter(magnitude, mine, narrow) * lax.rsqrt(norm_total)
    scale = jnp.transpose(scale, (1, 0, 2))
    high = lax.reduce_precision(scale, 8, 7)
    middle = lax.reduce_precision(scale - high, 8, 7)
    rest = scale - high - middle
    scale = jnp.concatenate(
        [high, middle, rest, jnp.zeros((2, 128 - 3 * scale.shape[1], narrow), jnp.float32)], axis=1
    ).astype(jnp.bfloat16)

    down = jnp.transpose(adapter_in, (0, 2, 1)).reshape(-1, adapter_in.shape[1])

    dots = functools.partial(
        dot_pair, weights=(w_gate, w_up), adapter_out=adapter_out, narrow=narrow, ids=ids
    )

    def swap(parts, pairs):
        return [lax.ppermute(part, "my", pairs) for part in parts]

    def send_far(chunk, pieces=1):
        rows = chunk[0].shape[0] // pieces
        parts = dots([chunk], flip=3, out_dtype=jnp.bfloat16, splits=(rows,) * pieces)
        got = swap(parts, near)
        part, = dots([chunk], flip=2, out_dtype=jnp.bfloat16, terms=got)
        return part, lax.ppermute(part, "my", across)

    *chunk0, = pack_rows(mx_count, CHUNKS[0], scalars, blocks[:3], down, after=(scale,))
    mark, far0 = send_far(chunk0)

    *chunk1, second, third = pack_rows(
        mx_count, CHUNKS[1], scalars, blocks, down, after=(mark,), passed=(3, 4), cost=LONG
    )
    blocks = [*blocks[:3], second, third, hop(second, 1, 2), hop(third, -1, 2)]
    mark, far1 = send_far(chunk1)

    parts = dots([chunk0, chunk1], flip=1, out_dtype=jnp.bfloat16, splits=(CHUNKS[2][0],), after=(mark,))
    early = swap(parts, near)

    *chunk2, = pack_rows(mx_count, CHUNKS[2], scalars, blocks, down, after=(parts[0], far0))
    mark, far2 = send_far(chunk2)

    first, last = CHUNKS[2][:2]
    parts = dots([chunk2], flip=1, out_dtype=jnp.bfloat16, splits=(last,), after=(mark, far1))
    late = swap(parts, near)
    hidden, = dots(
        [chunk0, chunk1], flip=0, out_dtype=jnp.bfloat16, terms=early, finish=((far0, far1), scale),
        after=(parts[0],),
    )
    sums, = dots([chunk2], flip=0, out_dtype=jnp.float32, terms=late, after=(hidden,))
    return last_rows(mx_count, first, scalars, sums, far2, chunk2[2], scale, hidden, block_rows.shape[0])


def adapter_low(rows_piece, aligned_row_total, adapter_in, block_tenant):
    row_count = rows_piece.shape[0]
    seg_rows = math.gcd(math.gcd(row_count, BLOCK_ROWS), aligned_row_total)
    seg_count = row_count // seg_rows
    seg_block = jnp.arange(seg_count, dtype=jnp.int32) * seg_rows // BLOCK_ROWS
    tenant_tables = adapter_in[block_tenant[seg_block]]
    grouped = rows_piece.reshape(seg_count, seg_rows, rows_piece.shape[1])
    low_terms = jnp.einsum(
        "skd,sdr->skr", grouped, tenant_tables, preferred_element_type=jnp.float32
    )
    return low_terms.reshape(row_count, tenant_tables.shape[2])


def finish_plain(
    summed, reduced_rank_factor, norm_total, mag_cols, adapter_cols, first_row, block_tenant, block_rows
):
    row_count = summed.shape[0]
    col_count = summed.shape[2]
    seg_rows = math.gcd(row_count, BLOCK_ROWS)
    seg_count = row_count // seg_rows
    seg_block = (first_row + jnp.arange(seg_count, dtype=jnp.int32) * seg_rows) // BLOCK_ROWS
    tenants = block_tenant[seg_block]
    col_scale = mag_cols * lax.rsqrt(norm_total)
    seg_scale = col_scale[tenants]
    seg_tables = adapter_cols[tenants]
    low_pair = reduced_rank_factor.reshape(seg_count, seg_rows, 2, RANK)
    adapted = jnp.einsum(
        "skpr,sprc->skpc", low_pair, seg_tables, preferred_element_type=jnp.float32
    )
    pre_act = (summed.reshape(seg_count, seg_rows, 2, col_count) + adapted) * seg_scale[:, None]
    hidden = jax.nn.silu(pre_act[:, :, 0]) * pre_act[:, :, 1]
    offsets = (first_row + jnp.arange(row_count, dtype=jnp.int32)).reshape(
        seg_count, seg_rows
    ) % BLOCK_ROWS
    live_mask = offsets < block_rows[seg_block][:, None]
    hidden = jnp.where(live_mask[:, :, None], hidden, jnp.zeros_like(hidden))
    return hidden.reshape(row_count, col_count).astype(jnp.bfloat16)


def plain(
    tokens, w_gate, w_up, adapter_in, adapter_out, magnitude, partial_norms, block_tenant, block_rows
):
    local_rows = tokens.shape[0]
    col_local = w_gate.shape[1]
    my_count = lax.axis_size("my")
    device_position = lax.axis_index("my")
    rows_piece = lax.all_gather(tokens, "mx", axis=0, tiled=True)
    gate_part = jnp.dot(rows_piece, w_gate, preferred_element_type=jnp.float32)
    up_part = jnp.dot(rows_piece, w_up, preferred_element_type=jnp.float32)
    main_part = jnp.stack((gate_part, up_part), axis=1)
    low_terms = adapter_low(rows_piece, local_rows, adapter_in, block_tenant)
    reduced_rank_factor = lax.psum(low_terms, "my").astype(jnp.bfloat16)
    summed = lax.psum_scatter(main_part, "my", scatter_dimension=2, tiled=True)
    norm_total = lax.psum_scatter(partial_norms[0], "my", scatter_dimension=2, tiled=True)
    narrow = col_local // my_count
    mag_cols = lax.dynamic_slice_in_dim(magnitude, device_position * narrow, narrow, 2)
    adapter_cols = lax.dynamic_slice_in_dim(adapter_out, device_position * narrow, narrow, 3)
    return finish_plain(
        summed, reduced_rank_factor, norm_total, mag_cols, adapter_cols, 0, block_tenant, block_rows
    )


def on_device(tokens, w_gate, *rest):
    my_count = lax.axis_size("my")
    fits = (
        my_count == 4
        and lax.axis_size("mx") == 4
        and tokens.shape[0] == 2 * BLOCK_ROWS
        and tokens.shape[1] % STEP_DEPTH == 0
        and tokens.shape[1] >= 4 * STEP_DEPTH
        and w_gate.shape[1] % (my_count * 128) == 0
    )
    return (pipelined if fits else plain)(tokens, w_gate, *rest)


def solution(mesh):
    return jax.shard_map(
        on_device,
        mesh=mesh,
        in_specs=(
            P(("groups", "mx"), "my"),
            P("my", "mx"),
            P("my", "mx"),
            P(None, "my", None),
            P(None, None, None, "mx"),
            P(None, None, "mx"),
            P("my", None, None, "mx"),
            P("groups"),
            P("groups"),
        ),
        out_specs=P("groups", ("mx", "my")),
        check_vma=False,
    )
```

```python
import functools
import math

import jax
import jax.numpy as jnp
from jax import lax
from jax.experimental import pallas as pl
from jax.experimental.pallas import tpu as pltpu
from jax.sharding import PartitionSpec as P

RANK = 16
BLOCK_ROWS = 128
LIVE_ROWS = 768
TILE = 256
AHEAD = 3
CUTS = 2
VMEM_LIMIT = 60 * 1024 * 1024

SLOTS = tuple((distance, half) for distance in (0, -1, 1, -2, 2, -3, 3) for half in range(2))
CHUNKS = ((0, 256, 6), (256, 256, 10), (512, 256, 14))
ANY = pl.BlockSpec(memory_space=pl.ANY)
COST = pl.CostEstimate(flops=0, bytes_accessed=0, transcendentals=0)
LONG = pl.CostEstimate(flops=10**12, bytes_accessed=0, transcendentals=0)


def fill_table(table, ids, rows, tenants, mx_count):
    start = jnp.int32(0)
    for slot, (distance, half) in enumerate(SLOTS):
        source = ids[0] + distance
        valid = (source >= 0) & (source < mx_count)
        block = jnp.clip(source, 0, mx_count - 1) * 2 + half
        count = jnp.where(valid, rows[block], 0)
        table[0, slot] = start
        table[1, slot] = count
        table[2, slot] = tenants[block]
        table[3, slot] = jnp.where(valid, block, -1)
        start = start + count


def pack_kernel(mx_count, first, rows_out, slots, passed, ids, rows, tenants, *refs):
    token_refs, down_ref = refs[:slots // 2], refs[slots // 2]
    outs, scratch = refs[-9 - passed:-6], refs[-6:]
    x_ref, low_ref, pick_ref = outs[:3]
    table, buffer, down, acc, sems, down_sem = scratch
    fill_table(table, ids, rows, tenants, mx_count)

    def needed(source):
        start, count = table[0, 2 * source], table[1, 2 * source] + table[1, 2 * source + 1]
        return (count > 0) & (start < first + rows_out) & (start + count > first)

    for source in range(slots // 2):
        @pl.when(needed(source))
        def _():
            pltpu.make_async_copy(token_refs[source], buffer.at[source], sems.at[source]).start()

    down_copy = pltpu.make_async_copy(down_ref, down, down_sem)
    down_copy.start()
    acc[...] = jnp.zeros_like(acc)

    @pl.loop(0, slots // 2)
    def _(source):
        @pl.when(needed(source))
        def _():
            pltpu.make_async_copy(buffer.at[source], buffer.at[source], sems.at[source]).wait()
            target = lax.broadcasted_iota(jnp.int32, (rows_out, 2 * BLOCK_ROWS), 0) + first
            place = lax.broadcasted_iota(jnp.int32, (rows_out, 2 * BLOCK_ROWS), 1)
            upper = place >= BLOCK_ROWS
            position = jnp.where(upper, place - BLOCK_ROWS, place)
            start = jnp.where(upper, table[0, 2 * source + 1], table[0, 2 * source])
            count = jnp.where(upper, table[1, 2 * source + 1], table[1, 2 * source])
            chosen = (position < count) & (target == position + start)
            acc[...] += jnp.dot(
                chosen.astype(jnp.bfloat16), buffer[source], preferred_element_type=jnp.float32
            )

    x_ref[...] = acc[...].astype(jnp.bfloat16)
    row = lax.broadcasted_iota(jnp.int32, (rows_out, 128), 0) + first

    def own(slot, tenant):
        start, count = table[0, slot], table[1, slot]
        return jnp.where((row >= start) & (row < start + count), table[2, slot], tenant)

    tenant = lax.fori_loop(0, slots, own, jnp.full((rows_out, 128), -1, jnp.int32))
    lane = lax.broadcasted_iota(jnp.int32, (rows_out, 128), 1)
    pick_ref[...] = ((lane % 8 == tenant) & (lane < 24)).astype(jnp.bfloat16)

    down_copy.wait()
    low = lax.dot_general(x_ref[...], down[...], (((1,), (1,)), ((), ())), preferred_element_type=jnp.float32)
    owner = jnp.concatenate([lane // 32, lane // 32 + 4], axis=1)
    low = jnp.where(owner == jnp.concatenate([tenant, tenant], axis=1), low, 0.0)
    high = low.astype(jnp.bfloat16)
    rest = (low - high.astype(jnp.float32)).astype(jnp.bfloat16)
    source = lax.broadcasted_iota(jnp.int32, (256, 256), 0)
    goal = lax.broadcasted_iota(jnp.int32, (256, 256), 1)
    place = source // 32 * RANK + source % RANK
    for side in range(2):
        mine = source // RANK % 2 == side
        to_high = (mine & (place == goal)).astype(jnp.bfloat16)
        to_rest = (mine & (place + 128 == goal)).astype(jnp.bfloat16)
        moved = jnp.dot(high, to_high, preferred_element_type=jnp.float32)
        moved += jnp.dot(rest, to_rest, preferred_element_type=jnp.float32)
        low_ref[side] = moved.astype(jnp.bfloat16)


def pack_rows(mx_count, chunk, scalars, tokens, down, after=(), passed=(), cost=COST):
    first, rows_out, slots = chunk
    width = down.shape[1]
    outs = [
        jax.ShapeDtypeStruct((rows_out, width), jnp.bfloat16),
        jax.ShapeDtypeStruct((2, rows_out, 256), jnp.bfloat16),
        jax.ShapeDtypeStruct((rows_out, 128), jnp.bfloat16),
    ]
    out_specs = [
        pl.BlockSpec((rows_out, width), lambda i, *_: (0, 0)),
        pl.BlockSpec((2, rows_out, 256), lambda i, *_: (0, 0, 0)),
        pl.BlockSpec((rows_out, 128), lambda i, *_: (0, 0)),
    ] + [ANY] * len(passed)
    return pl.pallas_call(
        functools.partial(pack_kernel, mx_count, first, rows_out, slots, len(passed)),
        out_shape=outs + [jax.ShapeDtypeStruct(tokens[i].shape, tokens[i].dtype) for i in passed],
        grid_spec=pltpu.PrefetchScalarGridSpec(
            num_scalar_prefetch=3,
            grid=(1,),
            in_specs=[ANY] * (len(tokens) + 1 + len(after)),
            out_specs=out_specs,
            scratch_shapes=[
                pltpu.SMEM((4, len(SLOTS)), jnp.int32),
                pltpu.VMEM((slots // 2, 2 * BLOCK_ROWS, width), jnp.bfloat16),
                pltpu.VMEM(down.shape, jnp.bfloat16),
                pltpu.VMEM((rows_out, width), jnp.float32),
                pltpu.SemaphoreType.DMA((slots // 2,)),
                pltpu.SemaphoreType.DMA,
            ],
        ),
        input_output_aliases={3 + place: 3 + i for i, place in enumerate(passed)},
        compiler_params=pltpu.CompilerParams(vmem_limit_bytes=VMEM_LIMIT),
        cost_estimate=cost,
        name="pack_rows",
    )(*scalars, *tokens, down, *after)


def activate(gate, up):
    return (gate * (1.0 / (1.0 + jnp.exp(-gate))) * up).astype(jnp.bfloat16)


def dot_kernel(flip, counts, splits, terms, far_counts, narrow, ids, *refs):
    parts = len(counts)
    finish = len(far_counts) > 0
    x_refs, low_refs, refs = refs[:parts], refs[parts:2 * parts], refs[2 * parts:]
    w_refs, up_ref, refs = refs[:2], refs[2], refs[3:]
    term_refs, refs = refs[:2 * terms], refs[2 * terms:]
    if finish:
        far_refs, refs = refs[:parts], refs[parts:]
        pick_refs, scale_ref, refs = refs[:parts], refs[parts], refs[parts + 1:]
    x, low, w, maps, term, out, far, pick, scale, in_sem, w_sem, out_sem = refs[-12:]
    outs = refs[-12 - max(1, 2 * len(splits)):-12]
    rows, depth = x.shape
    left = pl.multiple_of((ids[1] ^ flip) * narrow, 128)
    tiles = [(at, min(TILE, narrow - at)) for at in range(0, narrow, TILE)]
    whole = sum(size == TILE for _, size in tiles)

    loads = []

    def load(source, target):
        copy = pltpu.make_async_copy(source, target, in_sem.at[len(loads)])
        copy.start()
        loads.append(copy)

    def wait_loads(begin, end):
        for copy in loads[begin:end]:
            copy.wait()

    def pieces(at, size, place):
        cut = depth // CUTS
        return [
            pltpu.make_async_copy(
                w_refs[side].at[pl.ds(part * cut, cut), pl.ds(pl.multiple_of(left + at, 128), size)],
                w.at[place, pl.ds(part * cut, cut), pl.ds(side * size, size)], w_sem.at[place, side, part],
            )
            for part in range(CUTS) for side in range(2)
        ]

    def start_pieces(at, size, place):
        for copy in pieces(at, size, place):
            copy.start()

    def stores(at, size, place):
        columns = pl.ds(at, size)
        if finish:
            pairs = [(out.at[0, :, columns], outs[0].at[:, columns])]
        elif not splits:
            pairs = [(out.at[side, :, columns], outs[0].at[side, :, columns]) for side in range(2)]
        else:
            pairs = []
            for side in range(2):
                row = 0
                for part, count in enumerate(splits):
                    target = outs[side * len(splits) + part].at[:, columns]
                    pairs.append((out.at[side, pl.ds(row, count), columns], target))
                    row += count
        return [
            pltpu.make_async_copy(source, target, out_sem.at[place, i]) for i, (source, target) in enumerate(pairs)
        ]

    def tile(at, size, place, before_sums=lambda: None):
        columns = pl.ds(at, size)
        values = []
        for copy in pieces(at, size, place):
            copy.wait()
        both = jnp.dot(x[...], w[place, :, 0:2 * size], preferred_element_type=jnp.float32)
        before_sums()
        for side in range(2):
            value = both[:, side * size:(side + 1) * size]
            value += jnp.dot(
                low[side], maps[side, :, :, :, columns].reshape(256, size), preferred_element_type=jnp.float32
            )
            if terms:
                value += term[side, :, columns].astype(jnp.float32)
            if finish:
                value += far[side, :, columns].astype(jnp.float32)
                value *= jnp.dot(pick[...], scale[side, :, columns], preferred_element_type=jnp.float32)
                values.append(value)
            else:
                out[side, :, columns] = value.astype(out.dtype)
        if finish:
            out[0, :, columns] = activate(*values)
        for copy in stores(at, size, place):
            copy.start()

    row = 0
    for part, count in enumerate(counts):
        load(x_refs[part], x.at[pl.ds(row, count)])
        row += count
    first_loads = len(loads)
    for place in range(AHEAD):
        start_pieces(*tiles[place], place)
    row = 0
    for part, count in enumerate(counts):
        load(low_refs[part], low.at[:, pl.ds(row, count)])
        row += count
    for side in range(2):
        load(up_ref.at[:, side, :, pl.ds(left, narrow)], maps.at[side, 0])
    if terms:
        count = rows // terms
        for side in range(2):
            for part in range(terms):
                load(term_refs[side * terms + part], term.at[side, pl.ds(part * count, count)])
    if finish:
        row = 0
        for part, count in enumerate(counts):
            here = pl.ds(row, count)
            load(far_refs[part], far.at[:, here])
            load(pick_refs[part], pick.at[here])
            row += count
        load(scale_ref, scale)
    wait_loads(0, first_loads)

    def rest():
        start_pieces(*tiles[AHEAD], AHEAD)
        wait_loads(first_loads, len(loads))
        for side in range(2):
            maps[side, 1] = maps[side, 0]

    tile(*tiles[0], 0, rest)

    @pl.loop(1, whole)
    def _(place):
        at = pl.multiple_of(place * TILE, TILE)

        @pl.when(place + AHEAD < whole)
        def _():
            start_pieces(pl.multiple_of(at + AHEAD * TILE, TILE), TILE, place + AHEAD)

        if whole < len(tiles):
            @pl.when(place + AHEAD == whole)
            def _():
                start_pieces(*tiles[whole], whole)

        tile(at, TILE, place)

    for place in range(whole, len(tiles)):
        tile(*tiles[place], place)
    for place, (at, size) in enumerate(tiles):
        for copy in stores(at, size, place):
            copy.wait()


def dot_pair(chunks, weights, adapter_out, flip, narrow, ids, out_dtype, splits=(), terms=(), finish=None, after=(), cost=COST):
    xs, lows, picks = zip(*chunks)
    counts = tuple(x.shape[0] for x in xs)
    rows, depth = sum(counts), xs[0].shape[1]
    tenants = adapter_out.shape[0]
    operands = [ids, *xs, *lows, *weights, adapter_out, *terms]
    if finish is not None:
        operands += [*finish[0], *picks, finish[1]]
        out_shape = [jax.ShapeDtypeStruct((rows, narrow), out_dtype)]
    elif splits:
        out_shape = [jax.ShapeDtypeStruct((count, narrow), out_dtype) for _ in range(2) for count in splits]
    else:
        out_shape = [jax.ShapeDtypeStruct((2, rows, narrow), out_dtype)]
    operands += list(after)
    few = (8, 128)
    places = -(-narrow // TILE)
    return pl.pallas_call(
        functools.partial(
            dot_kernel, flip, counts, splits, len(terms) // 2, counts if finish is not None else (), narrow
        ),
        out_shape=out_shape,
        grid_spec=pltpu.PrefetchScalarGridSpec(
            num_scalar_prefetch=1,
            grid=(1,),
            in_specs=[ANY] * (len(operands) - 1),
            out_specs=[ANY] * len(out_shape),
            scratch_shapes=[
                pltpu.VMEM((rows, depth), jnp.bfloat16),
                pltpu.VMEM((2, rows, 256), jnp.bfloat16),
                pltpu.VMEM((places, depth, 2 * TILE), jnp.bfloat16),
                pltpu.VMEM((2, 2, tenants, RANK, narrow), jnp.bfloat16),
                pltpu.VMEM((2, rows, narrow) if terms else few, jnp.bfloat16),
                pltpu.VMEM((1 if finish is not None else 2, rows, narrow), out_dtype),
                pltpu.VMEM((2, rows, narrow) if finish is not None else few, jnp.bfloat16),
                pltpu.VMEM((rows, 128) if finish is not None else few, jnp.bfloat16),
                pltpu.VMEM((2, 128, narrow) if finish is not None else few, jnp.bfloat16),
                pltpu.SemaphoreType.DMA((4 * len(xs) + 8,)),
                pltpu.SemaphoreType.DMA((places, 2, CUTS)),
                pltpu.SemaphoreType.DMA((places, 4)),
            ],
        ),
        compiler_params=pltpu.CompilerParams(vmem_limit_bytes=VMEM_LIMIT),
        cost_estimate=cost,
        name="finish_dots" if finish is not None else "dot_pair",
    )(*operands)


def last_kernel(
    mx_count, first, ids, rows, tenants, sums_ref, far_ref, pick, scale, earlier_ref, out_ref, table, sums, far, held,
    tile_sem, held_sem,
):
    block = pl.program_id(0)
    tiles = far.shape[1] // 64

    def tile_copies(tile):
        here = pl.ds(pl.multiple_of(tile * 64, 64), 64)
        return [
            pltpu.make_async_copy(source.at[:, here], target.at[:, here], tile_sem.at[tile, i])
            for i, (source, target) in enumerate([(sums_ref, sums), (far_ref, far)])
        ]

    @pl.when(block == 0)
    def _():
        for tile in range(tiles):
            for copy in tile_copies(tile):
                copy.start()
        held_copy = pltpu.make_async_copy(earlier_ref, held.at[pl.ds(0, first)], held_sem)
        held_copy.start()
        fill_table(table, ids, rows, tenants, mx_count)
        held[LIVE_ROWS:, :] = jnp.zeros((BLOCK_ROWS, held.shape[1]), held.dtype)
        columns = held.shape[1]

        @pl.loop(0, tiles)
        def _(tile):
            for copy in tile_copies(tile):
                copy.wait()
            here = pl.ds(pl.multiple_of(tile * 64, 64), 64)
            there = pl.ds(pl.multiple_of(first + tile * 64, 64), 64)
            for left in range(0, columns, 2 * TILE):
                right = min(left + 2 * TILE, columns)
                pre = [
                    (sums[side, here, left:right] + far[side, here, left:right].astype(jnp.float32))
                    * jnp.dot(pick[here, :], scale[side, :, left:right], preferred_element_type=jnp.float32)
                    for side in range(2)
                ]
                held[there, left:right] = activate(*pre)

        held_copy.wait()

    def find(slot, start):
        return jnp.where(table[3, slot] == block, table[0, slot], start)

    start = lax.fori_loop(0, len(SLOTS), find, jnp.int32(0))
    count = rows[block]
    base = pl.multiple_of(jnp.minimum(start // BLOCK_ROWS * BLOCK_ROWS, LIVE_ROWS - BLOCK_ROWS), BLOCK_ROWS)
    shape = (BLOCK_ROWS, 2 * BLOCK_ROWS)
    position = lax.broadcasted_iota(jnp.int32, shape, 0)
    column = lax.broadcasted_iota(jnp.int32, shape, 1) + base
    chosen = (position < count) & (column == position + start)
    out_ref[...] = jnp.dot(
        chosen.astype(jnp.bfloat16), held[pl.ds(base, 2 * BLOCK_ROWS), :], preferred_element_type=jnp.float32
    ).astype(jnp.bfloat16)


def last_rows(mx_count, first, scalars, sums, far, pick, scale, earlier, blocks):
    narrow = far.shape[2]
    operands = (sums, far, pick, scale, earlier)
    return pl.pallas_call(
        functools.partial(last_kernel, mx_count, first),
        out_shape=jax.ShapeDtypeStruct((blocks * BLOCK_ROWS, narrow), jnp.bfloat16),
        grid_spec=pltpu.PrefetchScalarGridSpec(
            num_scalar_prefetch=3,
            grid=(blocks,),
            in_specs=[
                ANY, ANY,
                pl.BlockSpec(pick.shape, lambda i, *_: (0, 0)),
                pl.BlockSpec(scale.shape, lambda i, *_: (0, 0, 0)),
                ANY,
            ],
            out_specs=pl.BlockSpec((BLOCK_ROWS, narrow), lambda i, *_: (i, 0)),
            scratch_shapes=[
                pltpu.SMEM((4, len(SLOTS)), jnp.int32),
                pltpu.VMEM(sums.shape, sums.dtype),
                pltpu.VMEM(far.shape, far.dtype),
                pltpu.VMEM((LIVE_ROWS + BLOCK_ROWS, narrow), jnp.bfloat16),
                pltpu.SemaphoreType.DMA((far.shape[1] // 64, 2)),
                pltpu.SemaphoreType.DMA,
            ],
        ),
        compiler_params=pltpu.CompilerParams(vmem_limit_bytes=VMEM_LIMIT),
        cost_estimate=COST,
        name="last_rows",
    )(*scalars, *operands)


def quarter(array, index, narrow):
    return lax.dynamic_slice_in_dim(array, index * narrow, narrow, array.ndim - 1)


def pipelined(
    tokens, w_gate, w_up, adapter_in, adapter_out, magnitude, partial_norms, block_tenant, block_rows
):
    mx_count = lax.axis_size("mx")
    my_count = lax.axis_size("my")
    narrow = w_gate.shape[1] // my_count
    mine = lax.axis_index("my")
    ids = jnp.stack([lax.axis_index("mx"), mine]).astype(jnp.int32)
    scalars = (ids, block_rows, block_tenant)
    near = [(i, i ^ 1) for i in range(my_count)]
    across = [(i, i ^ 2) for i in range(my_count)]

    def hop(block, distance, least=0):
        if distance > 0:
            pairs = [(i, i + distance) for i in range(least, mx_count - distance)]
        else:
            pairs = [(i, i + distance) for i in range(-distance, mx_count - least)]
        return lax.ppermute(block, "mx", pairs)

    first_up, first_down = hop(tokens, 1), hop(tokens, -1)
    blocks = [tokens, first_up, first_down, hop(first_up, 1, 1), hop(first_down, -1, 1)]

    norms = partial_norms[0]
    pair = jnp.stack([quarter(norms, mine, narrow), quarter(norms, mine ^ 2, narrow)])
    other = jnp.stack([quarter(norms, mine ^ 1, narrow), quarter(norms, mine ^ 3, narrow)])
    pair = pair + lax.ppermute(other, "my", near)
    norm_total = pair[0] + lax.ppermute(pair[1], "my", across)
    scale = quarter(magnitude, mine, narrow) * lax.rsqrt(norm_total)
    scale = jnp.transpose(scale, (1, 0, 2))
    high = lax.reduce_precision(scale, 8, 7)
    middle = lax.reduce_precision(scale - high, 8, 7)
    rest = scale - high - middle
    scale = jnp.concatenate(
        [high, middle, rest, jnp.zeros((2, 128 - 3 * scale.shape[1], narrow), jnp.float32)], axis=1
    ).astype(jnp.bfloat16)

    down = jnp.transpose(adapter_in, (0, 2, 1)).reshape(-1, adapter_in.shape[1])

    dots = functools.partial(
        dot_pair, weights=(w_gate, w_up), adapter_out=adapter_out, narrow=narrow, ids=ids
    )

    def swap(parts, pairs):
        return [lax.ppermute(part, "my", pairs) for part in parts]

    def send_far(chunk, pieces=1):
        rows = chunk[0].shape[0] // pieces
        parts = dots([chunk], flip=3, out_dtype=jnp.bfloat16, splits=(rows,) * pieces)
        got = swap(parts, near)
        part, = dots([chunk], flip=2, out_dtype=jnp.bfloat16, terms=got)
        return part, lax.ppermute(part, "my", across)

    *chunk0, = pack_rows(mx_count, CHUNKS[0], scalars, blocks[:3], down, after=(scale,))
    mark, far0 = send_far(chunk0)

    *chunk1, second, third = pack_rows(
        mx_count, CHUNKS[1], scalars, blocks, down, after=(mark,), passed=(3, 4), cost=LONG
    )
    blocks = [*blocks[:3], second, third, hop(second, 1, 2), hop(third, -1, 2)]
    mark, far1 = send_far(chunk1)

    parts = dots([chunk0, chunk1], flip=1, out_dtype=jnp.bfloat16, splits=(CHUNKS[2][0],), after=(mark,))
    early = swap(parts, near)

    *chunk2, = pack_rows(mx_count, CHUNKS[2], scalars, blocks, down, after=(parts[0], far0))
    mark, far2 = send_far(chunk2)

    first, last = CHUNKS[2][:2]
    parts = dots([chunk2], flip=1, out_dtype=jnp.bfloat16, splits=(last,), after=(mark, far1))
    late = swap(parts, near)
    hidden, = dots(
        [chunk0, chunk1], flip=0, out_dtype=jnp.bfloat16, terms=early, finish=((far0, far1), scale),
        after=(parts[0],),
    )
    sums, = dots([chunk2], flip=0, out_dtype=jnp.float32, terms=late, after=(hidden,))
    return last_rows(mx_count, first, scalars, sums, far2, chunk2[2], scale, hidden, block_rows.shape[0])


def adapter_low(rows_piece, aligned_row_total, adapter_in, block_tenant):
    row_count = rows_piece.shape[0]
    seg_rows = math.gcd(math.gcd(row_count, BLOCK_ROWS), aligned_row_total)
    seg_count = row_count // seg_rows
    seg_block = jnp.arange(seg_count, dtype=jnp.int32) * seg_rows // BLOCK_ROWS
    tenant_tables = adapter_in[block_tenant[seg_block]]
    grouped = rows_piece.reshape(seg_count, seg_rows, rows_piece.shape[1])
    low_terms = jnp.einsum(
        "skd,sdr->skr", grouped, tenant_tables, preferred_element_type=jnp.float32
    )
    return low_terms.reshape(row_count, tenant_tables.shape[2])


def finish_plain(
    summed, reduced_rank_factor, norm_total, mag_cols, adapter_cols, first_row, block_tenant, block_rows
):
    row_count = summed.shape[0]
    col_count = summed.shape[2]
    seg_rows = math.gcd(row_count, BLOCK_ROWS)
    seg_count = row_count // seg_rows
    seg_block = (first_row + jnp.arange(seg_count, dtype=jnp.int32) * seg_rows) // BLOCK_ROWS
    tenants = block_tenant[seg_block]
    col_scale = mag_cols * lax.rsqrt(norm_total)
    seg_scale = col_scale[tenants]
    seg_tables = adapter_cols[tenants]
    low_pair = reduced_rank_factor.reshape(seg_count, seg_rows, 2, RANK)
    adapted = jnp.einsum(
        "skpr,sprc->skpc", low_pair, seg_tables, preferred_element_type=jnp.float32
    )
    pre_act = (summed.reshape(seg_count, seg_rows, 2, col_count) + adapted) * seg_scale[:, None]
    hidden = jax.nn.silu(pre_act[:, :, 0]) * pre_act[:, :, 1]
    offsets = (first_row + jnp.arange(row_count, dtype=jnp.int32)).reshape(
        seg_count, seg_rows
    ) % BLOCK_ROWS
    live_mask = offsets < block_rows[seg_block][:, None]
    hidden = jnp.where(live_mask[:, :, None], hidden, jnp.zeros_like(hidden))
    return hidden.reshape(row_count, col_count).astype(jnp.bfloat16)


def plain(
    tokens, w_gate, w_up, adapter_in, adapter_out, magnitude, partial_norms, block_tenant, block_rows
):
    local_rows = tokens.shape[0]
    col_local = w_gate.shape[1]
    my_count = lax.axis_size("my")
    device_position = lax.axis_index("my")
    rows_piece = lax.all_gather(tokens, "mx", axis=0, tiled=True)
    gate_part = jnp.dot(rows_piece, w_gate, preferred_element_type=jnp.float32)
    up_part = jnp.dot(rows_piece, w_up, preferred_element_type=jnp.float32)
    main_part = jnp.stack((gate_part, up_part), axis=1)
    low_terms = adapter_low(rows_piece, local_rows, adapter_in, block_tenant)
    reduced_rank_factor = lax.psum(low_terms, "my").astype(jnp.bfloat16)
    summed = lax.psum_scatter(main_part, "my", scatter_dimension=2, tiled=True)
    norm_total = lax.psum_scatter(partial_norms[0], "my", scatter_dimension=2, tiled=True)
    narrow = col_local // my_count
    mag_cols = lax.dynamic_slice_in_dim(magnitude, device_position * narrow, narrow, 2)
    adapter_cols = lax.dynamic_slice_in_dim(adapter_out, device_position * narrow, narrow, 3)
    return finish_plain(
        summed, reduced_rank_factor, norm_total, mag_cols, adapter_cols, 0, block_tenant, block_rows
    )


def on_device(tokens, w_gate, *rest):
    my_count = lax.axis_size("my")
    fits = (
        my_count == 4
        and lax.axis_size("mx") == 4
        and tokens.shape[0] == 2 * BLOCK_ROWS
        and tokens.shape[1] % 512 == 0
        and w_gate.shape[1] % (my_count * 128) == 0
        and w_gate.shape[1] // my_count >= (AHEAD + 1) * TILE
    )
    return (pipelined if fits else plain)(tokens, w_gate, *rest)


def solution(mesh):
    return jax.shard_map(
        on_device,
        mesh=mesh,
        in_specs=(
            P(("groups", "mx"), "my"),
            P("my", "mx"),
            P("my", "mx"),
            P(None, "my", None),
            P(None, None, None, "mx"),
            P(None, None, "mx"),
            P("my", None, None, "mx"),
            P("groups"),
            P("groups"),
        ),
        out_specs=P("groups", ("mx", "my")),
        check_vma=False,
    )
```

```python
import functools
import math

import jax
import jax.numpy as jnp
from jax import lax
from jax.experimental import pallas as pl
from jax.experimental.pallas import tpu as pltpu
from jax.sharding import PartitionSpec as P

RANK = 16
BLOCK_ROWS = 128
LIVE_ROWS = 768
STEP_DEPTH = 512
TILE = 512
VMEM_LIMIT = 66 * 10**6

SLOTS = tuple((distance, half) for distance in (0, -1, 1, -2, 2, -3, 3) for half in range(2))
CHUNKS = ((0, 256, 6), (256, 256, 10), (512, 256, 14))
ANY = pl.BlockSpec(memory_space=pl.ANY)
COST = pl.CostEstimate(flops=0, bytes_accessed=0, transcendentals=0)
LONG = pl.CostEstimate(flops=10**12, bytes_accessed=0, transcendentals=0)


def fill_table(table, ids, rows, tenants, mx_count):
    start = jnp.int32(0)
    for slot, (distance, half) in enumerate(SLOTS):
        source = ids[0] + distance
        valid = (source >= 0) & (source < mx_count)
        block = jnp.clip(source, 0, mx_count - 1) * 2 + half
        count = jnp.where(valid, rows[block], 0)
        table[0, slot] = start
        table[1, slot] = count
        table[2, slot] = tenants[block]
        table[3, slot] = jnp.where(valid, block, -1)
        start = start + count


def pack_kernel(mx_count, first, rows_out, slots, passed, ids, rows, tenants, *refs):
    token_refs, down_ref = refs[:slots // 2], refs[slots // 2]
    outs, scratch = refs[-9 - passed:-6], refs[-6:]
    x_ref, low_ref, pick_ref = outs[:3]
    table, buffer, down, acc, sems, down_sem = scratch
    fill_table(table, ids, rows, tenants, mx_count)

    def needed(source):
        start, count = table[0, 2 * source], table[1, 2 * source] + table[1, 2 * source + 1]
        return (count > 0) & (start < first + rows_out) & (start + count > first)

    for source in range(slots // 2):
        @pl.when(needed(source))
        def _():
            pltpu.make_async_copy(token_refs[source], buffer.at[source], sems.at[source]).start()

    down_copies = [
        pltpu.make_async_copy(
            down_ref.at[pl.ds((2 * place + side) * RANK, RANK)], down.at[pl.ds((8 * side + place) * RANK, RANK)],
            down_sem.at[side, place],
        )
        for side in range(2) for place in range(8)
    ]
    for copy in down_copies:
        copy.start()
    acc[...] = jnp.zeros_like(acc)

    @pl.loop(0, slots // 2)
    def _(source):
        @pl.when(needed(source))
        def _():
            pltpu.make_async_copy(buffer.at[source], buffer.at[source], sems.at[source]).wait()
            target = lax.broadcasted_iota(jnp.int32, (rows_out, 2 * BLOCK_ROWS), 0) + first
            place = lax.broadcasted_iota(jnp.int32, (rows_out, 2 * BLOCK_ROWS), 1)
            upper = place >= BLOCK_ROWS
            position = jnp.where(upper, place - BLOCK_ROWS, place)
            start = jnp.where(upper, table[0, 2 * source + 1], table[0, 2 * source])
            count = jnp.where(upper, table[1, 2 * source + 1], table[1, 2 * source])
            chosen = (position < count) & (target == position + start)
            acc[...] += jnp.dot(
                chosen.astype(jnp.bfloat16), buffer[source], preferred_element_type=jnp.float32
            )

    x_ref[...] = acc[...].astype(jnp.bfloat16)
    row = lax.broadcasted_iota(jnp.int32, (rows_out, 128), 0) + first

    def own(slot, tenant):
        start, count = table[0, slot], table[1, slot]
        return jnp.where((row >= start) & (row < start + count), table[2, slot], tenant)

    tenant = lax.fori_loop(0, slots, own, jnp.full((rows_out, 128), -1, jnp.int32))
    lane = lax.broadcasted_iota(jnp.int32, (rows_out, 128), 1)
    pick_ref[...] = ((lane % 8 == tenant) & (lane < 24)).astype(jnp.bfloat16)

    for copy in down_copies:
        copy.wait()
    low = lax.dot_general(x_ref[...], down[...], (((1,), (1,)), ((), ())), preferred_element_type=jnp.float32)
    for side in range(2):
        mine = jnp.where(lane // RANK == tenant, low[:, side * 128:(side + 1) * 128], 0.0)
        high = mine.astype(jnp.bfloat16)
        low_ref[side, :, 0:128] = high
        low_ref[side, :, 128:256] = (mine - high.astype(jnp.float32)).astype(jnp.bfloat16)


def pack_rows(mx_count, chunk, scalars, tokens, down, after=(), passed=(), cost=COST):
    first, rows_out, slots = chunk
    width = down.shape[1]
    outs = [
        jax.ShapeDtypeStruct((rows_out, width), jnp.bfloat16),
        jax.ShapeDtypeStruct((2, rows_out, 256), jnp.bfloat16),
        jax.ShapeDtypeStruct((rows_out, 128), jnp.bfloat16),
    ]
    out_specs = [
        pl.BlockSpec((rows_out, width), lambda i, *_: (0, 0)),
        pl.BlockSpec((2, rows_out, 256), lambda i, *_: (0, 0, 0)),
        pl.BlockSpec((rows_out, 128), lambda i, *_: (0, 0)),
    ] + [ANY] * len(passed)
    return pl.pallas_call(
        functools.partial(pack_kernel, mx_count, first, rows_out, slots, len(passed)),
        out_shape=outs + [jax.ShapeDtypeStruct(tokens[i].shape, tokens[i].dtype) for i in passed],
        grid_spec=pltpu.PrefetchScalarGridSpec(
            num_scalar_prefetch=3,
            grid=(1,),
            in_specs=[ANY] * (len(tokens) + 1 + len(after)),
            out_specs=out_specs,
            scratch_shapes=[
                pltpu.SMEM((4, len(SLOTS)), jnp.int32),
                pltpu.VMEM((slots // 2, 2 * BLOCK_ROWS, width), jnp.bfloat16),
                pltpu.VMEM(down.shape, jnp.bfloat16),
                pltpu.VMEM((rows_out, width), jnp.float32),
                pltpu.SemaphoreType.DMA((slots // 2,)),
                pltpu.SemaphoreType.DMA((2, 8)),
            ],
        ),
        input_output_aliases={3 + place: 3 + i for i, place in enumerate(passed)},
        compiler_params=pltpu.CompilerParams(vmem_limit_bytes=VMEM_LIMIT),
        cost_estimate=cost,
        name="pack_rows",
    )(*scalars, *tokens, down, *after)


def activate(gate, up):
    return (gate * (1.0 / (1.0 + jnp.exp(-gate))) * up).astype(jnp.bfloat16)


def dot_kernel(flip, counts, splits, term_counts, finished, narrow, ids, *refs):
    parts = len(counts)
    finish = finished > 0
    x_refs, low_refs, refs = refs[:parts], refs[parts:2 * parts], refs[2 * parts:]
    w_refs, up_ref, refs = refs[:2], refs[2], refs[3:]
    terms = len(term_counts)
    term_refs, refs = refs[:2 * terms], refs[2 * terms:]
    if finish:
        far_refs, refs = refs[:finished], refs[finished:]
        pick_refs, scale_ref, refs = refs[:finished], refs[finished], refs[finished + 1:]
    x, low, w, maps, term, acc, out, far, pick, scale, in_sem, w_sem, out_sem = refs[-13:]
    outs = refs[-13 - (2 if finish else max(1, 2 * len(splits))):-13]
    done = sum(counts[:finished])
    rows, depth = x.shape
    steps = depth // STEP_DEPTH
    left = pl.multiple_of((ids[1] ^ flip) * narrow, 128)
    tiles = [(at, min(TILE, narrow - at)) for at in range(0, narrow, TILE)]
    loads = []

    def load(source, target):
        copy = pltpu.make_async_copy(source, target, in_sem.at[len(loads)])
        copy.start()
        loads.append(copy)

    def piece(side, step):
        return pltpu.make_async_copy(
            w_refs[side].at[pl.ds(step * STEP_DEPTH, STEP_DEPTH), pl.ds(left, narrow)],
            w.at[side, step], w_sem.at[side, step],
        )

    def start_step(step):
        for side in range(2):
            piece(side, step).start()

    def stores(place):
        at, size = tiles[place]
        columns = pl.ds(at, size)
        if finish:
            pairs = [(out.at[0, :, columns], outs[0].at[:, columns])]
            pairs += [(acc.at[side, pl.ds(done, rows - done), columns], outs[1].at[side, :, columns]) for side in range(2)]
        elif not splits:
            pairs = [(out.at[side, :, columns], outs[0].at[side, :, columns]) for side in range(2)]
        else:
            pairs = []
            for side in range(2):
                row = 0
                for part, count in enumerate(splits):
                    target = outs[side * len(splits) + part].at[:, columns]
                    pairs.append((out.at[side, pl.ds(row, count), columns], target))
                    row += count
        return [
            pltpu.make_async_copy(source, target, out_sem.at[place, i]) for i, (source, target) in enumerate(pairs)
        ]

    def part_dot(side, step, columns):
        depths = pl.ds(step * STEP_DEPTH, STEP_DEPTH)
        return jnp.dot(x[:, depths], w[side, step, :, columns], preferred_element_type=jnp.float32)

    row = 0
    for part, count in enumerate(counts):
        load(x_refs[part], x.at[pl.ds(row, count)])
        row += count
    first_loads = len(loads)
    start_step(0)
    start_step(1)
    row = 0
    for part, count in enumerate(counts):
        load(low_refs[part], low.at[:, pl.ds(row, count)])
        row += count
    for side in range(2):
        load(up_ref.at[:, side, :, pl.ds(left, narrow)], maps.at[side, 0])
    if terms:
        for side in range(2):
            row = 0
            for part, count in enumerate(term_counts):
                load(term_refs[2 * part + side], term.at[side, pl.ds(row, count)])
                row += count
    if finish:
        row = 0
        for part, count in enumerate(counts[:finished]):
            here = pl.ds(row, count)
            load(far_refs[part], far.at[:, here])
            load(pick_refs[part], pick.at[here])
            row += count
        load(scale_ref, scale)

    for copy in loads[:first_loads]:
        copy.wait()
    for side in range(2):
        piece(side, 0).wait()
        if steps > 2:
            piece(side, 2).start()
        acc[side] = part_dot(side, 0, slice(None))

    @pl.loop(1, steps - 1)
    def _(step):
        for side in range(2):
            piece(side, step).wait()

            @pl.when(step + 2 < steps)
            def _():
                piece(side, step + 2).start()

            depths = pl.ds(pl.multiple_of(step * STEP_DEPTH, STEP_DEPTH), STEP_DEPTH)
            acc[side] += jnp.dot(x[:, depths], w[side, step], preferred_element_type=jnp.float32)

    for copy in loads[first_loads:]:
        copy.wait()
    for side in range(2):
        maps[side, 1] = maps[side, 0]
        piece(side, steps - 1).wait()
    for place, (at, size) in enumerate(tiles):
        columns = slice(at, at + size)
        values = []
        for side in range(2):
            value = acc[side, :, columns] + part_dot(side, steps - 1, columns)
            value += jnp.dot(
                low[side], maps[side, :, :, :, columns].reshape(256, size), preferred_element_type=jnp.float32
            )
            if terms:
                value += term[side, :, columns].astype(jnp.float32)
            if finish:
                acc[side, done:, columns] = value[done:]
                value = value[:done] + far[side, :, columns].astype(jnp.float32)
                value *= jnp.dot(pick[...], scale[side, :, columns], preferred_element_type=jnp.float32)
                values.append(value)
            else:
                out[side, :, columns] = value.astype(out.dtype)
        if finish:
            out[0, :, columns] = activate(*values)
        for copy in stores(place):
            copy.start()
    for place in range(len(tiles)):
        for copy in stores(place):
            copy.wait()


def dot_pair(chunks, weights, adapter_out, flip, narrow, ids, splits=(), terms=(), finish=None, after=()):
    xs, lows, picks = zip(*chunks)
    counts = tuple(x.shape[0] for x in xs)
    rows, depth = sum(counts), xs[0].shape[1]
    tenants = adapter_out.shape[0]
    term_counts = tuple(gate.shape[0] for gate, _ in terms)
    operands = [ids, *xs, *lows, *weights, adapter_out, *[array for pair in terms for array in pair]]
    finished = 0
    if finish is not None:
        finished = len(finish[0])
        done = sum(counts[:finished])
        operands += [*finish[0], *picks[:finished], finish[1]]
        out_shape = [
            jax.ShapeDtypeStruct((done, narrow), jnp.bfloat16),
            jax.ShapeDtypeStruct((2, rows - done, narrow), jnp.float32),
        ]
    elif splits:
        out_shape = [jax.ShapeDtypeStruct((count, narrow), jnp.bfloat16) for _ in range(2) for count in splits]
    else:
        out_shape = [jax.ShapeDtypeStruct((2, rows, narrow), jnp.bfloat16)]
    operands += list(after)
    few = (8, 128)
    steps = depth // STEP_DEPTH
    return pl.pallas_call(
        functools.partial(
            dot_kernel, flip, counts, splits, term_counts, finished, narrow
        ),
        out_shape=out_shape,
        grid_spec=pltpu.PrefetchScalarGridSpec(
            num_scalar_prefetch=1,
            grid=(1,),
            in_specs=[ANY] * (len(operands) - 1),
            out_specs=[ANY] * len(out_shape),
            scratch_shapes=[
                pltpu.VMEM((rows, depth), jnp.bfloat16),
                pltpu.VMEM((2, rows, 256), jnp.bfloat16),
                pltpu.VMEM((2, steps, STEP_DEPTH, narrow), jnp.bfloat16),
                pltpu.VMEM((2, 2, tenants, RANK, narrow), jnp.bfloat16),
                pltpu.VMEM((2, rows, narrow) if terms else few, jnp.bfloat16),
                pltpu.VMEM((2, rows, narrow), jnp.float32),
                pltpu.VMEM((1, done, narrow) if finished else (2, rows, narrow), jnp.bfloat16),
                pltpu.VMEM((2, done, narrow) if finished else few, jnp.bfloat16),
                pltpu.VMEM((done, 128) if finished else few, jnp.bfloat16),
                pltpu.VMEM((2, 128, narrow) if finished else few, jnp.bfloat16),
                pltpu.SemaphoreType.DMA((4 * len(xs) + 8,)),
                pltpu.SemaphoreType.DMA((2, steps)),
                pltpu.SemaphoreType.DMA((-(-narrow // TILE), 4)),
            ],
        ),
        compiler_params=pltpu.CompilerParams(vmem_limit_bytes=VMEM_LIMIT),
        cost_estimate=COST,
        name="finish_dots" if finished else "dot_pair",
    )(*operands)


def last_kernel(
    mx_count, first, ids, rows, tenants, sums_ref, far_ref, pick, scale, earlier_ref, out_ref, table, sums, far, held,
    tile_sem, held_sem,
):
    block = pl.program_id(0)
    tiles = far.shape[1] // 64

    def tile_copies(tile):
        here = pl.ds(pl.multiple_of(tile * 64, 64), 64)
        return [
            pltpu.make_async_copy(source.at[:, here], target.at[:, here], tile_sem.at[tile, i])
            for i, (source, target) in enumerate([(sums_ref, sums), (far_ref, far)])
        ]

    @pl.when(block == 0)
    def _():
        for tile in range(tiles):
            for copy in tile_copies(tile):
                copy.start()
        held_copy = pltpu.make_async_copy(earlier_ref, held.at[pl.ds(0, first)], held_sem)
        held_copy.start()
        fill_table(table, ids, rows, tenants, mx_count)
        held[LIVE_ROWS:, :] = jnp.zeros((BLOCK_ROWS, held.shape[1]), held.dtype)
        columns = held.shape[1]

        @pl.loop(0, tiles)
        def _(tile):
            for copy in tile_copies(tile):
                copy.wait()
            here = pl.ds(pl.multiple_of(tile * 64, 64), 64)
            there = pl.ds(pl.multiple_of(first + tile * 64, 64), 64)
            for left in range(0, columns, TILE):
                right = min(left + TILE, columns)
                pre = [
                    (sums[side, here, left:right] + far[side, here, left:right].astype(jnp.float32))
                    * jnp.dot(pick[here, :], scale[side, :, left:right], preferred_element_type=jnp.float32)
                    for side in range(2)
                ]
                held[there, left:right] = activate(*pre)

        held_copy.wait()

    def find(slot, start):
        return jnp.where(table[3, slot] == block, table[0, slot], start)

    start = lax.fori_loop(0, len(SLOTS), find, jnp.int32(0))
    count = rows[block]
    base = pl.multiple_of(jnp.minimum(start // BLOCK_ROWS * BLOCK_ROWS, LIVE_ROWS - BLOCK_ROWS), BLOCK_ROWS)
    shape = (BLOCK_ROWS, 2 * BLOCK_ROWS)
    position = lax.broadcasted_iota(jnp.int32, shape, 0)
    column = lax.broadcasted_iota(jnp.int32, shape, 1) + base
    chosen = (position < count) & (column == position + start)
    out_ref[...] = jnp.dot(
        chosen.astype(jnp.bfloat16), held[pl.ds(base, 2 * BLOCK_ROWS), :], preferred_element_type=jnp.float32
    ).astype(jnp.bfloat16)


def last_rows(mx_count, first, scalars, sums, far, pick, scale, earlier, blocks):
    narrow = far.shape[2]
    operands = (sums, far, pick, scale, earlier)
    return pl.pallas_call(
        functools.partial(last_kernel, mx_count, first),
        out_shape=jax.ShapeDtypeStruct((blocks * BLOCK_ROWS, narrow), jnp.bfloat16),
        grid_spec=pltpu.PrefetchScalarGridSpec(
            num_scalar_prefetch=3,
            grid=(blocks,),
            in_specs=[
                ANY, ANY,
                pl.BlockSpec(pick.shape, lambda i, *_: (0, 0)),
                pl.BlockSpec(scale.shape, lambda i, *_: (0, 0, 0)),
                ANY,
            ],
            out_specs=pl.BlockSpec((BLOCK_ROWS, narrow), lambda i, *_: (i, 0)),
            scratch_shapes=[
                pltpu.SMEM((4, len(SLOTS)), jnp.int32),
                pltpu.VMEM(sums.shape, sums.dtype),
                pltpu.VMEM(far.shape, far.dtype),
                pltpu.VMEM((LIVE_ROWS + BLOCK_ROWS, narrow), jnp.bfloat16),
                pltpu.SemaphoreType.DMA((far.shape[1] // 64, 2)),
                pltpu.SemaphoreType.DMA,
            ],
        ),
        compiler_params=pltpu.CompilerParams(vmem_limit_bytes=VMEM_LIMIT),
        cost_estimate=COST,
        name="last_rows",
    )(*scalars, *operands)


def quarter(array, index, narrow):
    return lax.dynamic_slice_in_dim(array, index * narrow, narrow, array.ndim - 1)


def pipelined(
    tokens, w_gate, w_up, adapter_in, adapter_out, magnitude, partial_norms, block_tenant, block_rows
):
    mx_count = lax.axis_size("mx")
    my_count = lax.axis_size("my")
    narrow = w_gate.shape[1] // my_count
    mine = lax.axis_index("my")
    ids = jnp.stack([lax.axis_index("mx"), mine]).astype(jnp.int32)
    scalars = (ids, block_rows, block_tenant)
    near = [(i, i ^ 1) for i in range(my_count)]
    across = [(i, i ^ 2) for i in range(my_count)]

    def hop(block, distance, least=0):
        if distance > 0:
            pairs = [(i, i + distance) for i in range(least, mx_count - distance)]
        else:
            pairs = [(i, i + distance) for i in range(-distance, mx_count - least)]
        return lax.ppermute(block, "mx", pairs)

    first_up, first_down = hop(tokens, 1), hop(tokens, -1)
    blocks = [tokens, first_up, first_down, hop(first_up, 1, 1), hop(first_down, -1, 1)]

    norms = partial_norms[0]
    pair = jnp.stack([quarter(norms, mine, narrow), quarter(norms, mine ^ 2, narrow)])
    other = jnp.stack([quarter(norms, mine ^ 1, narrow), quarter(norms, mine ^ 3, narrow)])
    pair = pair + lax.ppermute(other, "my", near)
    norm_total = pair[0] + lax.ppermute(pair[1], "my", across)
    scale = quarter(magnitude, mine, narrow) * lax.rsqrt(norm_total)
    scale = jnp.transpose(scale, (1, 0, 2))
    high = lax.reduce_precision(scale, 8, 7)
    middle = lax.reduce_precision(scale - high, 8, 7)
    rest = scale - high - middle
    scale = jnp.concatenate(
        [high, middle, rest, jnp.zeros((2, 128 - 3 * scale.shape[1], narrow), jnp.float32)], axis=1
    ).astype(jnp.bfloat16)

    down = jnp.transpose(adapter_in, (0, 2, 1)).reshape(-1, adapter_in.shape[1])

    dots = functools.partial(
        dot_pair, weights=(w_gate, w_up), adapter_out=adapter_out, narrow=narrow, ids=ids
    )

    def swap(parts, pairs):
        return [lax.ppermute(part, "my", pairs) for part in parts]

    def far_out(chunk, after=()):
        return dots([chunk], flip=3, splits=(chunk[0].shape[0],), after=after)

    def far_in(chunk, got, after=()):
        part, = dots([chunk], flip=2, terms=(got,), after=after)
        return part, lax.ppermute(part, "my", across)

    *chunk0, = pack_rows(mx_count, CHUNKS[0], scalars, blocks[:3], down, after=(scale,))
    mark, far0 = far_in(chunk0, swap(far_out(chunk0), near))

    *chunk1, second, third = pack_rows(
        mx_count, CHUNKS[1], scalars, blocks, down, after=(mark,), passed=(3, 4), cost=LONG
    )
    blocks = [*blocks[:3], second, third, hop(second, 1, 2), hop(third, -1, 2)]
    mark, far1 = far_in(chunk1, swap(far_out(chunk1), near))

    first, last = CHUNKS[2][:2]
    *chunk2, = pack_rows(mx_count, CHUNKS[2], scalars, blocks, down, after=(mark, far0))
    parts = far_out(chunk2)
    got = swap(parts, near)
    parts = dots([chunk0, chunk1], flip=1, splits=(first,), after=(parts[0],))
    early = swap(parts, near)
    mark, far2 = far_in(chunk2, got, after=(parts[0],))

    parts = dots([chunk2], flip=1, splits=(last,), after=(mark, far1))
    late = swap(parts, near)
    hidden, sums = dots([chunk0, chunk1, chunk2], flip=0, terms=(early, late), finish=((far0, far1), scale))
    return last_rows(mx_count, first, scalars, sums, far2, chunk2[2], scale, hidden, block_rows.shape[0])


def adapter_low(rows_piece, aligned_row_total, adapter_in, block_tenant):
    row_count = rows_piece.shape[0]
    seg_rows = math.gcd(math.gcd(row_count, BLOCK_ROWS), aligned_row_total)
    seg_count = row_count // seg_rows
    seg_block = jnp.arange(seg_count, dtype=jnp.int32) * seg_rows // BLOCK_ROWS
    tenant_tables = adapter_in[block_tenant[seg_block]]
    grouped = rows_piece.reshape(seg_count, seg_rows, rows_piece.shape[1])
    low_terms = jnp.einsum(
        "skd,sdr->skr", grouped, tenant_tables, preferred_element_type=jnp.float32
    )
    return low_terms.reshape(row_count, tenant_tables.shape[2])


def finish_plain(
    summed, reduced_rank_factor, norm_total, mag_cols, adapter_cols, first_row, block_tenant, block_rows
):
    row_count = summed.shape[0]
    col_count = summed.shape[2]
    seg_rows = math.gcd(row_count, BLOCK_ROWS)
    seg_count = row_count // seg_rows
    seg_block = (first_row + jnp.arange(seg_count, dtype=jnp.int32) * seg_rows) // BLOCK_ROWS
    tenants = block_tenant[seg_block]
    col_scale = mag_cols * lax.rsqrt(norm_total)
    seg_scale = col_scale[tenants]
    seg_tables = adapter_cols[tenants]
    low_pair = reduced_rank_factor.reshape(seg_count, seg_rows, 2, RANK)
    adapted = jnp.einsum(
        "skpr,sprc->skpc", low_pair, seg_tables, preferred_element_type=jnp.float32
    )
    pre_act = (summed.reshape(seg_count, seg_rows, 2, col_count) + adapted) * seg_scale[:, None]
    hidden = jax.nn.silu(pre_act[:, :, 0]) * pre_act[:, :, 1]
    offsets = (first_row + jnp.arange(row_count, dtype=jnp.int32)).reshape(
        seg_count, seg_rows
    ) % BLOCK_ROWS
    live_mask = offsets < block_rows[seg_block][:, None]
    hidden = jnp.where(live_mask[:, :, None], hidden, jnp.zeros_like(hidden))
    return hidden.reshape(row_count, col_count).astype(jnp.bfloat16)


def plain(
    tokens, w_gate, w_up, adapter_in, adapter_out, magnitude, partial_norms, block_tenant, block_rows
):
    local_rows = tokens.shape[0]
    col_local = w_gate.shape[1]
    my_count = lax.axis_size("my")
    device_position = lax.axis_index("my")
    rows_piece = lax.all_gather(tokens, "mx", axis=0, tiled=True)
    gate_part = jnp.dot(rows_piece, w_gate, preferred_element_type=jnp.float32)
    up_part = jnp.dot(rows_piece, w_up, preferred_element_type=jnp.float32)
    main_part = jnp.stack((gate_part, up_part), axis=1)
    low_terms = adapter_low(rows_piece, local_rows, adapter_in, block_tenant)
    reduced_rank_factor = lax.psum(low_terms, "my").astype(jnp.bfloat16)
    summed = lax.psum_scatter(main_part, "my", scatter_dimension=2, tiled=True)
    norm_total = lax.psum_scatter(partial_norms[0], "my", scatter_dimension=2, tiled=True)
    narrow = col_local // my_count
    mag_cols = lax.dynamic_slice_in_dim(magnitude, device_position * narrow, narrow, 2)
    adapter_cols = lax.dynamic_slice_in_dim(adapter_out, device_position * narrow, narrow, 3)
    return finish_plain(
        summed, reduced_rank_factor, norm_total, mag_cols, adapter_cols, 0, block_tenant, block_rows
    )


def on_device(tokens, w_gate, w_up, adapter_in, *rest):
    my_count = lax.axis_size("my")
    fits = (
        my_count == 4
        and lax.axis_size("mx") == 4
        and tokens.shape[0] == 2 * BLOCK_ROWS
        and adapter_in.shape[0] == 8
        and tokens.shape[1] % STEP_DEPTH == 0
        and tokens.shape[1] >= 2 * STEP_DEPTH
        and w_gate.shape[1] % (my_count * 128) == 0
    )
    return (pipelined if fits else plain)(tokens, w_gate, w_up, adapter_in, *rest)


def solution(mesh):
    return jax.shard_map(
        on_device,
        mesh=mesh,
        in_specs=(
            P(("groups", "mx"), "my"),
            P("my", "mx"),
            P("my", "mx"),
            P(None, "my", None),
            P(None, None, None, "mx"),
            P(None, None, "mx"),
            P("my", None, None, "mx"),
            P("groups"),
            P("groups"),
        ),
        out_specs=P("groups", ("mx", "my")),
        check_vma=False,
    )
```

```python
import functools
import math

import jax
import jax.numpy as jnp
from jax import lax
from jax.experimental import pallas as pl
from jax.experimental.pallas import tpu as pltpu
from jax.sharding import PartitionSpec as P

RANK = 16
BLOCK_ROWS = 128
LIVE_ROWS = 768
STEP_DEPTH = 512
TILE = 512
VMEM_LIMIT = 66 * 10**6

SLOTS = tuple((distance, half) for distance in (0, -1, 1, -2, 2, -3, 3) for half in range(2))
CHUNKS = ((0, 256, 6), (256, 256, 10), (512, 256, 14))
ANY = pl.BlockSpec(memory_space=pl.ANY)
COST = pl.CostEstimate(flops=0, bytes_accessed=0, transcendentals=0)
LONG = pl.CostEstimate(flops=10**12, bytes_accessed=0, transcendentals=0)


def fill_table(table, ids, rows, tenants, mx_count):
    start = jnp.int32(0)
    for slot, (distance, half) in enumerate(SLOTS):
        source = ids[0] + distance
        valid = (source >= 0) & (source < mx_count)
        block = jnp.clip(source, 0, mx_count - 1) * 2 + half
        count = jnp.where(valid, rows[block], 0)
        table[0, slot] = start
        table[1, slot] = count
        table[2, slot] = tenants[block]
        table[3, slot] = jnp.where(valid, block, -1)
        start = start + count


def pack_kernel(mx_count, first, rows_out, slots, passed, ids, rows, tenants, *refs):
    token_refs, down_ref = refs[:slots // 2], refs[slots // 2]
    outs, scratch = refs[-9 - passed:-6], refs[-6:]
    x_ref, low_ref, pick_ref = outs[:3]
    table, buffer, down, acc, sems, down_sem = scratch
    fill_table(table, ids, rows, tenants, mx_count)

    def needed(source):
        start, count = table[0, 2 * source], table[1, 2 * source] + table[1, 2 * source + 1]
        return (count > 0) & (start < first + rows_out) & (start + count > first)

    for source in range(slots // 2):
        @pl.when(needed(source))
        def _():
            pltpu.make_async_copy(token_refs[source], buffer.at[source], sems.at[source]).start()

    down_copies = [
        pltpu.make_async_copy(
            down_ref.at[pl.ds((2 * place + side) * RANK, RANK)], down.at[pl.ds((8 * side + place) * RANK, RANK)],
            down_sem.at[side, place],
        )
        for side in range(2) for place in range(8)
    ]
    for copy in down_copies:
        copy.start()
    acc[...] = jnp.zeros_like(acc)

    @pl.loop(0, slots // 2)
    def _(source):
        @pl.when(needed(source))
        def _():
            pltpu.make_async_copy(buffer.at[source], buffer.at[source], sems.at[source]).wait()
            target = lax.broadcasted_iota(jnp.int32, (rows_out, 2 * BLOCK_ROWS), 0) + first
            place = lax.broadcasted_iota(jnp.int32, (rows_out, 2 * BLOCK_ROWS), 1)
            upper = place >= BLOCK_ROWS
            position = jnp.where(upper, place - BLOCK_ROWS, place)
            start = jnp.where(upper, table[0, 2 * source + 1], table[0, 2 * source])
            count = jnp.where(upper, table[1, 2 * source + 1], table[1, 2 * source])
            chosen = (position < count) & (target == position + start)
            acc[...] += jnp.dot(
                chosen.astype(jnp.bfloat16), buffer[source], preferred_element_type=jnp.float32
            )

    x_ref[...] = acc[...].astype(jnp.bfloat16)
    row = lax.broadcasted_iota(jnp.int32, (rows_out, 128), 0) + first

    def own(slot, tenant):
        start, count = table[0, slot], table[1, slot]
        return jnp.where((row >= start) & (row < start + count), table[2, slot], tenant)

    tenant = lax.fori_loop(0, slots, own, jnp.full((rows_out, 128), -1, jnp.int32))
    lane = lax.broadcasted_iota(jnp.int32, (rows_out, 128), 1)
    pick_ref[...] = ((lane % 8 == tenant) & (lane < 24)).astype(jnp.bfloat16)

    for copy in down_copies:
        copy.wait()
    low = lax.dot_general(x_ref[...], down[...], (((1,), (1,)), ((), ())), preferred_element_type=jnp.float32)
    for side in range(2):
        mine = jnp.where(lane // RANK == tenant, low[:, side * 128:(side + 1) * 128], 0.0)
        high = mine.astype(jnp.bfloat16)
        low_ref[side, :, 0:128] = high
        low_ref[side, :, 128:256] = (mine - high.astype(jnp.float32)).astype(jnp.bfloat16)


def pack_rows(mx_count, chunk, scalars, tokens, down, after=(), passed=(), cost=COST):
    first, rows_out, slots = chunk
    width = down.shape[1]
    outs = [
        jax.ShapeDtypeStruct((rows_out, width), jnp.bfloat16),
        jax.ShapeDtypeStruct((2, rows_out, 256), jnp.bfloat16),
        jax.ShapeDtypeStruct((rows_out, 128), jnp.bfloat16),
    ]
    out_specs = [
        pl.BlockSpec((rows_out, width), lambda i, *_: (0, 0)),
        pl.BlockSpec((2, rows_out, 256), lambda i, *_: (0, 0, 0)),
        pl.BlockSpec((rows_out, 128), lambda i, *_: (0, 0)),
    ] + [ANY] * len(passed)
    return pl.pallas_call(
        functools.partial(pack_kernel, mx_count, first, rows_out, slots, len(passed)),
        out_shape=outs + [jax.ShapeDtypeStruct(tokens[i].shape, tokens[i].dtype) for i in passed],
        grid_spec=pltpu.PrefetchScalarGridSpec(
            num_scalar_prefetch=3,
            grid=(1,),
            in_specs=[ANY] * (len(tokens) + 1 + len(after)),
            out_specs=out_specs,
            scratch_shapes=[
                pltpu.SMEM((4, len(SLOTS)), jnp.int32),
                pltpu.VMEM((slots // 2, 2 * BLOCK_ROWS, width), jnp.bfloat16),
                pltpu.VMEM(down.shape, jnp.bfloat16),
                pltpu.VMEM((rows_out, width), jnp.float32),
                pltpu.SemaphoreType.DMA((slots // 2,)),
                pltpu.SemaphoreType.DMA((2, 8)),
            ],
        ),
        input_output_aliases={3 + place: 3 + i for i, place in enumerate(passed)},
        compiler_params=pltpu.CompilerParams(vmem_limit_bytes=VMEM_LIMIT),
        cost_estimate=cost,
        name="pack_rows",
    )(*scalars, *tokens, down, *after)


def activate(gate, up):
    return (gate * (1.0 / (1.0 + jnp.exp(-gate))) * up).astype(jnp.bfloat16)


def dot_kernel(flip, counts, splits, term_counts, finished, narrow, ids, *refs):
    parts = len(counts)
    finish = finished > 0
    x_refs, low_refs, refs = refs[:parts], refs[parts:2 * parts], refs[2 * parts:]
    w_refs, up_ref, refs = refs[:2], refs[2], refs[3:]
    terms = len(term_counts)
    term_refs, refs = refs[:2 * terms], refs[2 * terms:]
    if finish:
        far_refs, refs = refs[:finished], refs[finished:]
        pick_refs, scale_ref, refs = refs[:finished], refs[finished], refs[finished + 1:]
    x, low, w, maps, term, acc, out, far, pick, scale, in_sem, w_sem, out_sem = refs[-13:]
    outs = refs[-13 - (2 if finish else max(1, 2 * len(splits))):-13]
    done = sum(counts[:finished])
    rows, depth = x.shape
    steps = depth // STEP_DEPTH
    left = pl.multiple_of((ids[1] ^ flip) * narrow, 128)
    tiles = [(at, min(TILE, narrow - at)) for at in range(0, narrow, TILE)]
    loads = []

    def load(source, target):
        copy = pltpu.make_async_copy(source, target, in_sem.at[len(loads)])
        copy.start()
        loads.append(copy)

    def piece(side, step):
        return pltpu.make_async_copy(
            w_refs[side].at[pl.ds(step * STEP_DEPTH, STEP_DEPTH), pl.ds(left, narrow)],
            w.at[side, step], w_sem.at[side, step],
        )

    def start_step(step):
        for side in range(2):
            piece(side, step).start()

    def stores(place):
        at, size = tiles[place]
        columns = pl.ds(at, size)
        if finish:
            pairs = [(out.at[0, :, columns], outs[0].at[:, columns])]
            pairs += [(acc.at[side, pl.ds(done, rows - done), columns], outs[1].at[side, :, columns]) for side in range(2)]
        elif not splits:
            pairs = [(out.at[side, :, columns], outs[0].at[side, :, columns]) for side in range(2)]
        else:
            pairs = []
            for side in range(2):
                row = 0
                for part, count in enumerate(splits):
                    target = outs[side * len(splits) + part].at[:, columns]
                    pairs.append((out.at[side, pl.ds(row, count), columns], target))
                    row += count
        return [
            pltpu.make_async_copy(source, target, out_sem.at[place, i]) for i, (source, target) in enumerate(pairs)
        ]

    def part_dot(side, step, columns):
        depths = pl.ds(step * STEP_DEPTH, STEP_DEPTH)
        return jnp.dot(x[:, depths], w[side, step, :, columns], preferred_element_type=jnp.float32)

    row = 0
    for part, count in enumerate(counts):
        load(x_refs[part], x.at[pl.ds(row, count)])
        row += count
    first_loads = len(loads)
    start_step(0)
    start_step(1)
    row = 0
    for part, count in enumerate(counts):
        load(low_refs[part], low.at[:, pl.ds(row, count)])
        row += count
    for side in range(2):
        load(up_ref.at[:, side, :, pl.ds(left, narrow)], maps.at[side, 0])
    if terms:
        for side in range(2):
            row = 0
            for part, count in enumerate(term_counts):
                load(term_refs[2 * part + side], term.at[side, pl.ds(row, count)])
                row += count
    if finish:
        row = 0
        for part, count in enumerate(counts[:finished]):
            here = pl.ds(row, count)
            load(far_refs[part], far.at[:, here])
            load(pick_refs[part], pick.at[here])
            row += count
        load(scale_ref, scale)

    for copy in loads[:first_loads]:
        copy.wait()
    for side in range(2):
        piece(side, 0).wait()
        if steps > 2:
            piece(side, 2).start()
        acc[side] = part_dot(side, 0, slice(None))

    @pl.loop(1, steps - 1)
    def _(step):
        for side in range(2):
            piece(side, step).wait()

            @pl.when(step + 2 < steps)
            def _():
                piece(side, step + 2).start()

            depths = pl.ds(pl.multiple_of(step * STEP_DEPTH, STEP_DEPTH), STEP_DEPTH)
            acc[side] += jnp.dot(x[:, depths], w[side, step], preferred_element_type=jnp.float32)

    for copy in loads[first_loads:]:
        copy.wait()
    for side in range(2):
        maps[side, 1] = maps[side, 0]
        piece(side, steps - 1).wait()
    for place, (at, size) in enumerate(tiles):
        columns = slice(at, at + size)
        values = []
        for side in range(2):
            value = acc[side, :, columns] + part_dot(side, steps - 1, columns)
            value += jnp.dot(
                low[side], maps[side, :, :, :, columns].reshape(256, size), preferred_element_type=jnp.float32
            )
            if terms:
                value += term[side, :, columns].astype(jnp.float32)
            if finish:
                acc[side, done:, columns] = value[done:]
                value = value[:done] + far[side, :, columns].astype(jnp.float32)
                value *= jnp.dot(pick[...], scale[side, :, columns], preferred_element_type=jnp.float32)
                values.append(value)
            else:
                out[side, :, columns] = value.astype(out.dtype)
        if finish:
            out[0, :, columns] = activate(*values)
        for copy in stores(place):
            copy.start()
    for place in range(len(tiles)):
        for copy in stores(place):
            copy.wait()


def dot_pair(chunks, weights, adapter_out, flip, narrow, ids, splits=(), terms=(), finish=None, after=()):
    xs, lows, picks = zip(*chunks)
    counts = tuple(x.shape[0] for x in xs)
    rows, depth = sum(counts), xs[0].shape[1]
    tenants = adapter_out.shape[0]
    term_counts = tuple(gate.shape[0] for gate, _ in terms)
    operands = [ids, *xs, *lows, *weights, adapter_out, *[array for pair in terms for array in pair]]
    finished = 0
    if finish is not None:
        finished = len(finish[0])
        done = sum(counts[:finished])
        operands += [*finish[0], *picks[:finished], finish[1]]
        out_shape = [
            jax.ShapeDtypeStruct((done, narrow), jnp.bfloat16),
            jax.ShapeDtypeStruct((2, rows - done, narrow), jnp.float32),
        ]
    elif splits:
        out_shape = [jax.ShapeDtypeStruct((count, narrow), jnp.bfloat16) for _ in range(2) for count in splits]
    else:
        out_shape = [jax.ShapeDtypeStruct((2, rows, narrow), jnp.bfloat16)]
    operands += list(after)
    few = (8, 128)
    steps = depth // STEP_DEPTH
    return pl.pallas_call(
        functools.partial(
            dot_kernel, flip, counts, splits, term_counts, finished, narrow
        ),
        out_shape=out_shape,
        grid_spec=pltpu.PrefetchScalarGridSpec(
            num_scalar_prefetch=1,
            grid=(1,),
            in_specs=[ANY] * (len(operands) - 1),
            out_specs=[ANY] * len(out_shape),
            scratch_shapes=[
                pltpu.VMEM((rows, depth), jnp.bfloat16),
                pltpu.VMEM((2, rows, 256), jnp.bfloat16),
                pltpu.VMEM((2, steps, STEP_DEPTH, narrow), jnp.bfloat16),
                pltpu.VMEM((2, 2, tenants, RANK, narrow), jnp.bfloat16),
                pltpu.VMEM((2, rows, narrow) if terms else few, jnp.bfloat16),
                pltpu.VMEM((2, rows, narrow), jnp.float32),
                pltpu.VMEM((1, done, narrow) if finished else (2, rows, narrow), jnp.bfloat16),
                pltpu.VMEM((2, done, narrow) if finished else few, jnp.bfloat16),
                pltpu.VMEM((done, 128) if finished else few, jnp.bfloat16),
                pltpu.VMEM((2, 128, narrow) if finished else few, jnp.bfloat16),
                pltpu.SemaphoreType.DMA((4 * len(xs) + 8,)),
                pltpu.SemaphoreType.DMA((2, steps)),
                pltpu.SemaphoreType.DMA((-(-narrow // TILE), 4)),
            ],
        ),
        compiler_params=pltpu.CompilerParams(vmem_limit_bytes=VMEM_LIMIT),
        cost_estimate=COST,
        name="finish_dots" if finished else "dot_pair",
    )(*operands)


def last_kernel(
    mx_count, first, ids, rows, tenants, sums_ref, far_ref, pick, scale, earlier_ref, out_ref, table, sums, far, held,
    tile_sem, held_sem,
):
    block = pl.program_id(0)
    tiles = far.shape[1] // 64

    def tile_copies(tile):
        here = pl.ds(pl.multiple_of(tile * 64, 64), 64)
        return [
            pltpu.make_async_copy(source.at[:, here], target.at[:, here], tile_sem.at[tile, i])
            for i, (source, target) in enumerate([(sums_ref, sums), (far_ref, far)])
        ]

    @pl.when(block == 0)
    def _():
        for tile in range(tiles):
            for copy in tile_copies(tile):
                copy.start()
        held_copy = pltpu.make_async_copy(earlier_ref, held.at[pl.ds(0, first)], held_sem)
        held_copy.start()
        fill_table(table, ids, rows, tenants, mx_count)
        held[LIVE_ROWS:, :] = jnp.zeros((BLOCK_ROWS, held.shape[1]), held.dtype)
        columns = held.shape[1]

        @pl.loop(0, tiles)
        def _(tile):
            for copy in tile_copies(tile):
                copy.wait()
            here = pl.ds(pl.multiple_of(tile * 64, 64), 64)
            there = pl.ds(pl.multiple_of(first + tile * 64, 64), 64)
            for left in range(0, columns, TILE):
                right = min(left + TILE, columns)
                pre = [
                    (sums[side, here, left:right] + far[side, here, left:right].astype(jnp.float32))
                    * jnp.dot(pick[here, :], scale[side, :, left:right], preferred_element_type=jnp.float32)
                    for side in range(2)
                ]
                held[there, left:right] = activate(*pre)

        held_copy.wait()

    def find(slot, start):
        return jnp.where(table[3, slot] == block, table[0, slot], start)

    start = lax.fori_loop(0, len(SLOTS), find, jnp.int32(0))
    count = rows[block]
    base = pl.multiple_of(jnp.minimum(start // BLOCK_ROWS * BLOCK_ROWS, LIVE_ROWS - BLOCK_ROWS), BLOCK_ROWS)
    shape = (BLOCK_ROWS, 2 * BLOCK_ROWS)
    position = lax.broadcasted_iota(jnp.int32, shape, 0)
    column = lax.broadcasted_iota(jnp.int32, shape, 1) + base
    chosen = (position < count) & (column == position + start)
    out_ref[...] = jnp.dot(
        chosen.astype(jnp.bfloat16), held[pl.ds(base, 2 * BLOCK_ROWS), :], preferred_element_type=jnp.float32
    ).astype(jnp.bfloat16)


def last_rows(mx_count, first, scalars, sums, far, pick, scale, earlier, blocks):
    narrow = far.shape[2]
    operands = (sums, far, pick, scale, earlier)
    return pl.pallas_call(
        functools.partial(last_kernel, mx_count, first),
        out_shape=jax.ShapeDtypeStruct((blocks * BLOCK_ROWS, narrow), jnp.bfloat16),
        grid_spec=pltpu.PrefetchScalarGridSpec(
            num_scalar_prefetch=3,
            grid=(blocks,),
            in_specs=[
                ANY, ANY,
                pl.BlockSpec(pick.shape, lambda i, *_: (0, 0)),
                pl.BlockSpec(scale.shape, lambda i, *_: (0, 0, 0)),
                ANY,
            ],
            out_specs=pl.BlockSpec((BLOCK_ROWS, narrow), lambda i, *_: (i, 0)),
            scratch_shapes=[
                pltpu.SMEM((4, len(SLOTS)), jnp.int32),
                pltpu.VMEM(sums.shape, sums.dtype),
                pltpu.VMEM(far.shape, far.dtype),
                pltpu.VMEM((LIVE_ROWS + BLOCK_ROWS, narrow), jnp.bfloat16),
                pltpu.SemaphoreType.DMA((far.shape[1] // 64, 2)),
                pltpu.SemaphoreType.DMA,
            ],
        ),
        compiler_params=pltpu.CompilerParams(vmem_limit_bytes=VMEM_LIMIT),
        cost_estimate=COST,
        name="last_rows",
    )(*scalars, *operands)


def quarter(array, index, narrow):
    return lax.dynamic_slice_in_dim(array, index * narrow, narrow, array.ndim - 1)


def pipelined(
    tokens, w_gate, w_up, adapter_in, adapter_out, magnitude, partial_norms, block_tenant, block_rows
):
    mx_count = lax.axis_size("mx")
    my_count = lax.axis_size("my")
    narrow = w_gate.shape[1] // my_count
    mine = lax.axis_index("my")
    ids = jnp.stack([lax.axis_index("mx"), mine]).astype(jnp.int32)
    scalars = (ids, block_rows, block_tenant)
    near = [(i, i ^ 1) for i in range(my_count)]
    across = [(i, i ^ 2) for i in range(my_count)]

    def hop(block, distance, least=0):
        if distance > 0:
            pairs = [(i, i + distance) for i in range(least, mx_count - distance)]
        else:
            pairs = [(i, i + distance) for i in range(-distance, mx_count - least)]
        return lax.ppermute(block, "mx", pairs)

    blocks = [tokens, hop(tokens, 1), hop(tokens, -1)]

    norms = partial_norms[0]
    pair = jnp.stack([quarter(norms, mine, narrow), quarter(norms, mine ^ 2, narrow)])
    other = jnp.stack([quarter(norms, mine ^ 1, narrow), quarter(norms, mine ^ 3, narrow)])
    pair = pair + lax.ppermute(other, "my", near)
    norm_total = pair[0] + lax.ppermute(pair[1], "my", across)
    scale = quarter(magnitude, mine, narrow) * lax.rsqrt(norm_total)
    scale = jnp.transpose(scale, (1, 0, 2))
    high = lax.reduce_precision(scale, 8, 7)
    middle = lax.reduce_precision(scale - high, 8, 7)
    rest = scale - high - middle
    scale = jnp.concatenate(
        [high, middle, rest, jnp.zeros((2, 128 - 3 * scale.shape[1], narrow), jnp.float32)], axis=1
    ).astype(jnp.bfloat16)

    down = jnp.transpose(adapter_in, (0, 2, 1)).reshape(-1, adapter_in.shape[1])

    dots = functools.partial(
        dot_pair, weights=(w_gate, w_up), adapter_out=adapter_out, narrow=narrow, ids=ids
    )

    def swap(parts, pairs):
        return [lax.ppermute(part, "my", pairs) for part in parts]

    def far_out(chunk, after=()):
        return dots([chunk], flip=3, splits=(chunk[0].shape[0],), after=after)

    def far_in(chunk, got, after=()):
        part, = dots([chunk], flip=2, terms=(got,), after=after)
        return part, lax.ppermute(part, "my", across)

    *chunk0, up, down_line = pack_rows(
        mx_count, CHUNKS[0], scalars, blocks, down, after=(scale,), passed=(1, 2)
    )
    blocks = [tokens, up, down_line, hop(up, 1, 1), hop(down_line, -1, 1)]
    mark, far0 = far_in(chunk0, swap(far_out(chunk0), near))

    third_hop = [hop(blocks[3], 1, 2), hop(blocks[4], -1, 2)]
    *chunk1, = pack_rows(mx_count, CHUNKS[1], scalars, blocks, down, after=(mark,), cost=LONG)
    blocks += third_hop
    mark, far1 = far_in(chunk1, swap(far_out(chunk1), near))

    first, last = CHUNKS[2][:2]
    *chunk2, = pack_rows(mx_count, CHUNKS[2], scalars, blocks, down, after=(mark,))
    parts = far_out(chunk2, (far0,))
    got = swap(parts, near)
    parts = dots([chunk0, chunk1], flip=1, splits=(first,), after=(parts[0],))
    early = swap(parts, near)
    mark, far2 = far_in(chunk2, got, after=(parts[0],))

    parts = dots([chunk2], flip=1, splits=(last,), after=(mark,))
    late = swap(parts, near)
    hidden, sums = dots([chunk0, chunk1, chunk2], flip=0, terms=(early, late), finish=((far0, far1), scale))
    return last_rows(mx_count, first, scalars, sums, far2, chunk2[2], scale, hidden, block_rows.shape[0])


def adapter_low(rows_piece, aligned_row_total, adapter_in, block_tenant):
    row_count = rows_piece.shape[0]
    seg_rows = math.gcd(math.gcd(row_count, BLOCK_ROWS), aligned_row_total)
    seg_count = row_count // seg_rows
    seg_block = jnp.arange(seg_count, dtype=jnp.int32) * seg_rows // BLOCK_ROWS
    tenant_tables = adapter_in[block_tenant[seg_block]]
    grouped = rows_piece.reshape(seg_count, seg_rows, rows_piece.shape[1])
    low_terms = jnp.einsum(
        "skd,sdr->skr", grouped, tenant_tables, preferred_element_type=jnp.float32
    )
    return low_terms.reshape(row_count, tenant_tables.shape[2])


def finish_plain(
    summed, reduced_rank_factor, norm_total, mag_cols, adapter_cols, first_row, block_tenant, block_rows
):
    row_count = summed.shape[0]
    col_count = summed.shape[2]
    seg_rows = math.gcd(row_count, BLOCK_ROWS)
    seg_count = row_count // seg_rows
    seg_block = (first_row + jnp.arange(seg_count, dtype=jnp.int32) * seg_rows) // BLOCK_ROWS
    tenants = block_tenant[seg_block]
    col_scale = mag_cols * lax.rsqrt(norm_total)
    seg_scale = col_scale[tenants]
    seg_tables = adapter_cols[tenants]
    low_pair = reduced_rank_factor.reshape(seg_count, seg_rows, 2, RANK)
    adapted = jnp.einsum(
        "skpr,sprc->skpc", low_pair, seg_tables, preferred_element_type=jnp.float32
    )
    pre_act = (summed.reshape(seg_count, seg_rows, 2, col_count) + adapted) * seg_scale[:, None]
    hidden = jax.nn.silu(pre_act[:, :, 0]) * pre_act[:, :, 1]
    offsets = (first_row + jnp.arange(row_count, dtype=jnp.int32)).reshape(
        seg_count, seg_rows
    ) % BLOCK_ROWS
    live_mask = offsets < block_rows[seg_block][:, None]
    hidden = jnp.where(live_mask[:, :, None], hidden, jnp.zeros_like(hidden))
    return hidden.reshape(row_count, col_count).astype(jnp.bfloat16)


def plain(
    tokens, w_gate, w_up, adapter_in, adapter_out, magnitude, partial_norms, block_tenant, block_rows
):
    local_rows = tokens.shape[0]
    col_local = w_gate.shape[1]
    my_count = lax.axis_size("my")
    device_position = lax.axis_index("my")
    rows_piece = lax.all_gather(tokens, "mx", axis=0, tiled=True)
    gate_part = jnp.dot(rows_piece, w_gate, preferred_element_type=jnp.float32)
    up_part = jnp.dot(rows_piece, w_up, preferred_element_type=jnp.float32)
    main_part = jnp.stack((gate_part, up_part), axis=1)
    low_terms = adapter_low(rows_piece, local_rows, adapter_in, block_tenant)
    reduced_rank_factor = lax.psum(low_terms, "my").astype(jnp.bfloat16)
    summed = lax.psum_scatter(main_part, "my", scatter_dimension=2, tiled=True)
    norm_total = lax.psum_scatter(partial_norms[0], "my", scatter_dimension=2, tiled=True)
    narrow = col_local // my_count
    mag_cols = lax.dynamic_slice_in_dim(magnitude, device_position * narrow, narrow, 2)
    adapter_cols = lax.dynamic_slice_in_dim(adapter_out, device_position * narrow, narrow, 3)
    return finish_plain(
        summed, reduced_rank_factor, norm_total, mag_cols, adapter_cols, 0, block_tenant, block_rows
    )


def on_device(tokens, w_gate, w_up, adapter_in, *rest):
    my_count = lax.axis_size("my")
    fits = (
        my_count == 4
        and lax.axis_size("mx") == 4
        and tokens.shape[0] == 2 * BLOCK_ROWS
        and adapter_in.shape[0] == 8
        and tokens.shape[1] % STEP_DEPTH == 0
        and tokens.shape[1] >= 2 * STEP_DEPTH
        and w_gate.shape[1] % (my_count * 128) == 0
    )
    return (pipelined if fits else plain)(tokens, w_gate, w_up, adapter_in, *rest)


def solution(mesh):
    return jax.shard_map(
        on_device,
        mesh=mesh,
        in_specs=(
            P(("groups", "mx"), "my"),
            P("my", "mx"),
            P("my", "mx"),
            P(None, "my", None),
            P(None, None, None, "mx"),
            P(None, None, "mx"),
            P("my", None, None, "mx"),
            P("groups"),
            P("groups"),
        ),
        out_specs=P("groups", ("mx", "my")),
        check_vma=False,
    )
```

```python
import functools
import math

import jax
import jax.numpy as jnp
from jax import lax
from jax.experimental import pallas as pl
from jax.experimental.pallas import tpu as pltpu
from jax.sharding import PartitionSpec as P

RANK = 16
BLOCK_ROWS = 128
LIVE_ROWS = 768
STEP_DEPTH = 512
TILE = 512
VMEM_LIMIT = 66 * 10**6

SLOTS = tuple((distance, half) for distance in (0, -1, 1, -2, 2, -3, 3) for half in range(2))
CHUNKS = ((0, 256, 6), (256, 256, 10), (512, 256, 14))
ANY = pl.BlockSpec(memory_space=pl.ANY)
COST = pl.CostEstimate(flops=0, bytes_accessed=0, transcendentals=0)
LONG = pl.CostEstimate(flops=10**12, bytes_accessed=0, transcendentals=0)


def fill_table(table, ids, rows, tenants, mx_count):
    start = jnp.int32(0)
    for slot, (distance, half) in enumerate(SLOTS):
        source = ids[0] + distance
        valid = (source >= 0) & (source < mx_count)
        block = jnp.clip(source, 0, mx_count - 1) * 2 + half
        count = jnp.where(valid, rows[block], 0)
        table[0, slot] = start
        table[1, slot] = count
        table[2, slot] = tenants[block]
        table[3, slot] = jnp.where(valid, block, -1)
        start = start + count


def pack_kernel(mx_count, first, rows_out, slots, passed, ids, rows, tenants, *refs):
    token_refs, down_ref = refs[:slots // 2], refs[slots // 2]
    outs, scratch = refs[-9 - passed:-6], refs[-6:]
    x_ref, low_ref, pick_ref = outs[:3]
    table, buffer, down, acc, sems, down_sem = scratch
    fill_table(table, ids, rows, tenants, mx_count)

    def needed(source):
        start, count = table[0, 2 * source], table[1, 2 * source] + table[1, 2 * source + 1]
        return (count > 0) & (start < first + rows_out) & (start + count > first)

    for source in range(slots // 2):
        @pl.when(needed(source))
        def _():
            pltpu.make_async_copy(token_refs[source], buffer.at[source], sems.at[source]).start()

    down_copies = [
        pltpu.make_async_copy(
            down_ref.at[pl.ds((2 * place + side) * RANK, RANK)], down.at[pl.ds((8 * side + place) * RANK, RANK)],
            down_sem.at[side, place],
        )
        for side in range(2) for place in range(8)
    ]
    for copy in down_copies:
        copy.start()
    acc[...] = jnp.zeros_like(acc)

    @pl.loop(0, slots // 2)
    def _(source):
        @pl.when(needed(source))
        def _():
            pltpu.make_async_copy(buffer.at[source], buffer.at[source], sems.at[source]).wait()
            target = lax.broadcasted_iota(jnp.int32, (rows_out, 2 * BLOCK_ROWS), 0) + first
            place = lax.broadcasted_iota(jnp.int32, (rows_out, 2 * BLOCK_ROWS), 1)
            upper = place >= BLOCK_ROWS
            position = jnp.where(upper, place - BLOCK_ROWS, place)
            start = jnp.where(upper, table[0, 2 * source + 1], table[0, 2 * source])
            count = jnp.where(upper, table[1, 2 * source + 1], table[1, 2 * source])
            chosen = (position < count) & (target == position + start)
            acc[...] += jnp.dot(
                chosen.astype(jnp.bfloat16), buffer[source], preferred_element_type=jnp.float32
            )

    x_ref[...] = acc[...].astype(jnp.bfloat16)
    row = lax.broadcasted_iota(jnp.int32, (rows_out, 128), 0) + first

    def own(slot, tenant):
        start, count = table[0, slot], table[1, slot]
        return jnp.where((row >= start) & (row < start + count), table[2, slot], tenant)

    tenant = lax.fori_loop(0, slots, own, jnp.full((rows_out, 128), -1, jnp.int32))
    lane = lax.broadcasted_iota(jnp.int32, (rows_out, 128), 1)
    pick_ref[...] = ((lane % 8 == tenant) & (lane < 24)).astype(jnp.bfloat16)

    for copy in down_copies:
        copy.wait()
    low = lax.dot_general(x_ref[...], down[...], (((1,), (1,)), ((), ())), preferred_element_type=jnp.float32)
    for side in range(2):
        mine = jnp.where(lane // RANK == tenant, low[:, side * 128:(side + 1) * 128], 0.0)
        high = mine.astype(jnp.bfloat16)
        low_ref[side, :, 0:128] = high
        low_ref[side, :, 128:256] = (mine - high.astype(jnp.float32)).astype(jnp.bfloat16)


def pack_rows(mx_count, chunk, scalars, tokens, down, after=(), passed=(), cost=COST):
    first, rows_out, slots = chunk
    width = down.shape[1]
    outs = [
        jax.ShapeDtypeStruct((rows_out, width), jnp.bfloat16),
        jax.ShapeDtypeStruct((2, rows_out, 256), jnp.bfloat16),
        jax.ShapeDtypeStruct((rows_out, 128), jnp.bfloat16),
    ]
    out_specs = [
        pl.BlockSpec((rows_out, width), lambda i, *_: (0, 0)),
        pl.BlockSpec((2, rows_out, 256), lambda i, *_: (0, 0, 0)),
        pl.BlockSpec((rows_out, 128), lambda i, *_: (0, 0)),
    ] + [ANY] * len(passed)
    return pl.pallas_call(
        functools.partial(pack_kernel, mx_count, first, rows_out, slots, len(passed)),
        out_shape=outs + [jax.ShapeDtypeStruct(tokens[i].shape, tokens[i].dtype) for i in passed],
        grid_spec=pltpu.PrefetchScalarGridSpec(
            num_scalar_prefetch=3,
            grid=(1,),
            in_specs=[ANY] * (len(tokens) + 1 + len(after)),
            out_specs=out_specs,
            scratch_shapes=[
                pltpu.SMEM((4, len(SLOTS)), jnp.int32),
                pltpu.VMEM((slots // 2, 2 * BLOCK_ROWS, width), jnp.bfloat16),
                pltpu.VMEM(down.shape, jnp.bfloat16),
                pltpu.VMEM((rows_out, width), jnp.float32),
                pltpu.SemaphoreType.DMA((slots // 2,)),
                pltpu.SemaphoreType.DMA((2, 8)),
            ],
        ),
        input_output_aliases={3 + place: 3 + i for i, place in enumerate(passed)},
        compiler_params=pltpu.CompilerParams(vmem_limit_bytes=VMEM_LIMIT),
        cost_estimate=cost,
        name="pack_rows",
    )(*scalars, *tokens, down, *after)


def activate(gate, up):
    return (gate * (1.0 / (1.0 + jnp.exp(-gate))) * up).astype(jnp.bfloat16)


def dot_kernel(flip, counts, splits, term_counts, finished, narrow, ids, *refs):
    parts = len(counts)
    finish = finished > 0
    x_refs, low_refs, refs = refs[:parts], refs[parts:2 * parts], refs[2 * parts:]
    w_refs, up_ref, refs = refs[:2], refs[2], refs[3:]
    terms = len(term_counts)
    term_refs, refs = refs[:2 * terms], refs[2 * terms:]
    if finish:
        far_refs, refs = refs[:finished], refs[finished:]
        pick_refs, scale_ref, refs = refs[:finished], refs[finished], refs[finished + 1:]
    x, low, w, maps, term, acc, out, far, pick, scale, in_sem, w_sem, out_sem = refs[-13:]
    outs = refs[-13 - (2 if finish else max(1, 2 * len(splits))):-13]
    done = sum(counts[:finished])
    rows, depth = x.shape
    steps = depth // STEP_DEPTH
    left = pl.multiple_of((ids[1] ^ flip) * narrow, 128)
    tiles = [(at, min(TILE, narrow - at)) for at in range(0, narrow, TILE)]
    loads = []

    def load(source, target):
        copy = pltpu.make_async_copy(source, target, in_sem.at[len(loads)])
        copy.start()
        loads.append(copy)

    def piece(side, step):
        return pltpu.make_async_copy(
            w_refs[side].at[pl.ds(step * STEP_DEPTH, STEP_DEPTH), pl.ds(left, narrow)],
            w.at[side, step], w_sem.at[side, step],
        )

    def start_step(step):
        for side in range(2):
            piece(side, step).start()

    def stores(at, size, place):
        columns = pl.ds(at, size)
        if finish:
            pairs = [(out.at[0, :, columns], outs[0].at[:, columns])]
            pairs += [(acc.at[side, pl.ds(done, rows - done), columns], outs[1].at[side, :, columns]) for side in range(2)]
        elif not splits:
            pairs = [(out.at[side, :, columns], outs[0].at[side, :, columns]) for side in range(2)]
        else:
            pairs = []
            for side in range(2):
                row = 0
                for part, count in enumerate(splits):
                    target = outs[side * len(splits) + part].at[:, columns]
                    pairs.append((out.at[side, pl.ds(row, count), columns], target))
                    row += count
        return [
            pltpu.make_async_copy(source, target, out_sem.at[place, i]) for i, (source, target) in enumerate(pairs)
        ]

    row = 0
    for part, count in enumerate(counts):
        load(x_refs[part], x.at[pl.ds(row, count)])
        load(low_refs[part], low.at[:, pl.ds(row, count)])
        row += count
    for side in range(2):
        load(up_ref.at[:, side, :, pl.ds(left, narrow)], maps.at[side, 0])
    first_loads = len(loads)
    start_step(0)
    start_step(1)
    if terms:
        for side in range(2):
            row = 0
            for part, count in enumerate(term_counts):
                load(term_refs[2 * part + side], term.at[side, pl.ds(row, count)])
                row += count
    if finish:
        row = 0
        for part, count in enumerate(counts[:finished]):
            here = pl.ds(row, count)
            load(far_refs[part], far.at[:, here])
            load(pick_refs[part], pick.at[here])
            row += count
        load(scale_ref, scale)

    for copy in loads[:first_loads]:
        copy.wait()
    for side in range(2):
        maps[side, 1] = maps[side, 0]

    @pl.loop(0, 2)
    def _(side):
        acc[side] = jnp.dot(low[side], maps[side].reshape(256, narrow), preferred_element_type=jnp.float32)

    @pl.loop(0, steps - 1)
    def _(step):
        for side in range(2):
            piece(side, step).wait()

            @pl.when(step + 2 < steps)
            def _():
                piece(side, step + 2).start()

        depths = pl.ds(pl.multiple_of(step * STEP_DEPTH, STEP_DEPTH), STEP_DEPTH)

        @pl.loop(0, 2)
        def _(side):
            acc[side] += jnp.dot(x[:, depths], w[side, step], preferred_element_type=jnp.float32)

    for copy in loads[first_loads:]:
        copy.wait()
    for side in range(2):
        piece(side, steps - 1).wait()

    def last_step(at, size, place):
        columns = pl.ds(at, size)
        values = []
        for side in range(2):
            value = acc[side, :, columns] + jnp.dot(
                x[:, depth - STEP_DEPTH:], w[side, steps - 1, :, columns], preferred_element_type=jnp.float32
            )
            if terms:
                value += term[side, :, columns].astype(jnp.float32)
            if finish:
                acc[side, done:, columns] = value[done:]
                value = value[:done] + far[side, :, columns].astype(jnp.float32)
                value *= jnp.dot(pick[...], scale[side, :, columns], preferred_element_type=jnp.float32)
                values.append(value)
            else:
                out[side, :, columns] = value.astype(out.dtype)
        if finish:
            out[0, :, columns] = activate(*values)
        for copy in stores(at, size, place):
            copy.start()

    whole = narrow // TILE

    @pl.loop(0, whole)
    def _(place):
        last_step(pl.multiple_of(place * TILE, TILE), TILE, place)

    for place in range(whole, len(tiles)):
        last_step(*tiles[place], place)
    for place, (at, size) in enumerate(tiles):
        for copy in stores(at, size, place):
            copy.wait()


def dot_pair(chunks, weights, adapter_out, flip, narrow, ids, splits=(), terms=(), finish=None, after=()):
    xs, lows, picks = zip(*chunks)
    counts = tuple(x.shape[0] for x in xs)
    rows, depth = sum(counts), xs[0].shape[1]
    tenants = adapter_out.shape[0]
    term_counts = tuple(gate.shape[0] for gate, _ in terms)
    operands = [ids, *xs, *lows, *weights, adapter_out, *[array for pair in terms for array in pair]]
    finished = 0
    if finish is not None:
        finished = len(finish[0])
        done = sum(counts[:finished])
        operands += [*finish[0], *picks[:finished], finish[1]]
        out_shape = [
            jax.ShapeDtypeStruct((done, narrow), jnp.bfloat16),
            jax.ShapeDtypeStruct((2, rows - done, narrow), jnp.float32),
        ]
    elif splits:
        out_shape = [jax.ShapeDtypeStruct((count, narrow), jnp.bfloat16) for _ in range(2) for count in splits]
    else:
        out_shape = [jax.ShapeDtypeStruct((2, rows, narrow), jnp.bfloat16)]
    operands += list(after)
    few = (8, 128)
    steps = depth // STEP_DEPTH
    return pl.pallas_call(
        functools.partial(
            dot_kernel, flip, counts, splits, term_counts, finished, narrow
        ),
        out_shape=out_shape,
        grid_spec=pltpu.PrefetchScalarGridSpec(
            num_scalar_prefetch=1,
            grid=(1,),
            in_specs=[ANY] * (len(operands) - 1),
            out_specs=[ANY] * len(out_shape),
            scratch_shapes=[
                pltpu.VMEM((rows, depth), jnp.bfloat16),
                pltpu.VMEM((2, rows, 256), jnp.bfloat16),
                pltpu.VMEM((2, steps, STEP_DEPTH, narrow), jnp.bfloat16),
                pltpu.VMEM((2, 2, tenants, RANK, narrow), jnp.bfloat16),
                pltpu.VMEM((2, rows, narrow) if terms else few, jnp.bfloat16),
                pltpu.VMEM((2, rows, narrow), jnp.float32),
                pltpu.VMEM((1, done, narrow) if finished else (2, rows, narrow), jnp.bfloat16),
                pltpu.VMEM((2, done, narrow) if finished else few, jnp.bfloat16),
                pltpu.VMEM((done, 128) if finished else few, jnp.bfloat16),
                pltpu.VMEM((2, 128, narrow) if finished else few, jnp.bfloat16),
                pltpu.SemaphoreType.DMA((4 * len(xs) + 8,)),
                pltpu.SemaphoreType.DMA((2, steps)),
                pltpu.SemaphoreType.DMA((-(-narrow // TILE), 4)),
            ],
        ),
        compiler_params=pltpu.CompilerParams(vmem_limit_bytes=VMEM_LIMIT),
        cost_estimate=COST,
        name="finish_dots" if finished else "dot_pair",
    )(*operands)


def last_kernel(
    mx_count, first, ids, rows, tenants, sums_ref, far_ref, pick_ref, scale_ref, earlier_ref, out_ref,
    table, bases, sums, far, pick, scale, held, chosen, out, in_sem, tile_sem, out_sem,
):
    columns = held.shape[1]
    blocks = chosen.shape[0]
    tiles = [(at, min(TILE, columns - at)) for at in range(0, columns, TILE)]

    def reads(at, size, place):
        here = pl.ds(at, size)
        return [
            pltpu.make_async_copy(source.at[:, :, here], target.at[:, :, here], tile_sem.at[place, i])
            for i, (source, target) in enumerate([(sums_ref, sums), (far_ref, far)])
        ]

    def write(at, size, place):
        here = pl.ds(at, size)
        return pltpu.make_async_copy(out.at[:, here], out_ref.at[:, here], out_sem.at[place])

    loads = [
        pltpu.make_async_copy(source, target, in_sem.at[i])
        for i, (source, target) in enumerate(
            [(pick_ref, pick), (scale_ref, scale), (earlier_ref, held.at[pl.ds(0, first)])]
        )
    ]
    for copy in loads[:2]:
        copy.start()
    for place, (at, size) in enumerate(tiles):
        for copy in reads(at, size, place):
            copy.start()
        if place == 0:
            loads[2].start()
    fill_table(table, ids, rows, tenants, mx_count)
    held[LIVE_ROWS:, :] = jnp.zeros((BLOCK_ROWS, columns), held.dtype)

    @pl.loop(0, blocks)
    def _(block):
        def find(slot, start):
            return jnp.where(table[3, slot] == block, table[0, slot], start)

        start = lax.fori_loop(0, len(SLOTS), find, jnp.int32(0))
        count = rows[block]
        base = jnp.minimum(start // BLOCK_ROWS * BLOCK_ROWS, LIVE_ROWS - BLOCK_ROWS)
        bases[block] = base
        shape = (BLOCK_ROWS, 2 * BLOCK_ROWS)
        position = lax.broadcasted_iota(jnp.int32, shape, 0)
        column = lax.broadcasted_iota(jnp.int32, shape, 1) + base
        chosen[block] = ((position < count) & (column == position + start)).astype(jnp.bfloat16)

    for copy in loads:
        copy.wait()

    def work(at, size, place):
        here = pl.ds(at, size)
        for copy in reads(at, size, place):
            copy.wait()
        pre = [
            (sums[side, :, here] + far[side, :, here].astype(jnp.float32))
            * jnp.dot(pick[...], scale[side, :, here], preferred_element_type=jnp.float32)
            for side in range(2)
        ]
        held[first:LIVE_ROWS, here] = activate(*pre)

        @pl.loop(0, blocks)
        def _(block):
            window = pl.ds(pl.multiple_of(bases[block], BLOCK_ROWS), 2 * BLOCK_ROWS)
            there = pl.ds(pl.multiple_of(block * BLOCK_ROWS, BLOCK_ROWS), BLOCK_ROWS)
            out[there, here] = jnp.dot(
                chosen[block], held[window, here], preferred_element_type=jnp.float32
            ).astype(jnp.bfloat16)

        write(at, size, place).start()

    whole = columns // TILE

    @pl.loop(0, whole)
    def _(place):
        work(pl.multiple_of(place * TILE, TILE), TILE, place)

    for place in range(whole, len(tiles)):
        work(*tiles[place], place)
    for place, (at, size) in enumerate(tiles):
        write(at, size, place).wait()


def last_rows(mx_count, first, scalars, sums, far, pick, scale, earlier, blocks):
    narrow = far.shape[2]
    operands = (sums, far, pick, scale, earlier)
    places = -(-narrow // TILE)
    return pl.pallas_call(
        functools.partial(last_kernel, mx_count, first),
        out_shape=jax.ShapeDtypeStruct((blocks * BLOCK_ROWS, narrow), jnp.bfloat16),
        grid_spec=pltpu.PrefetchScalarGridSpec(
            num_scalar_prefetch=3,
            grid=(1,),
            in_specs=[ANY] * len(operands),
            out_specs=ANY,
            scratch_shapes=[
                pltpu.SMEM((4, len(SLOTS)), jnp.int32),
                pltpu.SMEM((blocks,), jnp.int32),
                pltpu.VMEM(sums.shape, sums.dtype),
                pltpu.VMEM(far.shape, far.dtype),
                pltpu.VMEM(pick.shape, pick.dtype),
                pltpu.VMEM(scale.shape, scale.dtype),
                pltpu.VMEM((LIVE_ROWS + BLOCK_ROWS, narrow), jnp.bfloat16),
                pltpu.VMEM((blocks, BLOCK_ROWS, 2 * BLOCK_ROWS), jnp.bfloat16),
                pltpu.VMEM((blocks * BLOCK_ROWS, narrow), jnp.bfloat16),
                pltpu.SemaphoreType.DMA((3,)),
                pltpu.SemaphoreType.DMA((places, 2)),
                pltpu.SemaphoreType.DMA((places,)),
            ],
        ),
        compiler_params=pltpu.CompilerParams(vmem_limit_bytes=VMEM_LIMIT),
        cost_estimate=COST,
        name="last_rows",
    )(*scalars, *operands)


def quarter(array, index, narrow):
    return lax.dynamic_slice_in_dim(array, index * narrow, narrow, array.ndim - 1)


def pipelined(
    tokens, w_gate, w_up, adapter_in, adapter_out, magnitude, partial_norms, block_tenant, block_rows
):
    mx_count = lax.axis_size("mx")
    my_count = lax.axis_size("my")
    narrow = w_gate.shape[1] // my_count
    mine = lax.axis_index("my")
    ids = jnp.stack([lax.axis_index("mx"), mine]).astype(jnp.int32)
    scalars = (ids, block_rows, block_tenant)
    near = [(i, i ^ 1) for i in range(my_count)]
    across = [(i, i ^ 2) for i in range(my_count)]

    def hop(block, distance, least=0):
        if distance > 0:
            pairs = [(i, i + distance) for i in range(least, mx_count - distance)]
        else:
            pairs = [(i, i + distance) for i in range(-distance, mx_count - least)]
        return lax.ppermute(block, "mx", pairs)

    blocks = [tokens, hop(tokens, 1), hop(tokens, -1)]

    norms = partial_norms[0]
    pair = jnp.stack([quarter(norms, mine, narrow), quarter(norms, mine ^ 2, narrow)])
    other = jnp.stack([quarter(norms, mine ^ 1, narrow), quarter(norms, mine ^ 3, narrow)])
    pair = pair + lax.ppermute(other, "my", near)
    norm_total = pair[0] + lax.ppermute(pair[1], "my", across)
    scale = quarter(magnitude, mine, narrow) * lax.rsqrt(norm_total)
    scale = jnp.transpose(scale, (1, 0, 2))
    high = lax.reduce_precision(scale, 8, 7)
    middle = lax.reduce_precision(scale - high, 8, 7)
    rest = scale - high - middle
    scale = jnp.concatenate(
        [high, middle, rest, jnp.zeros((2, 128 - 3 * scale.shape[1], narrow), jnp.float32)], axis=1
    ).astype(jnp.bfloat16)

    down = jnp.transpose(adapter_in, (0, 2, 1)).reshape(-1, adapter_in.shape[1])

    dots = functools.partial(
        dot_pair, weights=(w_gate, w_up), adapter_out=adapter_out, narrow=narrow, ids=ids
    )

    def swap(parts, pairs):
        return [lax.ppermute(part, "my", pairs) for part in parts]

    def far_out(chunk, after=()):
        return dots([chunk], flip=3, splits=(chunk[0].shape[0],), after=after)

    def far_in(chunk, got, after=()):
        part, = dots([chunk], flip=2, terms=(got,), after=after)
        return part, lax.ppermute(part, "my", across)

    *chunk0, up, down_line = pack_rows(
        mx_count, CHUNKS[0], scalars, blocks, down, after=(scale,), passed=(1, 2)
    )
    blocks = [tokens, up, down_line, hop(up, 1, 1), hop(down_line, -1, 1)]
    mark, far0 = far_in(chunk0, swap(far_out(chunk0), near))

    third_hop = [hop(blocks[3], 1, 2), hop(blocks[4], -1, 2)]
    *chunk1, = pack_rows(mx_count, CHUNKS[1], scalars, blocks, down, after=(mark,), cost=LONG)
    blocks += third_hop
    mark, far1 = far_in(chunk1, swap(far_out(chunk1), near))

    first, last = CHUNKS[2][:2]
    *chunk2, = pack_rows(mx_count, CHUNKS[2], scalars, blocks, down, after=(mark,))
    parts = far_out(chunk2, (far0,))
    got = swap(parts, near)
    parts = dots([chunk0, chunk1], flip=1, splits=(first,), after=(parts[0],))
    early = swap(parts, near)
    mark, far2 = far_in(chunk2, got, after=(parts[0],))

    parts = dots([chunk2], flip=1, splits=(last,), after=(mark,))
    late = swap(parts, near)
    hidden, sums = dots([chunk0, chunk1, chunk2], flip=0, terms=(early, late), finish=((far0, far1), scale))
    return last_rows(mx_count, first, scalars, sums, far2, chunk2[2], scale, hidden, block_rows.shape[0])


def adapter_low(rows_piece, aligned_row_total, adapter_in, block_tenant):
    row_count = rows_piece.shape[0]
    seg_rows = math.gcd(math.gcd(row_count, BLOCK_ROWS), aligned_row_total)
    seg_count = row_count // seg_rows
    seg_block = jnp.arange(seg_count, dtype=jnp.int32) * seg_rows // BLOCK_ROWS
    tenant_tables = adapter_in[block_tenant[seg_block]]
    grouped = rows_piece.reshape(seg_count, seg_rows, rows_piece.shape[1])
    low_terms = jnp.einsum(
        "skd,sdr->skr", grouped, tenant_tables, preferred_element_type=jnp.float32
    )
    return low_terms.reshape(row_count, tenant_tables.shape[2])


def finish_plain(
    summed, reduced_rank_factor, norm_total, mag_cols, adapter_cols, first_row, block_tenant, block_rows
):
    row_count = summed.shape[0]
    col_count = summed.shape[2]
    seg_rows = math.gcd(row_count, BLOCK_ROWS)
    seg_count = row_count // seg_rows
    seg_block = (first_row + jnp.arange(seg_count, dtype=jnp.int32) * seg_rows) // BLOCK_ROWS
    tenants = block_tenant[seg_block]
    col_scale = mag_cols * lax.rsqrt(norm_total)
    seg_scale = col_scale[tenants]
    seg_tables = adapter_cols[tenants]
    low_pair = reduced_rank_factor.reshape(seg_count, seg_rows, 2, RANK)
    adapted = jnp.einsum(
        "skpr,sprc->skpc", low_pair, seg_tables, preferred_element_type=jnp.float32
    )
    pre_act = (summed.reshape(seg_count, seg_rows, 2, col_count) + adapted) * seg_scale[:, None]
    hidden = jax.nn.silu(pre_act[:, :, 0]) * pre_act[:, :, 1]
    offsets = (first_row + jnp.arange(row_count, dtype=jnp.int32)).reshape(
        seg_count, seg_rows
    ) % BLOCK_ROWS
    live_mask = offsets < block_rows[seg_block][:, None]
    hidden = jnp.where(live_mask[:, :, None], hidden, jnp.zeros_like(hidden))
    return hidden.reshape(row_count, col_count).astype(jnp.bfloat16)


def plain(
    tokens, w_gate, w_up, adapter_in, adapter_out, magnitude, partial_norms, block_tenant, block_rows
):
    local_rows = tokens.shape[0]
    col_local = w_gate.shape[1]
    my_count = lax.axis_size("my")
    device_position = lax.axis_index("my")
    rows_piece = lax.all_gather(tokens, "mx", axis=0, tiled=True)
    gate_part = jnp.dot(rows_piece, w_gate, preferred_element_type=jnp.float32)
    up_part = jnp.dot(rows_piece, w_up, preferred_element_type=jnp.float32)
    main_part = jnp.stack((gate_part, up_part), axis=1)
    low_terms = adapter_low(rows_piece, local_rows, adapter_in, block_tenant)
    reduced_rank_factor = lax.psum(low_terms, "my").astype(jnp.bfloat16)
    summed = lax.psum_scatter(main_part, "my", scatter_dimension=2, tiled=True)
    norm_total = lax.psum_scatter(partial_norms[0], "my", scatter_dimension=2, tiled=True)
    narrow = col_local // my_count
    mag_cols = lax.dynamic_slice_in_dim(magnitude, device_position * narrow, narrow, 2)
    adapter_cols = lax.dynamic_slice_in_dim(adapter_out, device_position * narrow, narrow, 3)
    return finish_plain(
        summed, reduced_rank_factor, norm_total, mag_cols, adapter_cols, 0, block_tenant, block_rows
    )


def on_device(tokens, w_gate, w_up, adapter_in, *rest):
    my_count = lax.axis_size("my")
    fits = (
        my_count == 4
        and lax.axis_size("mx") == 4
        and tokens.shape[0] == 2 * BLOCK_ROWS
        and adapter_in.shape[0] == 8
        and tokens.shape[1] % STEP_DEPTH == 0
        and tokens.shape[1] >= 2 * STEP_DEPTH
        and w_gate.shape[1] % (my_count * 128) == 0
    )
    return (pipelined if fits else plain)(tokens, w_gate, w_up, adapter_in, *rest)


def solution(mesh):
    return jax.shard_map(
        on_device,
        mesh=mesh,
        in_specs=(
            P(("groups", "mx"), "my"),
            P("my", "mx"),
            P("my", "mx"),
            P(None, "my", None),
            P(None, None, None, "mx"),
            P(None, None, "mx"),
            P("my", None, None, "mx"),
            P("groups"),
            P("groups"),
        ),
        out_specs=P("groups", ("mx", "my")),
        check_vma=False,
    )
```

```python
import functools
import math

import jax
import jax.numpy as jnp
from jax import lax
from jax.experimental import pallas as pl
from jax.experimental.pallas import tpu as pltpu
from jax.sharding import PartitionSpec as P

RANK = 16
BLOCK_ROWS = 128
LIVE_ROWS = 768
STEP_DEPTH = 512
TILE = 512
VMEM_LIMIT = 66 * 10**6

SLOTS = tuple((distance, half) for distance in (0, -1, 1, -2, 2, -3, 3) for half in range(2))
CHUNKS = ((0, 256, 6), (256, 256, 10), (512, 256, 14))
ANY = pl.BlockSpec(memory_space=pl.ANY)
COST = pl.CostEstimate(flops=0, bytes_accessed=0, transcendentals=0)
LONG = pl.CostEstimate(flops=10**12, bytes_accessed=0, transcendentals=0)


def fill_table(table, ids, rows, tenants, mx_count):
    start = jnp.int32(0)
    for slot, (distance, half) in enumerate(SLOTS):
        source = ids[0] + distance
        valid = (source >= 0) & (source < mx_count)
        block = jnp.clip(source, 0, mx_count - 1) * 2 + half
        count = jnp.where(valid, rows[block], 0)
        table[0, slot] = start
        table[1, slot] = count
        table[2, slot] = tenants[block]
        table[3, slot] = jnp.where(valid, block, -1)
        start = start + count


def pack_kernel(mx_count, first, rows_out, slots, passed, ids, rows, tenants, *refs):
    token_refs, down_ref = refs[:slots // 2], refs[slots // 2]
    outs, scratch = refs[-9 - passed:-6], refs[-6:]
    x_ref, low_ref, pick_ref = outs[:3]
    table, buffer, down, acc, sems, down_sem = scratch
    fill_table(table, ids, rows, tenants, mx_count)

    def needed(source):
        start, count = table[0, 2 * source], table[1, 2 * source] + table[1, 2 * source + 1]
        return (count > 0) & (start < first + rows_out) & (start + count > first)

    for source in range(slots // 2):
        @pl.when(needed(source))
        def _():
            pltpu.make_async_copy(token_refs[source], buffer.at[source], sems.at[source]).start()

    down_copies = [
        pltpu.make_async_copy(
            down_ref.at[pl.ds((2 * place + side) * RANK, RANK)], down.at[pl.ds((8 * side + place) * RANK, RANK)],
            down_sem.at[side, place],
        )
        for side in range(2) for place in range(8)
    ]
    for copy in down_copies:
        copy.start()
    acc[...] = jnp.zeros_like(acc)

    @pl.loop(0, slots // 2)
    def _(source):
        @pl.when(needed(source))
        def _():
            pltpu.make_async_copy(buffer.at[source], buffer.at[source], sems.at[source]).wait()
            target = lax.broadcasted_iota(jnp.int32, (rows_out, 2 * BLOCK_ROWS), 0) + first
            place = lax.broadcasted_iota(jnp.int32, (rows_out, 2 * BLOCK_ROWS), 1)
            upper = place >= BLOCK_ROWS
            position = jnp.where(upper, place - BLOCK_ROWS, place)
            start = jnp.where(upper, table[0, 2 * source + 1], table[0, 2 * source])
            count = jnp.where(upper, table[1, 2 * source + 1], table[1, 2 * source])
            chosen = (position < count) & (target == position + start)
            acc[...] += jnp.dot(
                chosen.astype(jnp.bfloat16), buffer[source], preferred_element_type=jnp.float32
            )

    x_ref[...] = acc[...].astype(jnp.bfloat16)
    row = lax.broadcasted_iota(jnp.int32, (rows_out, 128), 0) + first

    def own(slot, tenant):
        start, count = table[0, slot], table[1, slot]
        return jnp.where((row >= start) & (row < start + count), table[2, slot], tenant)

    tenant = lax.fori_loop(0, slots, own, jnp.full((rows_out, 128), -1, jnp.int32))
    lane = lax.broadcasted_iota(jnp.int32, (rows_out, 128), 1)
    pick_ref[...] = ((lane % 8 == tenant) & (lane < 24)).astype(jnp.bfloat16)

    for copy in down_copies:
        copy.wait()
    low = lax.dot_general(x_ref[...], down[...], (((1,), (1,)), ((), ())), preferred_element_type=jnp.float32)
    for side in range(2):
        mine = jnp.where(lane // RANK == tenant, low[:, side * 128:(side + 1) * 128], 0.0)
        high = mine.astype(jnp.bfloat16)
        low_ref[side, :, 0:128] = high
        low_ref[side, :, 128:256] = (mine - high.astype(jnp.float32)).astype(jnp.bfloat16)


def pack_rows(mx_count, chunk, scalars, tokens, down, after=(), passed=(), cost=COST):
    first, rows_out, slots = chunk
    width = down.shape[1]
    outs = [
        jax.ShapeDtypeStruct((rows_out, width), jnp.bfloat16),
        jax.ShapeDtypeStruct((2, rows_out, 256), jnp.bfloat16),
        jax.ShapeDtypeStruct((rows_out, 128), jnp.bfloat16),
    ]
    out_specs = [
        pl.BlockSpec((rows_out, width), lambda i, *_: (0, 0)),
        pl.BlockSpec((2, rows_out, 256), lambda i, *_: (0, 0, 0)),
        pl.BlockSpec((rows_out, 128), lambda i, *_: (0, 0)),
    ] + [ANY] * len(passed)
    return pl.pallas_call(
        functools.partial(pack_kernel, mx_count, first, rows_out, slots, len(passed)),
        out_shape=outs + [jax.ShapeDtypeStruct(tokens[i].shape, tokens[i].dtype) for i in passed],
        grid_spec=pltpu.PrefetchScalarGridSpec(
            num_scalar_prefetch=3,
            grid=(1,),
            in_specs=[ANY] * (len(tokens) + 1 + len(after)),
            out_specs=out_specs,
            scratch_shapes=[
                pltpu.SMEM((4, len(SLOTS)), jnp.int32),
                pltpu.VMEM((slots // 2, 2 * BLOCK_ROWS, width), jnp.bfloat16),
                pltpu.VMEM(down.shape, jnp.bfloat16),
                pltpu.VMEM((rows_out, width), jnp.float32),
                pltpu.SemaphoreType.DMA((slots // 2,)),
                pltpu.SemaphoreType.DMA((2, 8)),
            ],
        ),
        input_output_aliases={3 + place: 3 + i for i, place in enumerate(passed)},
        compiler_params=pltpu.CompilerParams(vmem_limit_bytes=VMEM_LIMIT),
        cost_estimate=cost,
        name="pack_rows",
    )(*scalars, *tokens, down, *after)


def activate(gate, up):
    return (gate * (1.0 / (1.0 + jnp.exp(-gate))) * up).astype(jnp.bfloat16)


def dot_kernel(flip, counts, splits, term_counts, finished, narrow, ids, *refs):
    parts = len(counts)
    finish = finished > 0
    x_refs, low_refs, refs = refs[:parts], refs[parts:2 * parts], refs[2 * parts:]
    w_refs, up_ref, refs = refs[:2], refs[2], refs[3:]
    terms = len(term_counts)
    term_refs, refs = refs[:2 * terms], refs[2 * terms:]
    if finish:
        far_refs, refs = refs[:finished], refs[finished:]
        pick_refs, scale_ref, refs = refs[:finished], refs[finished], refs[finished + 1:]
    x, low, w, maps, term, acc, out, far, pick, scale, in_sem, w_sem, out_sem = refs[-13:]
    outs = refs[-13 - (2 if finish else max(1, 2 * len(splits))):-13]
    done = sum(counts[:finished])
    rows, depth = x.shape
    steps = depth // STEP_DEPTH
    left = pl.multiple_of((ids[1] ^ flip) * narrow, 128)
    tiles = [(at, min(TILE, narrow - at)) for at in range(0, narrow, TILE)]
    loads = []

    def load(source, target):
        copy = pltpu.make_async_copy(source, target, in_sem.at[len(loads)])
        copy.start()
        loads.append(copy)

    def piece(side, step):
        return pltpu.make_async_copy(
            w_refs[side].at[pl.ds(step * STEP_DEPTH, STEP_DEPTH), pl.ds(left, narrow)],
            w.at[side, step], w_sem.at[side, step],
        )

    def start_step(step):
        for side in range(2):
            piece(side, step).start()

    def stores(at, size, place):
        columns = pl.ds(at, size)
        if finish:
            pairs = [(out.at[0, :, columns], outs[0].at[:, columns])]
            pairs += [(acc.at[side, pl.ds(done, rows - done), columns], outs[1].at[side, :, columns]) for side in range(2)]
        elif not splits:
            pairs = [(out.at[side, :, columns], outs[0].at[side, :, columns]) for side in range(2)]
        else:
            pairs = []
            for side in range(2):
                row = 0
                for part, count in enumerate(splits):
                    target = outs[side * len(splits) + part].at[:, columns]
                    pairs.append((out.at[side, pl.ds(row, count), columns], target))
                    row += count
        return [
            pltpu.make_async_copy(source, target, out_sem.at[place, i]) for i, (source, target) in enumerate(pairs)
        ]

    row = 0
    for part, count in enumerate(counts):
        load(x_refs[part], x.at[pl.ds(row, count)])
        load(low_refs[part], low.at[:, pl.ds(row, count)])
        row += count
    for side in range(2):
        load(up_ref.at[:, side, :, pl.ds(left, narrow)], maps.at[side, 0])
    first_loads = len(loads)
    start_step(0)
    start_step(1)
    if terms:
        for side in range(2):
            row = 0
            for part, count in enumerate(term_counts):
                load(term_refs[2 * part + side], term.at[side, pl.ds(row, count)])
                row += count
    if finish:
        row = 0
        for part, count in enumerate(counts[:finished]):
            here = pl.ds(row, count)
            load(far_refs[part], far.at[:, here])
            load(pick_refs[part], pick.at[here])
            row += count
        load(scale_ref, scale)

    for copy in loads[:first_loads]:
        copy.wait()
    for side in range(2):
        maps[side, 1] = maps[side, 0]

    @pl.loop(0, 2)
    def _(side):
        acc[side] = jnp.dot(low[side], maps[side].reshape(256, narrow), preferred_element_type=jnp.float32)

    @pl.loop(0, steps - 1)
    def _(step):
        for side in range(2):
            piece(side, step).wait()

            @pl.when(step + 2 < steps)
            def _():
                piece(side, step + 2).start()

        depths = pl.ds(pl.multiple_of(step * STEP_DEPTH, STEP_DEPTH), STEP_DEPTH)

        @pl.loop(0, 2)
        def _(side):
            acc[side] += jnp.dot(x[:, depths], w[side, step], preferred_element_type=jnp.float32)

    for copy in loads[first_loads:]:
        copy.wait()
    for side in range(2):
        piece(side, steps - 1).wait()

    def last_step(at, size, place):
        columns = pl.ds(at, size)
        values = []
        for side in range(2):
            value = acc[side, :, columns] + jnp.dot(
                x[:, depth - STEP_DEPTH:], w[side, steps - 1, :, columns], preferred_element_type=jnp.float32
            )
            if terms:
                value += term[side, :, columns].astype(jnp.float32)
            if finish:
                acc[side, done:, columns] = value[done:]
                value = value[:done] + far[side, :, columns].astype(jnp.float32)
                value *= jnp.dot(pick[...], scale[side, :, columns], preferred_element_type=jnp.float32)
                values.append(value)
            else:
                out[side, :, columns] = value.astype(out.dtype)
        if finish:
            out[0, :, columns] = activate(*values)
        for copy in stores(at, size, place):
            copy.start()

    whole = narrow // TILE

    @pl.loop(0, whole)
    def _(place):
        last_step(pl.multiple_of(place * TILE, TILE), TILE, place)

    for place in range(whole, len(tiles)):
        last_step(*tiles[place], place)
    for place, (at, size) in enumerate(tiles):
        for copy in stores(at, size, place):
            copy.wait()


def dot_pair(chunks, weights, adapter_out, flip, narrow, ids, splits=(), terms=(), finish=None, after=()):
    xs, lows, picks = zip(*chunks)
    counts = tuple(x.shape[0] for x in xs)
    rows, depth = sum(counts), xs[0].shape[1]
    tenants = adapter_out.shape[0]
    term_counts = tuple(gate.shape[0] for gate, _ in terms)
    operands = [ids, *xs, *lows, *weights, adapter_out, *[array for pair in terms for array in pair]]
    finished = 0
    if finish is not None:
        finished = len(finish[0])
        done = sum(counts[:finished])
        operands += [*finish[0], *picks[:finished], finish[1]]
        out_shape = [
            jax.ShapeDtypeStruct((done, narrow), jnp.bfloat16),
            jax.ShapeDtypeStruct((2, rows - done, narrow), jnp.float32),
        ]
    elif splits:
        out_shape = [jax.ShapeDtypeStruct((count, narrow), jnp.bfloat16) for _ in range(2) for count in splits]
    else:
        out_shape = [jax.ShapeDtypeStruct((2, rows, narrow), jnp.bfloat16)]
    operands += list(after)
    few = (8, 128)
    steps = depth // STEP_DEPTH
    return pl.pallas_call(
        functools.partial(
            dot_kernel, flip, counts, splits, term_counts, finished, narrow
        ),
        out_shape=out_shape,
        grid_spec=pltpu.PrefetchScalarGridSpec(
            num_scalar_prefetch=1,
            grid=(1,),
            in_specs=[ANY] * (len(operands) - 1),
            out_specs=[ANY] * len(out_shape),
            scratch_shapes=[
                pltpu.VMEM((rows, depth), jnp.bfloat16),
                pltpu.VMEM((2, rows, 256), jnp.bfloat16),
                pltpu.VMEM((2, steps, STEP_DEPTH, narrow), jnp.bfloat16),
                pltpu.VMEM((2, 2, tenants, RANK, narrow), jnp.bfloat16),
                pltpu.VMEM((2, rows, narrow) if terms else few, jnp.bfloat16),
                pltpu.VMEM((2, rows, narrow), jnp.float32),
                pltpu.VMEM((1, done, narrow) if finished else (2, rows, narrow), jnp.bfloat16),
                pltpu.VMEM((2, done, narrow) if finished else few, jnp.bfloat16),
                pltpu.VMEM((done, 128) if finished else few, jnp.bfloat16),
                pltpu.VMEM((2, 128, narrow) if finished else few, jnp.bfloat16),
                pltpu.SemaphoreType.DMA((4 * len(xs) + 8,)),
                pltpu.SemaphoreType.DMA((2, steps)),
                pltpu.SemaphoreType.DMA((-(-narrow // TILE), 4)),
            ],
        ),
        compiler_params=pltpu.CompilerParams(vmem_limit_bytes=VMEM_LIMIT),
        cost_estimate=COST,
        name="finish_dots" if finished else "dot_pair",
    )(*operands)


def last_kernel(
    mx_count, first, ids, rows, tenants, sums_ref, far_ref, pick, scale, earlier_ref, out_ref, table, sums, far, held,
    tile_sem, held_sem,
):
    block = pl.program_id(0)
    tiles = far.shape[1] // BLOCK_ROWS

    def tile_copies(tile):
        here = pl.ds(pl.multiple_of(tile * BLOCK_ROWS, BLOCK_ROWS), BLOCK_ROWS)
        return [
            pltpu.make_async_copy(source.at[:, here], target.at[:, here], tile_sem.at[tile, i])
            for i, (source, target) in enumerate([(sums_ref, sums), (far_ref, far)])
        ]

    @pl.when(block == 0)
    def _():
        for tile in range(tiles):
            for copy in tile_copies(tile):
                copy.start()
        held_copy = pltpu.make_async_copy(earlier_ref, held.at[pl.ds(0, first)], held_sem)
        held_copy.start()
        fill_table(table, ids, rows, tenants, mx_count)
        held[LIVE_ROWS:, :] = jnp.zeros((BLOCK_ROWS, held.shape[1]), held.dtype)
        columns = held.shape[1]

        @pl.loop(0, tiles)
        def _(tile):
            for copy in tile_copies(tile):
                copy.wait()
            here = pl.ds(pl.multiple_of(tile * BLOCK_ROWS, BLOCK_ROWS), BLOCK_ROWS)
            there = pl.ds(pl.multiple_of(first + tile * BLOCK_ROWS, BLOCK_ROWS), BLOCK_ROWS)
            for left in range(0, columns, TILE):
                right = min(left + TILE, columns)
                pre = [
                    (sums[side, here, left:right] + far[side, here, left:right].astype(jnp.float32))
                    * jnp.dot(pick[here, :], scale[side, :, left:right], preferred_element_type=jnp.float32)
                    for side in range(2)
                ]
                held[there, left:right] = activate(*pre)

        held_copy.wait()

    def find(slot, start):
        return jnp.where(table[3, slot] == block, table[0, slot], start)

    start = lax.fori_loop(0, len(SLOTS), find, jnp.int32(0))
    count = rows[block]
    base = pl.multiple_of(jnp.minimum(start // BLOCK_ROWS * BLOCK_ROWS, LIVE_ROWS - BLOCK_ROWS), BLOCK_ROWS)
    shape = (BLOCK_ROWS, 2 * BLOCK_ROWS)
    position = lax.broadcasted_iota(jnp.int32, shape, 0)
    column = lax.broadcasted_iota(jnp.int32, shape, 1) + base
    chosen = (position < count) & (column == position + start)
    out_ref[...] = jnp.dot(
        chosen.astype(jnp.bfloat16), held[pl.ds(base, 2 * BLOCK_ROWS), :], preferred_element_type=jnp.float32
    ).astype(jnp.bfloat16)


def last_rows(mx_count, first, scalars, sums, far, pick, scale, earlier, blocks):
    narrow = far.shape[2]
    operands = (sums, far, pick, scale, earlier)
    return pl.pallas_call(
        functools.partial(last_kernel, mx_count, first),
        out_shape=jax.ShapeDtypeStruct((blocks * BLOCK_ROWS, narrow), jnp.bfloat16),
        grid_spec=pltpu.PrefetchScalarGridSpec(
            num_scalar_prefetch=3,
            grid=(blocks,),
            in_specs=[
                ANY, ANY,
                pl.BlockSpec(pick.shape, lambda i, *_: (0, 0)),
                pl.BlockSpec(scale.shape, lambda i, *_: (0, 0, 0)),
                ANY,
            ],
            out_specs=pl.BlockSpec((BLOCK_ROWS, narrow), lambda i, *_: (i, 0)),
            scratch_shapes=[
                pltpu.SMEM((4, len(SLOTS)), jnp.int32),
                pltpu.VMEM(sums.shape, sums.dtype),
                pltpu.VMEM(far.shape, far.dtype),
                pltpu.VMEM((LIVE_ROWS + BLOCK_ROWS, narrow), jnp.bfloat16),
                pltpu.SemaphoreType.DMA((far.shape[1] // BLOCK_ROWS, 2)),
                pltpu.SemaphoreType.DMA,
            ],
        ),
        compiler_params=pltpu.CompilerParams(vmem_limit_bytes=VMEM_LIMIT),
        cost_estimate=COST,
        name="last_rows",
    )(*scalars, *operands)


def quarter(array, index, narrow):
    return lax.dynamic_slice_in_dim(array, index * narrow, narrow, array.ndim - 1)


def pipelined(
    tokens, w_gate, w_up, adapter_in, adapter_out, magnitude, partial_norms, block_tenant, block_rows
):
    mx_count = lax.axis_size("mx")
    my_count = lax.axis_size("my")
    narrow = w_gate.shape[1] // my_count
    mine = lax.axis_index("my")
    ids = jnp.stack([lax.axis_index("mx"), mine]).astype(jnp.int32)
    scalars = (ids, block_rows, block_tenant)
    near = [(i, i ^ 1) for i in range(my_count)]
    across = [(i, i ^ 2) for i in range(my_count)]

    def hop(block, distance, least=0):
        if distance > 0:
            pairs = [(i, i + distance) for i in range(least, mx_count - distance)]
        else:
            pairs = [(i, i + distance) for i in range(-distance, mx_count - least)]
        return lax.ppermute(block, "mx", pairs)

    blocks = [tokens, hop(tokens, 1), hop(tokens, -1)]

    norms = partial_norms[0]
    pair = jnp.stack([quarter(norms, mine, narrow), quarter(norms, mine ^ 2, narrow)])
    other = jnp.stack([quarter(norms, mine ^ 1, narrow), quarter(norms, mine ^ 3, narrow)])
    pair = pair + lax.ppermute(other, "my", near)
    norm_total = pair[0] + lax.ppermute(pair[1], "my", across)
    scale = quarter(magnitude, mine, narrow) * lax.rsqrt(norm_total)
    scale = jnp.transpose(scale, (1, 0, 2))
    high = lax.reduce_precision(scale, 8, 7)
    middle = lax.reduce_precision(scale - high, 8, 7)
    rest = scale - high - middle
    scale = jnp.concatenate(
        [high, middle, rest, jnp.zeros((2, 128 - 3 * scale.shape[1], narrow), jnp.float32)], axis=1
    ).astype(jnp.bfloat16)

    down = jnp.transpose(adapter_in, (0, 2, 1)).reshape(-1, adapter_in.shape[1])

    dots = functools.partial(
        dot_pair, weights=(w_gate, w_up), adapter_out=adapter_out, narrow=narrow, ids=ids
    )

    def swap(parts, pairs):
        return [lax.ppermute(part, "my", pairs) for part in parts]

    def far_out(chunk, after=()):
        return dots([chunk], flip=3, splits=(chunk[0].shape[0],), after=after)

    def far_in(chunk, got, after=()):
        part, = dots([chunk], flip=2, terms=(got,), after=after)
        return part, lax.ppermute(part, "my", across)

    *chunk0, up, down_line = pack_rows(
        mx_count, CHUNKS[0], scalars, blocks, down, after=(scale,), passed=(1, 2)
    )
    blocks = [tokens, up, down_line, hop(up, 1, 1), hop(down_line, -1, 1)]
    mark, far0 = far_in(chunk0, swap(far_out(chunk0), near))

    third_hop = [hop(blocks[3], 1, 2), hop(blocks[4], -1, 2)]
    *chunk1, = pack_rows(mx_count, CHUNKS[1], scalars, blocks, down, after=(mark,), cost=LONG)
    blocks += third_hop
    mark, far1 = far_in(chunk1, swap(far_out(chunk1), near))

    first, last = CHUNKS[2][:2]
    *chunk2, = pack_rows(mx_count, CHUNKS[2], scalars, blocks, down, after=(mark,))
    parts = far_out(chunk2, (far0,))
    got = swap(parts, near)
    parts = dots([chunk0, chunk1], flip=1, splits=(first,), after=(parts[0],))
    early = swap(parts, near)
    mark, far2 = far_in(chunk2, got, after=(parts[0],))

    parts = dots([chunk2], flip=1, splits=(last,), after=(mark,))
    late = swap(parts, near)
    hidden, sums = dots([chunk0, chunk1, chunk2], flip=0, terms=(early, late), finish=((far0, far1), scale))
    return last_rows(mx_count, first, scalars, sums, far2, chunk2[2], scale, hidden, block_rows.shape[0])


def adapter_low(rows_piece, aligned_row_total, adapter_in, block_tenant):
    row_count = rows_piece.shape[0]
    seg_rows = math.gcd(math.gcd(row_count, BLOCK_ROWS), aligned_row_total)
    seg_count = row_count // seg_rows
    seg_block = jnp.arange(seg_count, dtype=jnp.int32) * seg_rows // BLOCK_ROWS
    tenant_tables = adapter_in[block_tenant[seg_block]]
    grouped = rows_piece.reshape(seg_count, seg_rows, rows_piece.shape[1])
    low_terms = jnp.einsum(
        "skd,sdr->skr", grouped, tenant_tables, preferred_element_type=jnp.float32
    )
    return low_terms.reshape(row_count, tenant_tables.shape[2])


def finish_plain(
    summed, reduced_rank_factor, norm_total, mag_cols, adapter_cols, first_row, block_tenant, block_rows
):
    row_count = summed.shape[0]
    col_count = summed.shape[2]
    seg_rows = math.gcd(row_count, BLOCK_ROWS)
    seg_count = row_count // seg_rows
    seg_block = (first_row + jnp.arange(seg_count, dtype=jnp.int32) * seg_rows) // BLOCK_ROWS
    tenants = block_tenant[seg_block]
    col_scale = mag_cols * lax.rsqrt(norm_total)
    seg_scale = col_scale[tenants]
    seg_tables = adapter_cols[tenants]
    low_pair = reduced_rank_factor.reshape(seg_count, seg_rows, 2, RANK)
    adapted = jnp.einsum(
        "skpr,sprc->skpc", low_pair, seg_tables, preferred_element_type=jnp.float32
    )
    pre_act = (summed.reshape(seg_count, seg_rows, 2, col_count) + adapted) * seg_scale[:, None]
    hidden = jax.nn.silu(pre_act[:, :, 0]) * pre_act[:, :, 1]
    offsets = (first_row + jnp.arange(row_count, dtype=jnp.int32)).reshape(
        seg_count, seg_rows
    ) % BLOCK_ROWS
    live_mask = offsets < block_rows[seg_block][:, None]
    hidden = jnp.where(live_mask[:, :, None], hidden, jnp.zeros_like(hidden))
    return hidden.reshape(row_count, col_count).astype(jnp.bfloat16)


def plain(
    tokens, w_gate, w_up, adapter_in, adapter_out, magnitude, partial_norms, block_tenant, block_rows
):
    local_rows = tokens.shape[0]
    col_local = w_gate.shape[1]
    my_count = lax.axis_size("my")
    device_position = lax.axis_index("my")
    rows_piece = lax.all_gather(tokens, "mx", axis=0, tiled=True)
    gate_part = jnp.dot(rows_piece, w_gate, preferred_element_type=jnp.float32)
    up_part = jnp.dot(rows_piece, w_up, preferred_element_type=jnp.float32)
    main_part = jnp.stack((gate_part, up_part), axis=1)
    low_terms = adapter_low(rows_piece, local_rows, adapter_in, block_tenant)
    reduced_rank_factor = lax.psum(low_terms, "my").astype(jnp.bfloat16)
    summed = lax.psum_scatter(main_part, "my", scatter_dimension=2, tiled=True)
    norm_total = lax.psum_scatter(partial_norms[0], "my", scatter_dimension=2, tiled=True)
    narrow = col_local // my_count
    mag_cols = lax.dynamic_slice_in_dim(magnitude, device_position * narrow, narrow, 2)
    adapter_cols = lax.dynamic_slice_in_dim(adapter_out, device_position * narrow, narrow, 3)
    return finish_plain(
        summed, reduced_rank_factor, norm_total, mag_cols, adapter_cols, 0, block_tenant, block_rows
    )


def on_device(tokens, w_gate, w_up, adapter_in, *rest):
    my_count = lax.axis_size("my")
    fits = (
        my_count == 4
        and lax.axis_size("mx") == 4
        and tokens.shape[0] == 2 * BLOCK_ROWS
        and adapter_in.shape[0] == 8
        and tokens.shape[1] % STEP_DEPTH == 0
        and tokens.shape[1] >= 2 * STEP_DEPTH
        and w_gate.shape[1] % (my_count * 128) == 0
    )
    return (pipelined if fits else plain)(tokens, w_gate, w_up, adapter_in, *rest)


def solution(mesh):
    return jax.shard_map(
        on_device,
        mesh=mesh,
        in_specs=(
            P(("groups", "mx"), "my"),
            P("my", "mx"),
            P("my", "mx"),
            P(None, "my", None),
            P(None, None, None, "mx"),
            P(None, None, "mx"),
            P("my", None, None, "mx"),
            P("groups"),
            P("groups"),
        ),
        out_specs=P("groups", ("mx", "my")),
        check_vma=False,
    )
```

```python
import functools
import math

import jax
import jax.numpy as jnp
from jax import lax
from jax.experimental import pallas as pl
from jax.experimental.pallas import tpu as pltpu
from jax.sharding import PartitionSpec as P

RANK = 16
BLOCK_ROWS = 128
LIVE_ROWS = 768
STEP_DEPTH = 512
TILE = 512
VMEM_LIMIT = 66 * 10**6

SLOTS = tuple((distance, half) for distance in (0, -1, 1, -2, 2, -3, 3) for half in range(2))
CHUNKS = ((0, 256, 6), (256, 256, 10), (512, 256, 14))
ANY = pl.BlockSpec(memory_space=pl.ANY)
COST = pl.CostEstimate(flops=0, bytes_accessed=0, transcendentals=0)
LONG = pl.CostEstimate(flops=10**12, bytes_accessed=0, transcendentals=0)


def fill_table(table, ids, rows, tenants, mx_count):
    start = jnp.int32(0)
    for slot, (distance, half) in enumerate(SLOTS):
        source = ids[0] + distance
        valid = (source >= 0) & (source < mx_count)
        block = jnp.clip(source, 0, mx_count - 1) * 2 + half
        count = jnp.where(valid, rows[block], 0)
        table[0, slot] = start
        table[1, slot] = count
        table[2, slot] = tenants[block]
        table[3, slot] = jnp.where(valid, block, -1)
        start = start + count


def pack_kernel(mx_count, first, rows_out, slots, passed, ids, rows, tenants, *refs):
    token_refs, down_ref = refs[:slots // 2], refs[slots // 2]
    outs, scratch = refs[-9 - passed:-6], refs[-6:]
    x_ref, low_ref, pick_ref = outs[:3]
    table, buffer, down, acc, sems, down_sem = scratch
    fill_table(table, ids, rows, tenants, mx_count)

    def needed(source):
        start, count = table[0, 2 * source], table[1, 2 * source] + table[1, 2 * source + 1]
        return (count > 0) & (start < first + rows_out) & (start + count > first)

    for source in range(slots // 2):
        @pl.when(needed(source))
        def _():
            pltpu.make_async_copy(token_refs[source], buffer.at[source], sems.at[source]).start()

    down_copies = [
        pltpu.make_async_copy(
            down_ref.at[pl.ds((2 * place + side) * RANK, RANK)], down.at[pl.ds((8 * side + place) * RANK, RANK)],
            down_sem.at[side, place],
        )
        for side in range(2) for place in range(8)
    ]
    for copy in down_copies:
        copy.start()
    acc[...] = jnp.zeros_like(acc)

    @pl.loop(0, slots // 2)
    def _(source):
        @pl.when(needed(source))
        def _():
            pltpu.make_async_copy(buffer.at[source], buffer.at[source], sems.at[source]).wait()
            target = lax.broadcasted_iota(jnp.int32, (rows_out, 2 * BLOCK_ROWS), 0) + first
            place = lax.broadcasted_iota(jnp.int32, (rows_out, 2 * BLOCK_ROWS), 1)
            upper = place >= BLOCK_ROWS
            position = jnp.where(upper, place - BLOCK_ROWS, place)
            start = jnp.where(upper, table[0, 2 * source + 1], table[0, 2 * source])
            count = jnp.where(upper, table[1, 2 * source + 1], table[1, 2 * source])
            chosen = (position < count) & (target == position + start)
            acc[...] += jnp.dot(
                chosen.astype(jnp.bfloat16), buffer[source], preferred_element_type=jnp.float32
            )

    x_ref[...] = acc[...].astype(jnp.bfloat16)
    row = lax.broadcasted_iota(jnp.int32, (rows_out, 128), 0) + first

    def own(slot, tenant):
        start, count = table[0, slot], table[1, slot]
        return jnp.where((row >= start) & (row < start + count), table[2, slot], tenant)

    tenant = lax.fori_loop(0, slots, own, jnp.full((rows_out, 128), -1, jnp.int32))
    lane = lax.broadcasted_iota(jnp.int32, (rows_out, 128), 1)
    pick_ref[...] = ((lane % 8 == tenant) & (lane < 24)).astype(jnp.bfloat16)

    for copy in down_copies:
        copy.wait()
    low = lax.dot_general(x_ref[...], down[...], (((1,), (1,)), ((), ())), preferred_element_type=jnp.float32)
    for side in range(2):
        mine = jnp.where(lane // RANK == tenant, low[:, side * 128:(side + 1) * 128], 0.0)
        high = mine.astype(jnp.bfloat16)
        low_ref[side, :, 0:128] = high
        low_ref[side, :, 128:256] = (mine - high.astype(jnp.float32)).astype(jnp.bfloat16)


def pack_rows(mx_count, chunk, scalars, tokens, down, after=(), passed=(), cost=COST):
    first, rows_out, slots = chunk
    width = down.shape[1]
    outs = [
        jax.ShapeDtypeStruct((rows_out, width), jnp.bfloat16),
        jax.ShapeDtypeStruct((2, rows_out, 256), jnp.bfloat16),
        jax.ShapeDtypeStruct((rows_out, 128), jnp.bfloat16),
    ]
    out_specs = [
        pl.BlockSpec((rows_out, width), lambda i, *_: (0, 0)),
        pl.BlockSpec((2, rows_out, 256), lambda i, *_: (0, 0, 0)),
        pl.BlockSpec((rows_out, 128), lambda i, *_: (0, 0)),
    ] + [ANY] * len(passed)
    return pl.pallas_call(
        functools.partial(pack_kernel, mx_count, first, rows_out, slots, len(passed)),
        out_shape=outs + [jax.ShapeDtypeStruct(tokens[i].shape, tokens[i].dtype) for i in passed],
        grid_spec=pltpu.PrefetchScalarGridSpec(
            num_scalar_prefetch=3,
            grid=(1,),
            in_specs=[ANY] * (len(tokens) + 1 + len(after)),
            out_specs=out_specs,
            scratch_shapes=[
                pltpu.SMEM((4, len(SLOTS)), jnp.int32),
                pltpu.VMEM((slots // 2, 2 * BLOCK_ROWS, width), jnp.bfloat16),
                pltpu.VMEM(down.shape, jnp.bfloat16),
                pltpu.VMEM((rows_out, width), jnp.float32),
                pltpu.SemaphoreType.DMA((slots // 2,)),
                pltpu.SemaphoreType.DMA((2, 8)),
            ],
        ),
        input_output_aliases={3 + place: 3 + i for i, place in enumerate(passed)},
        compiler_params=pltpu.CompilerParams(vmem_limit_bytes=VMEM_LIMIT),
        cost_estimate=cost,
        name="pack_rows",
    )(*scalars, *tokens, down, *after)


def activate(gate, up):
    half = 0.5 * gate
    return ((half + half * jnp.tanh(half)) * up).astype(jnp.bfloat16)


def dot_kernel(flip, counts, splits, term_counts, finished, narrow, ids, *refs):
    parts = len(counts)
    finish = finished > 0
    x_refs, low_refs, refs = refs[:parts], refs[parts:2 * parts], refs[2 * parts:]
    w_refs, up_ref, refs = refs[:2], refs[2], refs[3:]
    terms = len(term_counts)
    term_refs, refs = refs[:2 * terms], refs[2 * terms:]
    if finish:
        far_refs, refs = refs[:finished], refs[finished:]
        pick_refs, scale_ref, refs = refs[:finished], refs[finished], refs[finished + 1:]
    x, low, w, maps, term, acc, out, far, pick, scale, in_sem, w_sem, out_sem = refs[-13:]
    outs = refs[-13 - (2 if finish else max(1, 2 * len(splits))):-13]
    done = sum(counts[:finished])
    rows, depth = x.shape
    steps = depth // STEP_DEPTH
    left = pl.multiple_of((ids[1] ^ flip) * narrow, 128)
    tiles = [(at, min(TILE, narrow - at)) for at in range(0, narrow, TILE)]
    loads = []

    def load(source, target):
        copy = pltpu.make_async_copy(source, target, in_sem.at[len(loads)])
        copy.start()
        loads.append(copy)

    def piece(side, step):
        return pltpu.make_async_copy(
            w_refs[side].at[pl.ds(step * STEP_DEPTH, STEP_DEPTH), pl.ds(left, narrow)],
            w.at[side, step], w_sem.at[side, step],
        )

    def start_step(step):
        for side in range(2):
            piece(side, step).start()

    def stores(at, size, place):
        columns = pl.ds(at, size)
        if finish:
            pairs = [(out.at[0, :, columns], outs[0].at[:, columns])]
            pairs += [(acc.at[side, pl.ds(done, rows - done), columns], outs[1].at[side, :, columns]) for side in range(2)]
        elif not splits:
            pairs = [(out.at[side, :, columns], outs[0].at[side, :, columns]) for side in range(2)]
        else:
            pairs = []
            for side in range(2):
                row = 0
                for part, count in enumerate(splits):
                    target = outs[side * len(splits) + part].at[:, columns]
                    pairs.append((out.at[side, pl.ds(row, count), columns], target))
                    row += count
        return [
            pltpu.make_async_copy(source, target, out_sem.at[place, i]) for i, (source, target) in enumerate(pairs)
        ]

    row = 0
    for part, count in enumerate(counts):
        load(x_refs[part], x.at[pl.ds(row, count)])
        load(low_refs[part], low.at[:, pl.ds(row, count)])
        row += count
    for side in range(2):
        load(up_ref.at[:, side, :, pl.ds(left, narrow)], maps.at[side, 0])
    first_loads = len(loads)
    start_step(0)
    start_step(1)
    if terms:
        for side in range(2):
            row = 0
            for part, count in enumerate(term_counts):
                load(term_refs[2 * part + side], term.at[side, pl.ds(row, count)])
                row += count
    if finish:
        row = 0
        for part, count in enumerate(counts[:finished]):
            here = pl.ds(row, count)
            load(far_refs[part], far.at[:, here])
            load(pick_refs[part], pick.at[here])
            row += count
        load(scale_ref, scale)

    for copy in loads[:first_loads]:
        copy.wait()
    for side in range(2):
        maps[side, 1] = maps[side, 0]

    @pl.loop(0, 2)
    def _(side):
        acc[side] = jnp.dot(low[side], maps[side].reshape(256, narrow), preferred_element_type=jnp.float32)

    @pl.loop(0, steps - 1)
    def _(step):
        for side in range(2):
            piece(side, step).wait()

            @pl.when(step + 2 < steps)
            def _():
                piece(side, step + 2).start()

        depths = pl.ds(pl.multiple_of(step * STEP_DEPTH, STEP_DEPTH), STEP_DEPTH)

        @pl.loop(0, 2)
        def _(side):
            acc[side] += jnp.dot(x[:, depths], w[side, step], preferred_element_type=jnp.float32)

    for copy in loads[first_loads:]:
        copy.wait()
    for side in range(2):
        piece(side, steps - 1).wait()

    def last_step(at, size, place):
        columns = pl.ds(at, size)
        values = []
        for side in range(2):
            value = acc[side, :, columns] + jnp.dot(
                x[:, depth - STEP_DEPTH:], w[side, steps - 1, :, columns], preferred_element_type=jnp.float32
            )
            if terms:
                value += term[side, :, columns].astype(jnp.float32)
            if finish:
                acc[side, done:, columns] = value[done:]
                value = value[:done] + far[side, :, columns].astype(jnp.float32)
                value *= jnp.dot(pick[...], scale[side, :, columns], preferred_element_type=jnp.float32)
                values.append(value)
            else:
                out[side, :, columns] = value.astype(out.dtype)
        if finish:
            out[0, :, columns] = activate(*values)
        for copy in stores(at, size, place):
            copy.start()

    whole = narrow // TILE

    @pl.loop(0, whole)
    def _(place):
        last_step(pl.multiple_of(place * TILE, TILE), TILE, place)

    for place in range(whole, len(tiles)):
        last_step(*tiles[place], place)
    for place, (at, size) in enumerate(tiles):
        for copy in stores(at, size, place):
            copy.wait()


def dot_pair(chunks, weights, adapter_out, flip, narrow, ids, splits=(), terms=(), finish=None, after=()):
    xs, lows, picks = zip(*chunks)
    counts = tuple(x.shape[0] for x in xs)
    rows, depth = sum(counts), xs[0].shape[1]
    tenants = adapter_out.shape[0]
    term_counts = tuple(gate.shape[0] for gate, _ in terms)
    operands = [ids, *xs, *lows, *weights, adapter_out, *[array for pair in terms for array in pair]]
    finished = 0
    if finish is not None:
        finished = len(finish[0])
        done = sum(counts[:finished])
        operands += [*finish[0], *picks[:finished], finish[1]]
        out_shape = [
            jax.ShapeDtypeStruct((done, narrow), jnp.bfloat16),
            jax.ShapeDtypeStruct((2, rows - done, narrow), jnp.float32),
        ]
    elif splits:
        out_shape = [jax.ShapeDtypeStruct((count, narrow), jnp.bfloat16) for _ in range(2) for count in splits]
    else:
        out_shape = [jax.ShapeDtypeStruct((2, rows, narrow), jnp.bfloat16)]
    operands += list(after)
    few = (8, 128)
    steps = depth // STEP_DEPTH
    return pl.pallas_call(
        functools.partial(
            dot_kernel, flip, counts, splits, term_counts, finished, narrow
        ),
        out_shape=out_shape,
        grid_spec=pltpu.PrefetchScalarGridSpec(
            num_scalar_prefetch=1,
            grid=(1,),
            in_specs=[ANY] * (len(operands) - 1),
            out_specs=[ANY] * len(out_shape),
            scratch_shapes=[
                pltpu.VMEM((rows, depth), jnp.bfloat16),
                pltpu.VMEM((2, rows, 256), jnp.bfloat16),
                pltpu.VMEM((2, steps, STEP_DEPTH, narrow), jnp.bfloat16),
                pltpu.VMEM((2, 2, tenants, RANK, narrow), jnp.bfloat16),
                pltpu.VMEM((2, rows, narrow) if terms else few, jnp.bfloat16),
                pltpu.VMEM((2, rows, narrow), jnp.float32),
                pltpu.VMEM((1, done, narrow) if finished else (2, rows, narrow), jnp.bfloat16),
                pltpu.VMEM((2, done, narrow) if finished else few, jnp.bfloat16),
                pltpu.VMEM((done, 128) if finished else few, jnp.bfloat16),
                pltpu.VMEM((2, 128, narrow) if finished else few, jnp.bfloat16),
                pltpu.SemaphoreType.DMA((4 * len(xs) + 8,)),
                pltpu.SemaphoreType.DMA((2, steps)),
                pltpu.SemaphoreType.DMA((-(-narrow // TILE), 4)),
            ],
        ),
        compiler_params=pltpu.CompilerParams(vmem_limit_bytes=VMEM_LIMIT),
        cost_estimate=COST,
        name="finish_dots" if finished else "dot_pair",
    )(*operands)


def last_kernel(
    mx_count, first, ids, rows, tenants, sums_ref, far_ref, pick, scale, earlier_ref, out_ref, table, sums, far, held,
    tile_sem, held_sem,
):
    turn = pl.program_id(0)
    tiles = far.shape[1] // BLOCK_ROWS

    def tile_copies(tile):
        here = pl.ds(pl.multiple_of(tile * BLOCK_ROWS, BLOCK_ROWS), BLOCK_ROWS)
        return [
            pltpu.make_async_copy(source.at[:, here], target.at[:, here], tile_sem.at[tile, i])
            for i, (source, target) in enumerate([(sums_ref, sums), (far_ref, far)])
        ]

    @pl.when(turn == 0)
    def _():
        for tile in range(tiles):
            for copy in tile_copies(tile):
                copy.start()
        held_copy = pltpu.make_async_copy(earlier_ref, held.at[pl.ds(0, first)], held_sem)
        held_copy.start()
        fill_table(table, ids, rows, tenants, mx_count)
        held[LIVE_ROWS:, :] = jnp.zeros((BLOCK_ROWS, held.shape[1]), held.dtype)
        columns = held.shape[1]

        @pl.loop(0, tiles)
        def _(tile):
            for copy in tile_copies(tile):
                copy.wait()
            here = pl.ds(pl.multiple_of(tile * BLOCK_ROWS, BLOCK_ROWS), BLOCK_ROWS)
            there = pl.ds(pl.multiple_of(first + tile * BLOCK_ROWS, BLOCK_ROWS), BLOCK_ROWS)
            for left in range(0, columns, TILE):
                right = min(left + TILE, columns)
                pre = [
                    (sums[side, here, left:right] + far[side, here, left:right].astype(jnp.float32))
                    * jnp.dot(pick[here, :], scale[side, :, left:right], preferred_element_type=jnp.float32)
                    for side in range(2)
                ]
                held[there, left:right] = activate(*pre)

        held_copy.wait()

    for part in range(2):
        block = 2 * turn + part

        def find(slot, start, block=block):
            return jnp.where(table[3, slot] == block, table[0, slot], start)

        start = lax.fori_loop(0, len(SLOTS), find, jnp.int32(0))
        count = rows[block]
        base = pl.multiple_of(jnp.minimum(start // BLOCK_ROWS * BLOCK_ROWS, LIVE_ROWS - BLOCK_ROWS), BLOCK_ROWS)
        shape = (BLOCK_ROWS, 2 * BLOCK_ROWS)
        position = lax.broadcasted_iota(jnp.int32, shape, 0)
        column = lax.broadcasted_iota(jnp.int32, shape, 1) + base
        chosen = (position < count) & (column == position + start)
        out_ref[part * BLOCK_ROWS:(part + 1) * BLOCK_ROWS, :] = jnp.dot(
            chosen.astype(jnp.bfloat16), held[pl.ds(base, 2 * BLOCK_ROWS), :], preferred_element_type=jnp.float32
        ).astype(jnp.bfloat16)


def last_rows(mx_count, first, scalars, sums, far, pick, scale, earlier, blocks):
    narrow = far.shape[2]
    operands = (sums, far, pick, scale, earlier)
    return pl.pallas_call(
        functools.partial(last_kernel, mx_count, first),
        out_shape=jax.ShapeDtypeStruct((blocks * BLOCK_ROWS, narrow), jnp.bfloat16),
        grid_spec=pltpu.PrefetchScalarGridSpec(
            num_scalar_prefetch=3,
            grid=(blocks // 2,),
            in_specs=[
                ANY, ANY,
                pl.BlockSpec(pick.shape, lambda i, *_: (0, 0)),
                pl.BlockSpec(scale.shape, lambda i, *_: (0, 0, 0)),
                ANY,
            ],
            out_specs=pl.BlockSpec((2 * BLOCK_ROWS, narrow), lambda i, *_: (i, 0)),
            scratch_shapes=[
                pltpu.SMEM((4, len(SLOTS)), jnp.int32),
                pltpu.VMEM(sums.shape, sums.dtype),
                pltpu.VMEM(far.shape, far.dtype),
                pltpu.VMEM((LIVE_ROWS + BLOCK_ROWS, narrow), jnp.bfloat16),
                pltpu.SemaphoreType.DMA((far.shape[1] // BLOCK_ROWS, 2)),
                pltpu.SemaphoreType.DMA,
            ],
        ),
        compiler_params=pltpu.CompilerParams(vmem_limit_bytes=VMEM_LIMIT),
        cost_estimate=COST,
        name="last_rows",
    )(*scalars, *operands)


def quarter(array, index, narrow):
    return lax.dynamic_slice_in_dim(array, index * narrow, narrow, array.ndim - 1)


def pipelined(
    tokens, w_gate, w_up, adapter_in, adapter_out, magnitude, partial_norms, block_tenant, block_rows
):
    mx_count = lax.axis_size("mx")
    my_count = lax.axis_size("my")
    narrow = w_gate.shape[1] // my_count
    mine = lax.axis_index("my")
    ids = jnp.stack([lax.axis_index("mx"), mine]).astype(jnp.int32)
    scalars = (ids, block_rows, block_tenant)
    near = [(i, i ^ 1) for i in range(my_count)]
    across = [(i, i ^ 2) for i in range(my_count)]

    def hop(block, distance, least=0):
        if distance > 0:
            pairs = [(i, i + distance) for i in range(least, mx_count - distance)]
        else:
            pairs = [(i, i + distance) for i in range(-distance, mx_count - least)]
        return lax.ppermute(block, "mx", pairs)

    blocks = [tokens, hop(tokens, 1), hop(tokens, -1)]

    norms = partial_norms[0]
    pair = jnp.stack([quarter(norms, mine, narrow), quarter(norms, mine ^ 2, narrow)])
    other = jnp.stack([quarter(norms, mine ^ 1, narrow), quarter(norms, mine ^ 3, narrow)])
    pair = pair + lax.ppermute(other, "my", near)
    norm_total = pair[0] + lax.ppermute(pair[1], "my", across)
    scale = quarter(magnitude, mine, narrow) * lax.rsqrt(norm_total)
    scale = jnp.transpose(scale, (1, 0, 2))
    high = lax.reduce_precision(scale, 8, 7)
    middle = lax.reduce_precision(scale - high, 8, 7)
    rest = scale - high - middle
    scale = jnp.concatenate(
        [high, middle, rest, jnp.zeros((2, 128 - 3 * scale.shape[1], narrow), jnp.float32)], axis=1
    ).astype(jnp.bfloat16)

    down = jnp.transpose(adapter_in, (0, 2, 1)).reshape(-1, adapter_in.shape[1])

    dots = functools.partial(
        dot_pair, weights=(w_gate, w_up), adapter_out=adapter_out, narrow=narrow, ids=ids
    )

    def swap(parts, pairs):
        return [lax.ppermute(part, "my", pairs) for part in parts]

    def far_out(chunk, after=()):
        return dots([chunk], flip=3, splits=(chunk[0].shape[0],), after=after)

    def far_in(chunk, got, after=()):
        part, = dots([chunk], flip=2, terms=(got,), after=after)
        return part, lax.ppermute(part, "my", across)

    *chunk0, up, down_line = pack_rows(
        mx_count, CHUNKS[0], scalars, blocks, down, after=(scale,), passed=(1, 2)
    )
    blocks = [tokens, up, down_line, hop(up, 1, 1), hop(down_line, -1, 1)]
    mark, far0 = far_in(chunk0, swap(far_out(chunk0), near))

    third_hop = [hop(blocks[3], 1, 2), hop(blocks[4], -1, 2)]
    *chunk1, = pack_rows(mx_count, CHUNKS[1], scalars, blocks, down, after=(mark,), cost=LONG)
    blocks += third_hop
    mark, far1 = far_in(chunk1, swap(far_out(chunk1), near))

    first, last = CHUNKS[2][:2]
    *chunk2, = pack_rows(mx_count, CHUNKS[2], scalars, blocks, down, after=(mark,))
    parts = far_out(chunk2, (far0,))
    got = swap(parts, near)
    parts = dots([chunk0, chunk1], flip=1, splits=(first,), after=(parts[0],))
    early = swap(parts, near)
    mark, far2 = far_in(chunk2, got, after=(parts[0],))

    parts = dots([chunk2], flip=1, splits=(last,), after=(mark,))
    late = swap(parts, near)
    hidden, sums = dots([chunk0, chunk1, chunk2], flip=0, terms=(early, late), finish=((far0, far1), scale))
    return last_rows(mx_count, first, scalars, sums, far2, chunk2[2], scale, hidden, block_rows.shape[0])


def adapter_low(rows_piece, aligned_row_total, adapter_in, block_tenant):
    row_count = rows_piece.shape[0]
    seg_rows = math.gcd(math.gcd(row_count, BLOCK_ROWS), aligned_row_total)
    seg_count = row_count // seg_rows
    seg_block = jnp.arange(seg_count, dtype=jnp.int32) * seg_rows // BLOCK_ROWS
    tenant_tables = adapter_in[block_tenant[seg_block]]
    grouped = rows_piece.reshape(seg_count, seg_rows, rows_piece.shape[1])
    low_terms = jnp.einsum(
        "skd,sdr->skr", grouped, tenant_tables, preferred_element_type=jnp.float32
    )
    return low_terms.reshape(row_count, tenant_tables.shape[2])


def finish_plain(
    summed, reduced_rank_factor, norm_total, mag_cols, adapter_cols, first_row, block_tenant, block_rows
):
    row_count = summed.shape[0]
    col_count = summed.shape[2]
    seg_rows = math.gcd(row_count, BLOCK_ROWS)
    seg_count = row_count // seg_rows
    seg_block = (first_row + jnp.arange(seg_count, dtype=jnp.int32) * seg_rows) // BLOCK_ROWS
    tenants = block_tenant[seg_block]
    col_scale = mag_cols * lax.rsqrt(norm_total)
    seg_scale = col_scale[tenants]
    seg_tables = adapter_cols[tenants]
    low_pair = reduced_rank_factor.reshape(seg_count, seg_rows, 2, RANK)
    adapted = jnp.einsum(
        "skpr,sprc->skpc", low_pair, seg_tables, preferred_element_type=jnp.float32
    )
    pre_act = (summed.reshape(seg_count, seg_rows, 2, col_count) + adapted) * seg_scale[:, None]
    hidden = jax.nn.silu(pre_act[:, :, 0]) * pre_act[:, :, 1]
    offsets = (first_row + jnp.arange(row_count, dtype=jnp.int32)).reshape(
        seg_count, seg_rows
    ) % BLOCK_ROWS
    live_mask = offsets < block_rows[seg_block][:, None]
    hidden = jnp.where(live_mask[:, :, None], hidden, jnp.zeros_like(hidden))
    return hidden.reshape(row_count, col_count).astype(jnp.bfloat16)


def plain(
    tokens, w_gate, w_up, adapter_in, adapter_out, magnitude, partial_norms, block_tenant, block_rows
):
    local_rows = tokens.shape[0]
    col_local = w_gate.shape[1]
    my_count = lax.axis_size("my")
    device_position = lax.axis_index("my")
    rows_piece = lax.all_gather(tokens, "mx", axis=0, tiled=True)
    gate_part = jnp.dot(rows_piece, w_gate, preferred_element_type=jnp.float32)
    up_part = jnp.dot(rows_piece, w_up, preferred_element_type=jnp.float32)
    main_part = jnp.stack((gate_part, up_part), axis=1)
    low_terms = adapter_low(rows_piece, local_rows, adapter_in, block_tenant)
    reduced_rank_factor = lax.psum(low_terms, "my").astype(jnp.bfloat16)
    summed = lax.psum_scatter(main_part, "my", scatter_dimension=2, tiled=True)
    norm_total = lax.psum_scatter(partial_norms[0], "my", scatter_dimension=2, tiled=True)
    narrow = col_local // my_count
    mag_cols = lax.dynamic_slice_in_dim(magnitude, device_position * narrow, narrow, 2)
    adapter_cols = lax.dynamic_slice_in_dim(adapter_out, device_position * narrow, narrow, 3)
    return finish_plain(
        summed, reduced_rank_factor, norm_total, mag_cols, adapter_cols, 0, block_tenant, block_rows
    )


def on_device(tokens, w_gate, w_up, adapter_in, *rest):
    my_count = lax.axis_size("my")
    fits = (
        my_count == 4
        and lax.axis_size("mx") == 4
        and tokens.shape[0] == 2 * BLOCK_ROWS
        and adapter_in.shape[0] == 8
        and tokens.shape[1] % STEP_DEPTH == 0
        and tokens.shape[1] >= 2 * STEP_DEPTH
        and w_gate.shape[1] % (my_count * 128) == 0
    )
    return (pipelined if fits else plain)(tokens, w_gate, w_up, adapter_in, *rest)


def solution(mesh):
    return jax.shard_map(
        on_device,
        mesh=mesh,
        in_specs=(
            P(("groups", "mx"), "my"),
            P("my", "mx"),
            P("my", "mx"),
            P(None, "my", None),
            P(None, None, None, "mx"),
            P(None, None, "mx"),
            P("my", None, None, "mx"),
            P("groups"),
            P("groups"),
        ),
        out_specs=P("groups", ("mx", "my")),
        check_vma=False,
    )
```

```python
import functools
import math

import jax
import jax.numpy as jnp
from jax import lax
from jax.experimental import pallas as pl
from jax.experimental.pallas import tpu as pltpu
from jax.sharding import PartitionSpec as P

RANK = 16
BLOCK_ROWS = 128
LIVE_ROWS = 768
STEP_DEPTH = 512
TILE = 512
VMEM_LIMIT = 66 * 10**6

SLOTS = tuple((distance, half) for distance in (0, -1, 1, -2, 2, -3, 3) for half in range(2))
CHUNKS = ((0, 256, 6), (256, 256, 10), (512, 256, 14))
ANY = pl.BlockSpec(memory_space=pl.ANY)
COST = pl.CostEstimate(flops=0, bytes_accessed=0, transcendentals=0)
LONG = pl.CostEstimate(flops=10**12, bytes_accessed=0, transcendentals=0)


def fill_table(table, ids, rows, tenants, mx_count):
    start = jnp.int32(0)
    for slot, (distance, half) in enumerate(SLOTS):
        source = ids[0] + distance
        valid = (source >= 0) & (source < mx_count)
        block = jnp.clip(source, 0, mx_count - 1) * 2 + half
        count = jnp.where(valid, rows[block], 0)
        table[0, slot] = start
        table[1, slot] = count
        table[2, slot] = tenants[block]
        table[3, slot] = jnp.where(valid, block, -1)
        start = start + count


def pack_kernel(mx_count, first, rows_out, slots, passed, ids, rows, tenants, *refs):
    token_refs, down_ref = refs[:slots // 2], refs[slots // 2]
    outs, scratch = refs[-9 - passed:-6], refs[-6:]
    x_ref, low_ref, pick_ref = outs[:3]
    table, buffer, down, acc, sems, down_sem = scratch
    fill_table(table, ids, rows, tenants, mx_count)

    def needed(source):
        start, count = table[0, 2 * source], table[1, 2 * source] + table[1, 2 * source + 1]
        return (count > 0) & (start < first + rows_out) & (start + count > first)

    for source in range(slots // 2):
        @pl.when(needed(source))
        def _():
            pltpu.make_async_copy(token_refs[source], buffer.at[source], sems.at[source]).start()

    down_copies = [
        pltpu.make_async_copy(
            down_ref.at[pl.ds((2 * place + side) * RANK, RANK)], down.at[pl.ds((8 * side + place) * RANK, RANK)],
            down_sem.at[side, place],
        )
        for side in range(2) for place in range(8)
    ]
    for copy in down_copies:
        copy.start()
    acc[...] = jnp.zeros_like(acc)

    @pl.loop(0, slots // 2)
    def _(source):
        @pl.when(needed(source))
        def _():
            pltpu.make_async_copy(buffer.at[source], buffer.at[source], sems.at[source]).wait()
            target = lax.broadcasted_iota(jnp.int32, (rows_out, 2 * BLOCK_ROWS), 0) + first
            place = lax.broadcasted_iota(jnp.int32, (rows_out, 2 * BLOCK_ROWS), 1)
            upper = place >= BLOCK_ROWS
            position = jnp.where(upper, place - BLOCK_ROWS, place)
            start = jnp.where(upper, table[0, 2 * source + 1], table[0, 2 * source])
            count = jnp.where(upper, table[1, 2 * source + 1], table[1, 2 * source])
            chosen = (position < count) & (target == position + start)
            acc[...] += jnp.dot(
                chosen.astype(jnp.bfloat16), buffer[source], preferred_element_type=jnp.float32
            )

    x_ref[...] = acc[...].astype(jnp.bfloat16)
    row = lax.broadcasted_iota(jnp.int32, (rows_out, 128), 0) + first

    def own(slot, tenant):
        start, count = table[0, slot], table[1, slot]
        return jnp.where((row >= start) & (row < start + count), table[2, slot], tenant)

    tenant = lax.fori_loop(0, slots, own, jnp.full((rows_out, 128), -1, jnp.int32))
    lane = lax.broadcasted_iota(jnp.int32, (rows_out, 128), 1)
    pick_ref[...] = ((lane % 8 == tenant) & (lane < 24)).astype(jnp.bfloat16)

    for copy in down_copies:
        copy.wait()
    low = lax.dot_general(x_ref[...], down[...], (((1,), (1,)), ((), ())), preferred_element_type=jnp.float32)
    for side in range(2):
        mine = jnp.where(lane // RANK == tenant, low[:, side * 128:(side + 1) * 128], 0.0)
        high = mine.astype(jnp.bfloat16)
        low_ref[side, :, 0:128] = high
        low_ref[side, :, 128:256] = (mine - high.astype(jnp.float32)).astype(jnp.bfloat16)


def pack_rows(mx_count, chunk, scalars, tokens, down, after=(), passed=(), cost=COST):
    first, rows_out, slots = chunk
    width = down.shape[1]
    outs = [
        jax.ShapeDtypeStruct((rows_out, width), jnp.bfloat16),
        jax.ShapeDtypeStruct((2, rows_out, 256), jnp.bfloat16),
        jax.ShapeDtypeStruct((rows_out, 128), jnp.bfloat16),
    ]
    out_specs = [
        pl.BlockSpec((rows_out, width), lambda i, *_: (0, 0)),
        pl.BlockSpec((2, rows_out, 256), lambda i, *_: (0, 0, 0)),
        pl.BlockSpec((rows_out, 128), lambda i, *_: (0, 0)),
    ] + [ANY] * len(passed)
    return pl.pallas_call(
        functools.partial(pack_kernel, mx_count, first, rows_out, slots, len(passed)),
        out_shape=outs + [jax.ShapeDtypeStruct(tokens[i].shape, tokens[i].dtype) for i in passed],
        grid_spec=pltpu.PrefetchScalarGridSpec(
            num_scalar_prefetch=3,
            grid=(1,),
            in_specs=[ANY] * (len(tokens) + 1 + len(after)),
            out_specs=out_specs,
            scratch_shapes=[
                pltpu.SMEM((4, len(SLOTS)), jnp.int32),
                pltpu.VMEM((slots // 2, 2 * BLOCK_ROWS, width), jnp.bfloat16),
                pltpu.VMEM(down.shape, jnp.bfloat16),
                pltpu.VMEM((rows_out, width), jnp.float32),
                pltpu.SemaphoreType.DMA((slots // 2,)),
                pltpu.SemaphoreType.DMA((2, 8)),
            ],
        ),
        input_output_aliases={3 + place: 3 + i for i, place in enumerate(passed)},
        compiler_params=pltpu.CompilerParams(vmem_limit_bytes=VMEM_LIMIT),
        cost_estimate=cost,
        name="pack_rows",
    )(*scalars, *tokens, down, *after)


def activate(gate, up):
    half = 0.5 * gate
    return ((half + half * jnp.tanh(half)) * up).astype(jnp.bfloat16)


def dot_kernel(flip, counts, splits, term_counts, finished, narrow, ids, *refs):
    parts = len(counts)
    finish = finished > 0
    x_refs, low_refs, refs = refs[:parts], refs[parts:2 * parts], refs[2 * parts:]
    w_refs, up_ref, refs = refs[:2], refs[2], refs[3:]
    terms = len(term_counts)
    term_refs, refs = refs[:2 * terms], refs[2 * terms:]
    if finish:
        far_refs, refs = refs[:finished], refs[finished:]
        pick_refs, scale_ref, refs = refs[:finished], refs[finished], refs[finished + 1:]
    x, low, w, maps, term, acc, out, far, pick, scale, in_sem, w_sem, out_sem = refs[-13:]
    outs = refs[-13 - (2 if finish else max(1, 2 * len(splits))):-13]
    done = sum(counts[:finished])
    rows, depth = x.shape
    steps = depth // STEP_DEPTH
    left = pl.multiple_of((ids[1] ^ flip) * narrow, 128)
    tiles = [(at, min(TILE, narrow - at)) for at in range(0, narrow, TILE)]
    loads = []

    def load(source, target):
        copy = pltpu.make_async_copy(source, target, in_sem.at[len(loads)])
        copy.start()
        loads.append(copy)

    def piece(side, step):
        return pltpu.make_async_copy(
            w_refs[side].at[pl.ds(step * STEP_DEPTH, STEP_DEPTH), pl.ds(left, narrow)],
            w.at[side, step], w_sem.at[side, step],
        )

    def start_step(step):
        for side in range(2):
            piece(side, step).start()

    def stores(at, size, place):
        columns = pl.ds(at, size)
        if finish:
            pairs = [(out.at[0, :, columns], outs[0].at[:, columns])]
            pairs += [(acc.at[side, pl.ds(done, rows - done), columns], outs[1].at[side, :, columns]) for side in range(2)]
        elif not splits:
            pairs = [(out.at[side, :, columns], outs[0].at[side, :, columns]) for side in range(2)]
        else:
            pairs = []
            for side in range(2):
                row = 0
                for part, count in enumerate(splits):
                    target = outs[side * len(splits) + part].at[:, columns]
                    pairs.append((out.at[side, pl.ds(row, count), columns], target))
                    row += count
        return [
            pltpu.make_async_copy(source, target, out_sem.at[place, i]) for i, (source, target) in enumerate(pairs)
        ]

    row = 0
    for part, count in enumerate(counts):
        load(x_refs[part], x.at[pl.ds(row, count)])
        load(low_refs[part], low.at[:, pl.ds(row, count)])
        row += count
    for side in range(2):
        load(up_ref.at[:, side, :, pl.ds(left, narrow)], maps.at[side, 0])
    first_loads = len(loads)
    start_step(0)
    start_step(1)
    if terms:
        for side in range(2):
            row = 0
            for part, count in enumerate(term_counts):
                load(term_refs[2 * part + side], term.at[side, pl.ds(row, count)])
                row += count
    if finish:
        row = 0
        for part, count in enumerate(counts[:finished]):
            here = pl.ds(row, count)
            load(far_refs[part], far.at[:, here])
            load(pick_refs[part], pick.at[here])
            row += count
        load(scale_ref, scale)

    for copy in loads[:first_loads]:
        copy.wait()
    for side in range(2):
        maps[side, 1] = maps[side, 0]

    @pl.loop(0, 2)
    def _(side):
        acc[side] = jnp.dot(low[side], maps[side].reshape(256, narrow), preferred_element_type=jnp.float32)

    @pl.loop(0, steps - 1)
    def _(step):
        for side in range(2):
            piece(side, step).wait()

            @pl.when(step + 2 < steps)
            def _():
                piece(side, step + 2).start()

        depths = pl.ds(pl.multiple_of(step * STEP_DEPTH, STEP_DEPTH), STEP_DEPTH)

        for side in range(2):
            acc[side] += jnp.dot(x[:, depths], w[side, step], preferred_element_type=jnp.float32)

    for copy in loads[first_loads:]:
        copy.wait()
    for side in range(2):
        piece(side, steps - 1).wait()

    def last_step(at, size, place):
        columns = pl.ds(at, size)
        values = []
        for side in range(2):
            value = acc[side, :, columns] + jnp.dot(
                x[:, depth - STEP_DEPTH:], w[side, steps - 1, :, columns], preferred_element_type=jnp.float32
            )
            if terms:
                value += term[side, :, columns].astype(jnp.float32)
            if finish:
                acc[side, done:, columns] = value[done:]
                value = value[:done] + far[side, :, columns].astype(jnp.float32)
                value *= jnp.dot(pick[...], scale[side, :, columns], preferred_element_type=jnp.float32)
                values.append(value)
            else:
                out[side, :, columns] = value.astype(out.dtype)
        if finish:
            out[0, :, columns] = activate(*values)
        for copy in stores(at, size, place):
            copy.start()

    whole = narrow // TILE

    @pl.loop(0, whole)
    def _(place):
        last_step(pl.multiple_of(place * TILE, TILE), TILE, place)

    for place in range(whole, len(tiles)):
        last_step(*tiles[place], place)
    for place, (at, size) in enumerate(tiles):
        for copy in stores(at, size, place):
            copy.wait()


def dot_pair(chunks, weights, adapter_out, flip, narrow, ids, splits=(), terms=(), finish=None, after=()):
    xs, lows, picks = zip(*chunks)
    counts = tuple(x.shape[0] for x in xs)
    rows, depth = sum(counts), xs[0].shape[1]
    tenants = adapter_out.shape[0]
    term_counts = tuple(gate.shape[0] for gate, _ in terms)
    operands = [ids, *xs, *lows, *weights, adapter_out, *[array for pair in terms for array in pair]]
    finished = 0
    if finish is not None:
        finished = len(finish[0])
        done = sum(counts[:finished])
        operands += [*finish[0], *picks[:finished], finish[1]]
        out_shape = [
            jax.ShapeDtypeStruct((done, narrow), jnp.bfloat16),
            jax.ShapeDtypeStruct((2, rows - done, narrow), jnp.float32),
        ]
    elif splits:
        out_shape = [jax.ShapeDtypeStruct((count, narrow), jnp.bfloat16) for _ in range(2) for count in splits]
    else:
        out_shape = [jax.ShapeDtypeStruct((2, rows, narrow), jnp.bfloat16)]
    operands += list(after)
    few = (8, 128)
    steps = depth // STEP_DEPTH
    return pl.pallas_call(
        functools.partial(
            dot_kernel, flip, counts, splits, term_counts, finished, narrow
        ),
        out_shape=out_shape,
        grid_spec=pltpu.PrefetchScalarGridSpec(
            num_scalar_prefetch=1,
            grid=(1,),
            in_specs=[ANY] * (len(operands) - 1),
            out_specs=[ANY] * len(out_shape),
            scratch_shapes=[
                pltpu.VMEM((rows, depth), jnp.bfloat16),
                pltpu.VMEM((2, rows, 256), jnp.bfloat16),
                pltpu.VMEM((2, steps, STEP_DEPTH, narrow), jnp.bfloat16),
                pltpu.VMEM((2, 2, tenants, RANK, narrow), jnp.bfloat16),
                pltpu.VMEM((2, rows, narrow) if terms else few, jnp.bfloat16),
                pltpu.VMEM((2, rows, narrow), jnp.float32),
                pltpu.VMEM((1, done, narrow) if finished else (2, rows, narrow), jnp.bfloat16),
                pltpu.VMEM((2, done, narrow) if finished else few, jnp.bfloat16),
                pltpu.VMEM((done, 128) if finished else few, jnp.bfloat16),
                pltpu.VMEM((2, 128, narrow) if finished else few, jnp.bfloat16),
                pltpu.SemaphoreType.DMA((4 * len(xs) + 8,)),
                pltpu.SemaphoreType.DMA((2, steps)),
                pltpu.SemaphoreType.DMA((-(-narrow // TILE), 4)),
            ],
        ),
        compiler_params=pltpu.CompilerParams(vmem_limit_bytes=VMEM_LIMIT),
        cost_estimate=COST,
        name="finish_dots" if finished else "dot_pair",
    )(*operands)


def last_kernel(
    mx_count, first, ids, rows, tenants, sums_ref, far_ref, pick, scale, earlier_ref, out_ref, table, sums, far, held,
    tile_sem, held_sem,
):
    turn = pl.program_id(0)
    tiles = far.shape[1] // BLOCK_ROWS

    def tile_copies(tile):
        here = pl.ds(pl.multiple_of(tile * BLOCK_ROWS, BLOCK_ROWS), BLOCK_ROWS)
        return [
            pltpu.make_async_copy(source.at[:, here], target.at[:, here], tile_sem.at[tile, i])
            for i, (source, target) in enumerate([(sums_ref, sums), (far_ref, far)])
        ]

    @pl.when(turn == 0)
    def _():
        for tile in range(tiles):
            for copy in tile_copies(tile):
                copy.start()
        held_copy = pltpu.make_async_copy(earlier_ref, held.at[pl.ds(0, first)], held_sem)
        held_copy.start()
        fill_table(table, ids, rows, tenants, mx_count)
        held[LIVE_ROWS:, :] = jnp.zeros((BLOCK_ROWS, held.shape[1]), held.dtype)
        columns = held.shape[1]

        @pl.loop(0, tiles)
        def _(tile):
            for copy in tile_copies(tile):
                copy.wait()
            here = pl.ds(pl.multiple_of(tile * BLOCK_ROWS, BLOCK_ROWS), BLOCK_ROWS)
            there = pl.ds(pl.multiple_of(first + tile * BLOCK_ROWS, BLOCK_ROWS), BLOCK_ROWS)
            for left in range(0, columns, TILE):
                right = min(left + TILE, columns)
                pre = [
                    (sums[side, here, left:right] + far[side, here, left:right].astype(jnp.float32))
                    * jnp.dot(pick[here, :], scale[side, :, left:right], preferred_element_type=jnp.float32)
                    for side in range(2)
                ]
                held[there, left:right] = activate(*pre)

        held_copy.wait()

    for part in range(2):
        block = 2 * turn + part

        def find(slot, start, block=block):
            return jnp.where(table[3, slot] == block, table[0, slot], start)

        start = lax.fori_loop(0, len(SLOTS), find, jnp.int32(0))
        count = rows[block]
        base = pl.multiple_of(jnp.minimum(start // BLOCK_ROWS * BLOCK_ROWS, LIVE_ROWS - BLOCK_ROWS), BLOCK_ROWS)
        shape = (BLOCK_ROWS, 2 * BLOCK_ROWS)
        position = lax.broadcasted_iota(jnp.int32, shape, 0)
        column = lax.broadcasted_iota(jnp.int32, shape, 1) + base
        chosen = (position < count) & (column == position + start)
        out_ref[part * BLOCK_ROWS:(part + 1) * BLOCK_ROWS, :] = jnp.dot(
            chosen.astype(jnp.bfloat16), held[pl.ds(base, 2 * BLOCK_ROWS), :], preferred_element_type=jnp.float32
        ).astype(jnp.bfloat16)


def last_rows(mx_count, first, scalars, sums, far, pick, scale, earlier, blocks):
    narrow = far.shape[2]
    operands = (sums, far, pick, scale, earlier)
    return pl.pallas_call(
        functools.partial(last_kernel, mx_count, first),
        out_shape=jax.ShapeDtypeStruct((blocks * BLOCK_ROWS, narrow), jnp.bfloat16),
        grid_spec=pltpu.PrefetchScalarGridSpec(
            num_scalar_prefetch=3,
            grid=(blocks // 2,),
            in_specs=[
                ANY, ANY,
                pl.BlockSpec(pick.shape, lambda i, *_: (0, 0)),
                pl.BlockSpec(scale.shape, lambda i, *_: (0, 0, 0)),
                ANY,
            ],
            out_specs=pl.BlockSpec((2 * BLOCK_ROWS, narrow), lambda i, *_: (i, 0)),
            scratch_shapes=[
                pltpu.SMEM((4, len(SLOTS)), jnp.int32),
                pltpu.VMEM(sums.shape, sums.dtype),
                pltpu.VMEM(far.shape, far.dtype),
                pltpu.VMEM((LIVE_ROWS + BLOCK_ROWS, narrow), jnp.bfloat16),
                pltpu.SemaphoreType.DMA((far.shape[1] // BLOCK_ROWS, 2)),
                pltpu.SemaphoreType.DMA,
            ],
        ),
        compiler_params=pltpu.CompilerParams(vmem_limit_bytes=VMEM_LIMIT),
        cost_estimate=COST,
        name="last_rows",
    )(*scalars, *operands)


def quarter(array, index, narrow):
    return lax.dynamic_slice_in_dim(array, index * narrow, narrow, array.ndim - 1)


def pipelined(
    tokens, w_gate, w_up, adapter_in, adapter_out, magnitude, partial_norms, block_tenant, block_rows
):
    mx_count = lax.axis_size("mx")
    my_count = lax.axis_size("my")
    narrow = w_gate.shape[1] // my_count
    mine = lax.axis_index("my")
    ids = jnp.stack([lax.axis_index("mx"), mine]).astype(jnp.int32)
    scalars = (ids, block_rows, block_tenant)
    near = [(i, i ^ 1) for i in range(my_count)]
    across = [(i, i ^ 2) for i in range(my_count)]

    def hop(block, distance, least=0):
        if distance > 0:
            pairs = [(i, i + distance) for i in range(least, mx_count - distance)]
        else:
            pairs = [(i, i + distance) for i in range(-distance, mx_count - least)]
        return lax.ppermute(block, "mx", pairs)

    blocks = [tokens, hop(tokens, 1), hop(tokens, -1)]

    norms = partial_norms[0]
    pair = jnp.stack([quarter(norms, mine, narrow), quarter(norms, mine ^ 2, narrow)])
    other = jnp.stack([quarter(norms, mine ^ 1, narrow), quarter(norms, mine ^ 3, narrow)])
    pair = pair + lax.ppermute(other, "my", near)
    norm_total = pair[0] + lax.ppermute(pair[1], "my", across)
    scale = quarter(magnitude, mine, narrow) * lax.rsqrt(norm_total)
    scale = jnp.transpose(scale, (1, 0, 2))
    high = lax.reduce_precision(scale, 8, 7)
    middle = lax.reduce_precision(scale - high, 8, 7)
    rest = scale - high - middle
    scale = jnp.concatenate(
        [high, middle, rest, jnp.zeros((2, 128 - 3 * scale.shape[1], narrow), jnp.float32)], axis=1
    ).astype(jnp.bfloat16)

    down = jnp.transpose(adapter_in, (0, 2, 1)).reshape(-1, adapter_in.shape[1])

    dots = functools.partial(
        dot_pair, weights=(w_gate, w_up), adapter_out=adapter_out, narrow=narrow, ids=ids
    )

    def swap(parts, pairs):
        return [lax.ppermute(part, "my", pairs) for part in parts]

    def far_out(chunk, after=()):
        return dots([chunk], flip=3, splits=(chunk[0].shape[0],), after=after)

    def far_in(chunk, got, after=()):
        part, = dots([chunk], flip=2, terms=(got,), after=after)
        return part, lax.ppermute(part, "my", across)

    *chunk0, up, down_line = pack_rows(
        mx_count, CHUNKS[0], scalars, blocks, down, after=(scale,), passed=(1, 2)
    )
    blocks = [tokens, up, down_line, hop(up, 1, 1), hop(down_line, -1, 1)]
    mark, far0 = far_in(chunk0, swap(far_out(chunk0), near))

    third_hop = [hop(blocks[3], 1, 2), hop(blocks[4], -1, 2)]
    *chunk1, = pack_rows(mx_count, CHUNKS[1], scalars, blocks, down, after=(mark,), cost=LONG)
    blocks += third_hop
    mark, far1 = far_in(chunk1, swap(far_out(chunk1), near))

    first, last = CHUNKS[2][:2]
    *chunk2, = pack_rows(mx_count, CHUNKS[2], scalars, blocks, down, after=(mark,))
    parts = far_out(chunk2, (far0,))
    got = swap(parts, near)
    parts = dots([chunk0, chunk1], flip=1, splits=(first,), after=(parts[0],))
    early = swap(parts, near)
    mark, far2 = far_in(chunk2, got, after=(parts[0],))

    parts = dots([chunk2], flip=1, splits=(last,), after=(mark,))
    late = swap(parts, near)
    hidden, sums = dots([chunk0, chunk1, chunk2], flip=0, terms=(early, late), finish=((far0, far1), scale))
    return last_rows(mx_count, first, scalars, sums, far2, chunk2[2], scale, hidden, block_rows.shape[0])


def adapter_low(rows_piece, aligned_row_total, adapter_in, block_tenant):
    row_count = rows_piece.shape[0]
    seg_rows = math.gcd(math.gcd(row_count, BLOCK_ROWS), aligned_row_total)
    seg_count = row_count // seg_rows
    seg_block = jnp.arange(seg_count, dtype=jnp.int32) * seg_rows // BLOCK_ROWS
    tenant_tables = adapter_in[block_tenant[seg_block]]
    grouped = rows_piece.reshape(seg_count, seg_rows, rows_piece.shape[1])
    low_terms = jnp.einsum(
        "skd,sdr->skr", grouped, tenant_tables, preferred_element_type=jnp.float32
    )
    return low_terms.reshape(row_count, tenant_tables.shape[2])


def finish_plain(
    summed, reduced_rank_factor, norm_total, mag_cols, adapter_cols, first_row, block_tenant, block_rows
):
    row_count = summed.shape[0]
    col_count = summed.shape[2]
    seg_rows = math.gcd(row_count, BLOCK_ROWS)
    seg_count = row_count // seg_rows
    seg_block = (first_row + jnp.arange(seg_count, dtype=jnp.int32) * seg_rows) // BLOCK_ROWS
    tenants = block_tenant[seg_block]
    col_scale = mag_cols * lax.rsqrt(norm_total)
    seg_scale = col_scale[tenants]
    seg_tables = adapter_cols[tenants]
    low_pair = reduced_rank_factor.reshape(seg_count, seg_rows, 2, RANK)
    adapted = jnp.einsum(
        "skpr,sprc->skpc", low_pair, seg_tables, preferred_element_type=jnp.float32
    )
    pre_act = (summed.reshape(seg_count, seg_rows, 2, col_count) + adapted) * seg_scale[:, None]
    hidden = jax.nn.silu(pre_act[:, :, 0]) * pre_act[:, :, 1]
    offsets = (first_row + jnp.arange(row_count, dtype=jnp.int32)).reshape(
        seg_count, seg_rows
    ) % BLOCK_ROWS
    live_mask = offsets < block_rows[seg_block][:, None]
    hidden = jnp.where(live_mask[:, :, None], hidden, jnp.zeros_like(hidden))
    return hidden.reshape(row_count, col_count).astype(jnp.bfloat16)


def plain(
    tokens, w_gate, w_up, adapter_in, adapter_out, magnitude, partial_norms, block_tenant, block_rows
):
    local_rows = tokens.shape[0]
    col_local = w_gate.shape[1]
    my_count = lax.axis_size("my")
    device_position = lax.axis_index("my")
    rows_piece = lax.all_gather(tokens, "mx", axis=0, tiled=True)
    gate_part = jnp.dot(rows_piece, w_gate, preferred_element_type=jnp.float32)
    up_part = jnp.dot(rows_piece, w_up, preferred_element_type=jnp.float32)
    main_part = jnp.stack((gate_part, up_part), axis=1)
    low_terms = adapter_low(rows_piece, local_rows, adapter_in, block_tenant)
    reduced_rank_factor = lax.psum(low_terms, "my").astype(jnp.bfloat16)
    summed = lax.psum_scatter(main_part, "my", scatter_dimension=2, tiled=True)
    norm_total = lax.psum_scatter(partial_norms[0], "my", scatter_dimension=2, tiled=True)
    narrow = col_local // my_count
    mag_cols = lax.dynamic_slice_in_dim(magnitude, device_position * narrow, narrow, 2)
    adapter_cols = lax.dynamic_slice_in_dim(adapter_out, device_position * narrow, narrow, 3)
    return finish_plain(
        summed, reduced_rank_factor, norm_total, mag_cols, adapter_cols, 0, block_tenant, block_rows
    )


def on_device(tokens, w_gate, w_up, adapter_in, *rest):
    my_count = lax.axis_size("my")
    fits = (
        my_count == 4
        and lax.axis_size("mx") == 4
        and tokens.shape[0] == 2 * BLOCK_ROWS
        and adapter_in.shape[0] == 8
        and tokens.shape[1] % STEP_DEPTH == 0
        and tokens.shape[1] >= 2 * STEP_DEPTH
        and w_gate.shape[1] % (my_count * 128) == 0
    )
    return (pipelined if fits else plain)(tokens, w_gate, w_up, adapter_in, *rest)


def solution(mesh):
    return jax.shard_map(
        on_device,
        mesh=mesh,
        in_specs=(
            P(("groups", "mx"), "my"),
            P("my", "mx"),
            P("my", "mx"),
            P(None, "my", None),
            P(None, None, None, "mx"),
            P(None, None, "mx"),
            P("my", None, None, "mx"),
            P("groups"),
            P("groups"),
        ),
        out_specs=P("groups", ("mx", "my")),
        check_vma=False,
    )
```
